32 devices in a mesh: wide: 8 (over z, y), narrow: 4 (over x, core).
Axes of the slice: x: 2, y: 2, z: 4, core: 2. Of those that a mesh axis runs over, the one named last changes fastest.
Arguments:
- tables_in: bfloat16 [8192, 768], P(('wide', 'narrow')), may hold values from -6 to 6
- cotangent: bfloat16 [8192, 768], P(('wide', 'narrow')), may hold values from -6 to 6
- cell_ids: int32 [32, 256], P(('wide', 'narrow')), may hold values from 0 to 241, as said below
- lengths: int32 [32], P(('wide', 'narrow')), may hold values from 64 to 256
- qkv_weight: bfloat16 [2, 768, 2304], P(None, 'narrow'), may hold values from -0.21875 to 0.21875
- q_bias: bfloat16 [2, 768], P(None, 'narrow'), may hold values from -3 to 3
- v_bias: bfloat16 [2, 768], P(None, 'narrow'), may hold values from -3 to 3
- o_weight: bfloat16 [2, 768, 768], P(None, 'narrow'), may hold values from -0.875 to 0.875
- o_bias: bfloat16 [2, 768], P(None, 'narrow'), may hold values from -2 to 2
- norm1_gain: bfloat16 [2, 768], P(None, 'narrow'), may hold values from 0.5 to 1.5
- norm1_bias: bfloat16 [2, 768], P(None, 'narrow'), may hold values from -2 to 2
- in_weight: bfloat16 [2, 768, 3072], P(None, 'narrow'), may hold values from -0.21875 to 0.21875
- in_bias: bfloat16 [2, 3072], P(None, 'narrow'), may hold values from -3 to 3
- out_weight: bfloat16 [2, 3072, 768], P(None, 'narrow'), may hold values from -0.109375 to 0.109375
- out_bias: bfloat16 [2, 768], P(None, 'narrow'), may hold values from -2 to 2
- norm2_gain: bfloat16 [2, 768], P(None, 'narrow'), may hold values from 0.5 to 1.5
- norm2_bias: bfloat16 [2, 768], P(None, 'narrow'), may hold values from -2 to 2
Outputs:
- mixed_out: bfloat16 [8192, 768], P(('wide', 'narrow'))
- input_grad: bfloat16 [8192, 768], P(('wide', 'narrow'))
- qkv_grad: float32 [2, 768, 2304], P(None, 'narrow')
- q_bias_grad: float32 [2, 768], P(None, 'narrow')
- v_bias_grad: float32 [2, 768], P(None, 'narrow')
- o_weight_grad: float32 [2, 768, 768], P(None, 'narrow')
- o_bias_grad: float32 [2, 768], P(None, 'narrow')
- norm1_gain_grad: float32 [2, 768], P(None, 'narrow')
- norm1_bias_grad: float32 [2, 768], P(None, 'narrow')
- in_weight_grad: float32 [2, 768, 3072], P(None, 'narrow')
- in_bias_grad: float32 [2, 3072], P(None, 'narrow')
- out_weight_grad: float32 [2, 3072, 768], P(None, 'narrow')
- out_bias_grad: float32 [2, 768], P(None, 'narrow')
- norm2_gain_grad: float32 [2, 768], P(None, 'narrow')
- norm2_bias_grad: float32 [2, 768], P(None, 'narrow')
The draws below stay inside these ranges and needn't reach their ends.
Inputs may be any that keep to these rules, and one draw needn't show every extreme that they name: `cell_ids`: along a table the ids never fall; id 0 marks the question tokens at the table's head, never fewer than 16 of them; every other id marks one cell of that table.
All inputs are finite; a program needn't handle non-finite values.
Results may differ from the reference program's by a relative error of at most 0.023.
Values may be sent and summed in bfloat16 or wider, within the bound.
No kernel may reach another device: no remote copies, remote signals or barrier semaphores. Data moves between devices by JAX's collectives and lax.ppermute only.
A program may use at most 320 MiB of HBM per device.

```python
import math
import jax
import jax.numpy as jnp
from jax import lax

D = 768
HEADS = 12
FF = 3072
LEN = 256
LAYERS = 2
TABLES = 32
TOKENS = 8192


def draw_cell_ids(key, part):
    key = jax.random.fold_in(key, 11)
    head_key, size_key = jax.random.split(key)
    question = jax.random.randint(head_key, (TABLES, 1), LEN // 16, LEN // 4 + 1, dtype=jnp.int32)
    exponent = jax.random.randint(size_key, (TABLES, LEN), 0, 7, dtype=jnp.int32)
    cell_sizes = jnp.left_shift(jnp.ones((TABLES, LEN), jnp.int32), exponent)
    bounds = jnp.cumsum(cell_sizes, axis=1).astype(jnp.int32)
    offset = jnp.arange(LEN, dtype=jnp.int32)[None, :] - question
    counted = jax.vmap(lambda cell_edges, token_spots: jnp.searchsorted(cell_edges, token_spots, side='right'))(bounds, offset)
    drawn_ids = jnp.where(offset < 0, 0, 1 + counted.astype(jnp.int32)).astype(jnp.int32)
    last_spot = jnp.arange(LEN, dtype=jnp.int32)[None, :] == LEN - 1
    return jnp.where(last_spot, LEN - LEN // 16 + 1, drawn_ids).astype(jnp.int32)


def draw_lengths(key, part):
    key = jax.random.fold_in(key, 23)
    base_key, long_key, short_key = jax.random.split(key, 3)
    drawn_len = jax.random.randint(base_key, (TABLES,), LEN // 4, LEN + 1, dtype=jnp.int32)
    longest = jax.random.randint(long_key, (), 0, TABLES, dtype=jnp.int32)
    shortest = (longest + jax.random.randint(short_key, (), 1, TABLES, dtype=jnp.int32)) % TABLES
    table_index = jnp.arange(TABLES, dtype=jnp.int32)
    drawn_len = jnp.where(table_index == longest, LEN, drawn_len)
    return jnp.where(table_index == shortest, LEN // 4, drawn_len).astype(jnp.int32)


def levels(stream_key, dims, cuts, low, high):
    def one(dim, parts):
        draws = jax.random.uniform(jax.random.fold_in(jax.random.fold_in(stream_key, 6), dim), (parts,), jnp.float32, low / len(cuts), high / len(cuts))
        return jnp.repeat(jnp.exp(draws), dims[dim] // parts).reshape((-1,) + (1,) * (len(dims) - dim - 1))

    level = one(*cuts[0])
    for cut in cuts[1:]:
        level = level * one(*cut)
    return level


def scatter_about(key, shape, deviation, reach, shards=(), kind=jnp.bfloat16):
    level = levels(key, shape, shards, -0.22, 0.18) if shards else 1.0
    drawn = jax.random.normal(key, shape, jnp.float32) * deviation * level
    return jnp.minimum(jnp.maximum(drawn, -reach), reach).astype(kind)


def setup_inputs(seed: int = 0) -> dict:
    arg_keys = jax.random.split(jax.random.key(seed), 18)
    return {
        "tables_in": scatter_about(arg_keys[0], (TOKENS, D), 1.0, 6.0, ((0, 32),)),
        "cotangent": scatter_about(arg_keys[1], (TOKENS, D), 1.0, 6.0, ((0, 32),)),
        "cell_ids": draw_cell_ids(jax.random.fold_in(arg_keys[17], 71), 0),
        "lengths": draw_lengths(jax.random.fold_in(arg_keys[17], 71), 0),
        "qkv_weight": scatter_about(arg_keys[4], (LAYERS, D, 3 * D), D ** -0.5, 0.21875, ((1, 4),)),
        "q_bias": scatter_about(arg_keys[5], (LAYERS, D), 0.5, 3.0, ((1, 4),)),
        "v_bias": scatter_about(arg_keys[6], (LAYERS, D), 0.5, 3.0, ((1, 4),)),
        "o_weight": scatter_about(arg_keys[7], (LAYERS, D, D), (D // 16) ** -0.5, 0.875, ((1, 4),)),
        "o_bias": scatter_about(arg_keys[8], (LAYERS, D), 0.3, 2.0, ((1, 4),)),
        "norm1_gain": jnp.clip(1.0 + 0.1 * jax.random.normal(arg_keys[9], (LAYERS, D), jnp.float32), 0.5, 1.5).astype(jnp.bfloat16),
        "norm1_bias": scatter_about(arg_keys[10], (LAYERS, D), 0.3, 2.0, ((1, 4),)),
        "in_weight": scatter_about(arg_keys[11], (LAYERS, D, FF), D ** -0.5, 0.21875, ((1, 4),)),
        "in_bias": scatter_about(arg_keys[12], (LAYERS, FF), 0.5, 3.0, ((1, 4),)),
        "out_weight": scatter_about(arg_keys[13], (LAYERS, FF, D), FF ** -0.5, 0.109375, ((1, 4),)),
        "out_bias": scatter_about(arg_keys[14], (LAYERS, D), 0.3, 2.0, ((1, 4),)),
        "norm2_gain": jnp.clip(1.0 + 0.1 * jax.random.normal(arg_keys[15], (LAYERS, D), jnp.float32), 0.5, 1.5).astype(jnp.bfloat16),
        "norm2_bias": scatter_about(arg_keys[16], (LAYERS, D), 0.3, 2.0, ((1, 4),)),
    }


@jax.custom_vjp
def low(v):
    return lax.optimization_barrier(v.astype(jnp.bfloat16)).astype(jnp.float32)

@jax.custom_vjp
def low_back(v):
    return v

def low_keep(v):
    return (low(v), None)

def low_pass(kept, grad):
    return (grad,)

def back_keep(v):
    return (v, None)

def back_low(kept, grad):
    return (low(grad),)
low.defvjp(low_keep, low_pass)
low_back.defvjp(back_keep, back_low)
norm_eps = 1e-12
masked_score = -1000000000.0

def matmul(lhs_mat, rhs_mat):
    return jnp.dot(lhs_mat, rhs_mat, precision=lax.Precision.HIGHEST)

def layer_norm(residual, gain_vec, shift_bias):
    center = residual - lax.optimization_barrier(jnp.mean(residual, axis=-1, keepdims=True))
    spread = lax.optimization_barrier(jnp.mean(center * center, axis=-1, keepdims=True))
    return center * lax.rsqrt(spread + norm_eps) * gain_vec + shift_bias

def attend_table(query_rows, key_rows, value_rows, cell_row, length):
    head_size = D // HEADS
    score_scale = 1.0 / math.sqrt(head_size)
    query_h = query_rows.reshape(LEN, HEADS, head_size)
    key_h = key_rows.reshape(LEN, HEADS, head_size)
    value_h = value_rows.reshape(LEN, HEADS, head_size)
    raw_scores = jnp.einsum('qhd,khd->hqk', query_h, key_h, precision=lax.Precision.HIGHEST) * score_scale
    position = jnp.arange(LEN)
    same_cell = (cell_row[:, None] == cell_row[None, :]) | (cell_row[None, :] == 0) | (cell_row[:, None] == 0)
    allowed = same_cell & (position[None, :] < length)
    scores = low_back(jnp.where(allowed[None], raw_scores, masked_score))
    row_top = lax.optimization_barrier(jnp.max(scores, axis=-1, keepdims=True))
    shifted = jnp.exp(scores - row_top)
    attn_probs = low(shifted / lax.optimization_barrier(jnp.sum(shifted, axis=-1, keepdims=True)))
    context = jnp.einsum('hqk,khd->qhd', attn_probs, value_h, precision=lax.Precision.HIGHEST)
    return context.reshape(LEN, D)

def encoder_layer(inputs, params, cell_rows, length_rows):
    w_qkv, b_query, b_value, w_attn, b_attn, gain_one, bias_one, w_in, b_in, w_out, b_out, gain_two, bias_two = params
    tables = cell_rows.shape[0]
    projected = matmul(inputs, w_qkv)
    query_rows = low_back(low(projected[:, :D] + b_query))
    key_rows = low_back(low(projected[:, D:2 * D]))
    value_rows = low_back(low(projected[:, 2 * D:] + b_value))
    checked_attend = jax.checkpoint(attend_table)
    context = lax.map(lambda pieces: checked_attend(pieces[0], pieces[1], pieces[2], pieces[3], pieces[4]), (query_rows.reshape(tables, LEN, D), key_rows.reshape(tables, LEN, D), value_rows.reshape(tables, LEN, D), cell_rows, length_rows))
    context = low_back(low(context.reshape(tables * LEN, D)))
    attention = low_back(matmul(context, w_attn) + b_attn)
    normed = layer_norm(inputs + attention, gain_one, bias_one)
    pre_act = low_back(matmul(low(normed), w_in) + b_in)
    hidden = low(jax.nn.gelu(pre_act, approximate=False))
    ffn_out = low_back(matmul(hidden, w_out) + b_out)
    return layer_norm(normed + ffn_out, gain_two, bias_two)

def forward(rows_in, weights, cell_rows, length_rows):
    first_layer = tuple((weight[0] for weight in weights))
    second_layer = tuple((weight[1] for weight in weights))
    middle = low_back(low(encoder_layer(rows_in, first_layer, cell_rows, length_rows)))
    return encoder_layer(middle, second_layer, cell_rows, length_rows)

def reference(tables_in, cotangent, cell_ids, lengths, qkv_weight, q_bias, v_bias, o_weight, o_bias, norm1_gain, norm1_bias, in_weight, in_bias, out_weight, out_bias, norm2_gain, norm2_bias):
    weights = tuple((weight.astype(jnp.float32) for weight in (qkv_weight, q_bias, v_bias, o_weight, o_bias, norm1_gain, norm1_bias, in_weight, in_bias, out_weight, out_bias, norm2_gain, norm2_bias)))
    group_size = 8
    blocks = TABLES // group_size
    rows_in = tables_in.astype(jnp.float32).reshape(blocks, group_size * LEN, D)
    rows_grad = cotangent.astype(jnp.float32).reshape(blocks, group_size * LEN, D)
    cell_blocks = cell_ids.reshape(blocks, group_size, LEN)
    length_blocks = lengths.reshape(blocks, group_size)

    def one_block(running_sums, pieces):
        block_in, block_grad, block_cells, block_lengths = pieces
        outputs, pullback = jax.vjp(lambda values_in, params: forward(values_in, params, block_cells, block_lengths), block_in, weights)
        grad_in, grad_params = pullback(block_grad)
        running_sums = tuple((running + gradient for running, gradient in zip(running_sums, grad_params)))
        return (running_sums, (outputs.astype(jnp.bfloat16), grad_in.astype(jnp.bfloat16)))
    initial = tuple((jnp.zeros(weight.shape, jnp.float32) for weight in weights))
    totals, (outputs_all, grads_all) = lax.scan(one_block, initial, (rows_in, rows_grad, cell_blocks, length_blocks))
    return (outputs_all.reshape(TOKENS, D), grads_all.reshape(TOKENS, D), totals[0], totals[1], totals[2], totals[3], totals[4], totals[5], totals[6], totals[7], totals[8], totals[9], totals[10], totals[11], totals[12])
```

```python
import functools
import math

import jax
import jax.numpy as jnp
from jax import lax
from jax.experimental import pallas as pl
from jax.experimental.pallas import tpu as pltpu
from jax.sharding import PartitionSpec as P

HEADS = 12
norm_eps = 1e-12
masked_score = -1000000000.0
low = jnp.bfloat16
f32 = jnp.float32
VMEM_BYTES = 56 * 1024 * 1024
HALVINGS = 3


def swap(value, axis, bit):
    count = lax.axis_size(axis)
    return lax.ppermute(value, axis, [(i, i ^ bit) for i in range(count)])


def dot(a, b):
    return jnp.dot(a, b, preferred_element_type=f32)


def dot_nt(a, b):
    return lax.dot_general(a, b, (((1,), (1,)), ((), ())), preferred_element_type=f32)


def dot_tn(a, b):
    return lax.dot_general(a, b, (((0,), (0,)), ((), ())), preferred_element_type=f32)


def normalize(residual):
    center = residual - jnp.mean(residual, axis=-1, keepdims=True)
    inverse = lax.rsqrt(jnp.mean(center * center, axis=-1, keepdims=True) + norm_eps)
    return center * inverse, inverse


def normalize_back(grad_unit, unit, inverse):
    centered = grad_unit - jnp.mean(grad_unit, axis=-1, keepdims=True)
    return inverse * (centered - unit * jnp.mean(grad_unit * unit, axis=-1, keepdims=True))


def weight_copies(ids, layer, pieces, target, columns, sems, base):
    own, core, near_x, far_x, near_d, far_d = pieces
    rows = own.shape[1]
    half = rows // 2
    n, y = ids[0], ids[4]
    copies = []

    def add(source, start, count):
        where = target.at[pl.ds(pl.multiple_of(start, half), count), :]
        copies.append(pltpu.make_async_copy(source, where, sems.at[base + len(copies)]))

    def part(ref):
        return ref.at[:, pl.ds(columns, target.shape[1])]

    add(own.at[layer], n * rows, rows)
    add(core.at[layer], ids[1] * rows, rows)
    add(part(near_x), ids[2] * rows + y * half, half)
    add(part(far_x), ids[2] * rows + (1 - y) * half, half)
    add(part(near_d), ids[3] * rows + y * half, half)
    add(part(far_d), ids[3] * rows + (1 - y) * half, half)
    return copies


def begin(copies):
    for copy in copies:
        copy.start()


def finish(copies):
    for copy in copies:
        copy.wait()


def attn_copies(layer, ids, refs, w_qkv, w_o, sems):
    qkv_own, qkv_core, o_own, o_core, near_x, far_x, near_d, far_d = refs
    halves = (near_x, far_x, near_d, far_d)
    qkv = weight_copies(ids, layer, (qkv_own, qkv_core) + halves, w_qkv, 0, sems, 0)
    o = weight_copies(ids, layer, (o_own, o_core) + halves, w_o, w_qkv.shape[1], sems, 6)
    return qkv, o


def ffn_copies(layer, ids, refs, w_in, w_out, sems):
    in_copies = weight_copies(ids, layer, refs[:6], w_in, 0, sems, 0)
    out_copies = weight_copies(ids, layer, refs[6:], w_out, 0, sems, 6)
    return in_copies, out_copies


def attn_fwd_kernel(layer, ids, length, x, cell_row, cell_col, qkv_bias, small, *rest):
    weights, rest = rest[:8], rest[8:]
    qkv_rows, probs, context, unit_out, inverse_out, w_qkv, w_o, mask, sems = rest
    tokens, width = x.shape
    qkv_copies, o_copies = attn_copies(layer, ids, weights, w_qkv, w_o, sems)
    begin(qkv_copies)
    begin(o_copies)
    position = lax.broadcasted_iota(jnp.int32, (1, tokens), 1)
    key_cell, query_cell = cell_row[...], cell_col[...]
    allowed = (query_cell == key_cell) | (key_cell == 0) | (query_cell == 0)
    allowed = allowed & (position < length[0])
    mask[...] = jnp.where(allowed, 0.0, masked_score)
    scale = 1.0 / math.sqrt(width // HEADS)
    finish(qkv_copies)
    tile = width // 2

    @pl.loop(0, 6)
    def _(t):
        columns = pl.ds(pl.multiple_of(t * tile, tile), tile)
        rows = dot(x[...], w_qkv[:, columns]) + qkv_bias[:, columns]
        qkv_rows[:, columns] = (rows * jnp.where(t < 2, scale, 1.0)).astype(low)

    pair_width = 2 * width // HEADS
    first = lax.broadcasted_iota(jnp.int32, (1, pair_width), 1) < pair_width // 2

    @pl.loop(0, HEADS // 2)
    def _(pair):
        start = pl.multiple_of(pair * pair_width, pair_width)
        query = qkv_rows[:, pl.ds(start, pair_width)]
        key = qkv_rows[:, pl.ds(width + start, pair_width)]
        value = qkv_rows[:, pl.ds(2 * width + start, pair_width)]
        sides = []
        for side in range(2):
            mine = first if side == 0 else jnp.logical_not(first)
            scores = dot_nt(jnp.where(mine, query, jnp.zeros_like(query)), key) + mask[...]
            shifted = jnp.exp(scores - jnp.max(scores, axis=-1, keepdims=True))
            total = jnp.sum(shifted, axis=-1, keepdims=True)
            prob = (shifted / total).astype(low)
            probs[2 * pair + side] = prob
            sides.append(dot(prob, value))
        context[:, pl.ds(start, pair_width)] = jnp.where(first, sides[0], sides[1]).astype(low)

    finish(o_copies)
    residual = x[...].astype(f32) + (dot(context[...], w_o[...]) + small[2:3, :])
    unit, inverse = normalize(residual)
    unit_out[...] = unit
    inverse_out[...] = inverse


def ffn_fwd_kernel(layer, ids, unit_one, in_bias, small, *rest):
    weights, rest = rest[:12], rest[12:]
    hidden, slope, unit_out, inverse_out, result, w_in, w_out, normed_low, sems = rest
    in_copies, out_copies = ffn_copies(layer, ids, weights, w_in, w_out, sems)
    begin(in_copies)
    begin(out_copies)
    normed = unit_one[...] * small[3:4, :] + small[4:5, :]
    normed_low[...] = normed.astype(low)
    finish(in_copies)
    tile = w_in.shape[1] // 8

    @pl.loop(0, 8)
    def _(t):
        columns = pl.ds(pl.multiple_of(t * tile, tile), tile)
        pre = dot(normed_low[...], w_in[:, columns]) + in_bias[:, columns]
        cdf = 0.5 * (1.0 + lax.erf(pre * (1.0 / math.sqrt(2.0))))
        density = jnp.exp(-0.5 * pre * pre) * (1.0 / math.sqrt(2.0 * math.pi))
        hidden[:, columns] = (pre * cdf).astype(low)
        slope[:, columns] = cdf + pre * density

    finish(out_copies)
    residual = unit_one[...] * small[3:4, :] + small[4:5, :] + (dot(hidden[...], w_out[...]) + small[5:6, :])
    unit, inverse = normalize(residual)
    unit_out[...] = unit
    inverse_out[...] = inverse
    result[...] = (unit * small[6:7, :] + small[7:8, :]).astype(low)


def store_rows(stage, ids, product, piece, *more):
    share = product.shape[0] // 4
    for owner in range(4):
        away = ids[0] ^ owner
        block = product[owner * share : (owner + 1) * share].astype(low)
        stage[(away & 1, away >> 1, piece ^ ids[5]) + more] = block


def send_out(stage, kept, sent, sems):
    copies = [
        pltpu.make_async_copy(stage.at[1], sent, sems.at[0]),
        pltpu.make_async_copy(stage.at[0], kept, sems.at[1]),
    ]
    begin(copies)
    finish(copies)


def ffn_bwd_kernel(
    layer, ids, grad, unit_two, inverse_two, unit_one, inverse_one, hidden, slope, small, *rest
):
    weights, rest = rest[:12], rest[12:]
    d_resid, small_grads, in_bias_grad, kept, sent = rest[:5]
    w_in, w_out, d_ffn, d_resid_two, d_pre, normed_t, stage, sems, out_sems = rest[5:]
    in_copies, out_copies = ffn_copies(layer, ids, weights, w_in, w_out, sems)
    begin(out_copies)
    begin(in_copies)
    g = grad[...].astype(f32)
    unit = unit_two[...]
    small_grads[0:1, :] = jnp.sum(g * unit, axis=0, keepdims=True)
    small_grads[1:2, :] = jnp.sum(g, axis=0, keepdims=True)
    d_two = normalize_back(g * small[6:7, :], unit, inverse_two[...])
    d_resid_two[...] = d_two
    d_low = d_two.astype(low)
    d_ffn[...] = d_low
    small_grads[2:3, :] = jnp.sum(d_low.astype(f32), axis=0, keepdims=True)
    normed = unit_one[...] * small[3:4, :] + small[4:5, :]
    normed_t[...] = normed.astype(low).T
    finish(out_copies)
    tile = w_in.shape[1] // 8
    share = d_ffn.shape[1] // 4

    @pl.loop(0, 8)
    def _(t):
        columns = pl.ds(pl.multiple_of(t * tile, tile), tile)
        d_hidden = dot_nt(d_ffn[...], w_out[columns, :])
        d_tile = (d_hidden * slope[:, columns]).astype(low)
        d_pre[:, columns] = d_tile
        in_bias_grad[:, columns] = jnp.sum(d_tile.astype(f32), axis=0, keepdims=True)
        store_rows(stage, ids, dot(normed_t[...], d_tile), t, 0)
        out_grad = dot_tn(hidden[:, columns], d_ffn[...])
        away = ids[0] ^ (t // 2)
        for row_group in range(2):
            for column_group in range(2):
                piece = ((t % 2) * 2 + row_group) * 2 + column_group
                block = out_grad[
                    row_group * share : (row_group + 1) * share,
                    column_group * tile : (column_group + 1) * tile,
                ]
                stage[away & 1, away >> 1, piece ^ ids[5], 1] = block.astype(low)

    finish(in_copies)
    d_normed = d_resid_two[...] + dot_nt(d_pre[...], w_in[...])
    unit = unit_one[...]
    small_grads[3:4, :] = jnp.sum(d_normed * unit, axis=0, keepdims=True)
    small_grads[4:5, :] = jnp.sum(d_normed, axis=0, keepdims=True)
    small_grads[5:8, :] = jnp.zeros((3, unit.shape[1]), f32)
    d_resid[...] = normalize_back(d_normed * small[3:4, :], unit, inverse_one[...])
    send_out(stage, kept, sent, out_sems)


def attn_bwd_kernel(layer, ids, d_resid, x, qkv_rows, probs, context, *rest):
    weights, rest = rest[:8], rest[8:]
    d_input, small_grads, kept, sent = rest[:4]
    w_qkv, w_o, d_attn, d_context, d_qkv, x_t, stage, sems, out_sems = rest[4:]
    tokens, width = x.shape
    qkv_copies, o_copies = attn_copies(layer, ids, weights, w_qkv, w_o, sems)
    begin(o_copies)
    begin(qkv_copies)
    d_low = d_resid[...].astype(low)
    d_attn[...] = d_low
    small_grads[2:3, :] = jnp.sum(d_low.astype(f32), axis=0, keepdims=True)
    x_t[...] = x[...].T
    tile = width // 2
    for half in range(2):
        product = dot_tn(context[...], d_attn[:, half * tile : (half + 1) * tile])
        store_rows(stage, ids, product, 6 + half, 0)
    finish(o_copies)
    d_context[...] = dot_nt(d_attn[...], w_o[...]).astype(low)
    pair_width = 2 * width // HEADS
    first = lax.broadcasted_iota(jnp.int32, (1, pair_width), 1) < pair_width // 2
    scale = 1.0 / math.sqrt(width // HEADS)

    @pl.loop(0, HEADS // 2)
    def _(pair):
        start = pl.multiple_of(pair * pair_width, pair_width)
        at_query = pl.ds(start, pair_width)
        at_key = pl.ds(width + start, pair_width)
        at_value = pl.ds(2 * width + start, pair_width)
        query, key, value = qkv_rows[:, at_query], qkv_rows[:, at_key], qkv_rows[:, at_value]
        d_ctx = d_context[:, at_query]
        sides = []
        for side in range(2):
            mine = first if side == 0 else jnp.logical_not(first)
            prob_low = probs[2 * pair + side]
            prob = prob_low.astype(f32)
            d_prob = dot_nt(jnp.where(mine, d_ctx, jnp.zeros_like(d_ctx)), value)
            inner = jnp.sum(prob * d_prob, axis=-1, keepdims=True)
            d_scores = (prob * (d_prob - inner)).astype(low)
            sides.append((dot(d_scores, key), dot_tn(d_scores, query), dot_tn(prob_low, d_ctx)))
        d_qkv[:, at_query] = (jnp.where(first, sides[0][0], sides[1][0]) * scale).astype(low)
        d_qkv[:, at_key] = jnp.where(first, sides[0][1], sides[1][1]).astype(low)
        d_qkv[:, at_value] = jnp.where(first, sides[0][2], sides[1][2]).astype(low)

    @pl.loop(0, 6)
    def _(t):
        columns = pl.ds(pl.multiple_of(t * tile, tile), tile)
        store_rows(stage, ids, dot(x_t[...], d_qkv[:, columns]), t, 0)

    small_grads[0:1, :] = jnp.sum(d_qkv[:, :width].astype(f32), axis=0, keepdims=True)
    small_grads[1:2, :] = jnp.sum(d_qkv[:, 2 * width :].astype(f32), axis=0, keepdims=True)
    small_grads[3:8, :] = jnp.zeros((5, width), f32)
    finish(qkv_copies)
    d_input[...] = (d_resid[...] + dot_nt(d_qkv[...], w_qkv[...])).astype(low)
    send_out(stage, kept, sent, out_sems)


def unpack_kernel(ids, *rest):
    chunks, outs = rest[:8], rest[8:12]
    buffer, wide_buffer, in_sems, out_sems = rest[12:]
    qkv, o, w_in, w_out = outs
    share, tile = buffer.shape[2:]
    for layer in range(2):
        a_near, a_far, f_near, f_far = chunks[4 * layer : 4 * layer + 4]
        for piece in range(8):
            place = piece ^ ids[5]
            for slab in range(3):
                near, far = (a_near, a_far) if slab == 0 else (f_near, f_far)
                which = 0 if slab == 0 else slab - 1
                slot = (layer * 3 + slab) * 8 + piece

                @pl.when(place < 4)
                def _():
                    source = near.at[place, which]
                    pltpu.make_async_copy(source, buffer.at[slab * 8 + piece, layer], in_sems.at[slot]).start()

                @pl.when(place >= 4)
                def _():
                    source = far.at[place - 4, which]
                    pltpu.make_async_copy(source, buffer.at[slab * 8 + piece, layer], in_sems.at[slot]).start()

    copies = []
    for layer in range(2):
        a_near = chunks[4 * layer]
        for slab in range(3):
            for piece in range(8):
                slot = (layer * 3 + slab) * 8 + piece
                landed = buffer.at[slab * 8 + piece, layer]
                pltpu.make_async_copy(a_near.at[0, 0], landed, in_sems.at[slot]).wait()
                wide_buffer[slab * 8 + piece, layer] = landed[...].astype(f32)
                if slab == 0 and piece < 6:
                    target = qkv.at[layer, :, pl.ds(piece * tile, tile)]
                elif slab == 0:
                    target = o.at[layer, :, pl.ds((piece - 6) * tile, tile)]
                elif slab == 1:
                    target = w_in.at[layer, :, pl.ds(piece * tile, tile)]
                else:
                    rows = pl.ds((piece // 2) * share, share)
                    target = w_out.at[layer, rows, pl.ds((piece % 2) * tile, tile)]
                copy = pltpu.make_async_copy(wide_buffer.at[slab * 8 + piece, layer], target, out_sems.at[slot])
                copy.start()
                copies.append(copy)
    finish(copies)


SMEM = pl.BlockSpec(memory_space=pltpu.SMEM)
VMEM = pl.BlockSpec(memory_space=pltpu.VMEM)
ANY = pl.BlockSpec(memory_space=pl.ANY)


def call(kernel, name, in_specs, out_specs, out_shape, scratch, flops, moved, args):
    return pl.pallas_call(
        kernel,
        name=name,
        in_specs=in_specs,
        out_specs=out_specs,
        out_shape=out_shape,
        scratch_shapes=scratch,
        compiler_params=pltpu.CompilerParams(vmem_limit_bytes=VMEM_BYTES),
        cost_estimate=pl.CostEstimate(flops=flops, bytes_accessed=moved, transcendentals=0),
    )(*args)


def shape(dims, kind):
    return jax.ShapeDtypeStruct(dims, kind)


def reverse_bits(value, bits):
    result = jnp.zeros_like(value)
    for bit in range(bits):
        result = result | (((value >> bit) & 1) << (bits - 1 - bit))
    return result


def added(a, b):
    return (a.astype(f32) + b.astype(f32)).astype(low)


def reduce_chunk(kept, sent, wide_bits):
    split = (2,) * HALVINGS
    kept = kept.reshape((2,) + split + kept.shape[2:])
    sent = sent.reshape((2,) + split + sent.shape[2:])
    received = swap(sent, "narrow", 1)
    for axis, bit in [("narrow", 2)] + [("wide", 1 << b) for b in range(HALVINGS)]:
        send = added(kept[1], received[1])
        kept = added(kept[0], received[0])
        received = swap(send, axis, bit)
    piece = added(kept, received)
    for b in range(HALVINGS, wide_bits):
        piece = added(piece, swap(piece, "wide", 1 << b))
    block = piece[None]
    for b in range(HALVINGS - 1, 0, -1):
        block = jnp.concatenate([block, swap(block, "wide", 1 << b)], axis=0)
    return block, swap(block, "wide", 1)


def body(
    tables_in,
    cotangent,
    cell_ids,
    lengths,
    qkv_weight,
    q_bias,
    v_bias,
    o_weight,
    o_bias,
    norm1_gain,
    norm1_bias,
    in_weight,
    in_bias,
    out_weight,
    out_bias,
    norm2_gain,
    norm2_bias,
):
    tokens, width = tables_in.shape
    layers, share, ffn = in_weight.shape
    ffn_share = out_weight.shape[1]
    wide_count = lax.axis_size("wide")
    wide_bits = wide_count.bit_length() - 1
    assert wide_count == 1 << wide_bits and wide_bits >= HALVINGS and lax.axis_size("narrow") == 4
    tile = ffn // 8
    me = lax.axis_index("narrow").astype(jnp.int32)
    wide_me = lax.axis_index("wide").astype(jnp.int32)
    y = wide_me & 1
    order = reverse_bits(wide_me & (2**HALVINGS - 1), HALVINGS)
    ids = jnp.stack([me, me ^ 1, me ^ 2, me ^ 3, y, order])

    short = [q_bias, v_bias, o_bias, norm1_gain, norm1_bias, out_bias, norm2_gain, norm2_bias]
    packed = jnp.concatenate([jnp.stack(short, axis=1), in_bias.reshape(layers, 4, share)], axis=1)
    packed = lax.all_gather(packed, "narrow", axis=0).astype(f32)
    small = packed[:, :, :8].transpose(1, 2, 0, 3).reshape(layers, 8, width)
    full_in_bias = packed[:, :, 8:].transpose(1, 0, 2, 3).reshape(layers, 1, ffn)
    qkv_bias = jnp.concatenate([small[:, 0], jnp.zeros((layers, width), f32), small[:, 1]], axis=1)
    qkv_bias = qkv_bias.reshape(layers, 1, 3 * width)

    core = [swap(weight, "narrow", 1) for weight in (qkv_weight, o_weight, in_weight, out_weight)]

    def half_of(weight, layer):
        rows = weight.shape[1] // 2
        return lax.dynamic_slice(weight, (layer, y * rows, 0), (1, rows, weight.shape[2]))[0]

    def spread(half):
        near_x = swap(half, "narrow", 2)
        far_x = swap(near_x, "wide", 1)
        return near_x, far_x, swap(near_x, "narrow", 1), swap(far_x, "narrow", 1)

    attn_weights, ffn_weights = [], []
    for layer in range(layers):
        joint = jnp.concatenate([half_of(qkv_weight, layer), half_of(o_weight, layer)], axis=1)
        attn_weights.append((qkv_weight, core[0], o_weight, core[1]) + spread(joint))
        ffn_weights.append(
            (in_weight, core[2])
            + spread(half_of(in_weight, layer))
            + (out_weight, core[3])
            + spread(half_of(out_weight, layer))
        )

    cell_col = cell_ids.reshape(tokens, 1)
    w_qkv = pltpu.VMEM((width, 3 * width), low)
    w_o = pltpu.VMEM((width, width), low)
    w_in = pltpu.VMEM((width, ffn), low)
    w_out = pltpu.VMEM((ffn, width), low)
    copy_sems = pltpu.SemaphoreType.DMA((12,))
    pair_sems = pltpu.SemaphoreType.DMA((2,))
    rows_f32 = shape((tokens, width), f32)
    column_f32 = shape((tokens, 1), f32)
    rows_low = shape((tokens, width), low)
    attn_flops = 2 * tokens * width * (4 * width + 2 * tokens)
    ffn_flops = 4 * tokens * width * ffn
    attn_bytes = 8 * width * width
    ffn_bytes = 4 * width * ffn

    def attn_forward(layer, x):
        return call(
            functools.partial(attn_fwd_kernel, layer),
            "attn_fwd",
            [SMEM, SMEM] + [VMEM] * 5 + [ANY] * 8,
            [VMEM] * 5,
            [
                shape((tokens, 3 * width), low),
                shape((HEADS, tokens, tokens), low),
                rows_low,
                rows_f32,
                column_f32,
            ],
            [w_qkv, w_o, pltpu.VMEM((tokens, tokens), f32), copy_sems],
            attn_flops,
            2 * attn_bytes,
            (ids, lengths, x, cell_ids, cell_col, qkv_bias[layer], small[layer]) + attn_weights[layer],
        )

    def ffn_forward(layer, unit_one):
        return call(
            functools.partial(ffn_fwd_kernel, layer),
            "ffn_fwd",
            [SMEM] + [VMEM] * 3 + [ANY] * 12,
            [VMEM] * 5,
            [
                shape((tokens, ffn), low),
                shape((tokens, ffn), f32),
                rows_f32,
                column_f32,
                rows_low,
            ],
            [w_in, w_out, pltpu.VMEM((tokens, width), low), copy_sems],
            ffn_flops,
            2 * ffn_bytes,
            (ids, unit_one, full_in_bias[layer], small[layer]) + ffn_weights[layer],
        )

    def ffn_backward(layer, grad, unit_two, inverse_two, unit_one, inverse_one, hidden, slope):
        pieces = shape((2, 8, 2, share, tile), low)
        return call(
            functools.partial(ffn_bwd_kernel, layer),
            "ffn_bwd",
            [SMEM] + [VMEM] * 8 + [ANY] * 12,
            [VMEM] * 3 + [ANY] * 2,
            [rows_f32, shape((8, width), f32), shape((1, ffn), f32), pieces, pieces],
            [
                w_in,
                w_out,
                pltpu.VMEM((tokens, width), low),
                pltpu.VMEM((tokens, width), f32),
                pltpu.VMEM((tokens, ffn), low),
                pltpu.VMEM((width, tokens), low),
                pltpu.VMEM((2, 2, 8, 2, share, tile), low),
                copy_sems,
                pair_sems,
            ],
            2 * ffn_flops,
            3 * ffn_bytes,
            (ids, grad, unit_two, inverse_two, unit_one, inverse_one, hidden, slope, small[layer])
            + ffn_weights[layer],
        )

    def attn_backward(layer, d_resid, x, qkv_rows, probs, context):
        pieces = shape((2, 8, 1, share, tile), low)
        return call(
            functools.partial(attn_bwd_kernel, layer),
            "attn_bwd",
            [SMEM] + [VMEM] * 5 + [ANY] * 8,
            [VMEM] * 2 + [ANY] * 2,
            [rows_low, shape((8, width), f32), pieces, pieces],
            [
                w_qkv,
                w_o,
                pltpu.VMEM((tokens, width), low),
                pltpu.VMEM((tokens, width), low),
                pltpu.VMEM((tokens, 3 * width), low),
                pltpu.VMEM((width, tokens), low),
                pltpu.VMEM((2, 2, 8, 1, share, tile), low),
                copy_sems,
                pair_sems,
            ],
            2 * attn_flops,
            3 * attn_bytes,
            (ids, d_resid, x, qkv_rows, probs, context) + attn_weights[layer],
        )

    stored = []
    x = tables_in
    for layer in range(layers):
        qkv_rows, probs, context, unit_one, inverse_one = attn_forward(layer, x)
        hidden, slope, unit_two, inverse_two, result = ffn_forward(layer, unit_one)
        stored.append((x, qkv_rows, probs, context, unit_one, inverse_one, hidden, slope, unit_two, inverse_two))
        x = result
    mixed_out = x

    grad = cotangent
    chunks = [None] * (2 * layers)
    attn_small, ffn_small, in_bias_grads = [None] * layers, [None] * layers, [None] * layers
    for layer in reversed(range(layers)):
        x, qkv_rows, probs, context, unit_one, inverse_one, hidden, slope, unit_two, inverse_two = stored[layer]
        d_resid, ffn_small[layer], in_bias_grads[layer], kept, sent = ffn_backward(
            layer, grad, unit_two, inverse_two, unit_one, inverse_one, hidden, slope
        )
        chunks[2 * layer + 1] = reduce_chunk(kept, sent, wide_bits)
        grad, attn_small[layer], kept, sent = attn_backward(layer, d_resid, x, qkv_rows, probs, context)
        chunks[2 * layer] = reduce_chunk(kept, sent, wide_bits)

    flat = [part for pair in chunks for part in pair]
    qkv_grad, o_grad, in_grad, out_grad = call(
        unpack_kernel,
        "unpack",
        [SMEM] + [ANY] * 8,
        [ANY] * 4,
        [
            shape((layers, share, 3 * width), f32),
            shape((layers, share, width), f32),
            shape((layers, share, ffn), f32),
            shape((layers, ffn_share, width), f32),
        ],
        [
            pltpu.VMEM((24, layers, share, tile), low),
            pltpu.VMEM((24, layers, share, tile), f32),
            pltpu.SemaphoreType.DMA((48,)),
            pltpu.SemaphoreType.DMA((48,)),
        ],
        0,
        6 * layers * 3 * share * ffn,
        (ids, *flat),
    )

    rows = jnp.stack(
        [jnp.concatenate([attn_small[i][:3], ffn_small[i][:5]], axis=0) for i in range(layers)]
    )
    rows, in_rows = lax.psum((rows, jnp.stack(in_bias_grads)), ("wide", "narrow"))
    rows = lax.dynamic_slice(rows, (0, 0, me * share), (layers, 8, share))
    in_rows = lax.dynamic_slice(in_rows, (0, 0, me * ffn_share), (layers, 1, ffn_share))[:, 0]
    return (
        mixed_out,
        grad,
        qkv_grad,
        rows[:, 0],
        rows[:, 1],
        o_grad,
        rows[:, 2],
        rows[:, 6],
        rows[:, 7],
        in_grad,
        in_rows,
        out_grad,
        rows[:, 5],
        rows[:, 3],
        rows[:, 4],
    )


def solution(mesh):
    by_table = P(("wide", "narrow"), None)
    matrix = P(None, "narrow", None)
    vector = P(None, "narrow")
    return jax.shard_map(
        body,
        mesh=mesh,
        in_specs=(
            by_table,
            by_table,
            by_table,
            P(("wide", "narrow")),
            matrix,
            vector,
            vector,
            matrix,
            vector,
            vector,
            vector,
            matrix,
            vector,
            matrix,
            vector,
            vector,
            vector,
        ),
        out_specs=(
            by_table,
            by_table,
            matrix,
            vector,
            vector,
            matrix,
            vector,
            vector,
            vector,
            matrix,
            vector,
            matrix,
            vector,
            vector,
            vector,
        ),
        check_vma=False,
    )
```

```python
import functools
import math

import jax
import jax.numpy as jnp
from jax import lax
from jax.experimental import pallas as pl
from jax.experimental.pallas import tpu as pltpu
from jax.sharding import PartitionSpec as P

HEADS = 12
norm_eps = 1e-12
masked_score = -1000000000.0
low = jnp.bfloat16
f32 = jnp.float32
VMEM_BYTES = 56 * 1024 * 1024
HALVINGS = 3


def swap(value, axis, bit):
    count = lax.axis_size(axis)
    return lax.ppermute(value, axis, [(i, i ^ bit) for i in range(count)])


def dot(a, b):
    return jnp.dot(a, b, preferred_element_type=f32)


def dot_nt(a, b):
    return lax.dot_general(a, b, (((1,), (1,)), ((), ())), preferred_element_type=f32)


def dot_tn(a, b):
    return lax.dot_general(a, b, (((0,), (0,)), ((), ())), preferred_element_type=f32)


def normalize(residual):
    center = residual - jnp.mean(residual, axis=-1, keepdims=True)
    inverse = lax.rsqrt(jnp.mean(center * center, axis=-1, keepdims=True) + norm_eps)
    return center * inverse, inverse


def normalize_back(grad_unit, unit, inverse):
    centered = grad_unit - jnp.mean(grad_unit, axis=-1, keepdims=True)
    return inverse * (centered - unit * jnp.mean(grad_unit * unit, axis=-1, keepdims=True))


def weight_copies(ids, layer, pieces, target, columns, sems, base):
    own, core, near_x, far_x, near_d, far_d = pieces
    rows = own.shape[1]
    half = rows // 2
    n, y = ids[0], ids[4]
    copies = []

    def add(source, start, count):
        where = target.at[pl.ds(pl.multiple_of(start, half), count), :]
        copies.append(pltpu.make_async_copy(source, where, sems.at[base + len(copies)]))

    def part(ref):
        return ref.at[:, pl.ds(columns, target.shape[1])]

    add(own.at[layer], n * rows, rows)
    add(core.at[layer], ids[1] * rows, rows)
    add(part(near_x), ids[2] * rows + y * half, half)
    add(part(far_x), ids[2] * rows + (1 - y) * half, half)
    add(part(near_d), ids[3] * rows + y * half, half)
    add(part(far_d), ids[3] * rows + (1 - y) * half, half)
    return copies


def begin(copies):
    for copy in copies:
        copy.start()


def finish(copies):
    for copy in copies:
        copy.wait()


def attn_copies(layer, ids, refs, w_qkv, w_o, sems):
    qkv_own, qkv_core, o_own, o_core, near_x, far_x, near_d, far_d = refs
    halves = (near_x, far_x, near_d, far_d)
    qkv = weight_copies(ids, layer, (qkv_own, qkv_core) + halves, w_qkv, 0, sems, 0)
    o = weight_copies(ids, layer, (o_own, o_core) + halves, w_o, w_qkv.shape[1], sems, 6)
    return qkv, o


def ffn_copies(layer, ids, refs, w_in, w_out, sems):
    in_copies = weight_copies(ids, layer, refs[:6], w_in, 0, sems, 0)
    out_copies = weight_copies(ids, layer, refs[6:], w_out, 0, sems, 6)
    return in_copies, out_copies


def attn_fwd_kernel(layer, ids, length, x, cell_row, cell_col, qkv_bias, small, *rest):
    weights, rest = rest[:8], rest[8:]
    qkv_rows, probs, context, unit_out, inverse_out, w_qkv, w_o, mask, sems = rest
    tokens, width = x.shape
    qkv_copies, o_copies = attn_copies(layer, ids, weights, w_qkv, w_o, sems)
    begin(qkv_copies)
    begin(o_copies)
    position = lax.broadcasted_iota(jnp.int32, (1, tokens), 1)
    key_cell, query_cell = cell_row[...], cell_col[...]
    allowed = (query_cell == key_cell) | (key_cell == 0) | (query_cell == 0)
    allowed = allowed & (position < length[0])
    mask[...] = jnp.where(allowed, 0.0, masked_score)
    scale = 1.0 / math.sqrt(width // HEADS)
    finish(qkv_copies)
    tile = width // 2

    @pl.loop(0, 6)
    def _(t):
        columns = pl.ds(pl.multiple_of(t * tile, tile), tile)
        rows = dot(x[...], w_qkv[:, columns]) + qkv_bias[layer, :, columns]
        qkv_rows[:, columns] = (rows * jnp.where(t < 2, scale, 1.0)).astype(low)

    pair_width = 2 * width // HEADS
    first = lax.broadcasted_iota(jnp.int32, (1, pair_width), 1) < pair_width // 2

    @pl.loop(0, HEADS // 2)
    def _(pair):
        start = pl.multiple_of(pair * pair_width, pair_width)
        query = qkv_rows[:, pl.ds(start, pair_width)]
        key = qkv_rows[:, pl.ds(width + start, pair_width)]
        value = qkv_rows[:, pl.ds(2 * width + start, pair_width)]
        sides = []
        for side in range(2):
            mine = first if side == 0 else jnp.logical_not(first)
            scores = dot_nt(jnp.where(mine, query, jnp.zeros_like(query)), key) + mask[...]
            shifted = jnp.exp(scores - jnp.max(scores, axis=-1, keepdims=True))
            total = jnp.sum(shifted, axis=-1, keepdims=True)
            prob = (shifted / total).astype(low)
            probs[2 * pair + side] = prob
            sides.append(dot(prob, value))
        context[:, pl.ds(start, pair_width)] = jnp.where(first, sides[0], sides[1]).astype(low)

    finish(o_copies)
    residual = x[...].astype(f32) + (dot(context[...], w_o[...]) + small[layer, 2:3, :])
    unit, inverse = normalize(residual)
    unit_out[...] = unit
    inverse_out[...] = inverse


def ffn_fwd_kernel(layer, ids, unit_one, in_bias, small, *rest):
    weights, rest = rest[:12], rest[12:]
    hidden, slope, unit_out, inverse_out, result, w_in, w_out, normed_low, sems = rest
    in_copies, out_copies = ffn_copies(layer, ids, weights, w_in, w_out, sems)
    begin(in_copies)
    begin(out_copies)
    normed = unit_one[...] * small[layer, 3:4, :] + small[layer, 4:5, :]
    normed_low[...] = normed.astype(low)
    finish(in_copies)
    tile = w_in.shape[1] // 8

    @pl.loop(0, 8)
    def _(t):
        columns = pl.ds(pl.multiple_of(t * tile, tile), tile)
        pre = dot(normed_low[...], w_in[:, columns]) + in_bias[layer, :, columns]
        cdf = 0.5 * (1.0 + lax.erf(pre * (1.0 / math.sqrt(2.0))))
        density = jnp.exp(-0.5 * pre * pre) * (1.0 / math.sqrt(2.0 * math.pi))
        hidden[:, columns] = (pre * cdf).astype(low)
        slope[:, columns] = cdf + pre * density

    finish(out_copies)
    residual = unit_one[...] * small[layer, 3:4, :] + small[layer, 4:5, :] + (dot(hidden[...], w_out[...]) + small[layer, 5:6, :])
    unit, inverse = normalize(residual)
    unit_out[...] = unit
    inverse_out[...] = inverse
    result[...] = (unit * small[layer, 6:7, :] + small[layer, 7:8, :]).astype(low)


def store_rows(stage, ids, product, piece):
    share = product.shape[0] // 4
    for owner in range(4):
        away = ids[0] ^ owner
        block = product[owner * share : (owner + 1) * share].astype(low)
        stage[away & 1, away >> 1, piece ^ ids[5]] = block


def send_out(stage, kept, sent, sems, base):
    return [
        pltpu.make_async_copy(stage.at[1], sent, sems.at[base]),
        pltpu.make_async_copy(stage.at[0], kept, sems.at[base + 1]),
    ]


def ffn_bwd_kernel(
    layer, ids, grad, unit_two, inverse_two, unit_one, inverse_one, hidden, slope, small, *rest
):
    weights, rest = rest[:12], rest[12:]
    d_resid, small_grads, in_bias_grad, in_kept, in_sent, out_kept, out_sent = rest[:7]
    w_in, w_out, d_ffn, d_resid_two, d_pre, normed_t, in_stage, out_stage, sems, out_sems = rest[7:]
    in_copies, out_copies = ffn_copies(layer, ids, weights, w_in, w_out, sems)
    begin(out_copies)
    begin(in_copies)
    g = grad[...].astype(f32)
    unit = unit_two[...]
    small_grads[0:1, :] = jnp.sum(g * unit, axis=0, keepdims=True)
    small_grads[1:2, :] = jnp.sum(g, axis=0, keepdims=True)
    d_two = normalize_back(g * small[layer, 6:7, :], unit, inverse_two[...])
    d_resid_two[...] = d_two
    d_low = d_two.astype(low)
    d_ffn[...] = d_low
    small_grads[2:3, :] = jnp.sum(d_low.astype(f32), axis=0, keepdims=True)
    normed = unit_one[...] * small[layer, 3:4, :] + small[layer, 4:5, :]
    normed_t[...] = normed.astype(low).T
    finish(out_copies)
    tile = w_in.shape[1] // 8
    share = d_ffn.shape[1] // 4

    @pl.loop(0, 8)
    def _(t):
        columns = pl.ds(pl.multiple_of(t * tile, tile), tile)
        d_hidden = dot_nt(d_ffn[...], w_out[columns, :])
        d_tile = (d_hidden * slope[:, columns]).astype(low)
        d_pre[:, columns] = d_tile
        in_bias_grad[:, columns] = jnp.sum(d_tile.astype(f32), axis=0, keepdims=True)
        store_rows(in_stage, ids, dot(normed_t[...], d_tile), t)
        out_grad = dot_tn(hidden[:, columns], d_ffn[...])
        away = ids[0] ^ (t // 2)
        for row_group in range(2):
            for column_group in range(2):
                piece = ((t % 2) * 2 + row_group) * 2 + column_group
                block = out_grad[
                    row_group * share : (row_group + 1) * share,
                    column_group * tile : (column_group + 1) * tile,
                ]
                out_stage[away & 1, away >> 1, piece ^ ids[5]] = block.astype(low)

    going = send_out(out_stage, out_kept, out_sent, out_sems, 0)
    going += send_out(in_stage, in_kept, in_sent, out_sems, 2)
    begin(going)
    finish(in_copies)
    d_normed = d_resid_two[...] + dot_nt(d_pre[...], w_in[...])
    unit = unit_one[...]
    small_grads[3:4, :] = jnp.sum(d_normed * unit, axis=0, keepdims=True)
    small_grads[4:5, :] = jnp.sum(d_normed, axis=0, keepdims=True)
    small_grads[5:8, :] = jnp.zeros((3, unit.shape[1]), f32)
    d_resid[...] = normalize_back(d_normed * small[layer, 3:4, :], unit, inverse_one[...])
    finish(going)


def attn_bwd_kernel(layer, ids, d_resid, x, qkv_rows, probs, context, *rest):
    weights, rest = rest[:8], rest[8:]
    d_input, small_grads, kept, sent = rest[:4]
    w_qkv, w_o, d_attn, d_context, d_qkv, x_t, stage, sems, out_sems = rest[4:]
    tokens, width = x.shape
    qkv_copies, o_copies = attn_copies(layer, ids, weights, w_qkv, w_o, sems)
    begin(o_copies)
    begin(qkv_copies)
    d_low = d_resid[...].astype(low)
    d_attn[...] = d_low
    small_grads[2:3, :] = jnp.sum(d_low.astype(f32), axis=0, keepdims=True)
    x_t[...] = x[...].T
    tile = width // 2
    for half in range(2):
        product = dot_tn(context[...], d_attn[:, half * tile : (half + 1) * tile])
        store_rows(stage, ids, product, 6 + half)
    finish(o_copies)
    d_context[...] = dot_nt(d_attn[...], w_o[...]).astype(low)
    pair_width = 2 * width // HEADS
    first = lax.broadcasted_iota(jnp.int32, (1, pair_width), 1) < pair_width // 2
    scale = 1.0 / math.sqrt(width // HEADS)

    @pl.loop(0, HEADS // 2)
    def _(pair):
        start = pl.multiple_of(pair * pair_width, pair_width)
        at_query = pl.ds(start, pair_width)
        at_key = pl.ds(width + start, pair_width)
        at_value = pl.ds(2 * width + start, pair_width)
        query, key, value = qkv_rows[:, at_query], qkv_rows[:, at_key], qkv_rows[:, at_value]
        d_ctx = d_context[:, at_query]
        sides = []
        for side in range(2):
            mine = first if side == 0 else jnp.logical_not(first)
            prob_low = probs[2 * pair + side]
            prob = prob_low.astype(f32)
            d_prob = dot_nt(jnp.where(mine, d_ctx, jnp.zeros_like(d_ctx)), value)
            inner = jnp.sum(prob * d_prob, axis=-1, keepdims=True)
            d_scores = (prob * (d_prob - inner)).astype(low)
            sides.append((dot(d_scores, key), dot_tn(d_scores, query), dot_tn(prob_low, d_ctx)))
        d_qkv[:, at_query] = (jnp.where(first, sides[0][0], sides[1][0]) * scale).astype(low)
        d_qkv[:, at_key] = jnp.where(first, sides[0][1], sides[1][1]).astype(low)
        d_qkv[:, at_value] = jnp.where(first, sides[0][2], sides[1][2]).astype(low)

    @pl.loop(0, 6)
    def _(t):
        columns = pl.ds(pl.multiple_of(t * tile, tile), tile)
        store_rows(stage, ids, dot(x_t[...], d_qkv[:, columns]), t)

    going = send_out(stage, kept, sent, out_sems, 0)
    begin(going)
    small_grads[0:1, :] = jnp.sum(d_qkv[:, :width].astype(f32), axis=0, keepdims=True)
    small_grads[1:2, :] = jnp.sum(d_qkv[:, 2 * width :].astype(f32), axis=0, keepdims=True)
    small_grads[3:8, :] = jnp.zeros((5, width), f32)
    finish(qkv_copies)
    d_input[...] = (d_resid[...] + dot_nt(d_qkv[...], w_qkv[...])).astype(low)
    finish(going)


def unpack_kernel(layer, slab, ids, near, far, *rest):
    outs, scratch = rest[:-4], rest[-4:]
    outs = outs[len(outs) // 2 :] if layer == 0 else outs
    buffer, wide_buffer, in_sems, out_sems = scratch
    share, tile = buffer.shape[1:]
    for piece in range(8):
        place = piece ^ ids[5]

        @pl.when(place < 4)
        def _():
            pltpu.make_async_copy(near.at[place], buffer.at[piece], in_sems.at[piece]).start()

        @pl.when(place >= 4)
        def _():
            pltpu.make_async_copy(far.at[place - 4], buffer.at[piece], in_sems.at[piece]).start()

    copies = []
    for piece in range(8):
        pltpu.make_async_copy(near.at[0], buffer.at[piece], in_sems.at[piece]).wait()
        wide_buffer[piece] = buffer[piece].astype(f32)
        columns = pl.ds(piece * tile, tile)
        if slab == "in":
            target = outs[0].at[layer, :, columns]
        elif slab == "out":
            rows = pl.ds((piece // 2) * share, share)
            target = outs[0].at[layer, rows, pl.ds((piece % 2) * tile, tile)]
        elif piece < 6:
            target = outs[0].at[layer, :, columns]
        else:
            target = outs[1].at[layer, :, pl.ds((piece - 6) * tile, tile)]
        copies.append(pltpu.make_async_copy(wide_buffer.at[piece], target, out_sems.at[piece]))
        copies[-1].start()
    finish(copies)


SMEM = pl.BlockSpec(memory_space=pltpu.SMEM)
VMEM = pl.BlockSpec(memory_space=pltpu.VMEM)
ANY = pl.BlockSpec(memory_space=pl.ANY)


def call(kernel, name, in_specs, out_specs, out_shape, scratch, args, aliases=()):
    return pl.pallas_call(
        kernel,
        name=name,
        in_specs=in_specs,
        out_specs=out_specs,
        out_shape=out_shape,
        scratch_shapes=scratch,
        input_output_aliases=dict(aliases),
        compiler_params=pltpu.CompilerParams(vmem_limit_bytes=VMEM_BYTES),
        cost_estimate=pl.CostEstimate(flops=1, bytes_accessed=1, transcendentals=0),
    )(*args)


def shape(dims, kind):
    return jax.ShapeDtypeStruct(dims, kind)


def reverse_bits(value, bits):
    result = jnp.zeros_like(value)
    for bit in range(bits):
        result = result | (((value >> bit) & 1) << (bits - 1 - bit))
    return result


def added(a, b):
    return (a.astype(f32) + b.astype(f32)).astype(low)


class Order:
    def __init__(self):
        self.last = None

    def after(self, values):
        if self.last is None:
            return values
        values, self.last = lax.optimization_barrier((values, self.last))
        return values

    def wait(self, values):
        values = self.after(values)
        self.last = values
        return values


STEPS = {"x": ("narrow", 2, 0), "y": ("wide", 1, 1), "z": ("wide", 2, 2), "w": ("wide", 4, 3)}
BACK = "wzy"


class Slab:
    def __init__(self, way, wide_bits, kept, sent):
        self.way, self.wide_bits = way, wide_bits
        self.dims = "xyzw"
        self.kept = kept.reshape((2, 2, 2, 2) + kept.shape[2:])
        self.flying = swap(sent.reshape(self.kept.shape), "narrow", 1)
        self.stage = 0

    def step(self, order):
        received = order.after(self.flying)
        if self.stage < len(self.way):
            name = self.way[self.stage]
            at = self.dims.index(name)
            self.dims = self.dims.replace(name, "")
            kept, got = jnp.moveaxis(self.kept, at, 0), jnp.moveaxis(received, at, 0)
            send = added(kept[1], got[1])
            self.kept = added(kept[0], got[0])
            axis, bit, _ = STEPS[name]
            self.flying = swap(send, axis, bit)
            order.last = send
        elif self.stage == len(self.way):
            piece = added(self.kept, received)
            for b in range(HALVINGS, self.wide_bits):
                piece = added(piece, swap(piece, "wide", 1 << b))
            self.block = piece[None]
            order.last = self.block
            self.flying = swap(self.block, "wide", STEPS[BACK[0]][1])
        elif self.stage < len(self.way) + len(BACK):
            self.block = jnp.concatenate([self.block, received], axis=0)
            order.last = self.block
            self.flying = swap(self.block, "wide", STEPS[BACK[self.stage - len(self.way)]][1])
        else:
            self.far = received
        self.stage += 1


def plan(ways, kernels, megabytes):
    rate, core_rate = 0.091, 0.3
    trips = []
    for way in ways:
        size, trip = megabytes / 2, [("c", megabytes / 2 / core_rate)]
        for name in way:
            size /= 2
            trip.append((name, (4 if name == "w" else 2) * size / rate))
        for name in BACK:
            trip.append((name, (4 if name == "w" else 2) * size / rate))
            size *= 2
        trips.append(trip)
    free = dict.fromkeys("cxyzw", 0.0)
    now, flying, result, waiting = 0.0, [], [], list(kernels)

    def launch(slab, stage):
        name, time = trips[slab][stage]
        start = max(free[name], now)
        if name == "w":
            start = max(start, free["z"])
            free["z"] = start + time / 2
        free[name] = start + time
        flying.append((start + time + 0.7, slab, stage))

    while waiting or flying:
        landed = [event for event in flying if event[0] <= now]
        if not landed and waiting:
            kernel, time, slabs = waiting.pop(0)
            now += time
            result.append(("kernel", kernel))
            for slab in slabs:
                now += 0.8
                launch(slab, 0)
            continue
        event = min(landed, key=lambda e: e[1]) if landed else min(flying)
        flying.remove(event)
        done, slab, stage = event
        now = max(now, done) + (1.5 if stage <= len(ways[slab]) else 0.6)
        result.append(("step", slab))
        if stage + 1 < len(trips[slab]):
            now += 0.8
            launch(slab, stage + 1)
    return result


def body(
    tables_in,
    cotangent,
    cell_ids,
    lengths,
    qkv_weight,
    q_bias,
    v_bias,
    o_weight,
    o_bias,
    norm1_gain,
    norm1_bias,
    in_weight,
    in_bias,
    out_weight,
    out_bias,
    norm2_gain,
    norm2_bias,
):
    tokens, width = tables_in.shape
    layers, share, ffn = in_weight.shape
    ffn_share = out_weight.shape[1]
    wide_count = lax.axis_size("wide")
    wide_bits = wide_count.bit_length() - 1
    assert wide_count == 1 << wide_bits and wide_bits >= HALVINGS and lax.axis_size("narrow") == 4
    tile = ffn // 8
    me = lax.axis_index("narrow").astype(jnp.int32)
    wide_me = lax.axis_index("wide").astype(jnp.int32)
    y = wide_me & 1
    place = reverse_bits(wide_me & (2**HALVINGS - 1), HALVINGS)
    ids = jnp.stack([me, me ^ 1, me ^ 2, me ^ 3, y, place])

    short = [q_bias, v_bias, o_bias, norm1_gain, norm1_bias, out_bias, norm2_gain, norm2_bias]
    packed = jnp.concatenate([jnp.stack(short, axis=1), in_bias.reshape(layers, 4, share)], axis=1)
    packed = lax.all_gather(packed, "narrow", axis=0).astype(f32)
    small = packed[:, :, :8].transpose(1, 2, 0, 3).reshape(layers, 8, width)
    full_in_bias = packed[:, :, 8:].transpose(1, 0, 2, 3).reshape(layers, 1, ffn)
    qkv_bias = jnp.concatenate([small[:, 0], jnp.zeros((layers, width), f32), small[:, 1]], axis=1)
    qkv_bias = qkv_bias.reshape(layers, 1, 3 * width)
    cell_col = cell_ids.reshape(tokens, 1)
    order = Order()

    core = [swap(weight, "narrow", 1) for weight in (qkv_weight, o_weight, in_weight, out_weight)]

    def half_of(weight, layer):
        rows = weight.shape[1] // 2
        return lax.dynamic_slice(weight, (layer, y * rows, 0), (1, rows, weight.shape[2]))[0]

    halves = []
    for layer in range(layers):
        joint = jnp.concatenate([half_of(qkv_weight, layer), half_of(o_weight, layer)], axis=1)
        halves += [joint, half_of(in_weight, layer), half_of(out_weight, layer)]
    near_x = [swap(half, "narrow", 2) for half in halves]
    far_x, near_d, far_d = [None] * len(halves), [None] * len(halves), [None] * len(halves)
    ids, small, full_in_bias, qkv_bias, cell_col = order.wait((ids, small, full_in_bias, qkv_bias, cell_col))

    def arrive(*events):
        for kind, i in events:
            if kind == "x":
                near_x[i] = order.wait(near_x[i])
                far_x[i] = swap(near_x[i], "wide", 1)
                near_d[i] = swap(near_x[i], "narrow", 1)
            elif kind == "y":
                far_x[i] = order.wait(far_x[i])
                far_d[i] = swap(far_x[i], "narrow", 1)
            else:
                near_d[i], far_d[i] = order.wait((near_d[i], far_d[i]))

    def group(i):
        return near_x[i], far_x[i], near_d[i], far_d[i]

    def attn_weights(layer):
        return (qkv_weight, core[0], o_weight, core[1]) + group(3 * layer)

    def ffn_weights(layer):
        return (in_weight, core[2]) + group(3 * layer + 1) + (out_weight, core[3]) + group(3 * layer + 2)

    w_qkv = pltpu.VMEM((width, 3 * width), low)
    w_o = pltpu.VMEM((width, width), low)
    w_in = pltpu.VMEM((width, ffn), low)
    w_out = pltpu.VMEM((ffn, width), low)
    copy_sems = pltpu.SemaphoreType.DMA((12,))
    rows_f32 = shape((tokens, width), f32)
    rows_low = shape((tokens, width), low)
    column_f32 = shape((tokens, 1), f32)
    pieces = shape((2, 8, share, tile), low)
    stage = pltpu.VMEM((2, 2, 8, share, tile), low)

    def attn_forward(layer, x):
        x = order.after(x)
        outs = call(
            functools.partial(attn_fwd_kernel, layer),
            "attn_fwd",
            [SMEM, SMEM] + [VMEM] * 5 + [ANY] * 8,
            [VMEM] * 5,
            [shape((tokens, 3 * width), low), shape((HEADS, tokens, tokens), low), rows_low, rows_f32, column_f32],
            [w_qkv, w_o, pltpu.VMEM((tokens, tokens), f32), copy_sems],
            (ids, lengths, x, cell_ids, cell_col, qkv_bias, small) + attn_weights(layer),
        )
        order.last = outs[-1]
        return outs

    def ffn_forward(layer, unit_one):
        unit_one = order.after(unit_one)
        outs = call(
            functools.partial(ffn_fwd_kernel, layer),
            "ffn_fwd",
            [SMEM] + [VMEM] * 3 + [ANY] * 12,
            [VMEM] * 5,
            [shape((tokens, ffn), low), shape((tokens, ffn), f32), rows_f32, column_f32, rows_low],
            [w_in, w_out, pltpu.VMEM((tokens, width), low), copy_sems],
            (ids, unit_one, full_in_bias, small) + ffn_weights(layer),
        )
        order.last = outs[-2]
        return outs

    def ffn_backward(layer, grad, unit_two, inverse_two, unit_one, inverse_one, hidden, slope):
        grad = order.after(grad)
        outs = call(
            functools.partial(ffn_bwd_kernel, layer),
            "ffn_bwd",
            [SMEM] + [VMEM] * 8 + [ANY] * 12,
            [VMEM] * 3 + [ANY] * 4,
            [rows_f32, shape((8, width), f32), shape((1, ffn), f32)] + [pieces] * 4,
            [
                w_in,
                w_out,
                pltpu.VMEM((tokens, width), low),
                pltpu.VMEM((tokens, width), f32),
                pltpu.VMEM((tokens, ffn), low),
                pltpu.VMEM((width, tokens), low),
                stage,
                stage,
                copy_sems,
                pltpu.SemaphoreType.DMA((4,)),
            ],
            (ids, grad, unit_two, inverse_two, unit_one, inverse_one, hidden, slope, small) + ffn_weights(layer),
        )
        order.last = outs[1]
        return outs

    def attn_backward(layer, d_resid, x, qkv_rows, probs, context):
        d_resid = order.after(d_resid)
        outs = call(
            functools.partial(attn_bwd_kernel, layer),
            "attn_bwd",
            [SMEM] + [VMEM] * 5 + [ANY] * 8,
            [VMEM] * 2 + [ANY] * 2,
            [rows_low, shape((8, width), f32), pieces, pieces],
            [
                w_qkv,
                w_o,
                pltpu.VMEM((tokens, width), low),
                pltpu.VMEM((tokens, width), low),
                pltpu.VMEM((tokens, 3 * width), low),
                pltpu.VMEM((width, tokens), low),
                stage,
                copy_sems,
                pltpu.SemaphoreType.DMA((2,)),
            ],
            (ids, d_resid, x, qkv_rows, probs, context) + attn_weights(layer),
        )
        order.last = outs[1]
        return outs

    def unpack(layer, slab, near, far, earlier):
        dims = {
            "attn": [(layers, share, 3 * width), (layers, share, width)],
            "in": [(layers, share, ffn)],
            "out": [(layers, ffn_share, width)],
        }[slab]
        near, far = order.after((near, far))
        outs = call(
            functools.partial(unpack_kernel, layer, slab),
            "unpack",
            [SMEM] + [ANY] * (2 + len(earlier)),
            [ANY] * len(dims),
            [shape(d, f32) for d in dims],
            [
                pltpu.VMEM((8, share, tile), low),
                pltpu.VMEM((8, share, tile), f32),
                pltpu.SemaphoreType.DMA((8,)),
                pltpu.SemaphoreType.DMA((8,)),
            ],
            (ids, near, far, *earlier),
            {3 + i: i for i in range(len(earlier))},
        )
        return outs

    arrive(("x", 0), ("y", 0), ("x", 1), ("d", 0), ("x", 2))
    first_attn = attn_forward(0, tables_in)
    arrive(("x", 3), ("y", 1), ("y", 2), ("d", 1), ("d", 2))
    first_ffn = ffn_forward(0, first_attn[3])
    arrive(("x", 4), ("y", 3), ("d", 3))
    second_attn = attn_forward(1, first_ffn[4])
    arrive(("x", 5), ("y", 4), ("y", 5), ("d", 4), ("d", 5))
    second_ffn = ffn_forward(1, second_attn[3])
    mixed_out = second_ffn[4]
    inputs = (tables_in, first_ffn[4])
    attn_kept, ffn_kept = (first_attn, second_attn), (first_ffn, second_ffn)

    ways = ("xyzw", "yxzw", "xyzw", "xyzw", "xyzw", "yxzw")
    kernels = (("ffn1", 17, (0, 1)), ("attn1", 16, (2,)), ("ffn0", 17, (3, 4)), ("attn0", 16, (5,)))
    slabs = [None] * 6
    grad = cotangent
    attn_small, ffn_small, in_bias_grads = [None] * layers, [None] * layers, [None] * layers
    unpacked = {"attn": (), "in": (), "out": ()}
    small_sums = None
    small_steps = [("narrow", 1), ("narrow", 2)] + [("wide", 1 << b) for b in range(wide_bits)]
    steps_left = 0
    for action, which in plan(ways, kernels, width * ffn * 2e-6):
        if action == "kernel":
            layer = int(which[-1])
            _, _, _, unit_one, inverse_one = attn_kept[layer]
            if which[:-1] == "ffn":
                hidden, slope, unit_two, inverse_two, _ = ffn_kept[layer]
                d_resid, ffn_small[layer], in_bias_grads[layer], in_kept, in_sent, out_kept, out_sent = ffn_backward(
                    layer, grad, unit_two, inverse_two, unit_one, inverse_one, hidden, slope
                )
                base = 3 * (layers - 1 - layer)
                slabs[base] = Slab(ways[base], wide_bits, out_kept, out_sent)
                slabs[base + 1] = Slab(ways[base + 1], wide_bits, in_kept, in_sent)
            else:
                qkv_rows, probs, context, _, _ = attn_kept[layer]
                grad, attn_small[layer], kept, sent = attn_backward(
                    layer, d_resid, inputs[layer], qkv_rows, probs, context
                )
                base = 3 * (layers - 1 - layer) + 2
                slabs[base] = Slab(ways[base], wide_bits, kept, sent)
            if which == "attn0":
                small_sums = jnp.stack(
                    [
                        jnp.concatenate([attn_small[i][:3], ffn_small[i][:5], in_bias_grads[i].reshape(4, width)])
                        for i in range(layers)
                    ]
                )
                small_sums = order.after(small_sums)
                steps_left = len(small_steps)
            continue
        slab = slabs[which]
        slab.step(order)
        if steps_left:
            axis, bit = small_steps[-steps_left]
            small_sums = order.wait(small_sums + swap(small_sums, axis, bit))
            steps_left -= 1
            if not steps_left:
                rows = lax.dynamic_slice(small_sums, (0, 0, me * share), (layers, 8, share))
                in_rows = lax.dynamic_slice(small_sums, (0, 8 + me, 0), (layers, 1, ffn_share))
                vectors = [rows[:, i] for i in range(8)] + [in_rows[:, 0]]
        if slab.stage == len(ways[which]) + len(BACK) + 1:
            name = ("out", "in", "attn")[which % 3]
            if which == len(slabs) - 1:
                vectors = order.wait(vectors)
            unpacked[name] = unpack(
                layers - 1 - which // 3, name, slab.block, slab.far, unpacked[name]
            )
    qkv_grad, o_grad = unpacked["attn"]
    (in_grad,), (out_grad,) = unpacked["in"], unpacked["out"]
    return (
        mixed_out,
        grad,
        qkv_grad,
        vectors[0],
        vectors[1],
        o_grad,
        vectors[2],
        vectors[6],
        vectors[7],
        in_grad,
        vectors[8],
        out_grad,
        vectors[5],
        vectors[3],
        vectors[4],
    )


def solution(mesh):
    by_table = P(("wide", "narrow"), None)
    matrix = P(None, "narrow", None)
    vector = P(None, "narrow")
    return jax.shard_map(
        body,
        mesh=mesh,
        in_specs=(
            by_table,
            by_table,
            by_table,
            P(("wide", "narrow")),
            matrix,
            vector,
            vector,
            matrix,
            vector,
            vector,
            vector,
            matrix,
            vector,
            matrix,
            vector,
            vector,
            vector,
        ),
        out_specs=(
            by_table,
            by_table,
            matrix,
            vector,
            vector,
            matrix,
            vector,
            vector,
            vector,
            matrix,
            vector,
            matrix,
            vector,
            vector,
            vector,
        ),
        check_vma=False,
    )
```

```python
import functools
import math

import jax
import jax.numpy as jnp
from jax import lax
from jax.experimental import pallas as pl
from jax.experimental.pallas import tpu as pltpu
from jax.sharding import PartitionSpec as P

HEADS = 12
norm_eps = 1e-12
masked_score = -1000000000.0
low = jnp.bfloat16
f32 = jnp.float32
VMEM_BYTES = 56 * 1024 * 1024
HALVINGS = 3


def swap(value, axis, bit):
    count = lax.axis_size(axis)
    return lax.ppermute(value, axis, [(i, i ^ bit) for i in range(count)])


def dot(a, b):
    return jnp.dot(a, b, preferred_element_type=f32)


def dot_nt(a, b):
    return lax.dot_general(a, b, (((1,), (1,)), ((), ())), preferred_element_type=f32)


def dot_tn(a, b):
    return lax.dot_general(a, b, (((0,), (0,)), ((), ())), preferred_element_type=f32)


def normalize(residual):
    center = residual - jnp.mean(residual, axis=-1, keepdims=True)
    inverse = lax.rsqrt(jnp.mean(center * center, axis=-1, keepdims=True) + norm_eps)
    return center * inverse, inverse


def normalize_back(grad_unit, unit, inverse):
    centered = grad_unit - jnp.mean(grad_unit, axis=-1, keepdims=True)
    return inverse * (centered - unit * jnp.mean(grad_unit * unit, axis=-1, keepdims=True))


def weight_copies(ids, layer, pieces, target, columns, sems, base):
    own, core, near_x, far_x, diagonal = pieces
    rows = own.shape[1]
    half = rows // 2
    n, y = ids[0], ids[4]
    copies = []

    def add(source, start, count):
        where = target.at[pl.ds(pl.multiple_of(start, half), count), :]
        copies.append(pltpu.make_async_copy(source, where, sems.at[base + len(copies)]))

    at = pl.ds(columns, target.shape[1])
    add(own.at[layer], n * rows, rows)
    add(core.at[layer], ids[1] * rows, rows)
    add(near_x.at[:, at], ids[2] * rows + y * half, half)
    add(far_x.at[:, at], ids[2] * rows + (1 - y) * half, half)
    add(diagonal.at[pl.ds(0, half), at], ids[3] * rows + y * half, half)
    add(diagonal.at[pl.ds(half, half), at], ids[3] * rows + (1 - y) * half, half)
    return copies


def begin(copies):
    for copy in copies:
        copy.start()


def finish(copies):
    for copy in copies:
        copy.wait()


def attn_copies(layer, ids, refs, w_qkv, w_o, sems):
    qkv_own, qkv_core, o_own, o_core = refs[:4]
    halves = refs[4:]
    qkv = weight_copies(ids, layer, (qkv_own, qkv_core) + halves, w_qkv, 0, sems, 0)
    o = weight_copies(ids, layer, (o_own, o_core) + halves, w_o, w_qkv.shape[1], sems, 6)
    return qkv, o


def ffn_copies(layer, ids, refs, w_in, w_out, sems):
    in_copies = weight_copies(ids, layer, refs[:5], w_in, 0, sems, 0)
    out_copies = weight_copies(ids, layer, refs[5:], w_out, 0, sems, 6)
    return in_copies, out_copies


def attn_fwd_kernel(layer, ids, length, x, cell_row, small, *rest):
    weights, rest = rest[:7], rest[7:]
    qkv_rows, probs, context, unit_out, inverse_out, w_qkv, w_o, mask, sems = rest
    tokens, width = x.shape
    qkv_copies, o_copies = attn_copies(layer, ids, weights, w_qkv, w_o, sems)
    begin(qkv_copies)
    begin(o_copies)
    position = lax.broadcasted_iota(jnp.int32, (1, tokens), 1)
    key_cell = cell_row[...]
    square = (tokens, tokens)
    diagonal = lax.broadcasted_iota(jnp.int32, square, 0) == lax.broadcasted_iota(jnp.int32, square, 1)
    query_cell = jnp.sum(jnp.where(diagonal, key_cell, 0), axis=1, keepdims=True)
    allowed = (query_cell == key_cell) | (key_cell == 0) | (query_cell == 0)
    allowed = allowed & (position < length[0])
    mask[...] = jnp.where(allowed, 0.0, masked_score)
    scale = 1.0 / math.sqrt(width // HEADS)
    finish(qkv_copies)
    tile = width // 2

    for t in range(6):
        columns = slice(t * tile, (t + 1) * tile)
        rows = dot(x[...], w_qkv[:, columns])
        if t // 2 != 1:
            part = slice((t % 2) * tile, (t % 2 + 1) * tile)
            rows = rows + small[layer, t // 4 : t // 4 + 1, part]
        if t < 2:
            rows = rows * scale
        qkv_rows[:, columns] = rows.astype(low)

    pair_width = 2 * width // HEADS
    first = lax.broadcasted_iota(jnp.int32, (1, pair_width), 1) < pair_width // 2

    @pl.loop(0, HEADS // 2)
    def _(pair):
        start = pl.multiple_of(pair * pair_width, pair_width)
        query = qkv_rows[:, pl.ds(start, pair_width)]
        key = qkv_rows[:, pl.ds(width + start, pair_width)]
        value = qkv_rows[:, pl.ds(2 * width + start, pair_width)]
        sides = []
        for side in range(2):
            mine = first if side == 0 else jnp.logical_not(first)
            scores = dot_nt(jnp.where(mine, query, jnp.zeros_like(query)), key) + mask[...]
            shifted = jnp.exp(scores - jnp.max(scores, axis=-1, keepdims=True))
            total = jnp.sum(shifted, axis=-1, keepdims=True)
            prob = (shifted / total).astype(low)
            probs[2 * pair + side] = prob
            sides.append(dot(prob, value))
        context[:, pl.ds(start, pair_width)] = jnp.where(first, sides[0], sides[1]).astype(low)

    finish(o_copies)
    residual = x[...].astype(f32) + (dot(context[...], w_o[...]) + small[layer, 2:3, :])
    unit, inverse = normalize(residual)
    unit_out[...] = unit
    inverse_out[...] = inverse


def ffn_fwd_kernel(layer, ids, unit_one, in_bias, small, *rest):
    weights, rest = rest[:10], rest[10:]
    hidden, slope, unit_out, inverse_out, result, w_in, w_out, normed_low, sems = rest
    in_copies, out_copies = ffn_copies(layer, ids, weights, w_in, w_out, sems)
    begin(in_copies)
    begin(out_copies)
    normed = unit_one[...] * small[layer, 3:4, :] + small[layer, 4:5, :]
    normed_low[...] = normed.astype(low)
    finish(in_copies)
    tile = w_in.shape[1] // 8

    @pl.loop(0, 8)
    def _(t):
        columns = pl.ds(pl.multiple_of(t * tile, tile), tile)
        pre = dot(normed_low[...], w_in[:, columns]) + in_bias[layer, :, columns]
        cdf = 0.5 * (1.0 + lax.erf(pre * (1.0 / math.sqrt(2.0))))
        density = jnp.exp(-0.5 * pre * pre) * (1.0 / math.sqrt(2.0 * math.pi))
        hidden[:, columns] = (pre * cdf).astype(low)
        slope[:, columns] = cdf + pre * density

    finish(out_copies)
    residual = unit_one[...] * small[layer, 3:4, :] + small[layer, 4:5, :] + (dot(hidden[...], w_out[...]) + small[layer, 5:6, :])
    unit, inverse = normalize(residual)
    unit_out[...] = unit
    inverse_out[...] = inverse
    result[...] = (unit * small[layer, 6:7, :] + small[layer, 7:8, :]).astype(low)


WIDE_BIT = {"y": 2, "z": 1, "w": 0}


def place_of(ids, owner, piece, way):
    away, off = ids[0] ^ owner, piece ^ ids[5]
    return (away & 1,) + tuple(away >> 1 if name == "x" else (off >> WIDE_BIT[name]) & 1 for name in way)


def store_rows(stage, ids, product, piece, way):
    share = product.shape[0] // 4
    for owner in range(4):
        block = product[owner * share : (owner + 1) * share].astype(low)
        stage[place_of(ids, owner, piece, way) + (pl.ds(0, share),)] = block


def send_out(stage, kept, sent, sems):
    copies = [
        pltpu.make_async_copy(stage.at[1], sent, sems.at[0]),
        pltpu.make_async_copy(stage.at[0], kept, sems.at[1]),
    ]
    begin(copies)
    return copies


def out_bwd_kernel(layer, way, ids, grad, unit_two, inverse_two, hidden, small, *rest):
    d_ffn, d_resid_two, small_grads, kept, sent, stage, out_sems = rest
    g = grad[...].astype(f32)
    unit = unit_two[...]
    small_grads[0:1, :] = jnp.sum(g * unit, axis=0, keepdims=True)
    small_grads[1:2, :] = jnp.sum(g, axis=0, keepdims=True)
    d_two = normalize_back(g * small[layer, 6:7, :], unit, inverse_two[...])
    d_resid_two[...] = d_two
    d_low = d_two.astype(low)
    d_ffn[...] = d_low
    small_grads[2:3, :] = jnp.sum(d_low.astype(f32), axis=0, keepdims=True)
    small_grads[3:8, :] = jnp.zeros((5, unit.shape[1]), f32)
    tile = hidden.shape[1] // 8
    share = d_ffn.shape[1] // 4

    @pl.loop(0, 8)
    def _(t):
        columns = pl.ds(pl.multiple_of(t * tile, tile), tile)
        out_grad = dot_tn(hidden[:, columns], d_ffn[...])
        for row_group in range(2):
            for column_group in range(2):
                piece = ((t % 2) * 2 + row_group) * 2 + column_group
                block = out_grad[
                    row_group * share : (row_group + 1) * share,
                    column_group * tile : (column_group + 1) * tile,
                ]
                stage[place_of(ids, t // 2, piece, way)] = block.astype(low)

    finish(send_out(stage, kept, sent, out_sems))


def in_bwd_kernel(layer, way, ids, d_ffn, d_resid_two, unit_one, inverse_one, slope, small, *rest):
    weights, rest = rest[:10], rest[10:]
    d_resid, small_grads, in_bias_grad, kept, sent = rest[:5]
    w_in, w_out, d_pre, normed_t, stage, sems, out_sems = rest[5:]
    in_copies, out_copies = ffn_copies(layer, ids, weights, w_in, w_out, sems)
    begin(out_copies)
    begin(in_copies)
    normed = unit_one[...] * small[layer, 3:4, :] + small[layer, 4:5, :]
    normed_t[...] = normed.astype(low).T
    finish(out_copies)
    tile = w_in.shape[1] // 8

    @pl.loop(0, 8)
    def _(t):
        columns = pl.ds(pl.multiple_of(t * tile, tile), tile)
        d_hidden = dot_nt(d_ffn[...], w_out[columns, :])
        d_tile = (d_hidden * slope[:, columns]).astype(low)
        d_pre[:, columns] = d_tile
        in_bias_grad[:, columns] = jnp.sum(d_tile.astype(f32), axis=0, keepdims=True)
        store_rows(stage, ids, dot(normed_t[...], d_tile), t, way)

    going = send_out(stage, kept, sent, out_sems)
    finish(in_copies)
    d_normed = d_resid_two[...] + dot_nt(d_pre[...], w_in[...])
    unit = unit_one[...]
    small_grads[0:1, :] = jnp.sum(d_normed * unit, axis=0, keepdims=True)
    small_grads[1:2, :] = jnp.sum(d_normed, axis=0, keepdims=True)
    small_grads[2:8, :] = jnp.zeros((6, unit.shape[1]), f32)
    d_resid[...] = normalize_back(d_normed * small[layer, 3:4, :], unit, inverse_one[...])
    finish(going)


def attn_bwd_kernel(layer, way, ids, d_resid, x, qkv_rows, probs, context, *rest):
    weights, others, rest = rest[:7], rest[7:-13], rest[-13:]
    d_input, small_grads, kept, sent = rest[:4]
    w_qkv, w_o, d_attn, d_context, d_qkv, x_t, stage, sems, out_sems = rest[4:]
    tokens, width = x.shape
    qkv_copies, o_copies = attn_copies(layer, ids, weights, w_qkv, w_o, sems)
    begin(o_copies)
    begin(qkv_copies)
    d_low = d_resid[...].astype(low)
    d_attn[...] = d_low
    small_grads[2:3, :] = jnp.sum(d_low.astype(f32), axis=0, keepdims=True)
    x_t[...] = x[...].T
    tile = width // 2
    for half in range(2):
        product = dot_tn(context[...], d_attn[:, half * tile : (half + 1) * tile])
        store_rows(stage, ids, product, 6 + half, way)
    finish(o_copies)
    d_context[...] = dot_nt(d_attn[...], w_o[...]).astype(low)
    pair_width = 2 * width // HEADS
    first = lax.broadcasted_iota(jnp.int32, (1, pair_width), 1) < pair_width // 2
    scale = 1.0 / math.sqrt(width // HEADS)

    @pl.loop(0, HEADS // 2)
    def _(pair):
        start = pl.multiple_of(pair * pair_width, pair_width)
        at_query = pl.ds(start, pair_width)
        at_key = pl.ds(width + start, pair_width)
        at_value = pl.ds(2 * width + start, pair_width)
        query, key, value = qkv_rows[:, at_query], qkv_rows[:, at_key], qkv_rows[:, at_value]
        d_ctx = d_context[:, at_query]
        sides = []
        for side in range(2):
            mine = first if side == 0 else jnp.logical_not(first)
            prob_low = probs[2 * pair + side]
            prob = prob_low.astype(f32)
            d_prob = dot_nt(jnp.where(mine, d_ctx, jnp.zeros_like(d_ctx)), value)
            inner = jnp.sum(prob * d_prob, axis=-1, keepdims=True)
            d_scores = (prob * (d_prob - inner)).astype(low)
            sides.append((dot(d_scores, key), dot_tn(d_scores, query), dot_tn(prob_low, d_ctx)))
        d_qkv[:, at_query] = (jnp.where(first, sides[0][0], sides[1][0]) * scale).astype(low)
        d_qkv[:, at_key] = jnp.where(first, sides[0][1], sides[1][1]).astype(low)
        d_qkv[:, at_value] = jnp.where(first, sides[0][2], sides[1][2]).astype(low)

    @pl.loop(0, 6)
    def _(t):
        columns = pl.ds(pl.multiple_of(t * tile, tile), tile)
        store_rows(stage, ids, dot(x_t[...], d_qkv[:, columns]), t, way)

    small_grads[0:1, :] = jnp.sum(d_qkv[:, :width].astype(f32), axis=0, keepdims=True)
    small_grads[1:2, :] = jnp.sum(d_qkv[:, 2 * width :].astype(f32), axis=0, keepdims=True)
    small_grads[3:8, :] = jnp.zeros((5, width), f32)
    if others:
        share = width // 4
        sources = small_sources(layer, small_grads, others)
        for owner in range(4):
            for piece in range(8):
                lines = []
                for source, row, start, step in sources[3 * piece : 3 * piece + 3]:
                    line = source[row : row + 1, start + owner * step : start + owner * step + share]
                    lines.append(jnp.concatenate([line, jnp.zeros_like(line)], axis=1))
                lines.append(jnp.zeros((SMALL_ROWS - 3, tile), f32))
                block = jnp.concatenate(lines, axis=0).astype(low)
                stage[place_of(ids, owner, piece, way) + (pl.ds(share, SMALL_ROWS),)] = block
    going = send_out(stage, kept, sent, out_sems)
    finish(qkv_copies)
    d_input[...] = (d_resid[...] + dot_nt(d_qkv[...], w_qkv[...])).astype(low)
    finish(going)


SMALL_ROWS = 16
SMALL_LINES = (("attn", 0), ("attn", 1), ("attn", 2), ("in", 0), ("in", 1), ("out", 2), ("out", 0), ("out", 1))


def small_sources(layer, own, others):
    found = []
    out_0, in_0, bias_0, out_1, in_1, bias_1, attn_1 = others
    refs = ({"attn": own, "in": in_0, "out": out_0}, {"attn": attn_1, "in": in_1, "out": out_1})
    width = own.shape[1]
    for of_layer, bias in zip(refs, (bias_0, bias_1)):
        found += [(of_layer[name], row, 0, width // 4) for name, row in SMALL_LINES]
        found += [(bias, 0, i * (width // 4), width) for i in range(4)]
    return found


def unpack_kernel(layer, slab, back, earlier, ids, near, far, *rest):
    outs = rest[earlier:-4]
    buffer, wide_buffer, in_sems, out_sems = rest[-4:]
    share, tile = wide_buffer.shape[1:]

    def fetch(piece, ref, index):
        return pltpu.make_async_copy(ref.at[index], buffer.at[piece], in_sems.at[piece])

    for piece in range(8):
        off = piece ^ ids[5]
        bits = [(off >> WIDE_BIT[name]) & 1 for name in back]
        index = bits[1] * 2 + bits[0]

        @pl.when(bits[2] == 0)
        def _():
            fetch(piece, near, index).start()

        @pl.when(bits[2] == 1)
        def _():
            fetch(piece, far, index).start()

    copies = []
    for piece in range(8):
        fetch(piece, near, 0).wait()
        wide_buffer[piece] = buffer[piece, :share].astype(f32)
        columns = pl.ds(piece * tile, tile)
        if slab == "in":
            target = outs[0].at[layer, :, columns]
        elif slab == "out":
            rows = pl.ds((piece // 2) * share, share)
            target = outs[0].at[layer, rows, pl.ds((piece % 2) * tile, tile)]
        elif piece < 6:
            target = outs[0].at[layer, :, columns]
        else:
            target = outs[1].at[layer, :, pl.ds((piece - 6) * tile, tile)]
        copies.append(pltpu.make_async_copy(wide_buffer.at[piece], target, out_sems.at[piece]))
        copies[-1].start()
    if slab == "attn" and layer == 0:
        for line in range(24):
            of_layer, which = line // 12, line % 12
            row = share + line % 3
            values = buffer[line // 3, row : row + 1, :share].astype(f32)
            if which < 8:
                outs[2 + which][of_layer : of_layer + 1, :] = values
            else:
                at = (which - 8) * share
                outs[10][of_layer : of_layer + 1, at : at + share] = values
    else:
        outs[-1][...] = jnp.zeros(outs[-1].shape, f32)
    finish(copies)


SMEM = pl.BlockSpec(memory_space=pltpu.SMEM)
VMEM = pl.BlockSpec(memory_space=pltpu.VMEM)
ANY = pl.BlockSpec(memory_space=pl.ANY)


def call(kernel, name, in_specs, out_specs, out_shape, scratch, args, aliases=()):
    return pl.pallas_call(
        kernel,
        name=name,
        in_specs=in_specs,
        out_specs=out_specs,
        out_shape=out_shape,
        scratch_shapes=scratch,
        input_output_aliases=dict(aliases),
        compiler_params=pltpu.CompilerParams(vmem_limit_bytes=VMEM_BYTES),
        cost_estimate=pl.CostEstimate(flops=1, bytes_accessed=1, transcendentals=0),
    )(*args)


def shape(dims, kind):
    return jax.ShapeDtypeStruct(dims, kind)


def reverse_bits(value, bits):
    result = jnp.zeros_like(value)
    for bit in range(bits):
        result = result | (((value >> bit) & 1) << (bits - 1 - bit))
    return result


def added(a, b):
    return (a.astype(f32) + b.astype(f32)).astype(low)


WAYS = ("xyzw", "yxzw", "xyzw", "xyzw", "xyzw", "xyzw")
BACKS = ("wzy",) * 6
PLAN = (
    "out1", "in1", 0, "attn1", "out0", 0, 2, 1, 3, 0, "in0", 0, 2, 0, 0, 1, 2, 0, 3, 2, 4, 1, 0, "attn0", 2,
    3, 1, 5, 4, 3, 2, 3, 2, 4, 1, 3, 5, 4, 1, 3, 4, 5, 1, 5, 4, 5, 4, 5, 3, 5, 4, 1, 2, 5,
)


class Order:
    def __init__(self):
        self.last = None

    def after(self, values):
        if self.last is None:
            return values
        values, self.last = lax.optimization_barrier((values, self.last))
        return values

    def wait(self, values):
        values = self.after(values)
        self.last = values
        return values


STEPS = {"x": ("narrow", 2), "y": ("wide", 1), "z": ("wide", 2), "w": ("wide", 4)}


class Slab:
    def __init__(self, way, back, wide_bits, kept, sent):
        self.way, self.back, self.wide_bits = way, back, wide_bits
        self.kept = kept
        self.flying = swap(sent, "narrow", 1)
        self.stage = 0

    def step(self, order):
        received = order.after(self.flying)
        if self.stage < len(self.way):
            send = added(self.kept[1], received[1])
            self.kept = added(self.kept[0], received[0])
            self.flying = swap(send, *STEPS[self.way[self.stage]])
            order.last = send
        elif self.stage == len(self.way):
            piece = added(self.kept, received)
            for b in range(HALVINGS, self.wide_bits):
                piece = added(piece, swap(piece, "wide", 1 << b))
            self.block = piece[None]
            order.last = self.block
            self.flying = swap(self.block, *STEPS[self.back[0]])
        elif self.stage < len(self.way) + len(self.back):
            self.block = jnp.concatenate([self.block, received], axis=0)
            order.last = self.block
            self.flying = swap(self.block, *STEPS[self.back[self.stage - len(self.way)]])
        else:
            self.far = received
        self.stage += 1

    def ended(self):
        return self.stage == len(self.way) + len(self.back) + 1


def body(
    tables_in,
    cotangent,
    cell_ids,
    lengths,
    qkv_weight,
    q_bias,
    v_bias,
    o_weight,
    o_bias,
    norm1_gain,
    norm1_bias,
    in_weight,
    in_bias,
    out_weight,
    out_bias,
    norm2_gain,
    norm2_bias,
):
    tokens, width = tables_in.shape
    layers, share, ffn = in_weight.shape
    ffn_share = out_weight.shape[1]
    wide_count = lax.axis_size("wide")
    wide_bits = wide_count.bit_length() - 1
    assert wide_count == 1 << wide_bits and wide_bits >= HALVINGS and lax.axis_size("narrow") == 4
    tile = ffn // 8
    me = lax.axis_index("narrow").astype(jnp.int32)
    wide_me = lax.axis_index("wide").astype(jnp.int32)
    y = wide_me & 1
    place = reverse_bits(wide_me & (2**HALVINGS - 1), HALVINGS)
    ids = jnp.stack([me, me ^ 1, me ^ 2, me ^ 3, y, place])

    order = Order()

    def half_of(weight, layer):
        rows = weight.shape[1] // 2
        return lax.dynamic_slice(weight, (layer, y * rows, 0), (1, rows, weight.shape[2]))[0]

    halves = []
    for layer in range(layers):
        joint = jnp.concatenate([half_of(qkv_weight, layer), half_of(o_weight, layer)], axis=1)
        halves += [joint, half_of(in_weight, layer), half_of(out_weight, layer)]
    near_x, far_x, diagonal = [None] * len(halves), [None] * len(halves), [None] * len(halves)
    core = [None] * 4
    own = (qkv_weight, o_weight, in_weight, out_weight)

    def send_x(*which):
        for i in which:
            near_x[i] = swap(order.after(halves[i]), "narrow", 2)

    def send_core(i):
        core[i] = swap(order.after(own[i]), "narrow", 1)

    def arrive(*events):
        for kind, i in events:
            if kind == "x":
                near_x[i] = order.wait(near_x[i])
                far_x[i] = swap(near_x[i], "wide", 1)
            elif kind == "y":
                far_x[i] = order.wait(far_x[i])
                both = jnp.concatenate([near_x[i], far_x[i]], axis=0)
                order.last = both
                diagonal[i] = swap(both, "narrow", 1)
            elif kind == "d":
                diagonal[i] = order.wait(diagonal[i])
            else:
                core[i] = order.wait(core[i])

    def group(i):
        return near_x[i], far_x[i], diagonal[i]

    def attn_weights(layer):
        return (qkv_weight, core[0], o_weight, core[1]) + group(3 * layer)

    def ffn_weights(layer):
        return (in_weight, core[2]) + group(3 * layer + 1) + (out_weight, core[3]) + group(3 * layer + 2)

    send_x(0)
    short = [q_bias, v_bias, o_bias, norm1_gain, norm1_bias, out_bias, norm2_gain, norm2_bias]
    packed = jnp.concatenate([jnp.stack(short, axis=1), in_bias.reshape(layers, 4, share)], axis=1)
    others = [
        lax.ppermute(packed, "narrow", [(i, i ^ away) for i in range(4)]) for away in (1, 2, 3)
    ]
    send_core(0)
    arrive(("c", 0))
    near_x[0], others = order.wait((near_x[0], others))
    far_x[0] = swap(near_x[0], "wide", 1)
    send_x(1, 2)
    send_core(1)

    def in_order(low_one, high_one, bit):
        swapped = (me & bit) != 0
        return jnp.stack([jnp.where(swapped, high_one, low_one), jnp.where(swapped, low_one, high_one)])

    packed = in_order(in_order(packed, others[0], 1), in_order(others[1], others[2], 1), 2)
    packed = packed.reshape(4, layers, 12, share).astype(f32)
    small = packed[:, :, :8].transpose(1, 2, 0, 3).reshape(layers, 8, width)
    full_in_bias = packed[:, :, 8:].transpose(1, 0, 2, 3).reshape(layers, 1, ffn)
    ids, small, full_in_bias = order.wait((ids, small, full_in_bias))
    arrive(("c", 1))
    send_core(2)
    arrive(("c", 2))
    send_core(3)

    w_qkv = pltpu.VMEM((width, 3 * width), low)
    w_o = pltpu.VMEM((width, width), low)
    w_in = pltpu.VMEM((width, ffn), low)
    w_out = pltpu.VMEM((ffn, width), low)
    copy_sems = pltpu.SemaphoreType.DMA((12,))
    pair_sems = pltpu.SemaphoreType.DMA((2,))
    rows_f32 = shape((tokens, width), f32)
    rows_low = shape((tokens, width), low)
    column_f32 = shape((tokens, 1), f32)
    eight_f32 = shape((8, width), f32)

    def pieces(rows):
        return [shape((2, 2, 2, 2, rows, tile), low)] * 2

    def stage(rows):
        return pltpu.VMEM((2, 2, 2, 2, 2, rows, tile), low)

    def attn_forward(layer, x):
        x = order.after(x)
        outs = call(
            functools.partial(attn_fwd_kernel, layer),
            "attn_fwd",
            [SMEM, SMEM] + [VMEM] * 3 + [ANY] * 7,
            [VMEM] * 5,
            [shape((tokens, 3 * width), low), shape((HEADS, tokens, tokens), low), rows_low, rows_f32, column_f32],
            [w_qkv, w_o, pltpu.VMEM((tokens, tokens), f32), copy_sems],
            (ids, lengths, x, cell_ids, small) + attn_weights(layer),
        )
        order.last = outs[-1]
        return outs

    def ffn_forward(layer, unit_one):
        unit_one = order.after(unit_one)
        outs = call(
            functools.partial(ffn_fwd_kernel, layer),
            "ffn_fwd",
            [SMEM] + [VMEM] * 3 + [ANY] * 10,
            [VMEM] * 5,
            [shape((tokens, ffn), low), shape((tokens, ffn), f32), rows_f32, column_f32, rows_low],
            [w_in, w_out, pltpu.VMEM((tokens, width), low), copy_sems],
            (ids, unit_one, full_in_bias, small) + ffn_weights(layer),
        )
        order.last = outs[-2]
        return outs

    def out_backward(layer, way, grad, unit_two, inverse_two, hidden):
        grad = order.after(grad)
        outs = call(
            functools.partial(out_bwd_kernel, layer, way),
            "out_bwd",
            [SMEM] + [VMEM] * 5,
            [VMEM] * 3 + [ANY] * 2,
            [rows_low, rows_f32, eight_f32] + pieces(share),
            [stage(share), pair_sems],
            (ids, grad, unit_two, inverse_two, hidden, small),
        )
        order.last = outs[2]
        return outs

    def in_backward(layer, way, d_ffn, d_resid_two, unit_one, inverse_one, slope):
        d_ffn = order.after(d_ffn)
        outs = call(
            functools.partial(in_bwd_kernel, layer, way),
            "in_bwd",
            [SMEM] + [VMEM] * 6 + [ANY] * 10,
            [VMEM] * 3 + [ANY] * 2,
            [rows_f32, eight_f32, shape((1, ffn), f32)] + pieces(share),
            [
                w_in,
                w_out,
                pltpu.VMEM((tokens, ffn), low),
                pltpu.VMEM((width, tokens), low),
                stage(share),
                copy_sems,
                pair_sems,
            ],
            (ids, d_ffn, d_resid_two, unit_one, inverse_one, slope, small) + ffn_weights(layer),
        )
        order.last = outs[1]
        return outs

    def attn_backward(layer, way, d_resid, x, qkv_rows, probs, context, small_others):
        d_resid = order.after(d_resid)
        rows = share + (SMALL_ROWS if small_others else 0)
        outs = call(
            functools.partial(attn_bwd_kernel, layer, way),
            "attn_bwd",
            [SMEM] + [VMEM] * 5 + [ANY] * 7 + [VMEM] * len(small_others),
            [VMEM] * 2 + [ANY] * 2,
            [rows_low, eight_f32] + pieces(rows),
            [
                w_qkv,
                w_o,
                pltpu.VMEM((tokens, width), low),
                pltpu.VMEM((tokens, width), low),
                pltpu.VMEM((tokens, 3 * width), low),
                pltpu.VMEM((width, tokens), low),
                stage(rows),
                copy_sems,
                pair_sems,
            ],
            (ids, d_resid, x, qkv_rows, probs, context) + attn_weights(layer) + tuple(small_others),
        )
        order.last = outs[1]
        return outs

    def unpack(layer, name, slab, earlier):
        dims = {
            "attn": [(layers, share, 3 * width), (layers, share, width)],
            "in": [(layers, share, ffn)],
            "out": [(layers, ffn_share, width)],
        }[name]
        last = name == "attn" and layer == 0
        extra = [(layers, share)] * 8 + [(layers, ffn_share)] if last else [(8, 128)]
        near, far = order.after((slab.block, slab.far))
        rows = near.shape[1]
        outs = call(
            functools.partial(unpack_kernel, layer, name, slab.back, len(earlier)),
            "unpack",
            [SMEM] + [ANY] * (2 + len(earlier)),
            [ANY] * len(dims) + [VMEM] * len(extra),
            [shape(d, f32) for d in dims + extra],
            [
                pltpu.VMEM((8, rows, tile), low),
                pltpu.VMEM((8, share, tile), f32),
                pltpu.SemaphoreType.DMA((8,)),
                pltpu.SemaphoreType.DMA((8,)),
            ],
            (ids, near, far, *earlier),
            {3 + i: i for i in range(len(earlier))},
        )
        order.last = outs[-1]
        return tuple(outs)

    arrive(("y", 0), ("x", 1))
    send_x(3)
    arrive(("c", 3), ("d", 0), ("x", 2))
    send_x(4)
    first_attn = attn_forward(0, tables_in)
    arrive(("x", 3))
    send_x(5)
    arrive(("y", 1), ("y", 2), ("d", 1), ("d", 2))
    first_ffn = ffn_forward(0, first_attn[3])
    arrive(("x", 4), ("y", 3), ("d", 3), ("x", 5))
    second_attn = attn_forward(1, first_ffn[4])
    arrive(("y", 4), ("y", 5), ("d", 4), ("d", 5))
    second_ffn = ffn_forward(1, second_attn[3])
    mixed_out = second_ffn[4]
    inputs = (tables_in, first_ffn[4])
    attn_kept, ffn_kept = (first_attn, second_attn), (first_ffn, second_ffn)

    slabs = [None] * 6
    grad = cotangent
    small_out, small_in, small_attn, bias_grads = [None] * 2, [None] * 2, [None] * 2, [None] * 2
    unpacked = {"attn": (), "in": (), "out": ()}
    for action in PLAN:
        if isinstance(action, int):
            slab = slabs[action]
            slab.step(order)
            if slab.ended():
                name = ("out", "in", "attn")[action % 3]
                unpacked[name] = unpack(layers - 1 - action // 3, name, slab, unpacked[name][: 2 if name == "attn" else 1])
            continue
        name, layer = action[:-1], int(action[-1])
        which = 3 * (layers - 1 - layer) + ("out", "in", "attn").index(name)
        way = WAYS[which]
        qkv_rows, probs, context, unit_one, inverse_one = attn_kept[layer]
        hidden, slope, unit_two, inverse_two, _ = ffn_kept[layer]
        if name == "out":
            d_ffn, d_resid_two, small_out[layer], kept, sent = out_backward(
                layer, way, grad, unit_two, inverse_two, hidden
            )
        elif name == "in":
            d_resid, small_in[layer], bias_grads[layer], kept, sent = in_backward(
                layer, way, d_ffn, d_resid_two, unit_one, inverse_one, slope
            )
        else:
            small_others = ()
            if layer == 0:
                small_others = (
                    small_out[0],
                    small_in[0],
                    bias_grads[0],
                    small_out[1],
                    small_in[1],
                    bias_grads[1],
                    small_attn[1],
                )
            grad, small_attn[layer], kept, sent = attn_backward(
                layer, way, d_resid, inputs[layer], qkv_rows, probs, context, small_others
            )
        slabs[which] = Slab(way, BACKS[which], wide_bits, kept, sent)
    qkv_grad, o_grad, *vectors = unpacked["attn"]
    in_grad, out_grad = unpacked["in"][0], unpacked["out"][0]
    return (
        mixed_out,
        grad,
        qkv_grad,
        vectors[0],
        vectors[1],
        o_grad,
        vectors[2],
        vectors[3],
        vectors[4],
        in_grad,
        vectors[8],
        out_grad,
        vectors[5],
        vectors[6],
        vectors[7],
    )


def solution(mesh):
    by_table = P(("wide", "narrow"), None)
    matrix = P(None, "narrow", None)
    vector = P(None, "narrow")
    return jax.shard_map(
        body,
        mesh=mesh,
        in_specs=(
            by_table,
            by_table,
            by_table,
            P(("wide", "narrow")),
            matrix,
            vector,
            vector,
            matrix,
            vector,
            vector,
            vector,
            matrix,
            vector,
            matrix,
            vector,
            vector,
            vector,
        ),
        out_specs=(
            by_table,
            by_table,
            matrix,
            vector,
            vector,
            matrix,
            vector,
            vector,
            vector,
            matrix,
            vector,
            matrix,
            vector,
            vector,
            vector,
        ),
        check_vma=False,
    )
```

```python
import functools
import math

import jax
import jax.numpy as jnp
from jax import lax
from jax.experimental import pallas as pl
from jax.experimental.pallas import tpu as pltpu
from jax.sharding import PartitionSpec as P

HEADS = 12
norm_eps = 1e-12
masked_score = -1000000000.0
low = jnp.bfloat16
f32 = jnp.float32
VMEM_BYTES = 56 * 1024 * 1024
HALVINGS = 3


def swap(value, axis, bit):
    count = lax.axis_size(axis)
    return lax.ppermute(value, axis, [(i, i ^ bit) for i in range(count)])


def dot(a, b):
    return jnp.dot(a, b, preferred_element_type=f32)


def dot_nt(a, b):
    return lax.dot_general(a, b, (((1,), (1,)), ((), ())), preferred_element_type=f32)


def dot_tn(a, b):
    return lax.dot_general(a, b, (((0,), (0,)), ((), ())), preferred_element_type=f32)


def normalize(residual):
    center = residual - jnp.mean(residual, axis=-1, keepdims=True)
    inverse = lax.rsqrt(jnp.mean(center * center, axis=-1, keepdims=True) + norm_eps)
    return center * inverse, inverse


def normalize_back(grad_unit, unit, inverse):
    centered = grad_unit - jnp.mean(grad_unit, axis=-1, keepdims=True)
    return inverse * (centered - unit * jnp.mean(grad_unit * unit, axis=-1, keepdims=True))


def weight_copies(ids, layer, pieces, target, columns, sems, base):
    own, core, near_x, far_x, diagonal = pieces
    rows = own.shape[1]
    half = rows // 2
    n, y = ids[0], ids[4]
    copies = []

    def add(source, start, count):
        where = target.at[pl.ds(pl.multiple_of(start, half), count), :]
        copies.append(pltpu.make_async_copy(source, where, sems.at[base + len(copies)]))

    at = pl.ds(columns, target.shape[1])
    add(own.at[layer], n * rows, rows)
    add(core.at[layer], ids[1] * rows, rows)
    add(near_x.at[:, at], ids[2] * rows + y * half, half)
    add(far_x.at[:, at], ids[2] * rows + (1 - y) * half, half)
    add(diagonal.at[pl.ds(0, half), at], ids[3] * rows + y * half, half)
    add(diagonal.at[pl.ds(half, half), at], ids[3] * rows + (1 - y) * half, half)
    return copies


def begin(copies):
    for copy in copies:
        copy.start()


def finish(copies):
    for copy in copies:
        copy.wait()


def attn_copies(layer, ids, refs, w_qkv, w_o, sems):
    qkv_own, qkv_core, o_own, o_core = refs[:4]
    halves = refs[4:]
    qkv = weight_copies(ids, layer, (qkv_own, qkv_core) + halves, w_qkv, 0, sems, 0)
    o = weight_copies(ids, layer, (o_own, o_core) + halves, w_o, w_qkv.shape[1], sems, 6)
    return qkv, o


def ffn_copies(layer, ids, refs, w_in, w_out, sems):
    in_copies = weight_copies(ids, layer, refs[:5], w_in, 0, sems, 0)
    out_copies = weight_copies(ids, layer, refs[5:], w_out, 0, sems, 6)
    return in_copies, out_copies


def attn_fwd_kernel(layer, ids, length, x, cell_row, small, *rest):
    weights, rest = rest[:7], rest[7:]
    qkv_rows, probs, context, unit_out, inverse_out, w_qkv, w_o, mask, sems = rest
    tokens, width = x.shape
    qkv_copies, o_copies = attn_copies(layer, ids, weights, w_qkv, w_o, sems)
    begin(qkv_copies)
    begin(o_copies)
    position = lax.broadcasted_iota(jnp.int32, (1, tokens), 1)
    key_cell = cell_row[...]
    square = (tokens, tokens)
    diagonal = lax.broadcasted_iota(jnp.int32, square, 0) == lax.broadcasted_iota(jnp.int32, square, 1)
    query_cell = jnp.sum(jnp.where(diagonal, key_cell, 0), axis=1, keepdims=True)
    allowed = (query_cell == key_cell) | (key_cell == 0) | (query_cell == 0)
    allowed = allowed & (position < length[0])
    mask[...] = jnp.where(allowed, 0.0, masked_score)
    scale = 1.0 / math.sqrt(width // HEADS)
    finish(qkv_copies)
    tile = width // 2

    for t in range(6):
        columns = slice(t * tile, (t + 1) * tile)
        rows = dot(x[...], w_qkv[:, columns])
        if t // 2 != 1:
            part = slice((t % 2) * tile, (t % 2 + 1) * tile)
            rows = rows + small[layer, t // 4 : t // 4 + 1, part]
        if t < 2:
            rows = rows * scale
        qkv_rows[:, columns] = rows.astype(low)

    pair_width = 2 * width // HEADS
    first = lax.broadcasted_iota(jnp.int32, (1, pair_width), 1) < pair_width // 2

    @pl.loop(0, HEADS // 2)
    def _(pair):
        start = pl.multiple_of(pair * pair_width, pair_width)
        query = qkv_rows[:, pl.ds(start, pair_width)]
        key = qkv_rows[:, pl.ds(width + start, pair_width)]
        value = qkv_rows[:, pl.ds(2 * width + start, pair_width)]
        sides = []
        for side in range(2):
            mine = first if side == 0 else jnp.logical_not(first)
            scores = dot_nt(jnp.where(mine, query, jnp.zeros_like(query)), key) + mask[...]
            shifted = jnp.exp(scores - jnp.max(scores, axis=-1, keepdims=True))
            total = jnp.sum(shifted, axis=-1, keepdims=True)
            prob = (shifted / total).astype(low)
            probs[2 * pair + side] = prob
            sides.append(dot(prob, value))
        context[:, pl.ds(start, pair_width)] = jnp.where(first, sides[0], sides[1]).astype(low)

    finish(o_copies)
    residual = x[...].astype(f32) + (dot(context[...], w_o[...]) + small[layer, 2:3, :])
    unit, inverse = normalize(residual)
    unit_out[...] = unit
    inverse_out[...] = inverse


def ffn_fwd_kernel(layer, ids, unit_one, in_bias, small, *rest):
    weights, rest = rest[:10], rest[10:]
    hidden, slope, unit_out, inverse_out, result, w_in, w_out, normed_low, sems = rest
    in_copies, out_copies = ffn_copies(layer, ids, weights, w_in, w_out, sems)
    begin(in_copies)
    begin(out_copies)
    normed = unit_one[...] * small[layer, 3:4, :] + small[layer, 4:5, :]
    normed_low[...] = normed.astype(low)
    finish(in_copies)
    tile = w_in.shape[1] // 8

    @pl.loop(0, 8)
    def _(t):
        columns = pl.ds(pl.multiple_of(t * tile, tile), tile)
        pre = dot(normed_low[...], w_in[:, columns]) + in_bias[layer, :, columns]
        cdf = 0.5 * (1.0 + lax.erf(pre * (1.0 / math.sqrt(2.0))))
        density = jnp.exp(-0.5 * pre * pre) * (1.0 / math.sqrt(2.0 * math.pi))
        hidden[:, columns] = (pre * cdf).astype(low)
        slope[:, columns] = cdf + pre * density

    finish(out_copies)
    residual = unit_one[...] * small[layer, 3:4, :] + small[layer, 4:5, :] + (dot(hidden[...], w_out[...]) + small[layer, 5:6, :])
    unit, inverse = normalize(residual)
    unit_out[...] = unit
    inverse_out[...] = inverse
    result[...] = (unit * small[layer, 6:7, :] + small[layer, 7:8, :]).astype(low)


WIDE_BIT = {"y": 2, "z": 1, "w": 0}


def place_of(ids, owner, piece, way):
    away, off = ids[0] ^ owner, piece ^ ids[5]
    return (away & 1,) + tuple(away >> 1 if name == "x" else (off >> WIDE_BIT[name]) & 1 for name in way)


def store_rows(stage, ids, product, piece, way):
    share = product.shape[0] // 4
    for owner in range(4):
        block = product[owner * share : (owner + 1) * share].astype(low)
        stage[place_of(ids, owner, piece, way) + (pl.ds(0, share),)] = block


def send_out(stage, kept, sent, sems):
    copies = [
        pltpu.make_async_copy(stage.at[1], sent, sems.at[0]),
        pltpu.make_async_copy(stage.at[0], kept, sems.at[1]),
    ]
    begin(copies)
    return copies


def out_bwd_kernel(layer, way, ids, grad, unit_two, inverse_two, hidden, small, *rest):
    d_ffn, d_resid_two, small_grads, kept, sent, stage, out_sems = rest
    g = grad[...].astype(f32)
    unit = unit_two[...]
    small_grads[0:1, :] = jnp.sum(g * unit, axis=0, keepdims=True)
    small_grads[1:2, :] = jnp.sum(g, axis=0, keepdims=True)
    d_two = normalize_back(g * small[layer, 6:7, :], unit, inverse_two[...])
    d_resid_two[...] = d_two
    d_low = d_two.astype(low)
    d_ffn[...] = d_low
    small_grads[2:3, :] = jnp.sum(d_low.astype(f32), axis=0, keepdims=True)
    small_grads[3:8, :] = jnp.zeros((5, unit.shape[1]), f32)
    tile = hidden.shape[1] // 8
    share = d_ffn.shape[1] // 4

    @pl.loop(0, 8)
    def _(t):
        columns = pl.ds(pl.multiple_of(t * tile, tile), tile)
        out_grad = dot_tn(hidden[:, columns], d_ffn[...])
        for row_group in range(2):
            for column_group in range(2):
                piece = ((t % 2) * 2 + row_group) * 2 + column_group
                block = out_grad[
                    row_group * share : (row_group + 1) * share,
                    column_group * tile : (column_group + 1) * tile,
                ]
                stage[place_of(ids, t // 2, piece, way)] = block.astype(low)

    finish(send_out(stage, kept, sent, out_sems))


def in_bwd_kernel(layer, way, ids, d_ffn, d_resid_two, unit_one, inverse_one, slope, small, *rest):
    weights, rest = rest[:10], rest[10:]
    d_resid, small_grads, in_bias_grad, kept, sent = rest[:5]
    w_in, w_out, d_pre, normed_t, stage, sems, out_sems = rest[5:]
    in_copies, out_copies = ffn_copies(layer, ids, weights, w_in, w_out, sems)
    begin(out_copies)
    begin(in_copies)
    normed = unit_one[...] * small[layer, 3:4, :] + small[layer, 4:5, :]
    normed_t[...] = normed.astype(low).T
    finish(out_copies)
    tile = w_in.shape[1] // 8

    @pl.loop(0, 8)
    def _(t):
        columns = pl.ds(pl.multiple_of(t * tile, tile), tile)
        d_hidden = dot_nt(d_ffn[...], w_out[columns, :])
        d_tile = (d_hidden * slope[:, columns]).astype(low)
        d_pre[:, columns] = d_tile
        in_bias_grad[:, columns] = jnp.sum(d_tile.astype(f32), axis=0, keepdims=True)
        store_rows(stage, ids, dot(normed_t[...], d_tile), t, way)

    going = send_out(stage, kept, sent, out_sems)
    finish(in_copies)
    d_normed = d_resid_two[...] + dot_nt(d_pre[...], w_in[...])
    unit = unit_one[...]
    small_grads[0:1, :] = jnp.sum(d_normed * unit, axis=0, keepdims=True)
    small_grads[1:2, :] = jnp.sum(d_normed, axis=0, keepdims=True)
    small_grads[2:8, :] = jnp.zeros((6, unit.shape[1]), f32)
    d_resid[...] = normalize_back(d_normed * small[layer, 3:4, :], unit, inverse_one[...])
    finish(going)


def attn_bwd_kernel(layer, way, ids, d_resid, x, qkv_rows, probs, context, *rest):
    weights, others, rest = rest[:7], rest[7:-13], rest[-13:]
    d_input, small_grads, kept, sent = rest[:4]
    w_qkv, w_o, d_attn, d_context, d_qkv, x_t, stage, sems, out_sems = rest[4:]
    tokens, width = x.shape
    qkv_copies, o_copies = attn_copies(layer, ids, weights, w_qkv, w_o, sems)
    begin(o_copies)
    begin(qkv_copies)
    d_low = d_resid[...].astype(low)
    d_attn[...] = d_low
    small_grads[2:3, :] = jnp.sum(d_low.astype(f32), axis=0, keepdims=True)
    x_t[...] = x[...].T
    tile = width // 2
    for half in range(2):
        product = dot_tn(context[...], d_attn[:, half * tile : (half + 1) * tile])
        store_rows(stage, ids, product, 6 + half, way)
    finish(o_copies)
    d_context[...] = dot_nt(d_attn[...], w_o[...]).astype(low)
    pair_width = 2 * width // HEADS
    first = lax.broadcasted_iota(jnp.int32, (1, pair_width), 1) < pair_width // 2
    scale = 1.0 / math.sqrt(width // HEADS)

    @pl.loop(0, HEADS // 2)
    def _(pair):
        start = pl.multiple_of(pair * pair_width, pair_width)
        at_query = pl.ds(start, pair_width)
        at_key = pl.ds(width + start, pair_width)
        at_value = pl.ds(2 * width + start, pair_width)
        query, key, value = qkv_rows[:, at_query], qkv_rows[:, at_key], qkv_rows[:, at_value]
        d_ctx = d_context[:, at_query]
        sides = []
        for side in range(2):
            mine = first if side == 0 else jnp.logical_not(first)
            prob_low = probs[2 * pair + side]
            prob = prob_low.astype(f32)
            d_prob = dot_nt(jnp.where(mine, d_ctx, jnp.zeros_like(d_ctx)), value)
            inner = jnp.sum(prob * d_prob, axis=-1, keepdims=True)
            d_scores = (prob * (d_prob - inner)).astype(low)
            sides.append((dot(d_scores, key), dot_tn(d_scores, query), dot_tn(prob_low, d_ctx)))
        d_qkv[:, at_query] = (jnp.where(first, sides[0][0], sides[1][0]) * scale).astype(low)
        d_qkv[:, at_key] = jnp.where(first, sides[0][1], sides[1][1]).astype(low)
        d_qkv[:, at_value] = jnp.where(first, sides[0][2], sides[1][2]).astype(low)

    @pl.loop(0, 6)
    def _(t):
        columns = pl.ds(pl.multiple_of(t * tile, tile), tile)
        store_rows(stage, ids, dot(x_t[...], d_qkv[:, columns]), t, way)

    small_grads[0:1, :] = jnp.sum(d_qkv[:, :width].astype(f32), axis=0, keepdims=True)
    small_grads[1:2, :] = jnp.sum(d_qkv[:, 2 * width :].astype(f32), axis=0, keepdims=True)
    small_grads[3:8, :] = jnp.zeros((5, width), f32)
    if others:
        share = width // 4
        sources = small_sources(layer, small_grads, others)
        for owner in range(4):
            for piece in range(8):
                lines = []
                for source, row, start, step in sources[3 * piece : 3 * piece + 3]:
                    line = source[row : row + 1, start + owner * step : start + owner * step + share]
                    lines.append(jnp.concatenate([line, jnp.zeros_like(line)], axis=1))
                lines.append(jnp.zeros((SMALL_ROWS - 3, tile), f32))
                block = jnp.concatenate(lines, axis=0).astype(low)
                stage[place_of(ids, owner, piece, way) + (pl.ds(share, SMALL_ROWS),)] = block
    going = send_out(stage, kept, sent, out_sems)
    finish(qkv_copies)
    d_input[...] = (d_resid[...] + dot_nt(d_qkv[...], w_qkv[...])).astype(low)
    finish(going)


SMALL_ROWS = 16
SMALL_LINES = (("attn", 0), ("attn", 1), ("attn", 2), ("in", 0), ("in", 1), ("out", 2), ("out", 0), ("out", 1))


def small_sources(layer, own, others):
    found = []
    out_0, in_0, bias_0, out_1, in_1, bias_1, attn_1 = others
    refs = ({"attn": own, "in": in_0, "out": out_0}, {"attn": attn_1, "in": in_1, "out": out_1})
    width = own.shape[1]
    for of_layer, bias in zip(refs, (bias_0, bias_1)):
        found += [(of_layer[name], row, 0, width // 4) for name, row in SMALL_LINES]
        found += [(bias, 0, i * (width // 4), width) for i in range(4)]
    return found


def unpack_kernel(layer, slab, back, earlier, ids, near, far, *rest):
    outs = rest[earlier:-4]
    buffer, wide_buffer, in_sems, out_sems = rest[-4:]
    share, tile = wide_buffer.shape[1:]

    def fetch(piece, ref, index):
        return pltpu.make_async_copy(ref.at[index], buffer.at[piece], in_sems.at[piece])

    for piece in range(8):
        off = piece ^ ids[5]
        bits = [(off >> WIDE_BIT[name]) & 1 for name in back]
        index = bits[1] * 2 + bits[0]

        @pl.when(bits[2] == 0)
        def _():
            fetch(piece, near, index).start()

        @pl.when(bits[2] == 1)
        def _():
            fetch(piece, far, index).start()

    copies = []
    for piece in range(8):
        fetch(piece, near, 0).wait()
        wide_buffer[piece] = buffer[piece, :share].astype(f32)
        columns = pl.ds(piece * tile, tile)
        if slab == "in":
            target = outs[0].at[layer, :, columns]
        elif slab == "out":
            rows = pl.ds((piece // 2) * share, share)
            target = outs[0].at[layer, rows, pl.ds((piece % 2) * tile, tile)]
        elif piece < 6:
            target = outs[0].at[layer, :, columns]
        else:
            target = outs[1].at[layer, :, pl.ds((piece - 6) * tile, tile)]
        copies.append(pltpu.make_async_copy(wide_buffer.at[piece], target, out_sems.at[piece]))
        copies[-1].start()
    if slab == "attn" and layer == 0:
        for line in range(24):
            of_layer, which = line // 12, line % 12
            row = share + line % 3
            values = buffer[line // 3, row : row + 1, :share].astype(f32)
            if which < 8:
                outs[2 + which][of_layer : of_layer + 1, :] = values
            else:
                at = (which - 8) * share
                outs[10][of_layer : of_layer + 1, at : at + share] = values
    else:
        outs[-1][...] = jnp.zeros(outs[-1].shape, f32)
    finish(copies)


SMEM = pl.BlockSpec(memory_space=pltpu.SMEM)
VMEM = pl.BlockSpec(memory_space=pltpu.VMEM)
ANY = pl.BlockSpec(memory_space=pl.ANY)


def call(kernel, name, time, in_specs, out_specs, out_shape, scratch, args, aliases=()):
    return pl.pallas_call(
        kernel,
        name=name,
        in_specs=in_specs,
        out_specs=out_specs,
        out_shape=out_shape,
        scratch_shapes=scratch,
        input_output_aliases=dict(aliases),
        compiler_params=pltpu.CompilerParams(vmem_limit_bytes=VMEM_BYTES),
        cost_estimate=pl.CostEstimate(
            flops=int(time * 1.1e9), bytes_accessed=int(time * 3.6e6), transcendentals=0
        ),
    )(*args)


def shape(dims, kind):
    return jax.ShapeDtypeStruct(dims, kind)


def reverse_bits(value, bits):
    result = jnp.zeros_like(value)
    for bit in range(bits):
        result = result | (((value >> bit) & 1) << (bits - 1 - bit))
    return result


def added(a, b):
    return (a.astype(f32) + b.astype(f32)).astype(low)


WAYS = ("xyzw", "xyzw", "yxzw", "xyzw", "xyzw", "xyzw")
BACKS = ("wzy",) * 6
PLAN = (
    "out1", 0, "in1", "attn1", 0, 1, "out0", 0, 2, 0, 3, 1, 0, "in0", 0, 2, 4, 0, 1, 3, 2, 1, 0, "attn0", 1,
    3, 4, 5, 2, 1, 3, 2, 1, 4, 3, 2, 5, 1, 4, 3, 2, 4, 5, 3, 5, 4, 2, 5, 4, 3, 5, 5, 4, 5,
)


class Order:
    def __init__(self):
        self.last = None

    def after(self, values):
        if self.last is None:
            return values
        values, self.last = lax.optimization_barrier((values, self.last))
        return values

    def wait(self, values):
        values = self.after(values)
        self.last = values
        return values


STEPS = {"x": ("narrow", 2), "y": ("wide", 1), "z": ("wide", 2), "w": ("wide", 4)}


class Slab:
    def __init__(self, way, back, wide_bits, kept, sent):
        self.way, self.back, self.wide_bits = way, back, wide_bits
        self.kept = kept
        self.flying = swap(sent, "narrow", 1)
        self.stage = 0

    def step(self, order):
        received = order.after(self.flying)
        if self.stage < len(self.way):
            send = added(self.kept[1], received[1])
            self.kept = added(self.kept[0], received[0])
            self.flying = swap(send, *STEPS[self.way[self.stage]])
            order.last = send
        elif self.stage == len(self.way):
            piece = added(self.kept, received)
            for b in range(HALVINGS, self.wide_bits):
                piece = added(piece, swap(piece, "wide", 1 << b))
            self.block = piece[None]
            order.last = self.block
            self.flying = swap(self.block, *STEPS[self.back[0]])
        elif self.stage < len(self.way) + len(self.back):
            self.block = jnp.concatenate([self.block, received], axis=0)
            order.last = self.block
            self.flying = swap(self.block, *STEPS[self.back[self.stage - len(self.way)]])
        else:
            self.far = received
        self.stage += 1

    def ended(self):
        return self.stage == len(self.way) + len(self.back) + 1


def body(
    tables_in,
    cotangent,
    cell_ids,
    lengths,
    qkv_weight,
    q_bias,
    v_bias,
    o_weight,
    o_bias,
    norm1_gain,
    norm1_bias,
    in_weight,
    in_bias,
    out_weight,
    out_bias,
    norm2_gain,
    norm2_bias,
):
    tokens, width = tables_in.shape
    layers, share, ffn = in_weight.shape
    ffn_share = out_weight.shape[1]
    wide_count = lax.axis_size("wide")
    wide_bits = wide_count.bit_length() - 1
    assert wide_count == 1 << wide_bits and wide_bits >= HALVINGS and lax.axis_size("narrow") == 4
    tile = ffn // 8
    me = lax.axis_index("narrow").astype(jnp.int32)
    wide_me = lax.axis_index("wide").astype(jnp.int32)
    y = wide_me & 1
    place = reverse_bits(wide_me & (2**HALVINGS - 1), HALVINGS)
    ids = jnp.stack([me, me ^ 1, me ^ 2, me ^ 3, y, place])

    order = Order()

    def half_of(weight, layer):
        rows = weight.shape[1] // 2
        return lax.dynamic_slice(weight, (layer, y * rows, 0), (1, rows, weight.shape[2]))[0]

    halves = []
    for layer in range(layers):
        joint = jnp.concatenate([half_of(qkv_weight, layer), half_of(o_weight, layer)], axis=1)
        halves += [joint, half_of(in_weight, layer), half_of(out_weight, layer)]
    near_x, far_x, diagonal = [None] * len(halves), [None] * len(halves), [None] * len(halves)
    core = [None] * 4
    own = (qkv_weight, o_weight, in_weight, out_weight)

    def send_x(*which):
        for i in which:
            near_x[i] = swap(order.after(halves[i]), "narrow", 2)

    def send_core(i):
        core[i] = swap(order.after(own[i]), "narrow", 1)

    def arrive(*events):
        for kind, i in events:
            if kind == "x":
                near_x[i] = order.wait(near_x[i])
                far_x[i] = swap(near_x[i], "wide", 1)
            elif kind == "y":
                far_x[i] = order.wait(far_x[i])
                both = jnp.concatenate([near_x[i], far_x[i]], axis=0)
                order.last = both
                diagonal[i] = swap(both, "narrow", 1)
            elif kind == "d":
                diagonal[i] = order.wait(diagonal[i])
            else:
                core[i] = order.wait(core[i])

    def group(i):
        return near_x[i], far_x[i], diagonal[i]

    def attn_weights(layer):
        return (qkv_weight, core[0], o_weight, core[1]) + group(3 * layer)

    def ffn_weights(layer):
        return (in_weight, core[2]) + group(3 * layer + 1) + (out_weight, core[3]) + group(3 * layer + 2)

    send_x(0)
    short = [q_bias, v_bias, o_bias, norm1_gain, norm1_bias, out_bias, norm2_gain, norm2_bias]
    packed = jnp.concatenate([jnp.stack(short, axis=1), in_bias.reshape(layers, 4, share)], axis=1)
    others = [
        lax.ppermute(packed, "narrow", [(i, i ^ away) for i in range(4)]) for away in (1, 2, 3)
    ]
    send_core(0)
    halves[1:] = order.wait(halves[1:])
    arrive(("c", 0))
    send_core(1)
    near_x[0], others = order.wait((near_x[0], others))
    far_x[0] = swap(near_x[0], "wide", 1)
    send_x(1)

    def in_order(low_one, high_one, bit):
        swapped = (me & bit) != 0
        return jnp.stack([jnp.where(swapped, high_one, low_one), jnp.where(swapped, low_one, high_one)])

    packed = in_order(in_order(packed, others[0], 1), in_order(others[1], others[2], 1), 2)
    packed = packed.reshape(4, layers, 12, share).astype(f32)
    small = packed[:, :, :8].transpose(1, 2, 0, 3).reshape(layers, 8, width)
    full_in_bias = packed[:, :, 8:].transpose(1, 0, 2, 3).reshape(layers, 1, ffn)
    ids, small, full_in_bias = order.wait((ids, small, full_in_bias))
    arrive(("c", 1))
    send_core(2)
    arrive(("c", 2))
    send_core(3)

    w_qkv = pltpu.VMEM((width, 3 * width), low)
    w_o = pltpu.VMEM((width, width), low)
    w_in = pltpu.VMEM((width, ffn), low)
    w_out = pltpu.VMEM((ffn, width), low)
    copy_sems = pltpu.SemaphoreType.DMA((12,))
    pair_sems = pltpu.SemaphoreType.DMA((2,))
    rows_f32 = shape((tokens, width), f32)
    rows_low = shape((tokens, width), low)
    column_f32 = shape((tokens, 1), f32)
    eight_f32 = shape((8, width), f32)

    def pieces(rows):
        return [shape((2, 2, 2, 2, rows, tile), low)] * 2

    def stage(rows):
        return pltpu.VMEM((2, 2, 2, 2, 2, rows, tile), low)

    def attn_forward(layer, x):
        x = order.after(x)
        outs = call(
            functools.partial(attn_fwd_kernel, layer),
            "attn_fwd",
            13,
            [SMEM, SMEM] + [VMEM] * 3 + [ANY] * 7,
            [VMEM] * 5,
            [shape((tokens, 3 * width), low), shape((HEADS, tokens, tokens), low), rows_low, rows_f32, column_f32],
            [w_qkv, w_o, pltpu.VMEM((tokens, tokens), f32), copy_sems],
            (ids, lengths, x, cell_ids, small) + attn_weights(layer),
        )
        order.last = outs[-1]
        return outs

    def ffn_forward(layer, unit_one):
        unit_one = order.after(unit_one)
        outs = call(
            functools.partial(ffn_fwd_kernel, layer),
            "ffn_fwd",
            10,
            [SMEM] + [VMEM] * 3 + [ANY] * 10,
            [VMEM] * 5,
            [shape((tokens, ffn), low), shape((tokens, ffn), f32), rows_f32, column_f32, rows_low],
            [w_in, w_out, pltpu.VMEM((tokens, width), low), copy_sems],
            (ids, unit_one, full_in_bias, small) + ffn_weights(layer),
        )
        order.last = outs[-2]
        return outs

    def out_backward(layer, way, grad, unit_two, inverse_two, hidden):
        grad = order.after(grad)
        outs = call(
            functools.partial(out_bwd_kernel, layer, way),
            "out_bwd",
            8,
            [SMEM] + [VMEM] * 5,
            [VMEM] * 3 + [ANY] * 2,
            [rows_low, rows_f32, eight_f32] + pieces(share),
            [stage(share), pair_sems],
            (ids, grad, unit_two, inverse_two, hidden, small),
        )
        order.last = outs[2]
        return outs

    def in_backward(layer, way, d_ffn, d_resid_two, unit_one, inverse_one, slope):
        d_ffn = order.after(d_ffn)
        outs = call(
            functools.partial(in_bwd_kernel, layer, way),
            "in_bwd",
            14,
            [SMEM] + [VMEM] * 6 + [ANY] * 10,
            [VMEM] * 3 + [ANY] * 2,
            [rows_f32, eight_f32, shape((1, ffn), f32)] + pieces(share),
            [
                w_in,
                w_out,
                pltpu.VMEM((tokens, ffn), low),
                pltpu.VMEM((width, tokens), low),
                stage(share),
                copy_sems,
                pair_sems,
            ],
            (ids, d_ffn, d_resid_two, unit_one, inverse_one, slope, small) + ffn_weights(layer),
        )
        order.last = outs[1]
        return outs

    def attn_backward(layer, way, d_resid, x, qkv_rows, probs, context, small_others):
        d_resid = order.after(d_resid)
        rows = share + (SMALL_ROWS if small_others else 0)
        outs = call(
            functools.partial(attn_bwd_kernel, layer, way),
            "attn_bwd",
            16,
            [SMEM] + [VMEM] * 5 + [ANY] * 7 + [VMEM] * len(small_others),
            [VMEM] * 2 + [ANY] * 2,
            [rows_low, eight_f32] + pieces(rows),
            [
                w_qkv,
                w_o,
                pltpu.VMEM((tokens, width), low),
                pltpu.VMEM((tokens, width), low),
                pltpu.VMEM((tokens, 3 * width), low),
                pltpu.VMEM((width, tokens), low),
                stage(rows),
                copy_sems,
                pair_sems,
            ],
            (ids, d_resid, x, qkv_rows, probs, context) + attn_weights(layer) + tuple(small_others),
        )
        order.last = outs[1]
        return outs

    def unpack(layer, name, slab, earlier):
        dims = {
            "attn": [(layers, share, 3 * width), (layers, share, width)],
            "in": [(layers, share, ffn)],
            "out": [(layers, ffn_share, width)],
        }[name]
        last = name == "attn" and layer == 0
        extra = [(layers, share)] * 8 + [(layers, ffn_share)] if last else [(8, 128)]
        near, far = order.after((slab.block, slab.far))
        rows = near.shape[1]
        outs = call(
            functools.partial(unpack_kernel, layer, name, slab.back, len(earlier)),
            "unpack",
            4,
            [SMEM] + [ANY] * (2 + len(earlier)),
            [ANY] * len(dims) + [VMEM] * len(extra),
            [shape(d, f32) for d in dims + extra],
            [
                pltpu.VMEM((8, rows, tile), low),
                pltpu.VMEM((8, share, tile), f32),
                pltpu.SemaphoreType.DMA((8,)),
                pltpu.SemaphoreType.DMA((8,)),
            ],
            (ids, near, far, *earlier),
            {3 + i: i for i in range(len(earlier))},
        )
        order.last = outs[-1]
        return tuple(outs)

    arrive(("x", 1))
    send_x(2)
    arrive(("y", 0), ("c", 3), ("d", 0), ("x", 2))
    send_x(3)
    arrive(("y", 1))
    first_attn = attn_forward(0, tables_in)
    arrive(("x", 3))
    send_x(4)
    arrive(("y", 2), ("d", 1), ("d", 2))
    first_ffn = ffn_forward(0, first_attn[3])
    arrive(("x", 4))
    send_x(5)
    arrive(("y", 3), ("d", 3))
    second_attn = attn_forward(1, first_ffn[4])
    arrive(("x", 5), ("y", 4), ("y", 5), ("d", 4), ("d", 5))
    second_ffn = ffn_forward(1, second_attn[3])
    mixed_out = second_ffn[4]
    inputs = (tables_in, first_ffn[4])
    attn_kept, ffn_kept = (first_attn, second_attn), (first_ffn, second_ffn)

    slabs = [None] * 6
    grad = cotangent
    small_out, small_in, small_attn, bias_grads = [None] * 2, [None] * 2, [None] * 2, [None] * 2
    unpacked = {"attn": (), "in": (), "out": ()}
    for action in PLAN:
        if isinstance(action, int):
            slab = slabs[action]
            slab.step(order)
            if slab.ended():
                name = ("out", "in", "attn")[action % 3]
                unpacked[name] = unpack(layers - 1 - action // 3, name, slab, unpacked[name][: 2 if name == "attn" else 1])
            continue
        name, layer = action[:-1], int(action[-1])
        which = 3 * (layers - 1 - layer) + ("out", "in", "attn").index(name)
        way = WAYS[which]
        qkv_rows, probs, context, unit_one, inverse_one = attn_kept[layer]
        hidden, slope, unit_two, inverse_two, _ = ffn_kept[layer]
        if name == "out":
            d_ffn, d_resid_two, small_out[layer], kept, sent = out_backward(
                layer, way, grad, unit_two, inverse_two, hidden
            )
        elif name == "in":
            d_resid, small_in[layer], bias_grads[layer], kept, sent = in_backward(
                layer, way, d_ffn, d_resid_two, unit_one, inverse_one, slope
            )
        else:
            small_others = ()
            if layer == 0:
                small_others = (
                    small_out[0],
                    small_in[0],
                    bias_grads[0],
                    small_out[1],
                    small_in[1],
                    bias_grads[1],
                    small_attn[1],
                )
            grad, small_attn[layer], kept, sent = attn_backward(
                layer, way, d_resid, inputs[layer], qkv_rows, probs, context, small_others
            )
        slabs[which] = Slab(way, BACKS[which], wide_bits, kept, sent)
    qkv_grad, o_grad, *vectors = unpacked["attn"]
    in_grad, out_grad = unpacked["in"][0], unpacked["out"][0]
    return (
        mixed_out,
        grad,
        qkv_grad,
        vectors[0],
        vectors[1],
        o_grad,
        vectors[2],
        vectors[3],
        vectors[4],
        in_grad,
        vectors[8],
        out_grad,
        vectors[5],
        vectors[6],
        vectors[7],
    )


def solution(mesh):
    by_table = P(("wide", "narrow"), None)
    matrix = P(None, "narrow", None)
    vector = P(None, "narrow")
    return jax.shard_map(
        body,
        mesh=mesh,
        in_specs=(
            by_table,
            by_table,
            by_table,
            P(("wide", "narrow")),
            matrix,
            vector,
            vector,
            matrix,
            vector,
            vector,
            vector,
            matrix,
            vector,
            matrix,
            vector,
            vector,
            vector,
        ),
        out_specs=(
            by_table,
            by_table,
            matrix,
            vector,
            vector,
            matrix,
            vector,
            vector,
            vector,
            matrix,
            vector,
            matrix,
            vector,
            vector,
            vector,
        ),
        check_vma=False,
    )
```

```python
import functools
import math

import jax
import jax.numpy as jnp
from jax import lax
from jax.experimental import pallas as pl
from jax.experimental.pallas import tpu as pltpu
from jax.sharding import PartitionSpec as P

HEADS = 12
norm_eps = 1e-12
masked_score = -1000000000.0
low = jnp.bfloat16
f32 = jnp.float32
VMEM_BYTES = 56 * 1024 * 1024
HALVINGS = 3


def swap(value, axis, bit):
    count = lax.axis_size(axis)
    return lax.ppermute(value, axis, [(i, i ^ bit) for i in range(count)])


def dot(a, b):
    return jnp.dot(a, b, preferred_element_type=f32)


def dot_nt(a, b):
    return lax.dot_general(a, b, (((1,), (1,)), ((), ())), preferred_element_type=f32)


def dot_tn(a, b):
    return lax.dot_general(a, b, (((0,), (0,)), ((), ())), preferred_element_type=f32)


def normalize(residual):
    center = residual - jnp.mean(residual, axis=-1, keepdims=True)
    inverse = lax.rsqrt(jnp.mean(center * center, axis=-1, keepdims=True) + norm_eps)
    return center * inverse, inverse


def normalize_back(grad_unit, unit, inverse):
    centered = grad_unit - jnp.mean(grad_unit, axis=-1, keepdims=True)
    return inverse * (centered - unit * jnp.mean(grad_unit * unit, axis=-1, keepdims=True))


def weight_copies(ids, layer, pieces, target, columns, sems, base):
    at = pl.ds(columns, target.shape[1])
    if len(pieces) == 1:
        return [pltpu.make_async_copy(pieces[0].at[:, at], target, sems.at[base])]
    own, core, near_x, far_x, diagonal = pieces
    rows = own.shape[1]
    half = rows // 2
    n, y = ids[0], ids[4]
    copies = []

    def add(source, start, count):
        where = target.at[pl.ds(pl.multiple_of(start, half), count), :]
        copies.append(pltpu.make_async_copy(source, where, sems.at[base + len(copies)]))

    add(own.at[layer], n * rows, rows)
    add(core.at[layer], ids[1] * rows, rows)
    add(near_x.at[:, at], ids[2] * rows + y * half, half)
    add(far_x.at[:, at], ids[2] * rows + (1 - y) * half, half)
    add(diagonal.at[pl.ds(0, half), at], ids[3] * rows + y * half, half)
    add(diagonal.at[pl.ds(half, half), at], ids[3] * rows + (1 - y) * half, half)
    return copies


def begin(copies):
    for copy in copies:
        copy.start()


def finish(copies):
    for copy in copies:
        copy.wait()


def attn_copies(layer, ids, refs, w_qkv, w_o, sems):
    first, second = (refs, refs) if len(refs) == 1 else (refs[:2] + refs[4:], refs[2:])
    qkv = weight_copies(ids, layer, first, w_qkv, 0, sems, 0)
    o = weight_copies(ids, layer, second, w_o, w_qkv.shape[1], sems, 6)
    return qkv, o


def ffn_copies(layer, ids, refs, w_in, w_out, sems):
    in_copies = weight_copies(ids, layer, refs[:-5], w_in, 0, sems, 0)
    out_copies = weight_copies(ids, layer, refs[-5:], w_out, 0, sems, 6)
    return in_copies, out_copies


def pack_kernel(*refs):
    shorts, in_bias, packed = refs[:8], refs[8], refs[9]
    layers, share = shorts[0].shape
    for layer in range(layers):
        for i, short in enumerate(shorts):
            packed[layer, i : i + 1, :] = short[layer : layer + 1, :].astype(f32)
        for i in range(4):
            packed[layer, 8 + i : 9 + i, :] = in_bias[layer : layer + 1, i * share : (i + 1) * share].astype(f32)


def attn_fwd_kernel(layer, ids, length, x, cell_row, small, *rest):
    weights, rest = rest[:-9], rest[-9:]
    qkv_rows, probs, context, unit_out, inverse_out, w_qkv, w_o, mask, sems = rest
    tokens, width = x.shape
    qkv_copies, o_copies = attn_copies(layer, ids, weights, w_qkv, w_o, sems)
    begin(qkv_copies)
    begin(o_copies)
    position = lax.broadcasted_iota(jnp.int32, (1, tokens), 1)
    key_cell = cell_row[...]
    square = (tokens, tokens)
    diagonal = lax.broadcasted_iota(jnp.int32, square, 0) == lax.broadcasted_iota(jnp.int32, square, 1)
    query_cell = jnp.sum(jnp.where(diagonal, key_cell, 0), axis=1, keepdims=True)
    allowed = (query_cell == key_cell) | (key_cell == 0) | (query_cell == 0)
    allowed = allowed & (position < length[0])
    mask[...] = jnp.where(allowed, 0.0, masked_score)
    scale = 1.0 / math.sqrt(width // HEADS)
    finish(qkv_copies)
    tile = width // 2

    for t in range(6):
        columns = slice(t * tile, (t + 1) * tile)
        rows = dot(x[...], w_qkv[:, columns])
        if t // 2 != 1:
            part = slice((t % 2) * tile, (t % 2 + 1) * tile)
            rows = rows + small[layer, t // 4 : t // 4 + 1, part]
        if t < 2:
            rows = rows * scale
        qkv_rows[:, columns] = rows.astype(low)

    pair_width = 2 * width // HEADS
    first = lax.broadcasted_iota(jnp.int32, (1, pair_width), 1) < pair_width // 2

    @pl.loop(0, HEADS // 2)
    def _(pair):
        start = pl.multiple_of(pair * pair_width, pair_width)
        query = qkv_rows[:, pl.ds(start, pair_width)]
        key = qkv_rows[:, pl.ds(width + start, pair_width)]
        value = qkv_rows[:, pl.ds(2 * width + start, pair_width)]
        sides = []
        for side in range(2):
            mine = first if side == 0 else jnp.logical_not(first)
            scores = dot_nt(jnp.where(mine, query, jnp.zeros_like(query)), key) + mask[...]
            shifted = jnp.exp(scores - jnp.max(scores, axis=-1, keepdims=True))
            total = jnp.sum(shifted, axis=-1, keepdims=True)
            prob = (shifted / total).astype(low)
            probs[2 * pair + side] = prob
            sides.append(dot(prob, value))
        context[:, pl.ds(start, pair_width)] = jnp.where(first, sides[0], sides[1]).astype(low)

    finish(o_copies)
    residual = x[...].astype(f32) + (dot(context[...], w_o[...]) + small[layer, 2:3, :])
    unit, inverse = normalize(residual)
    unit_out[...] = unit
    inverse_out[...] = inverse


def ffn_fwd_kernel(layer, ids, unit_one, in_bias, small, *rest):
    weights, rest = rest[:-9], rest[-9:]
    hidden, slope, unit_out, inverse_out, result, w_in, w_out, normed_low, sems = rest
    in_copies, out_copies = ffn_copies(layer, ids, weights, w_in, w_out, sems)
    begin(in_copies)
    begin(out_copies)
    normed = unit_one[...] * small[layer, 3:4, :] + small[layer, 4:5, :]
    normed_low[...] = normed.astype(low)
    finish(in_copies)
    tile = w_in.shape[1] // 8

    @pl.loop(0, 8)
    def _(t):
        columns = pl.ds(pl.multiple_of(t * tile, tile), tile)
        pre = dot(normed_low[...], w_in[:, columns]) + in_bias[layer, :, columns]
        cdf = 0.5 * (1.0 + lax.erf(pre * (1.0 / math.sqrt(2.0))))
        density = jnp.exp(-0.5 * pre * pre) * (1.0 / math.sqrt(2.0 * math.pi))
        hidden[:, columns] = (pre * cdf).astype(low)
        slope[:, columns] = cdf + pre * density

    finish(out_copies)
    residual = unit_one[...] * small[layer, 3:4, :] + small[layer, 4:5, :] + (dot(hidden[...], w_out[...]) + small[layer, 5:6, :])
    unit, inverse = normalize(residual)
    unit_out[...] = unit
    inverse_out[...] = inverse
    result[...] = (unit * small[layer, 6:7, :] + small[layer, 7:8, :]).astype(low)


WIDE_BIT = {"y": 0, "z": 1, "w": 2}


def place_of(ids, owner, piece, way):
    away, off = ids[0] ^ owner, piece ^ ids[5]
    return (away & 1,) + tuple(away >> 1 if name == "x" else (off >> WIDE_BIT[name]) & 1 for name in way)


def store_rows(stage, ids, product, piece, way):
    share = product.shape[0] // 4
    for owner in range(4):
        block = product[owner * share : (owner + 1) * share].astype(low)
        stage[place_of(ids, owner, piece, way) + (pl.ds(0, share),)] = block


def send_out(stage, kept, sent, sems):
    copies = [
        pltpu.make_async_copy(stage.at[1], sent, sems.at[0]),
        pltpu.make_async_copy(stage.at[0], kept, sems.at[1]),
    ]
    begin(copies)
    return copies


def out_bwd_kernel(layer, way, ids, grad, unit_two, inverse_two, hidden, small, *rest):
    d_ffn, d_resid_two, small_grads, kept, sent, stage, out_sems = rest
    g = grad[...].astype(f32)
    unit = unit_two[...]
    small_grads[0:1, :] = jnp.sum(g * unit, axis=0, keepdims=True)
    small_grads[1:2, :] = jnp.sum(g, axis=0, keepdims=True)
    d_two = normalize_back(g * small[layer, 6:7, :], unit, inverse_two[...])
    d_resid_two[...] = d_two
    d_low = d_two.astype(low)
    d_ffn[...] = d_low
    small_grads[2:3, :] = jnp.sum(d_low.astype(f32), axis=0, keepdims=True)
    small_grads[3:8, :] = jnp.zeros((5, unit.shape[1]), f32)
    tile = hidden.shape[1] // 8
    share = d_ffn.shape[1] // 4

    @pl.loop(0, 8)
    def _(t):
        columns = pl.ds(pl.multiple_of(t * tile, tile), tile)
        out_grad = dot_tn(hidden[:, columns], d_ffn[...])
        for row_group in range(2):
            for column_group in range(2):
                piece = ((t % 2) * 2 + row_group) * 2 + column_group
                block = out_grad[
                    row_group * share : (row_group + 1) * share,
                    column_group * tile : (column_group + 1) * tile,
                ]
                stage[place_of(ids, t // 2, piece, way)] = block.astype(low)

    finish(send_out(stage, kept, sent, out_sems))


def in_bwd_kernel(layer, way, ids, d_ffn, d_resid_two, unit_one, inverse_one, slope, small, *rest):
    weights, rest = rest[:-12], rest[-12:]
    d_resid, small_grads, in_bias_grad, kept, sent = rest[:5]
    w_in, w_out, d_pre, normed_t, stage, sems, out_sems = rest[5:]
    in_copies, out_copies = ffn_copies(layer, ids, weights, w_in, w_out, sems)
    begin(out_copies)
    begin(in_copies)
    normed = unit_one[...] * small[layer, 3:4, :] + small[layer, 4:5, :]
    normed_t[...] = normed.astype(low).T
    finish(out_copies)
    tile = w_in.shape[1] // 8

    @pl.loop(0, 8)
    def _(t):
        columns = pl.ds(pl.multiple_of(t * tile, tile), tile)
        d_hidden = dot_nt(d_ffn[...], w_out[columns, :])
        d_tile = (d_hidden * slope[:, columns]).astype(low)
        d_pre[:, columns] = d_tile
        in_bias_grad[:, columns] = jnp.sum(d_tile.astype(f32), axis=0, keepdims=True)
        store_rows(stage, ids, dot(normed_t[...], d_tile), t, way)

    going = send_out(stage, kept, sent, out_sems)
    finish(in_copies)
    d_normed = d_resid_two[...] + dot_nt(d_pre[...], w_in[...])
    unit = unit_one[...]
    small_grads[0:1, :] = jnp.sum(d_normed * unit, axis=0, keepdims=True)
    small_grads[1:2, :] = jnp.sum(d_normed, axis=0, keepdims=True)
    small_grads[2:8, :] = jnp.zeros((6, unit.shape[1]), f32)
    d_resid[...] = normalize_back(d_normed * small[layer, 3:4, :], unit, inverse_one[...])
    finish(going)


def attn_bwd_kernel(layer, way, ids, d_resid, x, qkv_rows, probs, context, *rest):
    weights = rest[:-13][: 7 if layer == 0 else 1]
    others, rest = rest[len(weights) : -13], rest[-13:]
    d_input, small_grads, kept, sent = rest[:4]
    w_qkv, w_o, d_attn, d_context, d_qkv, x_t, stage, sems, out_sems = rest[4:]
    tokens, width = x.shape
    qkv_copies, o_copies = attn_copies(layer, ids, weights, w_qkv, w_o, sems)
    begin(o_copies)
    begin(qkv_copies)
    d_low = d_resid[...].astype(low)
    d_attn[...] = d_low
    small_grads[2:3, :] = jnp.sum(d_low.astype(f32), axis=0, keepdims=True)
    x_t[...] = x[...].T
    tile = width // 2
    for half in range(2):
        product = dot_tn(context[...], d_attn[:, half * tile : (half + 1) * tile])
        store_rows(stage, ids, product, 6 + half, way)
    finish(o_copies)
    d_context[...] = dot_nt(d_attn[...], w_o[...]).astype(low)
    pair_width = 2 * width // HEADS
    first = lax.broadcasted_iota(jnp.int32, (1, pair_width), 1) < pair_width // 2
    scale = 1.0 / math.sqrt(width // HEADS)

    @pl.loop(0, HEADS // 2)
    def _(pair):
        start = pl.multiple_of(pair * pair_width, pair_width)
        at_query = pl.ds(start, pair_width)
        at_key = pl.ds(width + start, pair_width)
        at_value = pl.ds(2 * width + start, pair_width)
        query, key, value = qkv_rows[:, at_query], qkv_rows[:, at_key], qkv_rows[:, at_value]
        d_ctx = d_context[:, at_query]
        sides = []
        for side in range(2):
            mine = first if side == 0 else jnp.logical_not(first)
            prob_low = probs[2 * pair + side]
            prob = prob_low.astype(f32)
            d_prob = dot_nt(jnp.where(mine, d_ctx, jnp.zeros_like(d_ctx)), value)
            inner = jnp.sum(prob * d_prob, axis=-1, keepdims=True)
            d_scores = (prob * (d_prob - inner)).astype(low)
            sides.append((dot(d_scores, key), dot_tn(d_scores, query), dot_tn(prob_low, d_ctx)))
        d_qkv[:, at_query] = (jnp.where(first, sides[0][0], sides[1][0]) * scale).astype(low)
        d_qkv[:, at_key] = jnp.where(first, sides[0][1], sides[1][1]).astype(low)
        d_qkv[:, at_value] = jnp.where(first, sides[0][2], sides[1][2]).astype(low)

    @pl.loop(0, 6)
    def _(t):
        columns = pl.ds(pl.multiple_of(t * tile, tile), tile)
        store_rows(stage, ids, dot(x_t[...], d_qkv[:, columns]), t, way)

    small_grads[0:1, :] = jnp.sum(d_qkv[:, :width].astype(f32), axis=0, keepdims=True)
    small_grads[1:2, :] = jnp.sum(d_qkv[:, 2 * width :].astype(f32), axis=0, keepdims=True)
    small_grads[3:8, :] = jnp.zeros((5, width), f32)
    if others:
        share = width // 4
        sources = small_sources(layer, small_grads, others)
        for owner in range(4):
            for piece in range(8):
                lines = []
                for source, row, start, step in sources[3 * piece : 3 * piece + 3]:
                    line = source[row : row + 1, start + owner * step : start + owner * step + share]
                    lines.append(jnp.concatenate([line, jnp.zeros_like(line)], axis=1))
                lines.append(jnp.zeros((SMALL_ROWS - 3, tile), f32))
                block = jnp.concatenate(lines, axis=0).astype(low)
                stage[place_of(ids, owner, piece, way) + (pl.ds(share, SMALL_ROWS),)] = block
    going = send_out(stage, kept, sent, out_sems)
    finish(qkv_copies)
    d_input[...] = (d_resid[...] + dot_nt(d_qkv[...], w_qkv[...])).astype(low)
    finish(going)


SMALL_ROWS = 16
SMALL_LINES = (("attn", 0), ("attn", 1), ("attn", 2), ("in", 0), ("in", 1), ("out", 2), ("out", 0), ("out", 1))


def small_sources(layer, own, others):
    found = []
    out_0, in_0, bias_0, out_1, in_1, bias_1, attn_1 = others
    refs = ({"attn": own, "in": in_0, "out": out_0}, {"attn": attn_1, "in": in_1, "out": out_1})
    width = own.shape[1]
    for of_layer, bias in zip(refs, (bias_0, bias_1)):
        found += [(of_layer[name], row, 0, width // 4) for name, row in SMALL_LINES]
        found += [(bias, 0, i * (width // 4), width) for i in range(4)]
    return found


def unpack_kernel(layer, slab, earlier, gathered, *rest):
    outs = rest[earlier:-4]
    buffer, wide_buffer, in_sems, out_sems = rest[-4:]
    share, tile = wide_buffer.shape[1:]
    arriving = [
        pltpu.make_async_copy(gathered.at[piece], buffer.at[piece], in_sems.at[piece]) for piece in range(8)
    ]
    begin(arriving)
    copies = []
    for piece in range(8):
        arriving[piece].wait()
        wide_buffer[piece] = buffer[piece, :share].astype(f32)
        columns = pl.ds(piece * tile, tile)
        if slab == "in":
            target = outs[0].at[layer, :, columns]
        elif slab == "out":
            rows = pl.ds((piece // 2) * share, share)
            target = outs[0].at[layer, rows, pl.ds((piece % 2) * tile, tile)]
        elif piece < 6:
            target = outs[0].at[layer, :, columns]
        else:
            target = outs[1].at[layer, :, pl.ds((piece - 6) * tile, tile)]
        copies.append(pltpu.make_async_copy(wide_buffer.at[piece], target, out_sems.at[piece]))
        copies[-1].start()
    if slab == "attn" and layer == 0:
        for line in range(24):
            of_layer, which = line // 12, line % 12
            row = share + line % 3
            values = buffer[line // 3, row : row + 1, :share].astype(f32)
            if which < 8:
                outs[2 + which][of_layer : of_layer + 1, :] = values
            else:
                at = (which - 8) * share
                outs[10][of_layer : of_layer + 1, at : at + share] = values
    else:
        outs[-1][...] = jnp.zeros(outs[-1].shape, f32)
    finish(copies)


SMEM = pl.BlockSpec(memory_space=pltpu.SMEM)
VMEM = pl.BlockSpec(memory_space=pltpu.VMEM)
ANY = pl.BlockSpec(memory_space=pl.ANY)


def call(kernel, name, time, in_specs, out_specs, out_shape, scratch, args, aliases=()):
    return pl.pallas_call(
        kernel,
        name=name,
        in_specs=in_specs,
        out_specs=out_specs,
        out_shape=out_shape,
        scratch_shapes=scratch,
        input_output_aliases=dict(aliases),
        compiler_params=pltpu.CompilerParams(vmem_limit_bytes=VMEM_BYTES),
        cost_estimate=pl.CostEstimate(
            flops=int(time * 1.1e9), bytes_accessed=int(time * 3.6e6), transcendentals=0
        ),
    )(*args)


def shape(dims, kind):
    return jax.ShapeDtypeStruct(dims, kind)


def added(a, b):
    return (a.astype(f32) + b.astype(f32)).astype(low)


WAYS = ("yxzw", "xyzw", "xyzw", "yxzw", "xyzw", "xyzw")
PLAN = (
    "out1", "in1", 0, 1, "attn1", "out0", 0, 2, 1, "in0", 0, 3, 4, 0, 1, 0, 2, 1, "attn0", 1, 3, 2, 5, 4, 2,
    0, 3, 2, 4, 3, 1, 4, 3, 5, 4, 2, 5, 5, 3, 5, 4, 5,
)


class Order:
    def __init__(self):
        self.last = None

    def after(self, values):
        if self.last is None:
            return values
        values, self.last = lax.optimization_barrier((values, self.last))
        return values

    def wait(self, values):
        values = self.after(values)
        self.last = values
        return values


STEPS = {"x": ("narrow", 2), "y": ("wide", 1), "z": ("wide", 2), "w": ("wide", 4)}


class Slab:
    def __init__(self, way, wide_count, kept, sent):
        self.way, self.wide_count = way, wide_count
        self.kept = kept
        self.flying = swap(sent, "narrow", 1)
        self.stage = 0

    def step(self, order):
        received = order.after(self.flying)
        if self.stage < len(self.way):
            send = added(self.kept[1], received[1])
            self.kept = added(self.kept[0], received[0])
            self.flying = swap(send, *STEPS[self.way[self.stage]])
            order.last = send
        elif self.stage == len(self.way):
            piece = added(self.kept, received)
            pieces = 1 << HALVINGS
            groups = None
            if self.wide_count > pieces:
                bit = pieces
                while bit < self.wide_count:
                    piece = added(piece, swap(piece, "wide", bit))
                    bit *= 2
                groups = [list(range(i, i + pieces)) for i in range(0, self.wide_count, pieces)]
            order.last = piece
            self.flying = lax.all_gather(piece, "wide", axis=0, axis_index_groups=groups)
        else:
            self.gathered = received
        self.stage += 1

    def ended(self):
        return self.stage == len(self.way) + 2


def body(
    tables_in,
    cotangent,
    cell_ids,
    lengths,
    qkv_weight,
    q_bias,
    v_bias,
    o_weight,
    o_bias,
    norm1_gain,
    norm1_bias,
    in_weight,
    in_bias,
    out_weight,
    out_bias,
    norm2_gain,
    norm2_bias,
):
    tokens, width = tables_in.shape
    layers, share, ffn = in_weight.shape
    ffn_share = out_weight.shape[1]
    wide_count = lax.axis_size("wide")
    assert wide_count & (wide_count - 1) == 0 and wide_count >= 1 << HALVINGS and lax.axis_size("narrow") == 4
    tile = ffn // 8
    me = lax.axis_index("narrow").astype(jnp.int32)
    wide_me = lax.axis_index("wide").astype(jnp.int32)
    y = wide_me & 1
    ids = jnp.stack([me, me ^ 1, me ^ 2, me ^ 3, y, wide_me & (2**HALVINGS - 1)])

    order = Order()

    def half_of(weight, layer):
        rows = weight.shape[1] // 2
        return lax.dynamic_slice(weight, (layer, y * rows, 0), (1, rows, weight.shape[2]))[0]

    own = (qkv_weight, o_weight, in_weight, out_weight)
    joint = jnp.concatenate([half_of(qkv_weight, 0), half_of(o_weight, 0)], axis=1)
    halves = [joint, half_of(in_weight, 0), half_of(out_weight, 0), half_of(out_weight, 1)]
    near_x, far_x, diagonal = [None] * 4, [None] * 4, [None] * 4
    core = [None] * 4

    def send_x(i):
        near_x[i] = swap(order.after(halves[i]), "narrow", 2)

    def send_core(i):
        core[i] = swap(order.after(own[i]), "narrow", 1)

    def arrive(*events):
        for kind, i in events:
            if kind == "x":
                near_x[i] = order.wait(near_x[i])
                far_x[i] = swap(near_x[i], "wide", 1)
            elif kind == "y":
                far_x[i] = order.wait(far_x[i])
                both = jnp.concatenate([near_x[i], far_x[i]], axis=0)
                order.last = both
                diagonal[i] = swap(both, "narrow", 1)
            elif kind == "d":
                diagonal[i] = order.wait(diagonal[i])
            else:
                core[i] = order.wait(core[i])

    def group(i):
        return near_x[i], far_x[i], diagonal[i]

    send_x(0)
    order.last = halves[0]
    send_core(0)
    second_attn_weights = lax.all_gather(
        jnp.concatenate([qkv_weight[1], o_weight[1]], axis=1), "narrow", axis=0, tiled=True
    )
    second_in_weight = lax.all_gather(in_weight[1], "narrow", axis=0, tiled=True)
    short = (q_bias, v_bias, o_bias, norm1_gain, norm1_bias, out_bias, norm2_gain, norm2_bias)
    packed = call(
        pack_kernel,
        "pack",
        1,
        [VMEM] * 9,
        VMEM,
        shape((layers, 12, share), f32),
        [],
        order.after(short) + (in_bias,),
    )
    others = [lax.ppermute(packed, "narrow", [(i, i ^ away) for i in range(4)]) for away in (1, 2, 3)]
    halves[1:] = order.wait(halves[1:])
    arrive(("c", 0))
    send_core(1)
    near_x[0], others = order.wait((near_x[0], others))
    far_x[0] = swap(near_x[0], "wide", 1)
    send_x(1)

    def in_order(low_one, high_one, bit):
        swapped = (me & bit) != 0
        return jnp.stack([jnp.where(swapped, high_one, low_one), jnp.where(swapped, low_one, high_one)])

    packed = in_order(in_order(packed, others[0], 1), in_order(others[1], others[2], 1), 2)
    packed = packed.reshape(4, layers, 12, share)
    small = packed[:, :, :8].transpose(1, 2, 0, 3).reshape(layers, 8, width)
    full_in_bias = packed[:, :, 8:].transpose(1, 0, 2, 3).reshape(layers, 1, ffn)
    ids, small, full_in_bias = order.wait((ids, small, full_in_bias))
    arrive(("c", 1))
    send_core(2)
    arrive(("c", 2))
    send_core(3)

    def attn_weights(layer):
        if layer == 1:
            return (second_attn_weights,)
        return (qkv_weight, core[0], o_weight, core[1]) + group(0)

    def ffn_weights(layer):
        in_refs = (second_in_weight,) if layer == 1 else (in_weight, core[2]) + group(1)
        return in_refs + (out_weight, core[3]) + group(2 + layer)

    w_qkv = pltpu.VMEM((width, 3 * width), low)
    w_o = pltpu.VMEM((width, width), low)
    w_in = pltpu.VMEM((width, ffn), low)
    w_out = pltpu.VMEM((ffn, width), low)
    copy_sems = pltpu.SemaphoreType.DMA((12,))
    pair_sems = pltpu.SemaphoreType.DMA((2,))
    rows_f32 = shape((tokens, width), f32)
    rows_low = shape((tokens, width), low)
    column_f32 = shape((tokens, 1), f32)
    eight_f32 = shape((8, width), f32)

    def pieces(rows):
        return [shape((2, 2, 2, 2, rows, tile), low)] * 2

    def stage(rows):
        return pltpu.VMEM((2, 2, 2, 2, 2, rows, tile), low)

    def attn_forward(layer, x):
        x = order.after(x)
        outs = call(
            functools.partial(attn_fwd_kernel, layer),
            "attn_fwd",
            13,
            [SMEM, SMEM] + [VMEM] * 3 + [ANY] * len(attn_weights(layer)),
            [VMEM] * 5,
            [shape((tokens, 3 * width), low), shape((HEADS, tokens, tokens), low), rows_low, rows_f32, column_f32],
            [w_qkv, w_o, pltpu.VMEM((tokens, tokens), f32), copy_sems],
            (ids, lengths, x, cell_ids, small) + attn_weights(layer),
        )
        order.last = outs[-1]
        return outs

    def ffn_forward(layer, unit_one):
        unit_one = order.after(unit_one)
        outs = call(
            functools.partial(ffn_fwd_kernel, layer),
            "ffn_fwd",
            10,
            [SMEM] + [VMEM] * 3 + [ANY] * len(ffn_weights(layer)),
            [VMEM] * 5,
            [shape((tokens, ffn), low), shape((tokens, ffn), f32), rows_f32, column_f32, rows_low],
            [w_in, w_out, pltpu.VMEM((tokens, width), low), copy_sems],
            (ids, unit_one, full_in_bias, small) + ffn_weights(layer),
        )
        order.last = outs[-2]
        return outs

    def out_backward(layer, way, grad, unit_two, inverse_two, hidden):
        grad = order.after(grad)
        outs = call(
            functools.partial(out_bwd_kernel, layer, way),
            "out_bwd",
            8,
            [SMEM] + [VMEM] * 5,
            [VMEM] * 3 + [ANY] * 2,
            [rows_low, rows_f32, eight_f32] + pieces(share),
            [stage(share), pair_sems],
            (ids, grad, unit_two, inverse_two, hidden, small),
        )
        order.last = outs[2]
        return outs

    def in_backward(layer, way, d_ffn, d_resid_two, unit_one, inverse_one, slope):
        d_ffn = order.after(d_ffn)
        outs = call(
            functools.partial(in_bwd_kernel, layer, way),
            "in_bwd",
            14,
            [SMEM] + [VMEM] * 6 + [ANY] * len(ffn_weights(layer)),
            [VMEM] * 3 + [ANY] * 2,
            [rows_f32, eight_f32, shape((1, ffn), f32)] + pieces(share),
            [
                w_in,
                w_out,
                pltpu.VMEM((tokens, ffn), low),
                pltpu.VMEM((width, tokens), low),
                stage(share),
                copy_sems,
                pair_sems,
            ],
            (ids, d_ffn, d_resid_two, unit_one, inverse_one, slope, small) + ffn_weights(layer),
        )
        order.last = outs[1]
        return outs

    def attn_backward(layer, way, d_resid, x, qkv_rows, probs, context, small_others):
        d_resid = order.after(d_resid)
        rows = share + (SMALL_ROWS if small_others else 0)
        outs = call(
            functools.partial(attn_bwd_kernel, layer, way),
            "attn_bwd",
            16,
            [SMEM] + [VMEM] * 5 + [ANY] * len(attn_weights(layer)) + [VMEM] * len(small_others),
            [VMEM] * 2 + [ANY] * 2,
            [rows_low, eight_f32] + pieces(rows),
            [
                w_qkv,
                w_o,
                pltpu.VMEM((tokens, width), low),
                pltpu.VMEM((tokens, width), low),
                pltpu.VMEM((tokens, 3 * width), low),
                pltpu.VMEM((width, tokens), low),
                stage(rows),
                copy_sems,
                pair_sems,
            ],
            (ids, d_resid, x, qkv_rows, probs, context) + attn_weights(layer) + tuple(small_others),
        )
        order.last = outs[1]
        return outs

    def unpack(layer, name, slab, earlier):
        dims = {
            "attn": [(layers, share, 3 * width), (layers, share, width)],
            "in": [(layers, share, ffn)],
            "out": [(layers, ffn_share, width)],
        }[name]
        last = name == "attn" and layer == 0
        extra = [(layers, share)] * 8 + [(layers, ffn_share)] if last else [(8, 128)]
        gathered = order.after(slab.gathered)
        rows = gathered.shape[1]
        outs = call(
            functools.partial(unpack_kernel, layer, name, len(earlier)),
            "unpack",
            4,
            [ANY] * (1 + len(earlier)),
            [ANY] * len(dims) + [VMEM] * len(extra),
            [shape(d, f32) for d in dims + extra],
            [
                pltpu.VMEM((8, rows, tile), low),
                pltpu.VMEM((8, share, tile), f32),
                pltpu.SemaphoreType.DMA((8,)),
                pltpu.SemaphoreType.DMA((8,)),
            ],
            (gathered, *earlier),
            {1 + i: i for i in range(len(earlier))},
        )
        order.last = outs[-1]
        return tuple(outs)

    arrive(("x", 1))
    send_x(2)
    arrive(("y", 0), ("c", 3), ("d", 0))
    first_attn = attn_forward(0, tables_in)
    arrive(("x", 2))
    send_x(3)
    arrive(("y", 1), ("y", 2), ("d", 1), ("d", 2))
    first_ffn = ffn_forward(0, first_attn[3])
    arrive(("x", 3))
    second_attn_weights = order.wait(second_attn_weights)
    second_attn = attn_forward(1, first_ffn[4])
    second_in_weight = order.wait(second_in_weight)
    arrive(("y", 3), ("d", 3))
    second_ffn = ffn_forward(1, second_attn[3])
    mixed_out = second_ffn[4]
    inputs = (tables_in, first_ffn[4])
    attn_kept, ffn_kept = (first_attn, second_attn), (first_ffn, second_ffn)

    slabs = [None] * 6
    grad = cotangent
    small_out, small_in, small_attn, bias_grads = [None] * 2, [None] * 2, [None] * 2, [None] * 2
    unpacked = {"attn": (), "in": (), "out": ()}
    for action in PLAN:
        if isinstance(action, int):
            slab = slabs[action]
            slab.step(order)
            if slab.ended():
                name = ("out", "in", "attn")[action % 3]
                unpacked[name] = unpack(layers - 1 - action // 3, name, slab, unpacked[name][: 2 if name == "attn" else 1])
            continue
        name, layer = action[:-1], int(action[-1])
        which = 3 * (layers - 1 - layer) + ("out", "in", "attn").index(name)
        way = WAYS[which]
        qkv_rows, probs, context, unit_one, inverse_one = attn_kept[layer]
        hidden, slope, unit_two, inverse_two, _ = ffn_kept[layer]
        if name == "out":
            d_ffn, d_resid_two, small_out[layer], kept, sent = out_backward(
                layer, way, grad, unit_two, inverse_two, hidden
            )
        elif name == "in":
            d_resid, small_in[layer], bias_grads[layer], kept, sent = in_backward(
                layer, way, d_ffn, d_resid_two, unit_one, inverse_one, slope
            )
        else:
            small_others = ()
            if layer == 0:
                small_others = (
                    small_out[0],
                    small_in[0],
                    bias_grads[0],
                    small_out[1],
                    small_in[1],
                    bias_grads[1],
                    small_attn[1],
                )
            grad, small_attn[layer], kept, sent = attn_backward(
                layer, way, d_resid, inputs[layer], qkv_rows, probs, context, small_others
            )
        slabs[which] = Slab(way, wide_count, kept, sent)
    qkv_grad, o_grad, *vectors = unpacked["attn"]
    in_grad, out_grad = unpacked["in"][0], unpacked["out"][0]
    return (
        mixed_out,
        grad,
        qkv_grad,
        vectors[0],
        vectors[1],
        o_grad,
        vectors[2],
        vectors[3],
        vectors[4],
        in_grad,
        vectors[8],
        out_grad,
        vectors[5],
        vectors[6],
        vectors[7],
    )


def solution(mesh):
    by_table = P(("wide", "narrow"), None)
    matrix = P(None, "narrow", None)
    vector = P(None, "narrow")
    return jax.shard_map(
        body,
        mesh=mesh,
        in_specs=(
            by_table,
            by_table,
            by_table,
            P(("wide", "narrow")),
            matrix,
            vector,
            vector,
            matrix,
            vector,
            vector,
            vector,
            matrix,
            vector,
            matrix,
            vector,
            vector,
            vector,
        ),
        out_specs=(
            by_table,
            by_table,
            matrix,
            vector,
            vector,
            matrix,
            vector,
            vector,
            vector,
            matrix,
            vector,
            matrix,
            vector,
            vector,
            vector,
        ),
        check_vma=False,
    )
```

```python
import functools
import math

import jax
import jax.numpy as jnp
from jax import lax
from jax.experimental import pallas as pl
from jax.experimental.pallas import tpu as pltpu
from jax.sharding import PartitionSpec as P

HEADS = 12
norm_eps = 1e-12
masked_score = -1000000000.0
low = jnp.bfloat16
f32 = jnp.float32
VMEM_BYTES = 56 * 1024 * 1024
HALVINGS = 2


def swap(value, axis, bit):
    count = lax.axis_size(axis)
    return lax.ppermute(value, axis, [(i, i ^ bit) for i in range(count)])


def dot(a, b):
    return jnp.dot(a, b, preferred_element_type=f32)


def dot_nt(a, b):
    return lax.dot_general(a, b, (((1,), (1,)), ((), ())), preferred_element_type=f32)


def dot_tn(a, b):
    return lax.dot_general(a, b, (((0,), (0,)), ((), ())), preferred_element_type=f32)


def normalize(residual):
    center = residual - jnp.mean(residual, axis=-1, keepdims=True)
    inverse = lax.rsqrt(jnp.mean(center * center, axis=-1, keepdims=True) + norm_eps)
    return center * inverse, inverse


def normalize_back(grad_unit, unit, inverse):
    centered = grad_unit - jnp.mean(grad_unit, axis=-1, keepdims=True)
    return inverse * (centered - unit * jnp.mean(grad_unit * unit, axis=-1, keepdims=True))


def weight_copies(ids, layer, pieces, target, columns, sems, base):
    own, core, near_x, far_x, diagonal = pieces
    rows = own.shape[1]
    half = rows // 2
    n, y = ids[0], ids[4]
    copies = []

    def add(source, start, count):
        where = target.at[pl.ds(pl.multiple_of(start, half), count), :]
        copies.append(pltpu.make_async_copy(source, where, sems.at[base + len(copies)]))

    at = pl.ds(columns, target.shape[1])
    add(own.at[layer], n * rows, rows)
    add(core.at[layer], ids[1] * rows, rows)
    add(near_x.at[:, at], ids[2] * rows + y * half, half)
    add(far_x.at[:, at], ids[2] * rows + (1 - y) * half, half)
    add(diagonal.at[pl.ds(0, half), at], ids[3] * rows + y * half, half)
    add(diagonal.at[pl.ds(half, half), at], ids[3] * rows + (1 - y) * half, half)
    return copies


def begin(copies):
    for copy in copies:
        copy.start()


def finish(copies):
    for copy in copies:
        copy.wait()


def attn_copies(layer, ids, refs, w_qkv, w_o, sems):
    qkv_own, qkv_core, o_own, o_core = refs[:4]
    halves = refs[4:]
    qkv = weight_copies(ids, layer, (qkv_own, qkv_core) + halves, w_qkv, 0, sems, 0)
    o = weight_copies(ids, layer, (o_own, o_core) + halves, w_o, w_qkv.shape[1], sems, 6)
    return qkv, o


def ffn_copies(layer, ids, refs, w_in, w_out, sems):
    in_copies = weight_copies(ids, layer, refs[:5], w_in, 0, sems, 0)
    out_copies = weight_copies(ids, layer, refs[5:], w_out, 0, sems, 6)
    return in_copies, out_copies


def pack_kernel(*refs):
    shorts, in_bias, packed = refs[:8], refs[8], refs[9]
    layers, share = shorts[0].shape
    for layer in range(layers):
        for i, short in enumerate(shorts):
            packed[layer, i : i + 1, :] = short[layer : layer + 1, :].astype(f32)
        for i in range(4):
            packed[layer, 8 + i : 9 + i, :] = in_bias[layer : layer + 1, i * share : (i + 1) * share].astype(f32)


def attn_fwd_kernel(layer, ids, length, x, cell_row, small, *rest):
    weights, rest = rest[:7], rest[7:]
    qkv_rows, probs, context, unit_out, inverse_out, w_qkv, w_o, mask, sems = rest
    tokens, width = x.shape
    qkv_copies, o_copies = attn_copies(layer, ids, weights, w_qkv, w_o, sems)
    begin(qkv_copies)
    begin(o_copies)
    position = lax.broadcasted_iota(jnp.int32, (1, tokens), 1)
    key_cell = cell_row[...]
    square = (tokens, tokens)
    diagonal = lax.broadcasted_iota(jnp.int32, square, 0) == lax.broadcasted_iota(jnp.int32, square, 1)
    query_cell = jnp.sum(jnp.where(diagonal, key_cell, 0), axis=1, keepdims=True)
    allowed = (query_cell == key_cell) | (key_cell == 0) | (query_cell == 0)
    allowed = allowed & (position < length[0])
    mask[...] = jnp.where(allowed, 0.0, masked_score)
    scale = 1.0 / math.sqrt(width // HEADS)
    finish(qkv_copies)
    tile = width // 2

    for t in range(6):
        columns = slice(t * tile, (t + 1) * tile)
        rows = dot(x[...], w_qkv[:, columns])
        if t // 2 != 1:
            part = slice((t % 2) * tile, (t % 2 + 1) * tile)
            rows = rows + small[layer, t // 4 : t // 4 + 1, part]
        if t < 2:
            rows = rows * scale
        qkv_rows[:, columns] = rows.astype(low)

    pair_width = 2 * width // HEADS
    first = lax.broadcasted_iota(jnp.int32, (1, pair_width), 1) < pair_width // 2

    for pair in range(HEADS // 2):
        at = slice(pair * pair_width, (pair + 1) * pair_width)
        query = qkv_rows[:, at]
        key = qkv_rows[:, width + at.start : width + at.stop]
        value = qkv_rows[:, 2 * width + at.start : 2 * width + at.stop]
        sides = []
        for side in range(2):
            mine = first if side == 0 else jnp.logical_not(first)
            scores = dot_nt(jnp.where(mine, query, jnp.zeros_like(query)), key) + mask[...]
            shifted = jnp.exp(scores - jnp.max(scores, axis=-1, keepdims=True))
            total = jnp.sum(shifted, axis=-1, keepdims=True)
            prob = (shifted * (1.0 / total)).astype(low)
            probs[2 * pair + side] = prob
            sides.append(dot(prob, value))
        context[:, at] = jnp.where(first, sides[0], sides[1]).astype(low)

    finish(o_copies)
    residual = x[...].astype(f32) + (dot(context[...], w_o[...]) + small[layer, 2:3, :])
    unit, inverse = normalize(residual)
    unit_out[...] = unit
    inverse_out[...] = inverse


def gelu_and_slope(x):
    t = 1.0 / (1.0 + (0.3275911 * math.sqrt(0.5)) * jnp.abs(x))
    bell = jnp.exp(-0.5 * x * x)
    series = 1.421413741 + t * (-1.453152027 + t * 1.061405429)
    series = t * (0.254829592 + t * (-0.284496736 + t * series))
    tail = 0.5 * series * bell
    cdf = jnp.where(x >= 0.0, 1.0 - tail, tail)
    return (x * cdf).astype(low), cdf + x * (bell * (1.0 / math.sqrt(2.0 * math.pi)))


def ffn_fwd_kernel(layer, ids, unit_one, in_bias, small, *rest):
    weights, rest = rest[:10], rest[10:]
    hidden, slope, unit_out, inverse_out, result, w_in, w_out, normed_low, sems = rest
    in_copies, out_copies = ffn_copies(layer, ids, weights, w_in, w_out, sems)
    begin(in_copies)
    begin(out_copies)
    normed = unit_one[...] * small[layer, 3:4, :] + small[layer, 4:5, :]
    normed_low[...] = normed.astype(low)
    finish(in_copies)
    tile = w_in.shape[1] // 8

    for t in range(8):
        columns = slice(t * tile, (t + 1) * tile)
        pre = dot(normed_low[...], w_in[:, columns]) + in_bias[layer, :, columns]
        hidden[:, columns], slope[:, columns] = gelu_and_slope(pre)

    finish(out_copies)
    residual = unit_one[...] * small[layer, 3:4, :] + small[layer, 4:5, :] + (dot(hidden[...], w_out[...]) + small[layer, 5:6, :])
    unit, inverse = normalize(residual)
    unit_out[...] = unit
    inverse_out[...] = inverse
    result[...] = (unit * small[layer, 6:7, :] + small[layer, 7:8, :]).astype(low)


WIDE_BIT = {"y": 0, "z": 1}


def place_of(ids, owner, piece, way):
    away = None if owner is None else ids[0] ^ owner
    off = None if piece is None else piece ^ ids[5]
    place = [None if away is None else away & 1]
    for name in way:
        if name == "x":
            place.append(pl.ds(0, 2) if away is None else away >> 1)
        else:
            place.append(pl.ds(0, 2) if off is None else (off >> WIDE_BIT[name]) & 1)
    return tuple(place) + (pl.ds(0, 2) if piece is None else piece >> 2,)


def store_rows(stage, ids, product, piece, way):
    share = product.shape[0] // 4
    for owner in range(4):
        block = product[owner * share : (owner + 1) * share].astype(low)
        stage[place_of(ids, owner, piece, way) + (pl.ds(0, share),)] = block


def piece_copies(stage, ids, piece, way, kept, sent, sems):
    at = place_of(ids, None, piece, way)[1:]
    copies = [
        pltpu.make_async_copy(stage.at[(1,) + at], sent.at[at], sems.at[2 * piece]),
        pltpu.make_async_copy(stage.at[(0,) + at], kept.at[at], sems.at[2 * piece + 1]),
    ]
    begin(copies)
    return copies


def out_bwd_kernel(layer, way, ids, grad, unit_two, inverse_two, hidden, small, *rest):
    d_ffn, d_resid_two, small_grads, kept, sent, stage, out_sems = rest
    g = grad[...].astype(f32)
    unit = unit_two[...]
    small_grads[0:1, :] = jnp.sum(g * unit, axis=0, keepdims=True)
    small_grads[1:2, :] = jnp.sum(g, axis=0, keepdims=True)
    d_two = normalize_back(g * small[layer, 6:7, :], unit, inverse_two[...])
    d_resid_two[...] = d_two
    d_low = d_two.astype(low)
    d_ffn[...] = d_low
    small_grads[2:3, :] = jnp.sum(d_low.astype(f32), axis=0, keepdims=True)
    small_grads[3:8, :] = jnp.zeros((5, unit.shape[1]), f32)
    tile = hidden.shape[1] // 8
    share = d_ffn.shape[1] // 4
    waits = []
    for owner in range(4):
        for half in range(2):
            columns = slice((2 * owner + half) * tile, (2 * owner + half + 1) * tile)
            out_grad = dot_tn(hidden[:, columns], d_ffn[...])
            for row_group in range(2):
                for column_group in range(2):
                    piece = (half * 2 + row_group) * 2 + column_group
                    block = out_grad[
                        row_group * share : (row_group + 1) * share,
                        column_group * tile : (column_group + 1) * tile,
                    ]
                    stage[place_of(ids, owner, piece, way)] = block.astype(low)
        core, *at = place_of(ids, owner, None, way)
        at = tuple(at)
        to_kept = pltpu.make_async_copy(stage.at[(0,) + at], kept.at[at], out_sems.at[owner])
        to_sent = pltpu.make_async_copy(stage.at[(1,) + at], sent.at[at], out_sems.at[owner])
        pl.when(core == 0)(to_kept.start)
        pl.when(core == 1)(to_sent.start)
        waits.append(to_kept)
    finish(waits)


def in_bwd_kernel(layer, way, ids, d_ffn, d_resid_two, unit_one, inverse_one, slope, small, *rest):
    weights, rest = rest[:10], rest[10:]
    d_resid, small_grads, in_bias_grad, kept, sent = rest[:5]
    w_in, w_out, d_pre, normed_t, stage, sems, out_sems = rest[5:]
    in_copies, out_copies = ffn_copies(layer, ids, weights, w_in, w_out, sems)
    begin(out_copies)
    begin(in_copies)
    normed = unit_one[...] * small[layer, 3:4, :] + small[layer, 4:5, :]
    normed_t[...] = normed.astype(low).T
    finish(out_copies)
    tile = w_in.shape[1] // 8
    going = []
    for t in range(8):
        columns = slice(t * tile, (t + 1) * tile)
        d_hidden = dot_nt(d_ffn[...], w_out[columns, :])
        d_tile = (d_hidden * slope[:, columns]).astype(low)
        d_pre[:, columns] = d_tile
        in_bias_grad[:, columns] = jnp.sum(d_tile.astype(f32), axis=0, keepdims=True)
        store_rows(stage, ids, dot(normed_t[...], d_tile), t, way)
        going += piece_copies(stage, ids, t, way, kept, sent, out_sems)
    finish(in_copies)
    d_normed = d_resid_two[...] + dot_nt(d_pre[...], w_in[...])
    unit = unit_one[...]
    small_grads[0:1, :] = jnp.sum(d_normed * unit, axis=0, keepdims=True)
    small_grads[1:2, :] = jnp.sum(d_normed, axis=0, keepdims=True)
    small_grads[2:8, :] = jnp.zeros((6, unit.shape[1]), f32)
    d_resid[...] = normalize_back(d_normed * small[layer, 3:4, :], unit, inverse_one[...])
    finish(going)


def attn_bwd_kernel(layer, way, ids, d_resid, x, qkv_rows, probs, context, *rest):
    weights, others, rest = rest[:7], rest[7:-13], rest[-13:]
    d_input, small_grads, kept, sent = rest[:4]
    w_qkv, w_o, d_attn, d_context, d_qkv, x_t, stage, sems, out_sems = rest[4:]
    tokens, width = x.shape
    qkv_copies, o_copies = attn_copies(layer, ids, weights, w_qkv, w_o, sems)
    begin(o_copies)
    begin(qkv_copies)
    d_low = d_resid[...].astype(low)
    d_attn[...] = d_low
    small_grads[2:3, :] = jnp.sum(d_low.astype(f32), axis=0, keepdims=True)
    x_t[...] = x[...].T
    tile = width // 2
    for half in range(2):
        product = dot_tn(context[...], d_attn[:, half * tile : (half + 1) * tile])
        store_rows(stage, ids, product, 6 + half, way)
    finish(o_copies)
    d_context[...] = dot_nt(d_attn[...], w_o[...]).astype(low)
    pair_width = 2 * width // HEADS
    first = lax.broadcasted_iota(jnp.int32, (1, pair_width), 1) < pair_width // 2
    scale = 1.0 / math.sqrt(width // HEADS)

    for pair in range(HEADS // 2):
        at_query = slice(pair * pair_width, (pair + 1) * pair_width)
        at_key = slice(width + at_query.start, width + at_query.stop)
        at_value = slice(2 * width + at_query.start, 2 * width + at_query.stop)
        query, key, value = qkv_rows[:, at_query], qkv_rows[:, at_key], qkv_rows[:, at_value]
        d_ctx = d_context[:, at_query]
        sides = []
        for side in range(2):
            mine = first if side == 0 else jnp.logical_not(first)
            prob_low = probs[2 * pair + side]
            prob = prob_low.astype(f32)
            d_prob = dot_nt(jnp.where(mine, d_ctx, jnp.zeros_like(d_ctx)), value)
            inner = jnp.sum(prob * d_prob, axis=-1, keepdims=True)
            d_scores = (prob * (d_prob - inner)).astype(low)
            sides.append((dot(d_scores, key), dot_tn(d_scores, query), dot_tn(prob_low, d_ctx)))
        d_qkv[:, at_query] = (jnp.where(first, sides[0][0], sides[1][0]) * scale).astype(low)
        d_qkv[:, at_key] = jnp.where(first, sides[0][1], sides[1][1]).astype(low)
        d_qkv[:, at_value] = jnp.where(first, sides[0][2], sides[1][2]).astype(low)

    small_grads[0:1, :] = jnp.sum(d_qkv[:, :width].astype(f32), axis=0, keepdims=True)
    small_grads[1:2, :] = jnp.sum(d_qkv[:, 2 * width :].astype(f32), axis=0, keepdims=True)
    small_grads[3:8, :] = jnp.zeros((5, width), f32)
    if others:
        share = width // 4
        sources = small_sources(layer, small_grads, others)
        for owner in range(4):
            for piece in range(8):
                lines = []
                for source, row, start, step in sources[3 * piece : 3 * piece + 3]:
                    line = source[row : row + 1, start + owner * step : start + owner * step + share]
                    lines.append(jnp.concatenate([line, jnp.zeros_like(line)], axis=1))
                lines.append(jnp.zeros((SMALL_ROWS - 3, tile), f32))
                block = jnp.concatenate(lines, axis=0).astype(low)
                stage[place_of(ids, owner, piece, way) + (pl.ds(share, SMALL_ROWS),)] = block
    going = []
    for piece in (6, 7, 0, 1, 2, 3, 4, 5):
        if piece < 6:
            store_rows(stage, ids, dot(x_t[...], d_qkv[:, piece * tile : (piece + 1) * tile]), piece, way)
        going += piece_copies(stage, ids, piece, way, kept, sent, out_sems)
    finish(qkv_copies)
    d_input[...] = (d_resid[...] + dot_nt(d_qkv[...], w_qkv[...])).astype(low)
    finish(going)


SMALL_ROWS = 16
SMALL_LINES = (("attn", 0), ("attn", 1), ("attn", 2), ("in", 0), ("in", 1), ("out", 2), ("out", 0), ("out", 1))


def small_sources(layer, own, others):
    found = []
    out_0, in_0, bias_0, out_1, in_1, bias_1, attn_1 = others
    refs = ({"attn": own, "in": in_0, "out": out_0}, {"attn": attn_1, "in": in_1, "out": out_1})
    width = own.shape[1]
    for of_layer, bias in zip(refs, (bias_0, bias_1)):
        found += [(of_layer[name], row, 0, width // 4) for name, row in SMALL_LINES]
        found += [(bias, 0, i * (width // 4), width) for i in range(4)]
    return found


def unpack_kernel(layer, slab, back, earlier, ids, near, far, *rest):
    outs = rest[earlier:-4]
    buffer, wide_buffer, in_sems, out_sems = rest[-4:]
    share, tile = wide_buffer.shape[1:]

    def fetch(piece, ref, index):
        return pltpu.make_async_copy(ref.at[index], buffer.at[piece], in_sems.at[piece])

    for piece in range(8):
        off = piece ^ ids[5]
        inner, outer = [(off >> WIDE_BIT[name]) & 1 for name in back]
        pl.when(outer == 0)(fetch(piece, near, (inner, piece >> 2)).start)
        pl.when(outer == 1)(fetch(piece, far, (inner, piece >> 2)).start)

    copies = []
    for piece in range(8):
        fetch(piece, near, (0, 0)).wait()
        wide_buffer[piece] = buffer[piece, :share].astype(f32)
        columns = pl.ds(piece * tile, tile)
        if slab == "in":
            target = outs[0].at[layer, :, columns]
        elif slab == "out":
            rows = pl.ds((piece // 2) * share, share)
            target = outs[0].at[layer, rows, pl.ds((piece % 2) * tile, tile)]
        elif piece < 6:
            target = outs[0].at[layer, :, columns]
        else:
            target = outs[1].at[layer, :, pl.ds((piece - 6) * tile, tile)]
        copies.append(pltpu.make_async_copy(wide_buffer.at[piece], target, out_sems.at[piece]))
        copies[-1].start()
    if slab == "attn" and layer == 0:
        for line in range(24):
            of_layer, which = line // 12, line % 12
            row = share + line % 3
            values = buffer[line // 3, row : row + 1, :share].astype(f32)
            if which < 8:
                outs[2 + which][of_layer : of_layer + 1, :] = values
            else:
                at = (which - 8) * share
                outs[10][of_layer : of_layer + 1, at : at + share] = values
    else:
        outs[-1][...] = jnp.zeros(outs[-1].shape, f32)
    finish(copies)


SMEM = pl.BlockSpec(memory_space=pltpu.SMEM)
VMEM = pl.BlockSpec(memory_space=pltpu.VMEM)
ANY = pl.BlockSpec(memory_space=pl.ANY)


def call(kernel, name, time, in_specs, out_specs, out_shape, scratch, args, aliases=()):
    return pl.pallas_call(
        kernel,
        name=name,
        in_specs=in_specs,
        out_specs=out_specs,
        out_shape=out_shape,
        scratch_shapes=scratch,
        input_output_aliases=dict(aliases),
        compiler_params=pltpu.CompilerParams(vmem_limit_bytes=VMEM_BYTES),
        cost_estimate=pl.CostEstimate(
            flops=int(time * 0.45e9), bytes_accessed=int(time * 1.4e6), transcendentals=0
        ),
    )(*args)


def shape(dims, kind):
    return jax.ShapeDtypeStruct(dims, kind)


def added(a, b):
    return (a.astype(f32) + b.astype(f32)).astype(low)


WAYS = ("xyz", "xzy", "xyz", "yzx", "xyz", "xyz")
BACKS = ("zy", "zy", "yz", "zy", "zy", "yz")
PLAN = (
    "out1", 0, "in1", "attn1", 0, 1, "out0", 2, 0, 3, 0, "in0", 0, 3, 0, 2, 4, 1, 3, 0, "attn0", 2, 4, 5, 1,
    3, 4, 1, 3, 2, 5, 3, 1, 4, 5, 2, 1, 5, 4, 3, 2, 5, 4, 5, 1, 2, 4, 5,
)


class Order:
    def __init__(self):
        self.last = None

    def after(self, values):
        if self.last is None:
            return values
        values, self.last = lax.optimization_barrier((values, self.last))
        return values

    def wait(self, values):
        values = self.after(values)
        self.last = values
        return values


STEPS = {"x": ("narrow", 2), "y": ("wide", 1), "z": ("wide", 2)}


class Slab:
    def __init__(self, way, back, wide_count, kept, sent):
        self.kept = kept
        self.way, self.back = way, back
        self.rest = [1 << b for b in range(HALVINGS, wide_count.bit_length() - 1)]
        self.flying = swap(sent, "narrow", 1)
        self.stage = 0

    def step(self, order):
        received = order.after(self.flying)
        stage, way = self.stage, self.way
        if stage < len(way):
            send = added(self.kept[1], received[1])
            self.kept = added(self.kept[0], received[0])
            self.flying = swap(send, *STEPS[way[stage]])
            order.last = send
        elif stage < len(way) + 1 + len(self.back):
            if stage == len(way):
                piece = added(self.kept, received)
                if not self.rest:
                    self.block = piece[None]
            elif stage == len(way) + 1 and self.rest:
                piece = added(self.kept, received)
                for bit in self.rest[1:]:
                    piece = added(piece, swap(piece, "wide", bit))
                self.block = piece[None]
            else:
                self.block = jnp.concatenate([self.block, received], axis=0)
                piece = self.block
            order.last = piece
            if stage == len(way) and self.rest:
                self.kept = piece
                self.flying = swap(piece, "wide", self.rest[0])
            else:
                self.flying = swap(self.block, *STEPS[self.back[stage - len(way) - 1]])
        else:
            self.far = received
        self.stage += 1

    def ended(self):
        return self.stage == len(self.way) + len(self.back) + 2


def body(
    tables_in,
    cotangent,
    cell_ids,
    lengths,
    qkv_weight,
    q_bias,
    v_bias,
    o_weight,
    o_bias,
    norm1_gain,
    norm1_bias,
    in_weight,
    in_bias,
    out_weight,
    out_bias,
    norm2_gain,
    norm2_bias,
):
    tokens, width = tables_in.shape
    layers, share, ffn = in_weight.shape
    ffn_share = out_weight.shape[1]
    wide_count = lax.axis_size("wide")
    assert wide_count & (wide_count - 1) == 0 and wide_count >= 1 << HALVINGS and lax.axis_size("narrow") == 4
    tile = ffn // 8
    me = lax.axis_index("narrow").astype(jnp.int32)
    wide_me = lax.axis_index("wide").astype(jnp.int32)
    y = wide_me & 1
    ids = jnp.stack([me, me ^ 1, me ^ 2, me ^ 3, y, wide_me & (2**HALVINGS - 1)])

    order = Order()

    def half_of(weight, layer):
        rows = weight.shape[1] // 2
        return lax.dynamic_slice(weight, (layer, y * rows, 0), (1, rows, weight.shape[2]))[0]

    halves = []
    for layer in range(layers):
        joint = jnp.concatenate([half_of(qkv_weight, layer), half_of(o_weight, layer)], axis=1)
        halves += [joint, half_of(in_weight, layer), half_of(out_weight, layer)]
    near_x, far_x, diagonal = [None] * len(halves), [None] * len(halves), [None] * len(halves)
    core = [None] * 4
    own = (qkv_weight, o_weight, in_weight, out_weight)

    def group(i):
        return near_x[i], far_x[i], diagonal[i]

    def attn_weights(layer):
        return (qkv_weight, core[0], o_weight, core[1]) + group(3 * layer)

    def ffn_weights(layer):
        return (in_weight, core[2]) + group(3 * layer + 1) + (out_weight, core[3]) + group(3 * layer + 2)

    def in_order(low_one, high_one, bit):
        swapped = (me & bit) != 0
        return jnp.stack([jnp.where(swapped, high_one, low_one), jnp.where(swapped, low_one, high_one)])

    near_x[0] = swap(halves[0], "narrow", 2)
    order.last = halves[0]
    core[0], core[1] = swap(own[0], "narrow", 1), swap(own[1], "narrow", 1)
    short = order.after((q_bias, v_bias, o_bias, norm1_gain, norm1_bias, out_bias, norm2_gain, norm2_bias))
    packed = call(
        pack_kernel, "pack", 1, [VMEM] * 9, VMEM, shape((layers, 12, share), f32), [], tuple(short) + (in_bias,)
    )
    others = [lax.ppermute(packed, "narrow", [(i, i ^ away) for i in range(4)]) for away in (1, 2, 3)]
    halves[1:] = order.wait(halves[1:])
    near_x[0], others, core[0], core[1] = order.wait((near_x[0], others, core[0], core[1]))

    far_x[0] = swap(near_x[0], "wide", 1)
    core[2] = swap(order.after(own[2]), "narrow", 1)
    near_x[1] = swap(order.after(halves[1]), "narrow", 2)
    packed = in_order(in_order(packed, others[0], 1), in_order(others[1], others[2], 1), 2)
    packed = packed.reshape(4, layers, 12, share)
    small = packed[:, :, :8].transpose(1, 2, 0, 3).reshape(layers, 8, width)
    full_in_bias = packed[:, :, 8:].transpose(1, 0, 2, 3).reshape(layers, 1, ffn)
    ids, small, full_in_bias = order.wait((ids, small, full_in_bias))
    far_x[0], near_x[1], core[2] = order.wait((far_x[0], near_x[1], core[2]))

    def join(i):
        both = jnp.concatenate([near_x[i], far_x[i]], axis=0)
        diagonal[i] = swap(both, "narrow", 1)
        return both

    def begin_round(i):
        both = join(i)
        if i + 1 < len(halves):
            far_x[i + 1] = swap(near_x[i + 1], "wide", 1)
        if i + 2 < len(halves):
            near_x[i + 2] = swap(order.after(halves[i + 2]), "narrow", 2)
        order.last = both

    def end_round(i):
        if i + 2 < len(halves):
            far_x[i + 1], near_x[i + 2] = order.wait((far_x[i + 1], near_x[i + 2]))
        elif i + 1 < len(halves):
            far_x[i + 1] = order.wait(far_x[i + 1])

    def arrive(i):
        diagonal[i] = order.wait(diagonal[i])

    begin_round(0)
    core[3] = swap(order.after(own[3]), "narrow", 1)
    arrive(0)
    core[3] = order.wait(core[3])
    end_round(0)

    w_qkv = pltpu.VMEM((width, 3 * width), low)
    w_o = pltpu.VMEM((width, width), low)
    w_in = pltpu.VMEM((width, ffn), low)
    w_out = pltpu.VMEM((ffn, width), low)
    copy_sems = pltpu.SemaphoreType.DMA((12,))
    piece_sems = pltpu.SemaphoreType.DMA((16,))
    rows_f32 = shape((tokens, width), f32)
    rows_low = shape((tokens, width), low)
    column_f32 = shape((tokens, 1), f32)
    eight_f32 = shape((8, width), f32)

    def pieces(rows):
        return [shape((2, 2, 2, 2, rows, tile), low)] * 2

    def stage(rows):
        return pltpu.VMEM((2, 2, 2, 2, 2, rows, tile), low)

    def attn_forward(layer, x):
        x = order.after(x)
        outs = call(
            functools.partial(attn_fwd_kernel, layer),
            "attn_fwd",
            13,
            [SMEM, SMEM] + [VMEM] * 3 + [ANY] * 7,
            [VMEM] * 5,
            [shape((tokens, 3 * width), low), shape((HEADS, tokens, tokens), low), rows_low, rows_f32, column_f32],
            [w_qkv, w_o, pltpu.VMEM((tokens, tokens), f32), copy_sems],
            (ids, lengths, x, cell_ids, small) + attn_weights(layer),
        )
        order.last = outs[-1]
        return outs

    def ffn_forward(layer, unit_one):
        unit_one = order.after(unit_one)
        outs = call(
            functools.partial(ffn_fwd_kernel, layer),
            "ffn_fwd",
            10,
            [SMEM] + [VMEM] * 3 + [ANY] * 10,
            [VMEM] * 5,
            [shape((tokens, ffn), low), shape((tokens, ffn), f32), rows_f32, column_f32, rows_low],
            [w_in, w_out, pltpu.VMEM((tokens, width), low), copy_sems],
            (ids, unit_one, full_in_bias, small) + ffn_weights(layer),
        )
        order.last = outs[-2]
        return outs

    def out_backward(layer, way, grad, unit_two, inverse_two, hidden):
        grad = order.after(grad)
        outs = call(
            functools.partial(out_bwd_kernel, layer, way),
            "out_bwd",
            8,
            [SMEM] + [VMEM] * 5,
            [VMEM] * 3 + [ANY] * 2,
            [rows_low, rows_f32, eight_f32] + pieces(share),
            [stage(share), pltpu.SemaphoreType.DMA((4,))],
            (ids, grad, unit_two, inverse_two, hidden, small),
        )
        order.last = outs[2]
        return outs

    def in_backward(layer, way, d_ffn, d_resid_two, unit_one, inverse_one, slope):
        d_ffn = order.after(d_ffn)
        outs = call(
            functools.partial(in_bwd_kernel, layer, way),
            "in_bwd",
            14,
            [SMEM] + [VMEM] * 6 + [ANY] * 10,
            [VMEM] * 3 + [ANY] * 2,
            [rows_f32, eight_f32, shape((1, ffn), f32)] + pieces(share),
            [
                w_in,
                w_out,
                pltpu.VMEM((tokens, ffn), low),
                pltpu.VMEM((width, tokens), low),
                stage(share),
                copy_sems,
                piece_sems,
            ],
            (ids, d_ffn, d_resid_two, unit_one, inverse_one, slope, small) + ffn_weights(layer),
        )
        order.last = outs[1]
        return outs

    def attn_backward(layer, way, d_resid, x, qkv_rows, probs, context, small_others):
        d_resid = order.after(d_resid)
        rows = share + (SMALL_ROWS if small_others else 0)
        outs = call(
            functools.partial(attn_bwd_kernel, layer, way),
            "attn_bwd",
            16,
            [SMEM] + [VMEM] * 5 + [ANY] * 7 + [VMEM] * len(small_others),
            [VMEM] * 2 + [ANY] * 2,
            [rows_low, eight_f32] + pieces(rows),
            [
                w_qkv,
                w_o,
                pltpu.VMEM((tokens, width), low),
                pltpu.VMEM((tokens, width), low),
                pltpu.VMEM((tokens, 3 * width), low),
                pltpu.VMEM((width, tokens), low),
                stage(rows),
                copy_sems,
                piece_sems,
            ],
            (ids, d_resid, x, qkv_rows, probs, context) + attn_weights(layer) + tuple(small_others),
        )
        order.last = outs[1]
        return outs

    def unpack(layer, name, slab, earlier):
        dims = {
            "attn": [(layers, share, 3 * width), (layers, share, width)],
            "in": [(layers, share, ffn)],
            "out": [(layers, ffn_share, width)],
        }[name]
        last = name == "attn" and layer == 0
        extra = [(layers, share)] * 8 + [(layers, ffn_share)] if last else [(8, 128)]
        near, far = order.after((slab.block, slab.far))
        rows = near.shape[2]
        outs = call(
            functools.partial(unpack_kernel, layer, name, slab.back, len(earlier)),
            "unpack",
            4,
            [SMEM] + [ANY] * (2 + len(earlier)),
            [ANY] * len(dims) + [VMEM] * len(extra),
            [shape(d, f32) for d in dims + extra],
            [
                pltpu.VMEM((8, rows, tile), low),
                pltpu.VMEM((8, share, tile), f32),
                pltpu.SemaphoreType.DMA((8,)),
                pltpu.SemaphoreType.DMA((8,)),
            ],
            (ids, near, far, *earlier),
            {3 + i: i for i in range(len(earlier))},
        )
        order.last = outs[-1]
        return tuple(outs)

    begin_round(1)
    first_attn = attn_forward(0, tables_in)
    arrive(1)
    end_round(1)
    begin_round(2)
    arrive(2)
    first_ffn = ffn_forward(0, first_attn[3])
    end_round(2)
    begin_round(3)
    arrive(3)
    second_attn = attn_forward(1, first_ffn[4])
    end_round(3)
    begin_round(4)
    arrive(4)
    end_round(4)
    begin_round(5)
    arrive(5)
    second_ffn = ffn_forward(1, second_attn[3])
    mixed_out = second_ffn[4]
    inputs = (tables_in, first_ffn[4])
    attn_kept, ffn_kept = (first_attn, second_attn), (first_ffn, second_ffn)

    slabs = [None] * 6
    grad = cotangent
    small_out, small_in, small_attn, bias_grads = [None] * 2, [None] * 2, [None] * 2, [None] * 2
    unpacked = {"attn": (), "in": (), "out": ()}
    for action in PLAN:
        if isinstance(action, int):
            slab = slabs[action]
            slab.step(order)
            if slab.ended():
                name = ("out", "in", "attn")[action % 3]
                unpacked[name] = unpack(layers - 1 - action // 3, name, slab, unpacked[name][: 2 if name == "attn" else 1])
            continue
        name, layer = action[:-1], int(action[-1])
        which = 3 * (layers - 1 - layer) + ("out", "in", "attn").index(name)
        way = WAYS[which]
        qkv_rows, probs, context, unit_one, inverse_one = attn_kept[layer]
        hidden, slope, unit_two, inverse_two, _ = ffn_kept[layer]
        if name == "out":
            d_ffn, d_resid_two, small_out[layer], kept, sent = out_backward(
                layer, way, grad, unit_two, inverse_two, hidden
            )
        elif name == "in":
            d_resid, small_in[layer], bias_grads[layer], kept, sent = in_backward(
                layer, way, d_ffn, d_resid_two, unit_one, inverse_one, slope
            )
        else:
            small_others = ()
            if layer == 0:
                small_others = (
                    small_out[0],
                    small_in[0],
                    bias_grads[0],
                    small_out[1],
                    small_in[1],
                    bias_grads[1],
                    small_attn[1],
                )
            grad, small_attn[layer], kept, sent = attn_backward(
                layer, way, d_resid, inputs[layer], qkv_rows, probs, context, small_others
            )
        slabs[which] = Slab(way, BACKS[which], wide_count, kept, sent)
    qkv_grad, o_grad, *vectors = unpacked["attn"]
    in_grad, out_grad = unpacked["in"][0], unpacked["out"][0]
    return (
        mixed_out,
        grad,
        qkv_grad,
        vectors[0],
        vectors[1],
        o_grad,
        vectors[2],
        vectors[3],
        vectors[4],
        in_grad,
        vectors[8],
        out_grad,
        vectors[5],
        vectors[6],
        vectors[7],
    )


def solution(mesh):
    by_table = P(("wide", "narrow"), None)
    matrix = P(None, "narrow", None)
    vector = P(None, "narrow")
    return jax.shard_map(
        body,
        mesh=mesh,
        in_specs=(
            by_table,
            by_table,
            by_table,
            P(("wide", "narrow")),
            matrix,
            vector,
            vector,
            matrix,
            vector,
            vector,
            vector,
            matrix,
            vector,
            matrix,
            vector,
            vector,
            vector,
        ),
        out_specs=(
            by_table,
            by_table,
            matrix,
            vector,
            vector,
            matrix,
            vector,
            vector,
            vector,
            matrix,
            vector,
            matrix,
            vector,
            vector,
            vector,
        ),
        check_vma=False,
    )
```

```python
import functools
import math

import jax
import jax.numpy as jnp
from jax import lax
from jax.experimental import pallas as pl
from jax.experimental.pallas import tpu as pltpu
from jax.sharding import PartitionSpec as P

HEADS = 12
norm_eps = 1e-12
masked_score = -1000000000.0
low = jnp.bfloat16
f32 = jnp.float32
VMEM_BYTES = 56 * 1024 * 1024
HALVINGS = 2


def swap(value, axis, bit):
    count = lax.axis_size(axis)
    return lax.ppermute(value, axis, [(i, i ^ bit) for i in range(count)])


def dot(a, b):
    return jnp.dot(a, b, preferred_element_type=f32)


def dot_nt(a, b):
    return lax.dot_general(a, b, (((1,), (1,)), ((), ())), preferred_element_type=f32)


def dot_tn(a, b):
    return lax.dot_general(a, b, (((0,), (0,)), ((), ())), preferred_element_type=f32)


def normalize(residual):
    center = residual - jnp.mean(residual, axis=-1, keepdims=True)
    inverse = lax.rsqrt(jnp.mean(center * center, axis=-1, keepdims=True) + norm_eps)
    return center * inverse, inverse


def normalize_back(grad_unit, unit, inverse):
    centered = grad_unit - jnp.mean(grad_unit, axis=-1, keepdims=True)
    return inverse * (centered - unit * jnp.mean(grad_unit * unit, axis=-1, keepdims=True))


def weight_copies(ids, layer, pieces, target, columns, sems, base):
    own, core, near_x, far_x, diagonal = pieces
    rows = own.shape[1]
    half = rows // 2
    n, y = ids[0], ids[4]
    copies = []

    def add(source, start, count):
        where = target.at[pl.ds(pl.multiple_of(start, half), count), :]
        copies.append(pltpu.make_async_copy(source, where, sems.at[base + len(copies)]))

    at = pl.ds(columns, target.shape[1])
    add(own.at[layer], n * rows, rows)
    add(core.at[layer], ids[1] * rows, rows)
    add(near_x.at[:, at], ids[2] * rows + y * half, half)
    add(far_x.at[:, at], ids[2] * rows + (1 - y) * half, half)
    add(diagonal.at[pl.ds(0, half), at], ids[3] * rows + y * half, half)
    add(diagonal.at[pl.ds(half, half), at], ids[3] * rows + (1 - y) * half, half)
    return copies


def begin(copies):
    for copy in copies:
        copy.start()


def finish(copies):
    for copy in copies:
        copy.wait()


def attn_copies(layer, ids, refs, w_qkv, w_o, sems):
    qkv_own, qkv_core, o_own, o_core = refs[:4]
    halves = refs[4:]
    qkv = weight_copies(ids, layer, (qkv_own, qkv_core) + halves, w_qkv, 0, sems, 0)
    o = weight_copies(ids, layer, (o_own, o_core) + halves, w_o, w_qkv.shape[1], sems, 6)
    return qkv, o


def ffn_copies(layer, ids, refs, w_in, w_out, sems):
    in_copies = weight_copies(ids, layer, refs[:5], w_in, 0, sems, 0)
    out_copies = weight_copies(ids, layer, refs[5:], w_out, 0, sems, 6)
    return in_copies, out_copies


def pack_kernel(*refs):
    shorts, in_bias, packed = refs[:8], refs[8], refs[9]
    layers, share = shorts[0].shape
    for layer in range(layers):
        for i, short in enumerate(shorts):
            packed[layer, i : i + 1, :] = short[layer : layer + 1, :].astype(f32)
        for i in range(4):
            packed[layer, 8 + i : 9 + i, :] = in_bias[layer : layer + 1, i * share : (i + 1) * share].astype(f32)


def attn_fwd_kernel(layer, ids, length, x, cell_row, small, *rest):
    weights, rest = rest[:7], rest[7:]
    qkv_rows, probs, context, unit_out, inverse_out, w_qkv, w_o, mask, sems = rest
    tokens, width = x.shape
    qkv_copies, o_copies = attn_copies(layer, ids, weights, w_qkv, w_o, sems)
    begin(qkv_copies)
    begin(o_copies)
    position = lax.broadcasted_iota(jnp.int32, (1, tokens), 1)
    key_cell = cell_row[...]
    square = (tokens, tokens)
    diagonal = lax.broadcasted_iota(jnp.int32, square, 0) == lax.broadcasted_iota(jnp.int32, square, 1)
    query_cell = jnp.sum(jnp.where(diagonal, key_cell, 0), axis=1, keepdims=True)
    allowed = (query_cell == key_cell) | (key_cell == 0) | (query_cell == 0)
    allowed = allowed & (position < length[0])
    mask[...] = jnp.where(allowed, 0.0, masked_score)
    scale = 1.0 / math.sqrt(width // HEADS)
    finish(qkv_copies)
    tile = width // 2

    for t in range(6):
        columns = slice(t * tile, (t + 1) * tile)
        rows = dot(x[...], w_qkv[:, columns])
        if t // 2 != 1:
            part = slice((t % 2) * tile, (t % 2 + 1) * tile)
            rows = rows + small[layer, t // 4 : t // 4 + 1, part]
        if t < 2:
            rows = rows * scale
        qkv_rows[:, columns] = rows.astype(low)

    pair_width = 2 * width // HEADS
    first = lax.broadcasted_iota(jnp.int32, (1, pair_width), 1) < pair_width // 2

    for pair in range(HEADS // 2):
        at = slice(pair * pair_width, (pair + 1) * pair_width)
        query = qkv_rows[:, at]
        key = qkv_rows[:, width + at.start : width + at.stop]
        value = qkv_rows[:, 2 * width + at.start : 2 * width + at.stop]
        sides = []
        for side in range(2):
            mine = first if side == 0 else jnp.logical_not(first)
            scores = dot_nt(jnp.where(mine, query, jnp.zeros_like(query)), key) + mask[...]
            shifted = jnp.exp(scores - jnp.max(scores, axis=-1, keepdims=True))
            total = jnp.sum(shifted, axis=-1, keepdims=True)
            prob = (shifted * (1.0 / total)).astype(low)
            probs[2 * pair + side] = prob
            sides.append(dot(prob, value))
        context[:, at] = jnp.where(first, sides[0], sides[1]).astype(low)

    finish(o_copies)
    residual = x[...].astype(f32) + (dot(context[...], w_o[...]) + small[layer, 2:3, :])
    unit, inverse = normalize(residual)
    unit_out[...] = unit
    inverse_out[...] = inverse


def gelu_and_slope(x):
    t = 1.0 / (1.0 + (0.3275911 * math.sqrt(0.5)) * jnp.abs(x))
    bell = jnp.exp(-0.5 * x * x)
    series = 1.421413741 + t * (-1.453152027 + t * 1.061405429)
    series = t * (0.254829592 + t * (-0.284496736 + t * series))
    tail = 0.5 * series * bell
    cdf = jnp.where(x >= 0.0, 1.0 - tail, tail)
    return (x * cdf).astype(low), cdf + x * (bell * (1.0 / math.sqrt(2.0 * math.pi)))


def ffn_fwd_kernel(layer, ids, unit_one, in_bias, small, *rest):
    weights, rest = rest[:10], rest[10:]
    hidden_out, slope_out, unit_out, inverse_out, result = rest[:5]
    w_in, w_out, normed_low, hidden, slope, sems, out_sems = rest[5:]
    in_copies, out_copies = ffn_copies(layer, ids, weights, w_in, w_out, sems)
    begin(in_copies)
    begin(out_copies)
    normed = unit_one[...] * small[layer, 3:4, :] + small[layer, 4:5, :]
    normed_low[...] = normed.astype(low)
    finish(in_copies)
    tile = w_in.shape[1] // 8
    going = []
    for t in range(8):
        columns = pl.ds(t * tile, tile)
        pre = dot(normed_low[...], w_in[:, columns]) + in_bias[layer, :, columns]
        hidden[:, columns], slope[:, columns] = gelu_and_slope(pre)
        leaving = [
            pltpu.make_async_copy(hidden.at[:, columns], hidden_out.at[:, columns], out_sems.at[2 * t]),
            pltpu.make_async_copy(slope.at[:, columns], slope_out.at[:, columns], out_sems.at[2 * t + 1]),
        ]
        begin(leaving)
        going += leaving

    finish(out_copies)
    residual = unit_one[...] * small[layer, 3:4, :] + small[layer, 4:5, :] + (dot(hidden[...], w_out[...]) + small[layer, 5:6, :])
    unit, inverse = normalize(residual)
    unit_out[...] = unit
    inverse_out[...] = inverse
    result[...] = (unit * small[layer, 6:7, :] + small[layer, 7:8, :]).astype(low)
    finish(going)


WIDE_BIT = {"y": 0, "z": 1}


def place_of(ids, owner, piece, way):
    away = None if owner is None else ids[0] ^ owner
    off = None if piece is None else piece ^ ids[5]
    place = [None if away is None else away & 1]
    for name in way:
        if name == "x":
            place.append(pl.ds(0, 2) if away is None else away >> 1)
        else:
            place.append(pl.ds(0, 2) if off is None else (off >> WIDE_BIT[name]) & 1)
    return tuple(place) + (pl.ds(0, 2) if piece is None else piece >> 2,)


def store_rows(stage, ids, product, piece, way):
    share = product.shape[0] // 4
    for owner in range(4):
        block = product[owner * share : (owner + 1) * share].astype(low)
        stage[place_of(ids, owner, piece, way) + (pl.ds(0, share),)] = block


def piece_copies(stage, ids, piece, way, kept, sent, sems, turn):
    at = place_of(ids, None, piece, way)[1:]
    copies = [
        pltpu.make_async_copy(stage.at[(1,) + at], sent.at[at], sems.at[2 * turn]),
        pltpu.make_async_copy(stage.at[(0,) + at], kept.at[at], sems.at[2 * turn + 1]),
    ]
    begin(copies)
    return copies


def out_bwd_kernel(layer, way, ids, grad, unit_two, inverse_two, hidden, small, *rest):
    d_ffn, d_resid_two, small_grads, kept, sent, stage, out_sems = rest
    g = grad[...].astype(f32)
    unit = unit_two[...]
    small_grads[0:1, :] = jnp.sum(g * unit, axis=0, keepdims=True)
    small_grads[1:2, :] = jnp.sum(g, axis=0, keepdims=True)
    d_two = normalize_back(g * small[layer, 6:7, :], unit, inverse_two[...])
    d_resid_two[...] = d_two
    d_low = d_two.astype(low)
    d_ffn[...] = d_low
    small_grads[2:3, :] = jnp.sum(d_low.astype(f32), axis=0, keepdims=True)
    small_grads[3:8, :] = jnp.zeros((5, unit.shape[1]), f32)
    tile = hidden.shape[1] // 8
    share = d_ffn.shape[1] // 4
    waits = []
    for owner in range(4):
        for half in range(2):
            columns = slice((2 * owner + half) * tile, (2 * owner + half + 1) * tile)
            out_grad = dot_tn(hidden[:, columns], d_ffn[...])
            for row_group in range(2):
                for column_group in range(2):
                    piece = (half * 2 + row_group) * 2 + column_group
                    block = out_grad[
                        row_group * share : (row_group + 1) * share,
                        column_group * tile : (column_group + 1) * tile,
                    ]
                    stage[place_of(ids, owner, piece, way)] = block.astype(low)
        core, *at = place_of(ids, owner, None, way)
        at = tuple(at)
        to_kept = pltpu.make_async_copy(stage.at[(0,) + at], kept.at[at], out_sems.at[owner])
        to_sent = pltpu.make_async_copy(stage.at[(1,) + at], sent.at[at], out_sems.at[owner])
        pl.when(core == 0)(to_kept.start)
        pl.when(core == 1)(to_sent.start)
        waits.append(to_kept)
    finish(waits)


def in_bwd_kernel(layer, way, ids, d_ffn, d_resid_two, unit_one, inverse_one, small, slope_in, *rest):
    weights, rest = rest[:10], rest[10:]
    d_resid, small_grads, in_bias_grad, kept, sent = rest[:5]
    w_in, w_out, d_pre, normed_t, slope, stage, sems, out_sems, slope_sem = rest[5:]
    in_copies, out_copies = ffn_copies(layer, ids, weights, w_in, w_out, sems)
    slope_copy = pltpu.make_async_copy(slope_in, slope, slope_sem.at[0])
    begin(out_copies[:2] + [slope_copy] + out_copies[2:] + in_copies)
    normed = unit_one[...] * small[layer, 3:4, :] + small[layer, 4:5, :]
    normed_t[...] = normed.astype(low).T
    tile = w_in.shape[1] // 8
    going = []
    slope_copy.wait()
    for turn in range(8):
        if turn % 2 == 0:
            finish(([out_copies[0]], [out_copies[1]], out_copies[2:4], out_copies[4:6])[turn // 2])
        t = 2 * ids[turn // 2] + turn % 2
        columns = pl.ds(pl.multiple_of(t * tile, tile), tile)
        d_hidden = dot_nt(d_ffn[...], w_out[columns, :])
        d_tile = (d_hidden * slope[:, columns]).astype(low)
        d_pre[:, columns] = d_tile
        in_bias_grad[:, columns] = jnp.sum(d_tile.astype(f32), axis=0, keepdims=True)
        store_rows(stage, ids, dot(normed_t[...], d_tile), t, way)
        going += piece_copies(stage, ids, t, way, kept, sent, out_sems, turn)
    finish(in_copies)
    d_normed = d_resid_two[...] + dot_nt(d_pre[...], w_in[...])
    unit = unit_one[...]
    small_grads[0:1, :] = jnp.sum(d_normed * unit, axis=0, keepdims=True)
    small_grads[1:2, :] = jnp.sum(d_normed, axis=0, keepdims=True)
    small_grads[2:8, :] = jnp.zeros((6, unit.shape[1]), f32)
    d_resid[...] = normalize_back(d_normed * small[layer, 3:4, :], unit, inverse_one[...])
    finish(going)


def attn_bwd_kernel(layer, way, ids, d_resid, x, qkv_rows, probs, context, *rest):
    weights, others, rest = rest[:7], rest[7:-13], rest[-13:]
    d_input, small_grads, kept, sent = rest[:4]
    w_qkv, w_o, d_attn, d_context, d_qkv, x_t, stage, sems, out_sems = rest[4:]
    tokens, width = x.shape
    qkv_copies, o_copies = attn_copies(layer, ids, weights, w_qkv, w_o, sems)
    begin(o_copies)
    begin(qkv_copies)
    d_low = d_resid[...].astype(low)
    d_attn[...] = d_low
    small_grads[2:3, :] = jnp.sum(d_low.astype(f32), axis=0, keepdims=True)
    x_t[...] = x[...].T
    tile = width // 2
    for half in range(2):
        product = dot_tn(context[...], d_attn[:, half * tile : (half + 1) * tile])
        store_rows(stage, ids, product, 6 + half, way)
    finish(o_copies)
    d_context[...] = dot_nt(d_attn[...], w_o[...]).astype(low)
    pair_width = 2 * width // HEADS
    first = lax.broadcasted_iota(jnp.int32, (1, pair_width), 1) < pair_width // 2
    scale = 1.0 / math.sqrt(width // HEADS)

    for pair in range(HEADS // 2):
        at_query = slice(pair * pair_width, (pair + 1) * pair_width)
        at_key = slice(width + at_query.start, width + at_query.stop)
        at_value = slice(2 * width + at_query.start, 2 * width + at_query.stop)
        query, key, value = qkv_rows[:, at_query], qkv_rows[:, at_key], qkv_rows[:, at_value]
        d_ctx = d_context[:, at_query]
        sides = []
        for side in range(2):
            mine = first if side == 0 else jnp.logical_not(first)
            prob_low = probs[2 * pair + side]
            prob = prob_low.astype(f32)
            d_prob = dot_nt(jnp.where(mine, d_ctx, jnp.zeros_like(d_ctx)), value)
            inner = jnp.sum(prob * d_prob, axis=-1, keepdims=True)
            d_scores = (prob * (d_prob - inner)).astype(low)
            sides.append((dot(d_scores, key), dot_tn(d_scores, query), dot_tn(prob_low, d_ctx)))
        d_qkv[:, at_query] = (jnp.where(first, sides[0][0], sides[1][0]) * scale).astype(low)
        d_qkv[:, at_key] = jnp.where(first, sides[0][1], sides[1][1]).astype(low)
        d_qkv[:, at_value] = jnp.where(first, sides[0][2], sides[1][2]).astype(low)

    small_grads[0:1, :] = jnp.sum(d_qkv[:, :width].astype(f32), axis=0, keepdims=True)
    small_grads[1:2, :] = jnp.sum(d_qkv[:, 2 * width :].astype(f32), axis=0, keepdims=True)
    small_grads[3:8, :] = jnp.zeros((5, width), f32)
    if others:
        share = width // 4
        sources = small_sources(layer, small_grads, others)
        for owner in range(4):
            for piece in range(8):
                lines = []
                for source, row, start, step in sources[3 * piece : 3 * piece + 3]:
                    line = source[row : row + 1, start + owner * step : start + owner * step + share]
                    lines.append(jnp.concatenate([line, jnp.zeros_like(line)], axis=1))
                lines.append(jnp.zeros((SMALL_ROWS - 3, tile), f32))
                block = jnp.concatenate(lines, axis=0).astype(low)
                stage[place_of(ids, owner, piece, way) + (pl.ds(share, SMALL_ROWS),)] = block
    going = []
    for piece in (6, 7, 0, 1, 2, 3, 4, 5):
        if piece < 6:
            store_rows(stage, ids, dot(x_t[...], d_qkv[:, piece * tile : (piece + 1) * tile]), piece, way)
        going += piece_copies(stage, ids, piece, way, kept, sent, out_sems, piece)
    finish(qkv_copies)
    d_input[...] = (d_resid[...] + dot_nt(d_qkv[...], w_qkv[...])).astype(low)
    finish(going)


SMALL_ROWS = 16
SMALL_LINES = (("attn", 0), ("attn", 1), ("attn", 2), ("in", 0), ("in", 1), ("out", 2), ("out", 0), ("out", 1))


def small_sources(layer, own, others):
    found = []
    out_0, in_0, bias_0, out_1, in_1, bias_1, attn_1 = others
    refs = ({"attn": own, "in": in_0, "out": out_0}, {"attn": attn_1, "in": in_1, "out": out_1})
    width = own.shape[1]
    for of_layer, bias in zip(refs, (bias_0, bias_1)):
        found += [(of_layer[name], row, 0, width // 4) for name, row in SMALL_LINES]
        found += [(bias, 0, i * (width // 4), width) for i in range(4)]
    return found


def unpack_kernel(layer, slab, back, earlier, ids, near, far, *rest):
    outs = rest[earlier:-4]
    buffer, wide_buffer, in_sems, out_sems = rest[-4:]
    share, tile = wide_buffer.shape[1:]

    def fetch(piece, ref, index):
        return pltpu.make_async_copy(ref.at[index], buffer.at[piece], in_sems.at[piece])

    for piece in range(8):
        off = piece ^ ids[5]
        inner, outer = [(off >> WIDE_BIT[name]) & 1 for name in back]
        pl.when(outer == 0)(fetch(piece, near, (inner, piece >> 2)).start)
        pl.when(outer == 1)(fetch(piece, far, (inner, piece >> 2)).start)

    copies = []
    for piece in range(8):
        fetch(piece, near, (0, 0)).wait()
        wide_buffer[piece] = buffer[piece, :share].astype(f32)
        columns = pl.ds(piece * tile, tile)
        if slab == "in":
            target = outs[0].at[layer, :, columns]
        elif slab == "out":
            rows = pl.ds((piece // 2) * share, share)
            target = outs[0].at[layer, rows, pl.ds((piece % 2) * tile, tile)]
        elif piece < 6:
            target = outs[0].at[layer, :, columns]
        else:
            target = outs[1].at[layer, :, pl.ds((piece - 6) * tile, tile)]
        copies.append(pltpu.make_async_copy(wide_buffer.at[piece], target, out_sems.at[piece]))
        copies[-1].start()
    if slab == "attn" and layer == 0:
        for line in range(24):
            of_layer, which = line // 12, line % 12
            row = share + line % 3
            values = buffer[line // 3, row : row + 1, :share].astype(f32)
            if which < 8:
                outs[2 + which][of_layer : of_layer + 1, :] = values
            else:
                at = (which - 8) * share
                outs[10][of_layer : of_layer + 1, at : at + share] = values
    else:
        outs[-1][...] = jnp.zeros(outs[-1].shape, f32)
    finish(copies)


SMEM = pl.BlockSpec(memory_space=pltpu.SMEM)
VMEM = pl.BlockSpec(memory_space=pltpu.VMEM)
ANY = pl.BlockSpec(memory_space=pl.ANY)


def call(kernel, name, time, in_specs, out_specs, out_shape, scratch, args, aliases=()):
    return pl.pallas_call(
        kernel,
        name=name,
        in_specs=in_specs,
        out_specs=out_specs,
        out_shape=out_shape,
        scratch_shapes=scratch,
        input_output_aliases=dict(aliases),
        compiler_params=pltpu.CompilerParams(vmem_limit_bytes=VMEM_BYTES),
        cost_estimate=pl.CostEstimate(
            flops=int(time * 0.22e9), bytes_accessed=int(time * 0.72e6), transcendentals=0
        ),
    )(*args)


def shape(dims, kind):
    return jax.ShapeDtypeStruct(dims, kind)


def added(a, b):
    return (a.astype(f32) + b.astype(f32)).astype(low)


WAYS = ("xyz", "zxy", "yxz", "xzy", "xyz", "xyz")
BACKS = ("zy", "zy", "zy", "zy", "yz", "zy")
PLAN = (
    "out1", "in1", 0, 1, "attn1", "out0", 0, 2, 1, 3, 0, 1, 0, "in0", 2, 0, 4, 1, 0, 3, "attn0", 0, 2, 1, 5,
    3, 2, 4, 1, 3, 4, 2, 5, 4, 3, 1, 2, 5, 3, 4, 5, 2, 3, 5, 4, 5, 4, 5,
)


class Order:
    def __init__(self):
        self.last = None

    def after(self, values):
        if self.last is None:
            return values
        values, self.last = lax.optimization_barrier((values, self.last))
        return values

    def wait(self, values):
        values = self.after(values)
        self.last = values
        return values


STEPS = {"x": ("narrow", 2), "y": ("wide", 1), "z": ("wide", 2)}


class Slab:
    def __init__(self, way, back, wide_count, kept, sent):
        self.kept = kept
        self.way, self.back = way, back
        self.rest = [1 << b for b in range(HALVINGS, wide_count.bit_length() - 1)]
        self.flying = swap(sent, "narrow", 1)
        self.stage = 0

    def step(self, order):
        received = order.after(self.flying)
        stage, way = self.stage, self.way
        if stage < len(way):
            send = added(self.kept[1], received[1])
            self.kept = added(self.kept[0], received[0])
            self.flying = swap(send, *STEPS[way[stage]])
            order.last = send
        elif stage < len(way) + 1 + len(self.back):
            if stage == len(way):
                piece = added(self.kept, received)
                if not self.rest:
                    self.block = piece[None]
            elif stage == len(way) + 1 and self.rest:
                piece = added(self.kept, received)
                for bit in self.rest[1:]:
                    piece = added(piece, swap(piece, "wide", bit))
                self.block = piece[None]
            else:
                self.block = jnp.concatenate([self.block, received], axis=0)
                piece = self.block
            order.last = piece
            if stage == len(way) and self.rest:
                self.kept = piece
                self.flying = swap(piece, "wide", self.rest[0])
            else:
                self.flying = swap(self.block, *STEPS[self.back[stage - len(way) - 1]])
        else:
            self.far = received
        self.stage += 1

    def ended(self):
        return self.stage == len(self.way) + len(self.back) + 2


def body(
    tables_in,
    cotangent,
    cell_ids,
    lengths,
    qkv_weight,
    q_bias,
    v_bias,
    o_weight,
    o_bias,
    norm1_gain,
    norm1_bias,
    in_weight,
    in_bias,
    out_weight,
    out_bias,
    norm2_gain,
    norm2_bias,
):
    tokens, width = tables_in.shape
    layers, share, ffn = in_weight.shape
    ffn_share = out_weight.shape[1]
    wide_count = lax.axis_size("wide")
    assert wide_count & (wide_count - 1) == 0 and wide_count >= 1 << HALVINGS and lax.axis_size("narrow") == 4
    tile = ffn // 8
    me = lax.axis_index("narrow").astype(jnp.int32)
    wide_me = lax.axis_index("wide").astype(jnp.int32)
    y = wide_me & 1
    ids = jnp.stack([me, me ^ 1, me ^ 2, me ^ 3, y, wide_me & (2**HALVINGS - 1)])

    order = Order()

    def half_of(weight, layer):
        rows = weight.shape[1] // 2
        return lax.dynamic_slice(weight, (layer, y * rows, 0), (1, rows, weight.shape[2]))[0]

    halves = []
    for layer in range(layers):
        joint = jnp.concatenate([half_of(qkv_weight, layer), half_of(o_weight, layer)], axis=1)
        halves += [joint, half_of(in_weight, layer), half_of(out_weight, layer)]
    near_x, far_x, diagonal = [None] * len(halves), [None] * len(halves), [None] * len(halves)
    core = [None] * 4
    own = (qkv_weight, o_weight, in_weight, out_weight)

    def group(i):
        return near_x[i], far_x[i], diagonal[i]

    def attn_weights(layer):
        return (qkv_weight, core[0], o_weight, core[1]) + group(3 * layer)

    def ffn_weights(layer):
        return (in_weight, core[2]) + group(3 * layer + 1) + (out_weight, core[3]) + group(3 * layer + 2)

    def in_order(low_one, high_one, bit):
        swapped = (me & bit) != 0
        return jnp.stack([jnp.where(swapped, high_one, low_one), jnp.where(swapped, low_one, high_one)])

    near_x[0] = swap(halves[0], "narrow", 2)
    order.last = halves[0]
    core[0], core[1] = swap(own[0], "narrow", 1), swap(own[1], "narrow", 1)
    short = order.after((q_bias, v_bias, o_bias, norm1_gain, norm1_bias, out_bias, norm2_gain, norm2_bias))
    packed = call(
        pack_kernel, "pack", 1, [VMEM] * 9, VMEM, shape((layers, 12, share), f32), [], tuple(short) + (in_bias,)
    )
    halves[1:], packed = order.wait((halves[1:], packed))
    near_x[0], core[0], core[1] = order.wait((near_x[0], core[0], core[1]))

    others = [
        lax.ppermute(order.after(packed), "narrow", [(i, i ^ away) for i in range(4)]) for away in (1, 2, 3)
    ]
    far_x[0] = swap(near_x[0], "wide", 1)
    near_x[1] = swap(order.after(halves[1]), "narrow", 2)
    far_x[0], near_x[1], others = order.wait((far_x[0], near_x[1], others))
    packed = in_order(in_order(packed, others[0], 1), in_order(others[1], others[2], 1), 2)
    packed = packed.reshape(4, layers, 12, share)
    small = packed[:, :, :8].transpose(1, 2, 0, 3).reshape(layers, 8, width)
    full_in_bias = packed[:, :, 8:].transpose(1, 0, 2, 3).reshape(layers, 1, ffn)

    def join(i):
        both = jnp.concatenate([near_x[i], far_x[i]], axis=0)
        diagonal[i] = swap(both, "narrow", 1)
        return both

    def begin_round(i):
        both = join(i)
        if i + 1 < len(halves):
            far_x[i + 1] = swap(near_x[i + 1], "wide", 1)
        if i + 2 < len(halves):
            near_x[i + 2] = swap(order.after(halves[i + 2]), "narrow", 2)
        order.last = both

    def end_round(i):
        if i + 2 < len(halves):
            far_x[i + 1], near_x[i + 2] = order.wait((far_x[i + 1], near_x[i + 2]))
        elif i + 1 < len(halves):
            far_x[i + 1] = order.wait(far_x[i + 1])

    def arrive(i):
        diagonal[i] = order.wait(diagonal[i])

    begin_round(0)
    core[2], core[3] = swap(order.after(own[2]), "narrow", 1), swap(order.after(own[3]), "narrow", 1)
    ids, small, full_in_bias = order.wait((ids, small, full_in_bias))
    arrive(0)
    core[2], core[3] = order.wait((core[2], core[3]))
    end_round(0)

    w_qkv = pltpu.VMEM((width, 3 * width), low)
    w_o = pltpu.VMEM((width, width), low)
    w_in = pltpu.VMEM((width, ffn), low)
    w_out = pltpu.VMEM((ffn, width), low)
    copy_sems = pltpu.SemaphoreType.DMA((12,))
    piece_sems = pltpu.SemaphoreType.DMA((16,))
    rows_f32 = shape((tokens, width), f32)
    rows_low = shape((tokens, width), low)
    column_f32 = shape((tokens, 1), f32)
    eight_f32 = shape((8, width), f32)

    def pieces(rows):
        return [shape((2, 2, 2, 2, rows, tile), low)] * 2

    def stage(rows):
        return pltpu.VMEM((2, 2, 2, 2, 2, rows, tile), low)

    def attn_forward(layer, x):
        x = order.after(x)
        outs = call(
            functools.partial(attn_fwd_kernel, layer),
            "attn_fwd",
            13,
            [SMEM, SMEM] + [VMEM] * 3 + [ANY] * 7,
            [VMEM] * 5,
            [shape((tokens, 3 * width), low), shape((HEADS, tokens, tokens), low), rows_low, rows_f32, column_f32],
            [w_qkv, w_o, pltpu.VMEM((tokens, tokens), f32), copy_sems],
            (ids, lengths, x, cell_ids, small) + attn_weights(layer),
        )
        order.last = outs[-1]
        return outs

    def ffn_forward(layer, unit_one):
        unit_one = order.after(unit_one)
        outs = call(
            functools.partial(ffn_fwd_kernel, layer),
            "ffn_fwd",
            10,
            [SMEM] + [VMEM] * 3 + [ANY] * 10,
            [ANY] * 2 + [VMEM] * 3,
            [shape((tokens, ffn), low), shape((tokens, ffn), f32), rows_f32, column_f32, rows_low],
            [
                w_in,
                w_out,
                pltpu.VMEM((tokens, width), low),
                pltpu.VMEM((tokens, ffn), low),
                pltpu.VMEM((tokens, ffn), f32),
                copy_sems,
                piece_sems,
            ],
            (ids, unit_one, full_in_bias, small) + ffn_weights(layer),
        )
        order.last = outs[-2]
        return outs

    def out_backward(layer, way, grad, unit_two, inverse_two, hidden):
        grad = order.after(grad)
        outs = call(
            functools.partial(out_bwd_kernel, layer, way),
            "out_bwd",
            8,
            [SMEM] + [VMEM] * 5,
            [VMEM] * 3 + [ANY] * 2,
            [rows_low, rows_f32, eight_f32] + pieces(share),
            [stage(share), pltpu.SemaphoreType.DMA((4,))],
            (ids, grad, unit_two, inverse_two, hidden, small),
        )
        order.last = outs[2]
        return outs

    def in_backward(layer, way, d_ffn, d_resid_two, unit_one, inverse_one, slope):
        d_ffn = order.after(d_ffn)
        outs = call(
            functools.partial(in_bwd_kernel, layer, way),
            "in_bwd",
            14,
            [SMEM] + [VMEM] * 5 + [ANY] * 11,
            [VMEM] * 3 + [ANY] * 2,
            [rows_f32, eight_f32, shape((1, ffn), f32)] + pieces(share),
            [
                w_in,
                w_out,
                pltpu.VMEM((tokens, ffn), low),
                pltpu.VMEM((width, tokens), low),
                pltpu.VMEM((tokens, ffn), f32),
                stage(share),
                copy_sems,
                piece_sems,
                pltpu.SemaphoreType.DMA((1,)),
            ],
            (ids, d_ffn, d_resid_two, unit_one, inverse_one, small, slope) + ffn_weights(layer),
        )
        order.last = outs[1]
        return outs

    def attn_backward(layer, way, d_resid, x, qkv_rows, probs, context, small_others):
        d_resid = order.after(d_resid)
        rows = share + (SMALL_ROWS if small_others else 0)
        outs = call(
            functools.partial(attn_bwd_kernel, layer, way),
            "attn_bwd",
            16,
            [SMEM] + [VMEM] * 5 + [ANY] * 7 + [VMEM] * len(small_others),
            [VMEM] * 2 + [ANY] * 2,
            [rows_low, eight_f32] + pieces(rows),
            [
                w_qkv,
                w_o,
                pltpu.VMEM((tokens, width), low),
                pltpu.VMEM((tokens, width), low),
                pltpu.VMEM((tokens, 3 * width), low),
                pltpu.VMEM((width, tokens), low),
                stage(rows),
                copy_sems,
                piece_sems,
            ],
            (ids, d_resid, x, qkv_rows, probs, context) + attn_weights(layer) + tuple(small_others),
        )
        order.last = outs[1]
        return outs

    def unpack(layer, name, slab, earlier):
        dims = {
            "attn": [(layers, share, 3 * width), (layers, share, width)],
            "in": [(layers, share, ffn)],
            "out": [(layers, ffn_share, width)],
        }[name]
        last = name == "attn" and layer == 0
        extra = [(layers, share)] * 8 + [(layers, ffn_share)] if last else [(8, 128)]
        near, far = order.after((slab.block, slab.far))
        rows = near.shape[2]
        outs = call(
            functools.partial(unpack_kernel, layer, name, slab.back, len(earlier)),
            "unpack",
            4,
            [SMEM] + [ANY] * (2 + len(earlier)),
            [ANY] * len(dims) + [VMEM] * len(extra),
            [shape(d, f32) for d in dims + extra],
            [
                pltpu.VMEM((8, rows, tile), low),
                pltpu.VMEM((8, share, tile), f32),
                pltpu.SemaphoreType.DMA((8,)),
                pltpu.SemaphoreType.DMA((8,)),
            ],
            (ids, near, far, *earlier),
            {3 + i: i for i in range(len(earlier))},
        )
        order.last = outs[-1]
        return tuple(outs)

    begin_round(1)
    first_attn = attn_forward(0, tables_in)
    arrive(1)
    end_round(1)
    begin_round(2)
    arrive(2)
    first_ffn = ffn_forward(0, first_attn[3])
    end_round(2)
    begin_round(3)
    arrive(3)
    second_attn = attn_forward(1, first_ffn[4])
    end_round(3)
    begin_round(4)
    arrive(4)
    end_round(4)
    begin_round(5)
    arrive(5)
    second_ffn = ffn_forward(1, second_attn[3])
    mixed_out = second_ffn[4]
    inputs = (tables_in, first_ffn[4])
    attn_kept, ffn_kept = (first_attn, second_attn), (first_ffn, second_ffn)

    slabs = [None] * 6
    grad = cotangent
    small_out, small_in, small_attn, bias_grads = [None] * 2, [None] * 2, [None] * 2, [None] * 2
    unpacked = {"attn": (), "in": (), "out": ()}
    for action in PLAN:
        if isinstance(action, int):
            slab = slabs[action]
            slab.step(order)
            if slab.ended():
                name = ("out", "in", "attn")[action % 3]
                unpacked[name] = unpack(layers - 1 - action // 3, name, slab, unpacked[name][: 2 if name == "attn" else 1])
            continue
        name, layer = action[:-1], int(action[-1])
        which = 3 * (layers - 1 - layer) + ("out", "in", "attn").index(name)
        way = WAYS[which]
        qkv_rows, probs, context, unit_one, inverse_one = attn_kept[layer]
        hidden, slope, unit_two, inverse_two, _ = ffn_kept[layer]
        if name == "out":
            d_ffn, d_resid_two, small_out[layer], kept, sent = out_backward(
                layer, way, grad, unit_two, inverse_two, hidden
            )
        elif name == "in":
            d_resid, small_in[layer], bias_grads[layer], kept, sent = in_backward(
                layer, way, d_ffn, d_resid_two, unit_one, inverse_one, slope
            )
        else:
            small_others = ()
            if layer == 0:
                small_others = (
                    small_out[0],
                    small_in[0],
                    bias_grads[0],
                    small_out[1],
                    small_in[1],
                    bias_grads[1],
                    small_attn[1],
                )
            grad, small_attn[layer], kept, sent = attn_backward(
                layer, way, d_resid, inputs[layer], qkv_rows, probs, context, small_others
            )
        slabs[which] = Slab(way, BACKS[which], wide_count, kept, sent)
    qkv_grad, o_grad, *vectors = unpacked["attn"]
    in_grad, out_grad = unpacked["in"][0], unpacked["out"][0]
    return (
        mixed_out,
        grad,
        qkv_grad,
        vectors[0],
        vectors[1],
        o_grad,
        vectors[2],
        vectors[3],
        vectors[4],
        in_grad,
        vectors[8],
        out_grad,
        vectors[5],
        vectors[6],
        vectors[7],
    )


def solution(mesh):
    by_table = P(("wide", "narrow"), None)
    matrix = P(None, "narrow", None)
    vector = P(None, "narrow")
    return jax.shard_map(
        body,
        mesh=mesh,
        in_specs=(
            by_table,
            by_table,
            by_table,
            P(("wide", "narrow")),
            matrix,
            vector,
            vector,
            matrix,
            vector,
            vector,
            vector,
            matrix,
            vector,
            matrix,
            vector,
            vector,
            vector,
        ),
        out_specs=(
            by_table,
            by_table,
            matrix,
            vector,
            vector,
            matrix,
            vector,
            vector,
            vector,
            matrix,
            vector,
            matrix,
            vector,
            vector,
            vector,
        ),
        check_vma=False,
    )
```

```python
import functools
import math

import jax
import jax.numpy as jnp
from jax import lax
from jax.experimental import pallas as pl
from jax.experimental.pallas import tpu as pltpu
from jax.sharding import PartitionSpec as P

HEADS = 12
norm_eps = 1e-12
masked_score = -1000000000.0
low = jnp.bfloat16
f32 = jnp.float32
VMEM_BYTES = 56 * 1024 * 1024


def swap(value, axis, bit):
    count = lax.axis_size(axis)
    return lax.ppermute(value, axis, [(i, i ^ bit) for i in range(count)])


def dot(a, b):
    return jnp.dot(a, b, preferred_element_type=f32)


def dot_nt(a, b):
    return lax.dot_general(a, b, (((1,), (1,)), ((), ())), preferred_element_type=f32)


def dot_tn(a, b):
    return lax.dot_general(a, b, (((0,), (0,)), ((), ())), preferred_element_type=f32)


def normalize(residual):
    center = residual - jnp.mean(residual, axis=-1, keepdims=True)
    inverse = lax.rsqrt(jnp.mean(center * center, axis=-1, keepdims=True) + norm_eps)
    return center * inverse, inverse


def normalize_back(grad_unit, unit, inverse):
    centered = grad_unit - jnp.mean(grad_unit, axis=-1, keepdims=True)
    return inverse * (centered - unit * jnp.mean(grad_unit * unit, axis=-1, keepdims=True))


ME, NEAR_CORE, NEAR_X, DIAGONAL, Z, SECTION = range(6)


def weight_copies(ids, pieces, target, columns, sems, base):
    own, core, near_x, far_x, diagonal = pieces
    rows = own.shape[1]
    half = rows // 2
    z = ids[Z]
    copies = []

    def add(source, start, count):
        where = target.at[pl.ds(pl.multiple_of(start, half), count), :]
        copies.append(pltpu.make_async_copy(source, where, sems.at[base + len(copies)]))

    at = pl.ds(columns, target.shape[1])
    add(own.at[ids[SECTION]], ids[ME] * rows, rows)
    add(core.at[ids[SECTION]], ids[NEAR_CORE] * rows, rows)
    add(near_x.at[:, at], ids[NEAR_X] * rows + z * half, half)
    add(far_x.at[:, at], ids[NEAR_X] * rows + (1 - z) * half, half)
    add(diagonal.at[pl.ds(0, half), at], ids[DIAGONAL] * rows + z * half, half)
    add(diagonal.at[pl.ds(half, half), at], ids[DIAGONAL] * rows + (1 - z) * half, half)
    return copies


def begin(copies):
    for copy in copies:
        copy.start()


def finish(copies):
    for copy in copies:
        copy.wait()


def attn_copies(ids, refs, w_qkv, w_o, sems):
    qkv_own, qkv_core, o_own, o_core = refs[:4]
    qkv = weight_copies(ids, (qkv_own, qkv_core) + refs[4:], w_qkv, 0, sems, 0)
    o = weight_copies(ids, (o_own, o_core) + refs[4:], w_o, w_qkv.shape[1], sems, 6)
    return qkv, o


def ffn_copies(ids, refs, w_in, w_out, sems):
    in_copies = weight_copies(ids, refs[:5], w_in, 0, sems, 0)
    out_copies = weight_copies(ids, refs[5:], w_out, 0, sems, 6)
    return in_copies, out_copies


def pack_kernel(*refs):
    shorts, in_bias, packed = refs[:8], refs[8], refs[9]
    layers, share = shorts[0].shape
    for layer in range(layers):
        for i, short in enumerate(shorts):
            packed[layer, i : i + 1, :] = short[layer : layer + 1, :].astype(f32)
        for i in range(4):
            packed[layer, 8 + i : 9 + i, :] = in_bias[layer : layer + 1, i * share : (i + 1) * share].astype(f32)


def leave(pairs, sems, base):
    copies = [pltpu.make_async_copy(a, b, sems.at[base + i]) for i, (a, b) in enumerate(pairs)]
    begin(copies)
    return copies


def on_section(kernel):
    @functools.wraps(kernel)
    def guarded(section, inputs, aliased, ids, *refs):
        refs = refs[:inputs] + refs[inputs + aliased + 1 :]

        @pl.when(ids[SECTION] == section)
        def _():
            kernel(ids, *refs)

    return guarded


@on_section
def attn_fwd_kernel(ids, length, x, cell_row, small, *rest):
    weights, rest = rest[:7], rest[7:]
    outs, (qkv_rows, probs, context, unit_one, inverse_one, w_qkv, w_o, mask, sems, out_sems) = rest[:5], rest[5:]
    tokens, width = x.shape
    layer = ids[SECTION]
    qkv_copies, o_copies = attn_copies(ids, weights, w_qkv, w_o, sems)
    begin(qkv_copies)
    begin(o_copies)
    position = lax.broadcasted_iota(jnp.int32, (1, tokens), 1)
    key_cell = cell_row[...]
    square = (tokens, tokens)
    diagonal = lax.broadcasted_iota(jnp.int32, square, 0) == lax.broadcasted_iota(jnp.int32, square, 1)
    query_cell = jnp.sum(jnp.where(diagonal, key_cell, 0), axis=1, keepdims=True)
    allowed = (query_cell == key_cell) | (key_cell == 0) | (query_cell == 0)
    allowed = allowed & (position < length[0])
    mask[...] = jnp.where(allowed, 0.0, masked_score)
    scale = 1.0 / math.sqrt(width // HEADS)
    finish(qkv_copies)
    tile = width // 2
    for t in range(6):
        columns = slice(t * tile, (t + 1) * tile)
        rows = dot(x[...], w_qkv[:, columns])
        if t // 2 != 1:
            part = slice((t % 2) * tile, (t % 2 + 1) * tile)
            rows = rows + small[layer, t // 4 : t // 4 + 1, part]
        if t < 2:
            rows = rows * scale
        qkv_rows[:, columns] = rows.astype(low)
    going = leave([(qkv_rows, outs[0])], out_sems, 0)

    pair_width = 2 * width // HEADS
    first = lax.broadcasted_iota(jnp.int32, (1, pair_width), 1) < pair_width // 2
    for pair in range(HEADS // 2):
        at = slice(pair * pair_width, (pair + 1) * pair_width)
        query = qkv_rows[:, at]
        key = qkv_rows[:, width + at.start : width + at.stop]
        value = qkv_rows[:, 2 * width + at.start : 2 * width + at.stop]
        sides = []
        for side in range(2):
            mine = first if side == 0 else jnp.logical_not(first)
            scores = dot_nt(jnp.where(mine, query, jnp.zeros_like(query)), key) + mask[...]
            shifted = jnp.exp(scores - jnp.max(scores, axis=-1, keepdims=True))
            total = jnp.sum(shifted, axis=-1, keepdims=True)
            prob = (shifted * (1.0 / total)).astype(low)
            probs[2 * pair + side] = prob
            sides.append(dot(prob, value))
        context[:, at] = jnp.where(first, sides[0], sides[1]).astype(low)

    going += leave([(probs, outs[1]), (context, outs[2])], out_sems, 1)
    finish(o_copies)
    residual = x[...].astype(f32) + (dot(context[...], w_o[...]) + small[layer, 2:3, :])
    unit, inverse = normalize(residual)
    unit_one[...] = unit
    inverse_one[...] = inverse
    finish(going + leave([(unit_one, outs[3]), (inverse_one, outs[4])], out_sems, 3))


def gelu_and_slope(x):
    t = 1.0 / (1.0 + (0.3275911 * math.sqrt(0.5)) * jnp.abs(x))
    bell = jnp.exp(-0.5 * x * x)
    series = 1.421413741 + t * (-1.453152027 + t * 1.061405429)
    series = t * (0.254829592 + t * (-0.284496736 + t * series))
    tail = 0.5 * series * bell
    cdf = jnp.where(x >= 0.0, 1.0 - tail, tail)
    return (x * cdf).astype(low), cdf + x * (bell * (1.0 / math.sqrt(2.0 * math.pi)))


@on_section
def ffn_fwd_kernel(ids, unit_one, in_bias, small, *rest):
    weights, rest = rest[:10], rest[10:]
    outs, rest = rest[:5], rest[5:]
    hidden, slope, unit_two, inverse_two, result, w_in, w_out, normed_low, sems, out_sems = rest
    layer = ids[SECTION]
    in_copies, out_copies = ffn_copies(ids, weights, w_in, w_out, sems)
    begin(in_copies)
    begin(out_copies)
    normed = unit_one[...] * small[layer, 3:4, :] + small[layer, 4:5, :]
    normed_low[...] = normed.astype(low)
    finish(in_copies)
    tile = w_in.shape[1] // 8
    for t in range(8):
        columns = slice(t * tile, (t + 1) * tile)
        pre = dot(normed_low[...], w_in[:, columns]) + in_bias[layer, :, columns]
        hidden[:, columns], slope[:, columns] = gelu_and_slope(pre)
    going = leave([(hidden, outs[0]), (slope, outs[1])], out_sems, 0)
    finish(out_copies)
    residual = unit_one[...] * small[layer, 3:4, :] + small[layer, 4:5, :]
    residual = residual + (dot(hidden[...], w_out[...]) + small[layer, 5:6, :])
    unit, inverse = normalize(residual)
    result[...] = (unit * small[layer, 6:7, :] + small[layer, 7:8, :]).astype(low)
    going += leave([(result, outs[4])], out_sems, 4)
    unit_two[...] = unit
    inverse_two[...] = inverse
    finish(going + leave([(unit_two, outs[2]), (inverse_two, outs[3])], out_sems, 2))


@on_section
def ffn_bwd_kernel(ids, grad, unit_two, inverse_two, unit_one, inverse_one, slope, small, *rest):
    weights, rest = rest[:10], rest[10:]
    outs, rest = rest[:5], rest[5:]
    d_ffn, d_pre, d_resid, small_grads, in_bias_grad, w_in, w_out, sems, out_sems = rest
    layer = ids[SECTION]
    in_copies, out_copies = ffn_copies(ids, weights, w_in, w_out, sems)
    begin(out_copies)
    begin(in_copies)
    g = grad[...].astype(f32)
    unit = unit_two[...]
    small_grads[0:1, :] = jnp.sum(g * unit, axis=0, keepdims=True)
    small_grads[1:2, :] = jnp.sum(g, axis=0, keepdims=True)
    d_two = normalize_back(g * small[layer, 6:7, :], unit, inverse_two[...])
    d_resid[...] = d_two
    d_low = d_two.astype(low)
    d_ffn[...] = d_low
    small_grads[2:3, :] = jnp.sum(d_low.astype(f32), axis=0, keepdims=True)
    going = leave([(d_ffn, outs[0])], out_sems, 0)
    finish(out_copies)
    tile = w_in.shape[1] // 8
    for t in range(8):
        columns = slice(t * tile, (t + 1) * tile)
        d_hidden = dot_nt(d_ffn[...], w_out[columns, :])
        d_tile = (d_hidden * slope[:, columns]).astype(low)
        d_pre[:, columns] = d_tile
        in_bias_grad[:, columns] = jnp.sum(d_tile.astype(f32), axis=0, keepdims=True)
    going += leave([(d_pre, outs[1])], out_sems, 1)
    finish(in_copies)
    d_normed = d_resid[...] + dot_nt(d_pre[...], w_in[...])
    unit = unit_one[...]
    small_grads[3:4, :] = jnp.sum(d_normed * unit, axis=0, keepdims=True)
    small_grads[4:5, :] = jnp.sum(d_normed, axis=0, keepdims=True)
    small_grads[5:8, :] = jnp.zeros((3, unit.shape[1]), f32)
    d_resid[...] = normalize_back(d_normed * small[layer, 3:4, :], unit, inverse_one[...])
    finish(going + leave([(d_resid, outs[2]), (small_grads, outs[3]), (in_bias_grad, outs[4])], out_sems, 2))


@on_section
def attn_bwd_kernel(ids, d_resid, qkv_rows, probs, *rest):
    weights, rest = rest[:7], rest[7:]
    outs, rest = rest[:4], rest[4:]
    d_attn, d_qkv, d_input, small_grads, w_qkv, w_o, d_context, sems, out_sems = rest
    tokens, width = d_resid.shape
    qkv_copies, o_copies = attn_copies(ids, weights, w_qkv, w_o, sems)
    begin(o_copies)
    begin(qkv_copies)
    d_low = d_resid[...].astype(low)
    d_attn[...] = d_low
    small_grads[2:3, :] = jnp.sum(d_low.astype(f32), axis=0, keepdims=True)
    going = leave([(d_attn, outs[0])], out_sems, 0)
    finish(o_copies)
    d_context[...] = dot_nt(d_attn[...], w_o[...]).astype(low)
    pair_width = 2 * width // HEADS
    first = lax.broadcasted_iota(jnp.int32, (1, pair_width), 1) < pair_width // 2
    scale = 1.0 / math.sqrt(width // HEADS)
    for pair in range(HEADS // 2):
        at_query = slice(pair * pair_width, (pair + 1) * pair_width)
        at_key = slice(width + at_query.start, width + at_query.stop)
        at_value = slice(2 * width + at_query.start, 2 * width + at_query.stop)
        query, key, value = qkv_rows[:, at_query], qkv_rows[:, at_key], qkv_rows[:, at_value]
        d_ctx = d_context[:, at_query]
        sides = []
        for side in range(2):
            mine = first if side == 0 else jnp.logical_not(first)
            prob_low = probs[2 * pair + side]
            prob = prob_low.astype(f32)
            d_prob = dot_nt(jnp.where(mine, d_ctx, jnp.zeros_like(d_ctx)), value)
            inner = jnp.sum(prob * d_prob, axis=-1, keepdims=True)
            d_scores = (prob * (d_prob - inner)).astype(low)
            sides.append((dot(d_scores, key), dot_tn(d_scores, query), dot_tn(prob_low, d_ctx)))
        d_qkv[:, at_query] = (jnp.where(first, sides[0][0], sides[1][0]) * scale).astype(low)
        d_qkv[:, at_key] = jnp.where(first, sides[0][1], sides[1][1]).astype(low)
        d_qkv[:, at_value] = jnp.where(first, sides[0][2], sides[1][2]).astype(low)

    going += leave([(d_qkv, outs[1])], out_sems, 1)
    finish(qkv_copies)
    d_input[...] = (d_resid[...] + dot_nt(d_qkv[...], w_qkv[...])).astype(low)
    going += leave([(d_input, outs[2])], out_sems, 2)
    small_grads[0:1, :] = jnp.sum(d_qkv[:, :width].astype(f32), axis=0, keepdims=True)
    small_grads[1:2, :] = jnp.sum(d_qkv[:, 2 * width :].astype(f32), axis=0, keepdims=True)
    small_grads[3:8, :] = jnp.zeros((5, width), f32)
    finish(going + leave([(small_grads, outs[3])], out_sems, 3))


def place_of(ids, owner, piece, way):
    away = None if owner is None else ids[ME] ^ owner
    place = [None if away is None else away & 1]
    for name in way:
        if name == "x":
            place.append(pl.ds(0, 2) if away is None else away >> 1)
        else:
            place.append(pl.ds(0, 2) if piece is None else (piece & 1) ^ ids[Z])
    return tuple(place) + (pl.ds(0, 4) if piece is None else piece >> 1,)


def store_rows(stage, ids, product, piece, way):
    share = product.shape[0] // 4
    for owner in range(4):
        block = product[owner * share : (owner + 1) * share].astype(low)
        stage[place_of(ids, owner, piece, way) + (pl.ds(0, share),)] = block


def piece_copies(stage, ids, piece, way, kept, sent, sems):
    at = place_of(ids, None, piece, way)[1:]
    return leave([(stage.at[(1,) + at], sent.at[at]), (stage.at[(0,) + at], kept.at[at])], sems, 2 * piece)


def out_grad_kernel(way, ids, hidden_0, hidden_1, d_ffn_0, d_ffn_1, kept, sent, stage, out_sems):
    tile = hidden_0.shape[1] // 8
    share = d_ffn_0.shape[1] // 4
    waits = []
    for owner in range(4):
        for half in range(2):
            columns = slice((2 * owner + half) * tile, (2 * owner + half + 1) * tile)
            out_grad = dot_tn(hidden_0[:, columns], d_ffn_0[...]) + dot_tn(hidden_1[:, columns], d_ffn_1[...])
            for row_group in range(2):
                for column_group in range(2):
                    piece = (half * 2 + row_group) * 2 + column_group
                    block = out_grad[
                        row_group * share : (row_group + 1) * share,
                        column_group * tile : (column_group + 1) * tile,
                    ]
                    stage[place_of(ids, owner, piece, way)] = block.astype(low)
        core, *at = place_of(ids, owner, None, way)
        at = tuple(at)
        to_kept = pltpu.make_async_copy(stage.at[(0,) + at], kept.at[at], out_sems.at[owner])
        to_sent = pltpu.make_async_copy(stage.at[(1,) + at], sent.at[at], out_sems.at[owner])
        pl.when(core == 0)(to_kept.start)
        pl.when(core == 1)(to_sent.start)
        waits.append(to_kept)
    finish(waits)


def in_grad_kernel(way, ids, unit_0, unit_1, d_pre_0, d_pre_1, small, kept, sent, normed_t, stage, out_sems):
    layer = ids[SECTION]
    gain, shift = small[layer, 3:4, :], small[layer, 4:5, :]
    for i, unit in enumerate((unit_0, unit_1)):
        normed_t[i] = (unit[...] * gain + shift).astype(low).T
    tile = d_pre_0.shape[1] // 8
    going = []
    for t in range(8):
        columns = slice(t * tile, (t + 1) * tile)
        product = dot(normed_t[0], d_pre_0[:, columns]) + dot(normed_t[1], d_pre_1[:, columns])
        store_rows(stage, ids, product, t, way)
        going += piece_copies(stage, ids, t, way, kept, sent, out_sems)
    finish(going)


SMALL_ROWS = 16
SMALL_LINES = ((True, 0), (True, 1), (True, 2), (False, 3), (False, 4), (False, 2), (False, 0), (False, 1))


def attn_grad_kernel(way, ids, *refs):
    x, context, d_qkv, d_attn, small_attn, small_ffn, in_bias = [refs[2 * i : 2 * i + 2] for i in range(7)]
    kept, sent, x_t, stage, out_sems = refs[14:]
    tokens, width = x[0].shape
    share, tile = width // 4, width // 2
    attn_lines, ffn_lines = [a[0][...] + a[1][...] for a in (small_attn, small_ffn)]
    bias_line = in_bias[0][...] + in_bias[1][...]
    for i in range(2):
        x_t[i] = x[i][...].T
    for owner in range(4):
        lines = []
        for attention, line in SMALL_LINES:
            source = attn_lines if attention else ffn_lines
            lines.append(source[line : line + 1, owner * share : (owner + 1) * share])
        for i in range(4):
            lines.append(bias_line[:, owner * width + i * share : owner * width + (i + 1) * share])
        for piece in range(8):
            mine = lines[2 * piece : 2 * piece + 2]
            rows = [jnp.concatenate([line, jnp.zeros_like(line)], axis=1) for line in mine]
            rows.append(jnp.zeros((SMALL_ROWS - len(mine), tile), f32))
            block = jnp.concatenate(rows, axis=0).astype(low)
            stage[place_of(ids, owner, piece, way) + (pl.ds(share, SMALL_ROWS),)] = block
    going = []
    for piece in range(8):
        if piece < 6:
            at = slice(piece * tile, (piece + 1) * tile)
            product = dot(x_t[0], d_qkv[0][:, at]) + dot(x_t[1], d_qkv[1][:, at])
        else:
            at = slice((piece - 6) * tile, (piece - 5) * tile)
            product = dot_tn(context[0][...], d_attn[0][:, at]) + dot_tn(context[1][...], d_attn[1][:, at])
        store_rows(stage, ids, product, piece, way)
        going += piece_copies(stage, ids, piece, way, kept, sent, out_sems)
    finish(going)


def unpack_kernel(slab, ids, mine, other, *rest):
    outs, (buffer, wide_buffer, in_sems, out_sems) = rest[:-4], rest[-4:]
    share, tile = wide_buffer.shape[2:]
    arriving, copies = [], []
    for i, source in enumerate((mine, other)):
        for piece in range(8):
            place = ((piece & 1) ^ ids[Z], piece >> 1)
            arriving.append(
                pltpu.make_async_copy(source.at[place], buffer.at[i, piece], in_sems.at[8 * i + piece])
            )
    begin(arriving)
    for i in range(2):
        layer = ids[SECTION] if i == 0 else 1 - ids[SECTION]
        for piece in range(8):
            arriving[8 * i + piece].wait()
            wide_buffer[i, piece] = buffer[i, piece, :share].astype(f32)
            columns = pl.ds(piece * tile, tile)
            if slab == "in":
                target = outs[0].at[layer, :, columns]
            elif slab == "out":
                rows = pl.ds((piece // 2) * share, share)
                target = outs[0].at[layer, rows, pl.ds((piece % 2) * tile, tile)]
            elif piece < 6:
                target = outs[0].at[layer, :, columns]
            else:
                target = outs[1].at[layer, :, pl.ds((piece - 6) * tile, tile)]
            copies += leave([(wide_buffer.at[i, piece], target)], out_sems, 8 * i + piece)
    if slab == "attn":
        first = ids[SECTION] == 0
        for line in range(12):
            row = share + line % 2
            mine_line, other_line = [buffer[i, line // 2, row : row + 1, :share].astype(f32) for i in range(2)]
            out = outs[2 + min(line, 8)]
            at = slice(0, share) if line < 8 else slice((line - 8) * share, (line - 7) * share)
            out[0:1, at] = jnp.where(first, mine_line, other_line)
            out[1:2, at] = jnp.where(first, other_line, mine_line)
    if slab != "attn":
        outs[-1][...] = jnp.zeros(outs[-1].shape, f32)
    finish(copies)


SMEM = pl.BlockSpec(memory_space=pltpu.SMEM)
VMEM = pl.BlockSpec(memory_space=pltpu.VMEM)
ANY = pl.BlockSpec(memory_space=pl.ANY)


def call(kernel, name, time, in_specs, out_specs, out_shape, scratch, args, aliases=()):
    return pl.pallas_call(
        kernel,
        name=name,
        in_specs=in_specs,
        out_specs=out_specs,
        out_shape=out_shape,
        scratch_shapes=scratch,
        input_output_aliases=dict(aliases),
        compiler_params=pltpu.CompilerParams(vmem_limit_bytes=VMEM_BYTES),
        cost_estimate=pl.CostEstimate(
            flops=int(time * 1.1e9), bytes_accessed=int(time * 3.6e6), transcendentals=0
        ),
    )(*args)


def shape(dims, kind):
    return jax.ShapeDtypeStruct(dims, kind)


def added(a, b):
    return (a.astype(f32) + b.astype(f32)).astype(low)


class Order:
    def __init__(self):
        self.last = None

    def after(self, values):
        if self.last is None:
            return values
        values, self.last = lax.optimization_barrier((values, self.last))
        return values

    def wait(self, values):
        values = self.after(values)
        self.last = values
        return values


STEPS = {"x": ("narrow", 2), "z": ("wide", 2)}
PLAN = (1, 2, 0, -1, 1, 0, 0, 1, 2, 0, 1, 2, 0, 1, 2, 1, 2, 2)


class Slab:
    def __init__(self, way, wide_count, kept, sent):
        self.way, self.kept = way, kept
        self.rest = [1 << b for b in range(2, wide_count.bit_length() - 1)]
        self.flying = swap(sent, "narrow", 1)
        self.stage = 0

    def step(self, order):
        received = order.after(self.flying)
        if self.stage < 2:
            send = added(self.kept[1], received[1])
            self.kept = added(self.kept[0], received[0])
            self.flying = swap(send, *STEPS[self.way[self.stage]])
            order.last = send
        elif self.stage == 2:
            self.kept = added(self.kept, received)
            for bit in self.rest[:-1]:
                self.kept = added(self.kept, swap(self.kept, "wide", bit))
            order.last = self.kept
            self.flying = swap(self.kept, "wide", self.rest[-1])
        elif self.stage == 3:
            self.kept = added(self.kept, received)
            order.last = self.kept
            self.flying = swap(self.kept, "wide", 2)
        elif self.stage == 4:
            self.mine = jnp.stack([self.kept, received])
            order.last = self.mine
            self.flying = swap(self.mine, "wide", 1)
        else:
            self.other = received
        self.stage += 1


def body(
    tables_in,
    cotangent,
    cell_ids,
    lengths,
    qkv_weight,
    q_bias,
    v_bias,
    o_weight,
    o_bias,
    norm1_gain,
    norm1_bias,
    in_weight,
    in_bias,
    out_weight,
    out_bias,
    norm2_gain,
    norm2_bias,
):
    tokens, width = tables_in.shape
    layers, share, ffn = in_weight.shape
    ffn_share = out_weight.shape[1]
    tile = ffn // 8
    wide_count = lax.axis_size("wide")
    assert wide_count & (wide_count - 1) == 0 and wide_count >= 8 and lax.axis_size("narrow") == 4
    assert cell_ids.shape == (1, tokens) and layers == 2
    me = lax.axis_index("narrow").astype(jnp.int32)
    wide_me = lax.axis_index("wide").astype(jnp.int32)
    section, z = wide_me & 1, (wide_me >> 1) & 1
    is_first = section == 0
    ids = jnp.stack([me, me ^ 1, me ^ 2, me ^ 3, z, section])
    order = Order()


    def half_of(weight):
        rows = weight.shape[1] // 2
        return lax.dynamic_slice(weight, (section, z * rows, 0), (1, rows, weight.shape[2]))[0]

    own = (qkv_weight, o_weight, in_weight, out_weight)
    joint = jnp.concatenate([half_of(qkv_weight), half_of(o_weight)], axis=1)
    halves = [joint, half_of(in_weight), half_of(out_weight)]
    near_x, far_x, diagonal, core = [None] * 3, [None] * 3, [None] * 3, [None] * 4
    near_x[0] = swap(halves[0], "narrow", 2)
    order.last = halves[0]
    core[0], core[1] = swap(own[0], "narrow", 1), swap(own[1], "narrow", 1)
    swapped = swap(order.after(jnp.where(is_first, cotangent, tables_in)), "wide", 1)
    numbers = jnp.concatenate([cell_ids, jnp.broadcast_to(lengths[:, None], (1, 128))], axis=1)
    others_numbers = swap(order.after(numbers), "wide", 1)
    short = order.after((q_bias, v_bias, o_bias, norm1_gain, norm1_bias, out_bias, norm2_gain, norm2_bias))
    packed = call(
        pack_kernel, "pack", 1, [VMEM] * 9, VMEM, shape((layers, 12, share), f32), [], tuple(short) + (in_bias,)
    )
    halves[1:], packed = order.wait((halves[1:], packed))
    near_x[0], core[0], core[1], swapped, others_numbers = order.wait(
        (near_x[0], core[0], core[1], swapped, others_numbers)
    )

    others = [
        lax.ppermute(order.after(packed), "narrow", [(i, i ^ away) for i in range(4)]) for away in (1, 2, 3)
    ]
    far_x[0] = swap(near_x[0], "wide", 2)
    near_x[1] = swap(order.after(halves[1]), "narrow", 2)
    far_x[0], near_x[1], others = order.wait((far_x[0], near_x[1], others))

    def in_order(low_one, high_one, bit):
        swap_them = (me & bit) != 0
        return jnp.stack([jnp.where(swap_them, high_one, low_one), jnp.where(swap_them, low_one, high_one)])

    def join(i):
        both = jnp.concatenate([near_x[i], far_x[i]], axis=0)
        diagonal[i] = swap(both, "narrow", 1)
        return both

    both = join(0)
    far_x[1] = swap(near_x[1], "wide", 2)
    near_x[2] = swap(order.after(halves[2]), "narrow", 2)
    core[2], core[3] = swap(order.after(own[2]), "narrow", 1), swap(order.after(own[3]), "narrow", 1)
    order.last = both
    packed = in_order(in_order(packed, others[0], 1), in_order(others[1], others[2], 1), 2)
    packed = packed.reshape(4, layers, 12, share)
    small = packed[:, :, :8].transpose(1, 2, 0, 3).reshape(layers, 8, width)
    full_in_bias = packed[:, :, 8:].transpose(1, 0, 2, 3).reshape(layers, 1, ffn)
    other_cells, other_lengths = others_numbers[:, :tokens], others_numbers[0, tokens : tokens + 1]
    cells = (jnp.where(is_first, cell_ids, other_cells), jnp.where(is_first, other_cells, cell_ids))
    spans = (jnp.where(is_first, lengths, other_lengths), jnp.where(is_first, other_lengths, lengths))
    ids, small, full_in_bias, cells, spans = order.wait((ids, small, full_in_bias, cells, spans))
    diagonal[0] = order.wait(diagonal[0])


    w_qkv = pltpu.VMEM((width, 3 * width), low)
    w_o = pltpu.VMEM((width, width), low)
    w_in = pltpu.VMEM((width, ffn), low)
    w_out = pltpu.VMEM((ffn, width), low)
    copy_sems = pltpu.SemaphoreType.DMA((12,))
    out_sems = pltpu.SemaphoreType.DMA((5,))
    piece_sems = pltpu.SemaphoreType.DMA((16,))
    rows_f32, rows_low = ((tokens, width), f32), ((tokens, width), low)
    column_f32, eight_f32, line_f32 = ((tokens, 1), f32), ((8, width), f32), ((1, ffn), f32)
    wide_low, wide_f32 = ((tokens, ffn), low), ((tokens, ffn), f32)
    qkv_low, probs_low = ((tokens, 3 * width), low), ((HEADS, tokens, tokens), low)

    def guarded(kernel, name, time, of_section, inputs, weights, outs, scratch, earlier, lead=0):
        inputs = list(inputs)
        inputs[lead] = order.after(inputs[lead])
        specs = [SMEM] + [SMEM if v.ndim == 1 else VMEM for v in inputs]
        specs += [ANY] * (len(weights) + len(earlier))
        results = call(
            functools.partial(kernel, of_section, len(inputs) + len(weights), len(earlier)),
            name,
            time,
            specs,
            [VMEM] + [ANY] * len(outs),
            [shape((8, 128), f32)] + [shape(*out) for out in outs],
            scratch,
            (ids, *inputs, *weights, *earlier),
            {1 + len(inputs) + len(weights) + i: 1 + i for i in range(len(earlier))},
        )
        order.last = results[0]
        return tuple(results[1:])

    def attn_weights():
        return (qkv_weight, core[0], o_weight, core[1], near_x[0], far_x[0], diagonal[0])

    def ffn_weights():
        in_refs = (in_weight, core[2], near_x[1], far_x[1], diagonal[1])
        return in_refs + (out_weight, core[3], near_x[2], far_x[2], diagonal[2])

    def attn_forward(of_section, table, x, earlier=()):
        outs = [qkv_low, probs_low, rows_low, rows_f32, column_f32]
        return guarded(
            attn_fwd_kernel,
            "attn_fwd",
            8,
            of_section,
            (spans[table], x, cells[table], small),
            attn_weights(),
            outs,
            [pltpu.VMEM(*out) for out in outs] + [w_qkv, w_o, pltpu.VMEM((tokens, tokens), f32), copy_sems, out_sems],
            earlier,
            lead=1,
        )

    def ffn_forward(of_section, unit_one, earlier=()):
        outs = [wide_low, wide_f32, rows_f32, column_f32, rows_low]
        return guarded(
            ffn_fwd_kernel,
            "ffn_fwd",
            10,
            of_section,
            (unit_one, full_in_bias, small),
            ffn_weights(),
            outs,
            [pltpu.VMEM(*out) for out in outs] + [w_in, w_out, pltpu.VMEM(*rows_low), copy_sems, out_sems],
            earlier,
        )

    def ffn_backward(of_section, grad, attn_kept, ffn_kept, earlier=()):
        outs = [rows_low, wide_low, rows_f32, eight_f32, line_f32]
        _, slope, unit_two, inverse_two, _ = ffn_kept
        return guarded(
            ffn_bwd_kernel,
            "ffn_bwd",
            10,
            of_section,
            (grad, unit_two, inverse_two, attn_kept[3], attn_kept[4], slope, small),
            ffn_weights(),
            outs,
            [pltpu.VMEM(*out) for out in outs] + [w_in, w_out, copy_sems, out_sems],
            earlier,
        )

    def attn_backward(of_section, d_resid, attn_kept, earlier=()):
        outs = [rows_low, qkv_low, rows_low, eight_f32]
        return guarded(
            attn_bwd_kernel,
            "attn_bwd",
            10,
            of_section,
            (d_resid, attn_kept[0], attn_kept[1]),
            attn_weights(),
            outs,
            [pltpu.VMEM(*out) for out in outs] + [w_qkv, w_o, pltpu.VMEM(*rows_low), copy_sems, out_sems],
            earlier,
        )

    def hop(value, forth):
        pairs = [(i, i + 1) if forth else (i + 1, i) for i in range(0, wide_count, 2)]
        return lax.ppermute(value, "wide", pairs)

    def weight_grad(kernel, name, time, way, inputs, rows, scratch, sems):
        inputs = list(inputs)
        inputs[0] = order.after(inputs[0])
        pieces = shape((2, 2, 4, rows, tile), low)
        _, kept, sent = call(
            lambda i, *refs: kernel(way, i, *refs[: len(inputs)], *refs[len(inputs) + 1 :]),
            name,
            time,
            [SMEM] + [VMEM] * len(inputs),
            [VMEM, ANY, ANY],
            [shape((8, 128), f32), pieces, pieces],
            scratch + [pltpu.VMEM((2, 2, 2, 4, rows, tile), low), sems],
            (ids, *inputs),
        )
        order.last = _
        return Slab(way, wide_count, kept, sent)

    def unpack(name, slab):
        dims = {
            "attn": [(layers, share, 3 * width), (layers, share, width)],
            "in": [(layers, share, ffn)],
            "out": [(layers, ffn_share, width)],
        }[name]
        extra = [(layers, share)] * 8 + [(layers, ffn_share)] if name == "attn" else [(8, 128)]
        mine, other = order.after((slab.mine, slab.other))
        rows = mine.shape[2]
        outs = call(
            functools.partial(unpack_kernel, name),
            "unpack",
            5,
            [SMEM] + [ANY] * 2,
            [ANY] * len(dims) + [VMEM] * len(extra),
            [shape(d, f32) for d in dims + extra],
            [
                pltpu.VMEM((2, 8, rows, tile), low),
                pltpu.VMEM((2, 8, share, tile), f32),
                pltpu.SemaphoreType.DMA((16,)),
                pltpu.SemaphoreType.DMA((16,)),
            ],
            (ids, mine, other),
        )
        order.last = outs[-1]
        return outs


    first_attn = [attn_forward(0, 0, tables_in), attn_forward(0, 1, swapped)]
    far_x[1], near_x[2], core[2], core[3] = order.wait((far_x[1], near_x[2], core[2], core[3]))
    order.last = join(1)
    far_x[2] = swap(near_x[2], "wide", 2)
    diagonal[1], far_x[2] = order.wait((diagonal[1], far_x[2]))
    order.last = join(2)
    diagonal[2] = order.wait(diagonal[2])
    first_ffn = [ffn_forward(0, first_attn[0][3]), None]
    hops = [order.wait(hop(first_ffn[0][4], True)), None]
    first_ffn[1] = ffn_forward(0, first_attn[1][3])
    hops[1] = hop(first_ffn[1][4], True)

    attn_kept, ffn_kept, ffn_back, attn_back, returned = [[None] * 2 for _ in range(5)]
    attn_kept[0] = attn_forward(1, 0, hops[0], first_attn[0])
    ffn_kept[0] = ffn_forward(1, attn_kept[0][3], first_ffn[0])
    ffn_back[0] = ffn_backward(1, swapped, attn_kept[0], ffn_kept[0])
    attn_back[0] = attn_backward(1, ffn_back[0][2], attn_kept[0])
    returned[0] = hop(attn_back[0][2], False)
    hops[1] = order.wait(hops[1])
    attn_kept[1] = attn_forward(1, 1, hops[1], first_attn[1])
    returned[0] = order.wait(returned[0])
    ffn_kept[1] = ffn_forward(1, attn_kept[1][3], first_ffn[1])
    ffn_back[1] = ffn_backward(1, cotangent, attn_kept[1], ffn_kept[1])
    attn_back[1] = attn_backward(1, ffn_back[1][2], attn_kept[1])
    returned[1] = hop(attn_back[1][2], False)

    ffn_back[0] = ffn_backward(0, returned[0], attn_kept[0], ffn_kept[0], ffn_back[0])
    attn_back[0] = attn_backward(0, ffn_back[0][2], attn_kept[0], attn_back[0])
    returned[1] = order.wait(returned[1])
    ffn_back[1] = ffn_backward(0, returned[1], attn_kept[1], ffn_kept[1], ffn_back[1])

    way = "xz"
    slabs = [None] * 3
    slabs[0] = weight_grad(
        out_grad_kernel,
        "out_grad",
        7,
        way,
        (ffn_kept[0][0], ffn_kept[1][0], ffn_back[0][0], ffn_back[1][0]),
        share,
        [],
        pltpu.SemaphoreType.DMA((4,)),
    )
    turned = pltpu.VMEM((2, width, tokens), low)
    slabs[1] = weight_grad(
        in_grad_kernel,
        "in_grad",
        6,
        way,
        (attn_kept[0][3], attn_kept[1][3], ffn_back[0][1], ffn_back[1][1], small),
        share,
        [turned],
        piece_sems,
    )
    slabs[0].step(order)
    attn_back[1] = attn_backward(0, ffn_back[1][2], attn_kept[1], attn_back[1])
    layer_inputs = (jnp.where(is_first, tables_in, hops[0]), jnp.where(is_first, swapped, hops[1]))
    slabs[2] = weight_grad(
        attn_grad_kernel,
        "attn_grad",
        7,
        way,
        layer_inputs
        + (attn_kept[0][2], attn_kept[1][2])
        + (attn_back[0][1], attn_back[1][1], attn_back[0][0], attn_back[1][0])
        + (attn_back[0][3], attn_back[1][3], ffn_back[0][3], ffn_back[1][3], ffn_back[0][4], ffn_back[1][4]),
        share + SMALL_ROWS,
        [turned],
        piece_sems,
    )
    handed = swap(order.after(jnp.where(is_first, attn_back[1][2], ffn_kept[0][4])), "wide", 1)
    names = ("out", "in", "attn")
    results = {}
    for which in PLAN:
        if which < 0:
            handed = order.wait(handed)
            mixed_out = jnp.where(is_first, handed, ffn_kept[1][4])
            input_grad = jnp.where(is_first, attn_back[0][2], handed)
            mixed_out, input_grad = order.wait((mixed_out, input_grad))
            continue
        slabs[which].step(order)
        if slabs[which].stage == 6:
            results[names[which]] = unpack(names[which], slabs[which])
    qkv_grad, o_grad, *vectors = results["attn"]
    return (
        mixed_out,
        input_grad,
        qkv_grad,
        vectors[0],
        vectors[1],
        o_grad,
        vectors[2],
        vectors[3],
        vectors[4],
        results["in"][0],
        vectors[8],
        results["out"][0],
        vectors[5],
        vectors[6],
        vectors[7],
    )


def solution(mesh):
    by_table = P(("wide", "narrow"), None)
    matrix = P(None, "narrow", None)
    vector = P(None, "narrow")
    return jax.shard_map(
        body,
        mesh=mesh,
        in_specs=(
            by_table,
            by_table,
            by_table,
            P(("wide", "narrow")),
            matrix,
            vector,
            vector,
            matrix,
            vector,
            vector,
            vector,
            matrix,
            vector,
            matrix,
            vector,
            vector,
            vector,
        ),
        out_specs=(
            by_table,
            by_table,
            matrix,
            vector,
            vector,
            matrix,
            vector,
            vector,
            vector,
            matrix,
            vector,
            matrix,
            vector,
            vector,
            vector,
        ),
        check_vma=False,
    )
```

```python
import functools
import math

import jax
import jax.numpy as jnp
from jax import lax
from jax.experimental import pallas as pl
from jax.experimental.pallas import tpu as pltpu
from jax.sharding import PartitionSpec as P

HEADS = 12
norm_eps = 1e-12
masked_score = -1000000000.0
low = jnp.bfloat16
f32 = jnp.float32
VMEM_BYTES = 56 * 1024 * 1024
HALVINGS = 2


def swap(value, axis, bit):
    count = lax.axis_size(axis)
    return lax.ppermute(value, axis, [(i, i ^ bit) for i in range(count)])


def dot(a, b):
    return jnp.dot(a, b, preferred_element_type=f32)


def dot_nt(a, b):
    return lax.dot_general(a, b, (((1,), (1,)), ((), ())), preferred_element_type=f32)


def dot_tn(a, b):
    return lax.dot_general(a, b, (((0,), (0,)), ((), ())), preferred_element_type=f32)


def normalize(residual):
    center = residual - jnp.mean(residual, axis=-1, keepdims=True)
    inverse = lax.rsqrt(jnp.mean(center * center, axis=-1, keepdims=True) + norm_eps)
    return center * inverse, inverse


def normalize_back(grad_unit, unit, inverse):
    centered = grad_unit - jnp.mean(grad_unit, axis=-1, keepdims=True)
    return inverse * (centered - unit * jnp.mean(grad_unit * unit, axis=-1, keepdims=True))


def weight_copies(ids, layer, pieces, target, columns, sems, base):
    own, core, near_x, far_x, diagonal = pieces
    rows = own.shape[1]
    half = rows // 2
    n, y = ids[0], ids[4]
    copies = []

    def add(source, start, count):
        where = target.at[pl.ds(pl.multiple_of(start, half), count), :]
        copies.append(pltpu.make_async_copy(source, where, sems.at[base + len(copies)]))

    at = pl.ds(columns, target.shape[1])
    add(own.at[layer], n * rows, rows)
    add(core.at[layer], ids[1] * rows, rows)
    add(near_x.at[:, at], ids[2] * rows + y * half, half)
    add(far_x.at[:, at], ids[2] * rows + (1 - y) * half, half)
    add(diagonal.at[pl.ds(0, half), at], ids[3] * rows + y * half, half)
    add(diagonal.at[pl.ds(half, half), at], ids[3] * rows + (1 - y) * half, half)
    return copies


def begin(copies):
    for copy in copies:
        copy.start()


def finish(copies):
    for copy in copies:
        copy.wait()


def attn_copies(layer, ids, refs, w_qkv, w_o, sems):
    qkv_own, qkv_core, o_own, o_core = refs[:4]
    halves = refs[4:]
    qkv = weight_copies(ids, layer, (qkv_own, qkv_core) + halves, w_qkv, 0, sems, 0)
    o = weight_copies(ids, layer, (o_own, o_core) + halves, w_o, w_qkv.shape[1], sems, 6)
    return qkv, o


def ffn_copies(layer, ids, refs, w_in, w_out, sems):
    in_copies = weight_copies(ids, layer, refs[:5], w_in, 0, sems, 0)
    out_copies = weight_copies(ids, layer, refs[5:], w_out, 0, sems, 6)
    return in_copies, out_copies


def pack_kernel(*refs):
    shorts, in_bias, packed = refs[:8], refs[8], refs[9]
    layers, share = shorts[0].shape
    for layer in range(layers):
        for i, short in enumerate(shorts):
            packed[layer, i : i + 1, :] = short[layer : layer + 1, :].astype(f32)
        for i in range(4):
            packed[layer, 8 + i : 9 + i, :] = in_bias[layer : layer + 1, i * share : (i + 1) * share].astype(f32)


def attn_fwd_kernel(layer, ids, length, x, cell_row, small, *rest):
    weights, rest = rest[:7], rest[7:]
    qkv_rows, probs, context, unit_out, inverse_out, w_qkv, w_o, mask, sems = rest
    tokens, width = x.shape
    qkv_copies, o_copies = attn_copies(layer, ids, weights, w_qkv, w_o, sems)
    begin(qkv_copies)
    begin(o_copies)
    position = lax.broadcasted_iota(jnp.int32, (1, tokens), 1)
    key_cell = cell_row[...]
    square = (tokens, tokens)
    diagonal = lax.broadcasted_iota(jnp.int32, square, 0) == lax.broadcasted_iota(jnp.int32, square, 1)
    query_cell = jnp.sum(jnp.where(diagonal, key_cell, 0), axis=1, keepdims=True)
    allowed = (query_cell == key_cell) | (key_cell == 0) | (query_cell == 0)
    allowed = allowed & (position < length[0])
    mask[...] = jnp.where(allowed, 0.0, masked_score)
    scale = 1.0 / math.sqrt(width // HEADS)
    finish(qkv_copies)
    tile = width // 2

    for t in range(6):
        columns = slice(t * tile, (t + 1) * tile)
        rows = dot(x[...], w_qkv[:, columns])
        if t // 2 != 1:
            part = slice((t % 2) * tile, (t % 2 + 1) * tile)
            rows = rows + small[layer, t // 4 : t // 4 + 1, part]
        if t < 2:
            rows = rows * scale
        qkv_rows[:, columns] = rows.astype(low)

    pair_width = 2 * width // HEADS
    first = lax.broadcasted_iota(jnp.int32, (1, pair_width), 1) < pair_width // 2

    for pair in range(HEADS // 2):
        at = slice(pair * pair_width, (pair + 1) * pair_width)
        query = qkv_rows[:, at]
        key = qkv_rows[:, width + at.start : width + at.stop]
        value = qkv_rows[:, 2 * width + at.start : 2 * width + at.stop]
        sides = []
        for side in range(2):
            mine = first if side == 0 else jnp.logical_not(first)
            scores = dot_nt(jnp.where(mine, query, jnp.zeros_like(query)), key) + mask[...]
            shifted = jnp.exp(scores - jnp.max(scores, axis=-1, keepdims=True))
            total = jnp.sum(shifted, axis=-1, keepdims=True)
            prob = (shifted * (1.0 / total)).astype(low)
            probs[2 * pair + side] = prob
            sides.append(dot(prob, value))
        context[:, at] = jnp.where(first, sides[0], sides[1]).astype(low)

    finish(o_copies)
    residual = x[...].astype(f32) + (dot(context[...], w_o[...]) + small[layer, 2:3, :])
    unit, inverse = normalize(residual)
    unit_out[...] = unit
    inverse_out[...] = inverse


def gelu_and_slope(x):
    t = 1.0 / (1.0 + (0.3275911 * math.sqrt(0.5)) * jnp.abs(x))
    bell = jnp.exp(-0.5 * x * x)
    series = 1.421413741 + t * (-1.453152027 + t * 1.061405429)
    series = t * (0.254829592 + t * (-0.284496736 + t * series))
    tail = 0.5 * series * bell
    cdf = jnp.where(x >= 0.0, 1.0 - tail, tail)
    return (x * cdf).astype(low), cdf + x * (bell * (1.0 / math.sqrt(2.0 * math.pi)))


def ffn_fwd_kernel(layer, ids, unit_one, in_bias, small, *rest):
    weights, rest = rest[:10], rest[10:]
    hidden_out, slope_out, unit_out, inverse_out, result = rest[:5]
    w_in, w_out, normed_low, hidden, slope, sems, out_sems = rest[5:]
    in_copies, out_copies = ffn_copies(layer, ids, weights, w_in, w_out, sems)
    begin(in_copies)
    begin(out_copies)
    normed = unit_one[...] * small[layer, 3:4, :] + small[layer, 4:5, :]
    normed_low[...] = normed.astype(low)
    finish(in_copies)
    tile = w_in.shape[1] // 8
    going = []
    for t in range(8):
        columns = pl.ds(t * tile, tile)
        pre = dot(normed_low[...], w_in[:, columns]) + in_bias[layer, :, columns]
        hidden[:, columns], slope[:, columns] = gelu_and_slope(pre)
        leaving = [
            pltpu.make_async_copy(hidden.at[:, columns], hidden_out.at[:, columns], out_sems.at[2 * t]),
            pltpu.make_async_copy(slope.at[:, columns], slope_out.at[:, columns], out_sems.at[2 * t + 1]),
        ]
        begin(leaving)
        going += leaving

    finish(out_copies)
    residual = unit_one[...] * small[layer, 3:4, :] + small[layer, 4:5, :] + (dot(hidden[...], w_out[...]) + small[layer, 5:6, :])
    unit, inverse = normalize(residual)
    unit_out[...] = unit
    inverse_out[...] = inverse
    result[...] = (unit * small[layer, 6:7, :] + small[layer, 7:8, :]).astype(low)
    finish(going)


WIDE_BIT = {"y": 0, "z": 1}


def place_of(ids, owner, piece, way):
    away = None if owner is None else ids[0] ^ owner
    off = None if piece is None else piece ^ ids[5]
    place = [None if away is None else away & 1]
    for name in way:
        if name == "x":
            place.append(pl.ds(0, 2) if away is None else away >> 1)
        else:
            place.append(pl.ds(0, 2) if off is None else (off >> WIDE_BIT[name]) & 1)
    return tuple(place) + (pl.ds(0, 2) if piece is None else piece >> 2,)


def store_rows(stage, ids, product, piece, way):
    share = product.shape[0] // 4
    for owner in range(4):
        block = product[owner * share : (owner + 1) * share].astype(low)
        stage[place_of(ids, owner, piece, way) + (pl.ds(0, share),)] = block


def piece_copies(stage, ids, piece, way, kept, sent, sems, turn):
    at = place_of(ids, None, piece, way)[1:]
    copies = [
        pltpu.make_async_copy(stage.at[(1,) + at], sent.at[at], sems.at[2 * turn]),
        pltpu.make_async_copy(stage.at[(0,) + at], kept.at[at], sems.at[2 * turn + 1]),
    ]
    begin(copies)
    return copies


def out_bwd_kernel(layer, way, ids, grad, unit_two, inverse_two, hidden, small, *rest):
    d_ffn, d_resid_two, small_grads, kept, sent, stage, out_sems = rest
    g = grad[...].astype(f32)
    unit = unit_two[...]
    small_grads[0:1, :] = jnp.sum(g * unit, axis=0, keepdims=True)
    small_grads[1:2, :] = jnp.sum(g, axis=0, keepdims=True)
    d_two = normalize_back(g * small[layer, 6:7, :], unit, inverse_two[...])
    d_resid_two[...] = d_two
    d_low = d_two.astype(low)
    d_ffn[...] = d_low
    small_grads[2:3, :] = jnp.sum(d_low.astype(f32), axis=0, keepdims=True)
    small_grads[3:8, :] = jnp.zeros((5, unit.shape[1]), f32)
    tile = hidden.shape[1] // 8
    share = d_ffn.shape[1] // 4
    waits = []
    for owner in range(4):
        for half in range(2):
            columns = slice((2 * owner + half) * tile, (2 * owner + half + 1) * tile)
            out_grad = dot_tn(hidden[:, columns], d_ffn[...])
            for row_group in range(2):
                for column_group in range(2):
                    piece = (half * 2 + row_group) * 2 + column_group
                    block = out_grad[
                        row_group * share : (row_group + 1) * share,
                        column_group * tile : (column_group + 1) * tile,
                    ]
                    stage[place_of(ids, owner, piece, way)] = block.astype(low)
        core, *at = place_of(ids, owner, None, way)
        at = tuple(at)
        to_kept = pltpu.make_async_copy(stage.at[(0,) + at], kept.at[at], out_sems.at[owner])
        to_sent = pltpu.make_async_copy(stage.at[(1,) + at], sent.at[at], out_sems.at[owner])
        pl.when(core == 0)(to_kept.start)
        pl.when(core == 1)(to_sent.start)
        waits.append(to_kept)
    finish(waits)


def in_bwd_kernel(layer, way, ids, d_ffn, d_resid_two, unit_one, inverse_one, slope, small, *rest):
    weights, rest = rest[:10], rest[10:]
    d_resid, small_grads, in_bias_grad, kept, sent = rest[:5]
    w_in, w_out, d_pre, normed_t, stage, sems, out_sems = rest[5:]
    in_copies, out_copies = ffn_copies(layer, ids, weights, w_in, w_out, sems)
    begin(out_copies)
    begin(in_copies)
    normed = unit_one[...] * small[layer, 3:4, :] + small[layer, 4:5, :]
    normed_t[...] = normed.astype(low).T
    finish(out_copies)
    tile = w_in.shape[1] // 8
    going = []
    for t in range(8):
        columns = slice(t * tile, (t + 1) * tile)
        d_hidden = dot_nt(d_ffn[...], w_out[columns, :])
        d_tile = (d_hidden * slope[:, columns]).astype(low)
        d_pre[:, columns] = d_tile
        in_bias_grad[:, columns] = jnp.sum(d_tile.astype(f32), axis=0, keepdims=True)
        store_rows(stage, ids, dot(normed_t[...], d_tile), t, way)
        going += piece_copies(stage, ids, t, way, kept, sent, out_sems, t)
    finish(in_copies)
    d_normed = d_resid_two[...] + dot_nt(d_pre[...], w_in[...])
    unit = unit_one[...]
    small_grads[0:1, :] = jnp.sum(d_normed * unit, axis=0, keepdims=True)
    small_grads[1:2, :] = jnp.sum(d_normed, axis=0, keepdims=True)
    small_grads[2:8, :] = jnp.zeros((6, unit.shape[1]), f32)
    d_resid[...] = normalize_back(d_normed * small[layer, 3:4, :], unit, inverse_one[...])
    finish(going)


def attn_bwd_kernel(layer, way, ids, d_resid, x, qkv_rows, probs, context, *rest):
    weights, others, rest = rest[:7], rest[7:-13], rest[-13:]
    d_input, small_grads, kept, sent = rest[:4]
    w_qkv, w_o, d_attn, d_context, d_qkv, x_t, stage, sems, out_sems = rest[4:]
    tokens, width = x.shape
    qkv_copies, o_copies = attn_copies(layer, ids, weights, w_qkv, w_o, sems)
    begin(o_copies)
    begin(qkv_copies)
    d_low = d_resid[...].astype(low)
    d_attn[...] = d_low
    small_grads[2:3, :] = jnp.sum(d_low.astype(f32), axis=0, keepdims=True)
    x_t[...] = x[...].T
    tile = width // 2
    for half in range(2):
        product = dot_tn(context[...], d_attn[:, half * tile : (half + 1) * tile])
        store_rows(stage, ids, product, 6 + half, way)
    finish(o_copies)
    d_context[...] = dot_nt(d_attn[...], w_o[...]).astype(low)
    pair_width = 2 * width // HEADS
    first = lax.broadcasted_iota(jnp.int32, (1, pair_width), 1) < pair_width // 2
    scale = 1.0 / math.sqrt(width // HEADS)

    for pair in range(HEADS // 2):
        at_query = slice(pair * pair_width, (pair + 1) * pair_width)
        at_key = slice(width + at_query.start, width + at_query.stop)
        at_value = slice(2 * width + at_query.start, 2 * width + at_query.stop)
        query, key, value = qkv_rows[:, at_query], qkv_rows[:, at_key], qkv_rows[:, at_value]
        d_ctx = d_context[:, at_query]
        sides = []
        for side in range(2):
            mine = first if side == 0 else jnp.logical_not(first)
            prob_low = probs[2 * pair + side]
            prob = prob_low.astype(f32)
            d_prob = dot_nt(jnp.where(mine, d_ctx, jnp.zeros_like(d_ctx)), value)
            inner = jnp.sum(prob * d_prob, axis=-1, keepdims=True)
            d_scores = (prob * (d_prob - inner)).astype(low)
            sides.append((dot(d_scores, key), dot_tn(d_scores, query), dot_tn(prob_low, d_ctx)))
        d_qkv[:, at_query] = (jnp.where(first, sides[0][0], sides[1][0]) * scale).astype(low)
        d_qkv[:, at_key] = jnp.where(first, sides[0][1], sides[1][1]).astype(low)
        d_qkv[:, at_value] = jnp.where(first, sides[0][2], sides[1][2]).astype(low)

    small_grads[0:1, :] = jnp.sum(d_qkv[:, :width].astype(f32), axis=0, keepdims=True)
    small_grads[1:2, :] = jnp.sum(d_qkv[:, 2 * width :].astype(f32), axis=0, keepdims=True)
    small_grads[3:8, :] = jnp.zeros((5, width), f32)
    if others:
        share = width // 4
        sources = small_sources(layer, small_grads, others)
        for owner in range(4):
            for piece in range(8):
                lines = []
                for source, row, start, step in sources[3 * piece : 3 * piece + 3]:
                    line = source[row : row + 1, start + owner * step : start + owner * step + share]
                    lines.append(jnp.concatenate([line, jnp.zeros_like(line)], axis=1))
                lines.append(jnp.zeros((SMALL_ROWS - 3, tile), f32))
                block = jnp.concatenate(lines, axis=0).astype(low)
                stage[place_of(ids, owner, piece, way) + (pl.ds(share, SMALL_ROWS),)] = block
    going = []
    for piece in (6, 7, 0, 1, 2, 3, 4, 5):
        if piece < 6:
            store_rows(stage, ids, dot(x_t[...], d_qkv[:, piece * tile : (piece + 1) * tile]), piece, way)
        going += piece_copies(stage, ids, piece, way, kept, sent, out_sems, piece)
    finish(qkv_copies)
    d_input[...] = (d_resid[...] + dot_nt(d_qkv[...], w_qkv[...])).astype(low)
    finish(going)


SMALL_ROWS = 16
SMALL_LINES = (("attn", 0), ("attn", 1), ("attn", 2), ("in", 0), ("in", 1), ("out", 2), ("out", 0), ("out", 1))


def small_sources(layer, own, others):
    found = []
    out_0, in_0, bias_0, out_1, in_1, bias_1, attn_1 = others
    refs = ({"attn": own, "in": in_0, "out": out_0}, {"attn": attn_1, "in": in_1, "out": out_1})
    width = own.shape[1]
    for of_layer, bias in zip(refs, (bias_0, bias_1)):
        found += [(of_layer[name], row, 0, width // 4) for name, row in SMALL_LINES]
        found += [(bias, 0, i * (width // 4), width) for i in range(4)]
    return found


def unpack_kernel(layer, slab, back, earlier, ids, near, far, *rest):
    outs = rest[earlier:-4]
    buffer, wide_buffer, in_sems, out_sems = rest[-4:]
    share, tile = wide_buffer.shape[1:]

    def fetch(piece, ref, index):
        return pltpu.make_async_copy(ref.at[index], buffer.at[piece], in_sems.at[piece])

    for piece in range(8):
        off = piece ^ ids[5]
        inner, outer = [(off >> WIDE_BIT[name]) & 1 for name in back]
        pl.when(outer == 0)(fetch(piece, near, (inner, piece >> 2)).start)
        pl.when(outer == 1)(fetch(piece, far, (inner, piece >> 2)).start)

    copies = []
    for piece in range(8):
        fetch(piece, near, (0, 0)).wait()
        wide_buffer[piece] = buffer[piece, :share].astype(f32)
        columns = pl.ds(piece * tile, tile)
        if slab == "in":
            target = outs[0].at[layer, :, columns]
        elif slab == "out":
            rows = pl.ds((piece // 2) * share, share)
            target = outs[0].at[layer, rows, pl.ds((piece % 2) * tile, tile)]
        elif piece < 6:
            target = outs[0].at[layer, :, columns]
        else:
            target = outs[1].at[layer, :, pl.ds((piece - 6) * tile, tile)]
        copies.append(pltpu.make_async_copy(wide_buffer.at[piece], target, out_sems.at[piece]))
        copies[-1].start()
    if slab == "attn" and layer == 0:
        for line in range(24):
            of_layer, which = line // 12, line % 12
            row = share + line % 3
            values = buffer[line // 3, row : row + 1, :share].astype(f32)
            if which < 8:
                outs[2 + which][of_layer : of_layer + 1, :] = values
            else:
                at = (which - 8) * share
                outs[10][of_layer : of_layer + 1, at : at + share] = values
    else:
        outs[-1][...] = jnp.zeros(outs[-1].shape, f32)
    finish(copies)


SMEM = pl.BlockSpec(memory_space=pltpu.SMEM)
VMEM = pl.BlockSpec(memory_space=pltpu.VMEM)
ANY = pl.BlockSpec(memory_space=pl.ANY)


def call(kernel, name, time, in_specs, out_specs, out_shape, scratch, args, aliases=()):
    return pl.pallas_call(
        kernel,
        name=name,
        in_specs=in_specs,
        out_specs=out_specs,
        out_shape=out_shape,
        scratch_shapes=scratch,
        input_output_aliases=dict(aliases),
        compiler_params=pltpu.CompilerParams(vmem_limit_bytes=VMEM_BYTES),
        cost_estimate=pl.CostEstimate(
            flops=int(time * 1.1e9), bytes_accessed=int(time * 3.6e6), transcendentals=0
        ),
    )(*args)


def shape(dims, kind):
    return jax.ShapeDtypeStruct(dims, kind)


def added(a, b):
    return (a.astype(f32) + b.astype(f32)).astype(low)


WAYS = ("xyz", "zxy", "yxz", "xzy", "xyz", "xyz")
BACKS = ("zy", "zy", "zy", "zy", "yz", "zy")
PLAN = (
    "out1", "in1", 0, 1, "attn1", "out0", 0, 2, 1, 3, 0, 1, 0, "in0", 2, 0, 4, 1, 0, 3, "attn0", 0, 2, 1, 5,
    3, 2, 4, 1, 3, 4, 2, 5, 4, 3, 1, 2, 5, 3, 4, 5, 2, 3, 5, 4, 5, 4, 5,
)


class Order:
    def __init__(self, ids):
        self.ids = ids

    def wait(self, values):
        values, self.ids = lax.optimization_barrier((values, self.ids))
        return values


STEPS = {"x": ("narrow", 2), "y": ("wide", 1), "z": ("wide", 2)}


class Slab:
    def __init__(self, way, back, wide_count, kept, sent):
        self.kept = kept
        self.way, self.back = way, back
        self.rest = [1 << b for b in range(HALVINGS, wide_count.bit_length() - 1)]
        self.flying = swap(sent, "narrow", 1)
        self.stage = 0

    def step(self, order):
        received = order.wait(self.flying)
        stage, way = self.stage, self.way
        if stage < len(way):
            send = order.wait(added(self.kept[1], received[1]))
            self.kept = added(self.kept[0], received[0])
            self.flying = swap(send, *STEPS[way[stage]])
        elif stage < len(way) + 1 + len(self.back):
            if stage == len(way):
                piece = added(self.kept, received)
                for bit in self.rest[:-1]:
                    piece = added(piece, swap(piece, "wide", bit))
                self.kept = order.wait(piece)
                self.flying = swap(self.kept, "wide", self.rest[-1])
            else:
                if stage == len(way) + 1:
                    self.block = added(self.kept, received)[None]
                else:
                    self.block = jnp.concatenate([self.block, received], axis=0)
                self.block = order.wait(self.block)
                self.flying = swap(self.block, *STEPS[self.back[stage - len(way) - 1]])
        else:
            self.far = received
        self.stage += 1

    def ended(self):
        return self.stage == len(self.way) + len(self.back) + 2


def body(
    tables_in,
    cotangent,
    cell_ids,
    lengths,
    qkv_weight,
    q_bias,
    v_bias,
    o_weight,
    o_bias,
    norm1_gain,
    norm1_bias,
    in_weight,
    in_bias,
    out_weight,
    out_bias,
    norm2_gain,
    norm2_bias,
):
    tokens, width = tables_in.shape
    layers, share, ffn = in_weight.shape
    ffn_share = out_weight.shape[1]
    wide_count = lax.axis_size("wide")
    assert wide_count & (wide_count - 1) == 0 and wide_count > 1 << HALVINGS and lax.axis_size("narrow") == 4
    tile = ffn // 8
    me = lax.axis_index("narrow").astype(jnp.int32)
    wide_me = lax.axis_index("wide").astype(jnp.int32)
    y = wide_me & 1
    ids = jnp.stack([me, me ^ 1, me ^ 2, me ^ 3, y, wide_me & (2**HALVINGS - 1)])

    order = Order(ids)

    def half_of(weight, layer):
        rows = weight.shape[1] // 2
        return lax.dynamic_slice(weight, (layer, y * rows, 0), (1, rows, weight.shape[2]))[0]

    halves = []
    for layer in range(layers):
        joint = jnp.concatenate([half_of(qkv_weight, layer), half_of(o_weight, layer)], axis=1)
        halves += [joint, half_of(in_weight, layer), half_of(out_weight, layer)]
    near_x, far_x, diagonal = [None] * len(halves), [None] * len(halves), [None] * len(halves)
    core = [None] * 4
    own = (qkv_weight, o_weight, in_weight, out_weight)

    def group(i):
        return near_x[i], far_x[i], diagonal[i]

    def attn_weights(layer):
        return (qkv_weight, core[0], o_weight, core[1]) + group(3 * layer)

    def ffn_weights(layer):
        return (in_weight, core[2]) + group(3 * layer + 1) + (out_weight, core[3]) + group(3 * layer + 2)

    def in_order(low_one, high_one, bit):
        swapped = (me & bit) != 0
        return jnp.stack([jnp.where(swapped, high_one, low_one), jnp.where(swapped, low_one, high_one)])

    def send_x(*which):
        for i in which:
            near_x[i] = swap(order.wait(halves[i]), "narrow", 2)

    def send_core(i):
        core[i] = swap(order.wait(own[i]), "narrow", 1)

    def arrive(*events):
        for kind, i in events:
            if kind == "x":
                near_x[i] = order.wait(near_x[i])
                far_x[i] = swap(near_x[i], "wide", 1)
            elif kind == "y":
                far_x[i] = order.wait(far_x[i])
                diagonal[i] = swap(order.wait(jnp.concatenate([near_x[i], far_x[i]], axis=0)), "narrow", 1)
            elif kind == "d":
                diagonal[i] = order.wait(diagonal[i])
            else:
                core[i] = order.wait(core[i])

    send_x(0)
    short = order.wait((q_bias, v_bias, o_bias, norm1_gain, norm1_bias, out_bias, norm2_gain, norm2_bias))
    packed = call(
        pack_kernel, "pack", 1, [VMEM] * 9, VMEM, shape((layers, 12, share), f32), [], tuple(short) + (in_bias,)
    )
    packed = order.wait(packed)
    others = [lax.ppermute(packed, "narrow", [(i, i ^ away) for i in range(4)]) for away in (1, 2, 3)]
    send_x(1)
    halves[2:] = order.wait(halves[2:])
    others[0] = order.wait(others[0])
    send_core(0)
    arrive(("x", 0))
    others[1:] = order.wait(others[1:])
    send_x(2)
    send_core(1)
    packed = in_order(in_order(packed, others[0], 1), in_order(others[1], others[2], 1), 2)
    packed = packed.reshape(4, layers, 12, share)
    small = packed[:, :, :8].transpose(1, 2, 0, 3).reshape(layers, 8, width)
    full_in_bias = packed[:, :, 8:].transpose(1, 0, 2, 3).reshape(layers, 1, ffn)
    small, full_in_bias = order.wait((small, full_in_bias))
    arrive(("c", 0), ("x", 1))
    send_x(3)
    arrive(("c", 1))
    send_core(2)
    arrive(("y", 0), ("c", 2))
    send_core(3)
    arrive(("d", 0))

    w_qkv = pltpu.VMEM((width, 3 * width), low)
    w_o = pltpu.VMEM((width, width), low)
    w_in = pltpu.VMEM((width, ffn), low)
    w_out = pltpu.VMEM((ffn, width), low)
    copy_sems = pltpu.SemaphoreType.DMA((12,))
    piece_sems = pltpu.SemaphoreType.DMA((16,))
    rows_f32 = shape((tokens, width), f32)
    rows_low = shape((tokens, width), low)
    column_f32 = shape((tokens, 1), f32)
    eight_f32 = shape((8, width), f32)

    def pieces(rows):
        return [shape((2, 2, 2, 2, rows, tile), low)] * 2

    def stage(rows):
        return pltpu.VMEM((2, 2, 2, 2, 2, rows, tile), low)

    def tie(outs, which):
        outs = list(outs)
        outs[which] = order.wait(outs[which])
        return outs

    def attn_forward(layer, x):
        x = order.wait(x)
        outs = call(
            functools.partial(attn_fwd_kernel, layer),
            "attn_fwd",
            13,
            [SMEM, SMEM] + [VMEM] * 3 + [ANY] * 7,
            [VMEM] * 5,
            [shape((tokens, 3 * width), low), shape((HEADS, tokens, tokens), low), rows_low, rows_f32, column_f32],
            [w_qkv, w_o, pltpu.VMEM((tokens, tokens), f32), copy_sems],
            (order.ids, lengths, x, cell_ids, small) + attn_weights(layer),
        )
        return tie(outs, 3)

    def ffn_forward(layer, unit_one):
        unit_one = order.wait(unit_one)
        outs = call(
            functools.partial(ffn_fwd_kernel, layer),
            "ffn_fwd",
            10,
            [SMEM] + [VMEM] * 3 + [ANY] * 10,
            [ANY] * 2 + [VMEM] * 3,
            [shape((tokens, ffn), low), shape((tokens, ffn), f32), rows_f32, column_f32, rows_low],
            [
                w_in,
                w_out,
                pltpu.VMEM((tokens, width), low),
                pltpu.VMEM((tokens, ffn), low),
                pltpu.VMEM((tokens, ffn), f32),
                copy_sems,
                piece_sems,
            ],
            (order.ids, unit_one, full_in_bias, small) + ffn_weights(layer),
        )
        return tie(outs, 4)

    def out_backward(layer, way, grad, unit_two, inverse_two, hidden):
        grad = order.wait(grad)
        outs = call(
            functools.partial(out_bwd_kernel, layer, way),
            "out_bwd",
            8,
            [SMEM] + [VMEM] * 5,
            [VMEM] * 3 + [ANY] * 2,
            [rows_low, rows_f32, eight_f32] + pieces(share),
            [stage(share), pltpu.SemaphoreType.DMA((4,))],
            (order.ids, grad, unit_two, inverse_two, hidden, small),
        )
        return tie(outs, 0)

    def in_backward(layer, way, d_ffn, d_resid_two, unit_one, inverse_one, slope):
        d_ffn = order.wait(d_ffn)
        outs = call(
            functools.partial(in_bwd_kernel, layer, way),
            "in_bwd",
            14,
            [SMEM] + [VMEM] * 6 + [ANY] * 10,
            [VMEM] * 3 + [ANY] * 2,
            [rows_f32, eight_f32, shape((1, ffn), f32)] + pieces(share),
            [
                w_in,
                w_out,
                pltpu.VMEM((tokens, ffn), low),
                pltpu.VMEM((width, tokens), low),
                stage(share),
                copy_sems,
                piece_sems,
            ],
            (order.ids, d_ffn, d_resid_two, unit_one, inverse_one, slope, small) + ffn_weights(layer),
        )
        return tie(outs, 0)

    def attn_backward(layer, way, d_resid, x, qkv_rows, probs, context, small_others):
        d_resid = order.wait(d_resid)
        rows = share + (SMALL_ROWS if small_others else 0)
        outs = call(
            functools.partial(attn_bwd_kernel, layer, way),
            "attn_bwd",
            16,
            [SMEM] + [VMEM] * 5 + [ANY] * 7 + [VMEM] * len(small_others),
            [VMEM] * 2 + [ANY] * 2,
            [rows_low, eight_f32] + pieces(rows),
            [
                w_qkv,
                w_o,
                pltpu.VMEM((tokens, width), low),
                pltpu.VMEM((tokens, width), low),
                pltpu.VMEM((tokens, 3 * width), low),
                pltpu.VMEM((width, tokens), low),
                stage(rows),
                copy_sems,
                piece_sems,
            ],
            (order.ids, d_resid, x, qkv_rows, probs, context) + attn_weights(layer) + tuple(small_others),
        )
        return tie(outs, 0)

    def unpack(layer, name, slab, earlier):
        dims = {
            "attn": [(layers, share, 3 * width), (layers, share, width)],
            "in": [(layers, share, ffn)],
            "out": [(layers, ffn_share, width)],
        }[name]
        last = name == "attn" and layer == 0
        extra = [(layers, share)] * 8 + [(layers, ffn_share)] if last else [(8, 128)]
        near, far = order.wait((slab.block, slab.far))
        rows = near.shape[2]
        outs = call(
            functools.partial(unpack_kernel, layer, name, slab.back, len(earlier)),
            "unpack",
            4,
            [SMEM] + [ANY] * (2 + len(earlier)),
            [ANY] * len(dims) + [VMEM] * len(extra),
            [shape(d, f32) for d in dims + extra],
            [
                pltpu.VMEM((8, rows, tile), low),
                pltpu.VMEM((8, share, tile), f32),
                pltpu.SemaphoreType.DMA((8,)),
                pltpu.SemaphoreType.DMA((8,)),
            ],
            (order.ids, near, far, *earlier),
            {3 + i: i for i in range(len(earlier))},
        )
        return tuple(tie(outs, 0))

    first_attn = attn_forward(0, tables_in)
    arrive(("x", 2))
    send_x(4)
    arrive(("y", 1), ("c", 3), ("d", 1), ("x", 3))
    send_x(5)
    arrive(("y", 2), ("d", 2))
    first_ffn = ffn_forward(0, first_attn[3])
    arrive(("x", 4), ("y", 3), ("d", 3))
    second_attn = attn_forward(1, first_ffn[4])
    arrive(("x", 5), ("y", 4), ("y", 5), ("d", 4), ("d", 5))
    second_ffn = ffn_forward(1, second_attn[3])
    mixed_out = second_ffn[4]
    inputs = (tables_in, first_ffn[4])
    attn_kept, ffn_kept = (first_attn, second_attn), (first_ffn, second_ffn)

    slabs = [None] * 6
    grad = cotangent
    small_out, small_in, small_attn, bias_grads = [None] * 2, [None] * 2, [None] * 2, [None] * 2
    unpacked = {"attn": (), "in": (), "out": ()}
    for action in PLAN:
        if isinstance(action, int):
            slab = slabs[action]
            slab.step(order)
            if slab.ended():
                name = ("out", "in", "attn")[action % 3]
                unpacked[name] = unpack(layers - 1 - action // 3, name, slab, unpacked[name][: 2 if name == "attn" else 1])
            continue
        name, layer = action[:-1], int(action[-1])
        which = 3 * (layers - 1 - layer) + ("out", "in", "attn").index(name)
        way = WAYS[which]
        qkv_rows, probs, context, unit_one, inverse_one = attn_kept[layer]
        hidden, slope, unit_two, inverse_two, _ = ffn_kept[layer]
        if name == "out":
            d_ffn, d_resid_two, small_out[layer], kept, sent = out_backward(
                layer, way, grad, unit_two, inverse_two, hidden
            )
        elif name == "in":
            d_resid, small_in[layer], bias_grads[layer], kept, sent = in_backward(
                layer, way, d_ffn, d_resid_two, unit_one, inverse_one, slope
            )
        else:
            small_others = ()
            if layer == 0:
                small_others = (
                    small_out[0],
                    small_in[0],
                    bias_grads[0],
                    small_out[1],
                    small_in[1],
                    bias_grads[1],
                    small_attn[1],
                )
            grad, small_attn[layer], kept, sent = attn_backward(
                layer, way, d_resid, inputs[layer], qkv_rows, probs, context, small_others
            )
        slabs[which] = Slab(way, BACKS[which], wide_count, kept, sent)
    qkv_grad, o_grad, *vectors = unpacked["attn"]
    in_grad, out_grad = unpacked["in"][0], unpacked["out"][0]
    return (
        mixed_out,
        grad,
        qkv_grad,
        vectors[0],
        vectors[1],
        o_grad,
        vectors[2],
        vectors[3],
        vectors[4],
        in_grad,
        vectors[8],
        out_grad,
        vectors[5],
        vectors[6],
        vectors[7],
    )


def solution(mesh):
    by_table = P(("wide", "narrow"), None)
    matrix = P(None, "narrow", None)
    vector = P(None, "narrow")
    return jax.shard_map(
        body,
        mesh=mesh,
        in_specs=(
            by_table,
            by_table,
            by_table,
            P(("wide", "narrow")),
            matrix,
            vector,
            vector,
            matrix,
            vector,
            vector,
            vector,
            matrix,
            vector,
            matrix,
            vector,
            vector,
            vector,
        ),
        out_specs=(
            by_table,
            by_table,
            matrix,
            vector,
            vector,
            matrix,
            vector,
            vector,
            vector,
            matrix,
            vector,
            matrix,
            vector,
            vector,
            vector,
        ),
        check_vma=False,
    )
```

```python
import functools
import math

import jax
import jax.numpy as jnp
from jax import lax
from jax.experimental import pallas as pl
from jax.experimental.pallas import tpu as pltpu
from jax.sharding import PartitionSpec as P

HEADS = 12
norm_eps = 1e-12
masked_score = -1000000000.0
low = jnp.bfloat16
f32 = jnp.float32
VMEM_BYTES = 56 * 1024 * 1024
HALVINGS = 2


def swap(value, axis, bit):
    count = lax.axis_size(axis)
    return lax.ppermute(value, axis, [(i, i ^ bit) for i in range(count)])


def dot(a, b):
    return jnp.dot(a, b, preferred_element_type=f32)


def dot_nt(a, b):
    return lax.dot_general(a, b, (((1,), (1,)), ((), ())), preferred_element_type=f32)


def dot_tn(a, b):
    return lax.dot_general(a, b, (((0,), (0,)), ((), ())), preferred_element_type=f32)


def normalize(residual):
    center = residual - jnp.mean(residual, axis=-1, keepdims=True)
    inverse = lax.rsqrt(jnp.mean(center * center, axis=-1, keepdims=True) + norm_eps)
    return center * inverse, inverse


def normalize_back(grad_unit, unit, inverse):
    centered = grad_unit - jnp.mean(grad_unit, axis=-1, keepdims=True)
    return inverse * (centered - unit * jnp.mean(grad_unit * unit, axis=-1, keepdims=True))


def weight_copies(ids, layer, pieces, target, columns, sems, base):
    own, core, near_x, far_x, diagonal = pieces
    rows = own.shape[1]
    half = rows // 2
    n, y = ids[0], ids[4]
    copies = []

    def add(source, start, count):
        where = target.at[pl.ds(pl.multiple_of(start, half), count), :]
        copies.append(pltpu.make_async_copy(source, where, sems.at[base + len(copies)]))

    at = pl.ds(columns, target.shape[1])
    add(own.at[layer], n * rows, rows)
    add(core.at[layer], ids[1] * rows, rows)
    add(near_x.at[:, at], ids[2] * rows + y * half, half)
    add(far_x.at[:, at], ids[2] * rows + (1 - y) * half, half)
    add(diagonal.at[pl.ds(0, half), at], ids[3] * rows + y * half, half)
    add(diagonal.at[pl.ds(half, half), at], ids[3] * rows + (1 - y) * half, half)
    return copies


def begin(copies):
    for copy in copies:
        copy.start()


def finish(copies):
    for copy in copies:
        copy.wait()


def attn_copies(layer, ids, refs, w_qkv, w_o, sems):
    qkv_own, qkv_core, o_own, o_core = refs[:4]
    halves = refs[4:]
    qkv = weight_copies(ids, layer, (qkv_own, qkv_core) + halves, w_qkv, 0, sems, 0)
    o = weight_copies(ids, layer, (o_own, o_core) + halves, w_o, w_qkv.shape[1], sems, 6)
    return qkv, o


def ffn_copies(layer, ids, refs, w_in, w_out, sems):
    in_copies = weight_copies(ids, layer, refs[:5], w_in, 0, sems, 0)
    out_copies = weight_copies(ids, layer, refs[5:], w_out, 0, sems, 6)
    return in_copies, out_copies


def pack_kernel(*refs):
    shorts, in_bias, packed = refs[:8], refs[8], refs[9]
    layers, share = shorts[0].shape
    for layer in range(layers):
        for i, short in enumerate(shorts):
            packed[layer, i : i + 1, :] = short[layer : layer + 1, :].astype(f32)
        for i in range(4):
            packed[layer, 8 + i : 9 + i, :] = in_bias[layer : layer + 1, i * share : (i + 1) * share].astype(f32)


def attn_fwd_kernel(layer, ids, length, x, cell_row, small, *rest):
    weights, rest = rest[:7], rest[7:]
    qkv_rows, probs, context, unit_out, inverse_out, w_qkv, w_o, mask, sems = rest
    tokens, width = x.shape
    qkv_copies, o_copies = attn_copies(layer, ids, weights, w_qkv, w_o, sems)
    begin(qkv_copies)
    begin(o_copies)
    position = lax.broadcasted_iota(jnp.int32, (1, tokens), 1)
    key_cell = cell_row[...]
    square = (tokens, tokens)
    diagonal = lax.broadcasted_iota(jnp.int32, square, 0) == lax.broadcasted_iota(jnp.int32, square, 1)
    query_cell = jnp.sum(jnp.where(diagonal, key_cell, 0), axis=1, keepdims=True)
    allowed = (query_cell == key_cell) | (key_cell == 0) | (query_cell == 0)
    allowed = allowed & (position < length[0])
    mask[...] = jnp.where(allowed, 0.0, masked_score)
    scale = 1.0 / math.sqrt(width // HEADS)
    finish(qkv_copies)
    tile = width // 2

    for t in range(6):
        columns = slice(t * tile, (t + 1) * tile)
        rows = dot(x[...], w_qkv[:, columns])
        if t // 2 != 1:
            part = slice((t % 2) * tile, (t % 2 + 1) * tile)
            rows = rows + small[layer, t // 4 : t // 4 + 1, part]
        if t < 2:
            rows = rows * scale
        qkv_rows[:, columns] = rows.astype(low)

    pair_width = 2 * width // HEADS
    first = lax.broadcasted_iota(jnp.int32, (1, pair_width), 1) < pair_width // 2

    for pair in range(HEADS // 2):
        at = slice(pair * pair_width, (pair + 1) * pair_width)
        query = qkv_rows[:, at]
        key = qkv_rows[:, width + at.start : width + at.stop]
        value = qkv_rows[:, 2 * width + at.start : 2 * width + at.stop]
        sides = []
        for side in range(2):
            mine = first if side == 0 else jnp.logical_not(first)
            scores = dot_nt(jnp.where(mine, query, jnp.zeros_like(query)), key) + mask[...]
            shifted = jnp.exp(scores - jnp.max(scores, axis=-1, keepdims=True))
            total = jnp.sum(shifted, axis=-1, keepdims=True)
            prob = (shifted * (1.0 / total)).astype(low)
            probs[2 * pair + side] = prob
            sides.append(dot(prob, value))
        context[:, at] = jnp.where(first, sides[0], sides[1]).astype(low)

    finish(o_copies)
    residual = x[...].astype(f32) + (dot(context[...], w_o[...]) + small[layer, 2:3, :])
    unit, inverse = normalize(residual)
    unit_out[...] = unit
    inverse_out[...] = inverse


def gelu_and_slope(x):
    t = 1.0 / (1.0 + (0.3275911 * math.sqrt(0.5)) * jnp.abs(x))
    bell = jnp.exp(-0.5 * x * x)
    series = 1.421413741 + t * (-1.453152027 + t * 1.061405429)
    series = t * (0.254829592 + t * (-0.284496736 + t * series))
    tail = 0.5 * series * bell
    cdf = jnp.where(x >= 0.0, 1.0 - tail, tail)
    return (x * cdf).astype(low), cdf + x * (bell * (1.0 / math.sqrt(2.0 * math.pi)))


def ffn_fwd_kernel(layer, ids, unit_one, in_bias, small, *rest):
    weights, rest = rest[:10], rest[10:]
    hidden_out, slope_out, unit_out, inverse_out, result = rest[:5]
    w_in, w_out, normed_low, hidden, slope, sems, out_sems = rest[5:]
    in_copies, out_copies = ffn_copies(layer, ids, weights, w_in, w_out, sems)
    begin(in_copies)
    begin(out_copies)
    normed = unit_one[...] * small[layer, 3:4, :] + small[layer, 4:5, :]
    normed_low[...] = normed.astype(low)
    finish(in_copies)
    tile = w_in.shape[1] // 8
    going = []
    for t in range(8):
        columns = pl.ds(t * tile, tile)
        pre = dot(normed_low[...], w_in[:, columns]) + in_bias[layer, :, columns]
        hidden[:, columns], slope[:, columns] = gelu_and_slope(pre)
        leaving = [
            pltpu.make_async_copy(hidden.at[:, columns], hidden_out.at[:, columns], out_sems.at[2 * t]),
            pltpu.make_async_copy(slope.at[:, columns], slope_out.at[:, columns], out_sems.at[2 * t + 1]),
        ]
        begin(leaving)
        going += leaving

    finish(out_copies)
    residual = unit_one[...] * small[layer, 3:4, :] + small[layer, 4:5, :] + (dot(hidden[...], w_out[...]) + small[layer, 5:6, :])
    unit, inverse = normalize(residual)
    unit_out[...] = unit
    inverse_out[...] = inverse
    result[...] = (unit * small[layer, 6:7, :] + small[layer, 7:8, :]).astype(low)
    finish(going)


WIDE_BIT = {"y": 0, "z": 1}


def place_of(ids, owner, piece, way):
    away = None if owner is None else ids[0] ^ owner
    off = None if piece is None else piece ^ ids[5]
    place = [None if away is None else away & 1]
    for name in way:
        if name == "x":
            place.append(pl.ds(0, 2) if away is None else away >> 1)
        else:
            place.append(pl.ds(0, 2) if off is None else (off >> WIDE_BIT[name]) & 1)
    return tuple(place) + (pl.ds(0, 2) if piece is None else piece >> 2,)


def store_rows(stage, ids, product, piece, way):
    share = product.shape[0] // 4
    for owner in range(4):
        block = product[owner * share : (owner + 1) * share].astype(low)
        stage[place_of(ids, owner, piece, way) + (pl.ds(0, share),)] = block


def piece_copies(stage, ids, piece, way, kept, sent, sems, turn):
    at = place_of(ids, None, piece, way)[1:]
    copies = [
        pltpu.make_async_copy(stage.at[(1,) + at], sent.at[at], sems.at[2 * turn]),
        pltpu.make_async_copy(stage.at[(0,) + at], kept.at[at], sems.at[2 * turn + 1]),
    ]
    begin(copies)
    return copies


def out_bwd_kernel(layer, way, ids, grad, unit_two, inverse_two, hidden, small, *rest):
    d_ffn, d_resid_two, small_grads, kept, sent, stage, out_sems = rest
    g = grad[...].astype(f32)
    unit = unit_two[...]
    small_grads[0:1, :] = jnp.sum(g * unit, axis=0, keepdims=True)
    small_grads[1:2, :] = jnp.sum(g, axis=0, keepdims=True)
    d_two = normalize_back(g * small[layer, 6:7, :], unit, inverse_two[...])
    d_resid_two[...] = d_two
    d_low = d_two.astype(low)
    d_ffn[...] = d_low
    small_grads[2:3, :] = jnp.sum(d_low.astype(f32), axis=0, keepdims=True)
    small_grads[3:8, :] = jnp.zeros((5, unit.shape[1]), f32)
    tile = hidden.shape[1] // 8
    share = d_ffn.shape[1] // 4
    waits = []
    for owner in range(4):
        for half in range(2):
            columns = slice((2 * owner + half) * tile, (2 * owner + half + 1) * tile)
            out_grad = dot_tn(hidden[:, columns], d_ffn[...])
            for row_group in range(2):
                for column_group in range(2):
                    piece = (half * 2 + row_group) * 2 + column_group
                    block = out_grad[
                        row_group * share : (row_group + 1) * share,
                        column_group * tile : (column_group + 1) * tile,
                    ]
                    stage[place_of(ids, owner, piece, way)] = block.astype(low)
        core, *at = place_of(ids, owner, None, way)
        at = tuple(at)
        to_kept = pltpu.make_async_copy(stage.at[(0,) + at], kept.at[at], out_sems.at[owner])
        to_sent = pltpu.make_async_copy(stage.at[(1,) + at], sent.at[at], out_sems.at[owner])
        pl.when(core == 0)(to_kept.start)
        pl.when(core == 1)(to_sent.start)
        waits.append(to_kept)
    finish(waits)


def in_bwd_kernel(layer, way, ids, d_ffn, d_resid_two, unit_one, inverse_one, slope, small, *rest):
    weights, rest = rest[:10], rest[10:]
    d_resid, small_grads, in_bias_grad, kept, sent = rest[:5]
    w_in, w_out, d_pre, normed_t, stage, sems, out_sems = rest[5:]
    in_copies, out_copies = ffn_copies(layer, ids, weights, w_in, w_out, sems)
    begin(out_copies)
    begin(in_copies)
    normed = unit_one[...] * small[layer, 3:4, :] + small[layer, 4:5, :]
    normed_t[...] = normed.astype(low).T
    finish(out_copies)
    tile = w_in.shape[1] // 8
    going = []
    for t in range(8):
        columns = slice(t * tile, (t + 1) * tile)
        d_hidden = dot_nt(d_ffn[...], w_out[columns, :])
        d_tile = (d_hidden * slope[:, columns]).astype(low)
        d_pre[:, columns] = d_tile
        in_bias_grad[:, columns] = jnp.sum(d_tile.astype(f32), axis=0, keepdims=True)
        store_rows(stage, ids, dot(normed_t[...], d_tile), t, way)
        going += piece_copies(stage, ids, t, way, kept, sent, out_sems, t)
    finish(in_copies)
    d_normed = d_resid_two[...] + dot_nt(d_pre[...], w_in[...])
    unit = unit_one[...]
    small_grads[0:1, :] = jnp.sum(d_normed * unit, axis=0, keepdims=True)
    small_grads[1:2, :] = jnp.sum(d_normed, axis=0, keepdims=True)
    small_grads[2:8, :] = jnp.zeros((6, unit.shape[1]), f32)
    d_resid[...] = normalize_back(d_normed * small[layer, 3:4, :], unit, inverse_one[...])
    finish(going)


def attn_bwd_kernel(layer, way, ids, d_resid, x, qkv_rows, probs, context, *rest):
    weights, others, rest = rest[:7], rest[7:-13], rest[-13:]
    d_input, small_grads, kept, sent = rest[:4]
    w_qkv, w_o, d_attn, d_context, d_qkv, x_t, stage, sems, out_sems = rest[4:]
    tokens, width = x.shape
    qkv_copies, o_copies = attn_copies(layer, ids, weights, w_qkv, w_o, sems)
    begin(o_copies)
    begin(qkv_copies)
    d_low = d_resid[...].astype(low)
    d_attn[...] = d_low
    small_grads[2:3, :] = jnp.sum(d_low.astype(f32), axis=0, keepdims=True)
    x_t[...] = x[...].T
    tile = width // 2
    for half in range(2):
        product = dot_tn(context[...], d_attn[:, half * tile : (half + 1) * tile])
        store_rows(stage, ids, product, 6 + half, way)
    finish(o_copies)
    d_context[...] = dot_nt(d_attn[...], w_o[...]).astype(low)
    pair_width = 2 * width // HEADS
    first = lax.broadcasted_iota(jnp.int32, (1, pair_width), 1) < pair_width // 2
    scale = 1.0 / math.sqrt(width // HEADS)

    for pair in range(HEADS // 2):
        at_query = slice(pair * pair_width, (pair + 1) * pair_width)
        at_key = slice(width + at_query.start, width + at_query.stop)
        at_value = slice(2 * width + at_query.start, 2 * width + at_query.stop)
        query, key, value = qkv_rows[:, at_query], qkv_rows[:, at_key], qkv_rows[:, at_value]
        d_ctx = d_context[:, at_query]
        sides = []
        for side in range(2):
            mine = first if side == 0 else jnp.logical_not(first)
            prob_low = probs[2 * pair + side]
            prob = prob_low.astype(f32)
            d_prob = dot_nt(jnp.where(mine, d_ctx, jnp.zeros_like(d_ctx)), value)
            inner = jnp.sum(prob * d_prob, axis=-1, keepdims=True)
            d_scores = (prob * (d_prob - inner)).astype(low)
            sides.append((dot(d_scores, key), dot_tn(d_scores, query), dot_tn(prob_low, d_ctx)))
        d_qkv[:, at_query] = (jnp.where(first, sides[0][0], sides[1][0]) * scale).astype(low)
        d_qkv[:, at_key] = jnp.where(first, sides[0][1], sides[1][1]).astype(low)
        d_qkv[:, at_value] = jnp.where(first, sides[0][2], sides[1][2]).astype(low)

    small_grads[0:1, :] = jnp.sum(d_qkv[:, :width].astype(f32), axis=0, keepdims=True)
    small_grads[1:2, :] = jnp.sum(d_qkv[:, 2 * width :].astype(f32), axis=0, keepdims=True)
    small_grads[3:8, :] = jnp.zeros((5, width), f32)
    if others:
        share = width // 4
        sources = small_sources(layer, small_grads, others)
        for owner in range(4):
            for piece in range(8):
                lines = []
                for source, row, start, step in sources[3 * piece : 3 * piece + 3]:
                    line = source[row : row + 1, start + owner * step : start + owner * step + share]
                    lines.append(jnp.concatenate([line, jnp.zeros_like(line)], axis=1))
                lines.append(jnp.zeros((SMALL_ROWS - 3, tile), f32))
                block = jnp.concatenate(lines, axis=0).astype(low)
                stage[place_of(ids, owner, piece, way) + (pl.ds(share, SMALL_ROWS),)] = block
    going = []
    for piece in (6, 7, 0, 1, 2, 3, 4, 5):
        if piece < 6:
            store_rows(stage, ids, dot(x_t[...], d_qkv[:, piece * tile : (piece + 1) * tile]), piece, way)
        going += piece_copies(stage, ids, piece, way, kept, sent, out_sems, piece)
    finish(qkv_copies)
    d_input[...] = (d_resid[...] + dot_nt(d_qkv[...], w_qkv[...])).astype(low)
    finish(going)


SMALL_ROWS = 16
SMALL_LINES = (("attn", 0), ("attn", 1), ("attn", 2), ("in", 0), ("in", 1), ("out", 2), ("out", 0), ("out", 1))


def small_sources(layer, own, others):
    found = []
    out_0, in_0, bias_0, out_1, in_1, bias_1, attn_1 = others
    refs = ({"attn": own, "in": in_0, "out": out_0}, {"attn": attn_1, "in": in_1, "out": out_1})
    width = own.shape[1]
    for of_layer, bias in zip(refs, (bias_0, bias_1)):
        found += [(of_layer[name], row, 0, width // 4) for name, row in SMALL_LINES]
        found += [(bias, 0, i * (width // 4), width) for i in range(4)]
    return found


def unpack_kernel(layer, slab, back, earlier, ids, near, far, *rest):
    outs = rest[earlier:-4]
    buffer, wide_buffer, in_sems, out_sems = rest[-4:]
    share, tile = wide_buffer.shape[1:]

    def fetch(piece, ref, index):
        return pltpu.make_async_copy(ref.at[index], buffer.at[piece], in_sems.at[piece])

    for piece in range(8):
        off = piece ^ ids[5]
        inner, outer = [(off >> WIDE_BIT[name]) & 1 for name in back]
        pl.when(outer == 0)(fetch(piece, near, (inner, piece >> 2)).start)
        pl.when(outer == 1)(fetch(piece, far, (inner, piece >> 2)).start)

    copies = []
    for piece in range(8):
        fetch(piece, near, (0, 0)).wait()
        wide_buffer[piece] = buffer[piece, :share].astype(f32)
        columns = pl.ds(piece * tile, tile)
        if slab == "in":
            target = outs[0].at[layer, :, columns]
        elif slab == "out":
            rows = pl.ds((piece // 2) * share, share)
            target = outs[0].at[layer, rows, pl.ds((piece % 2) * tile, tile)]
        elif piece < 6:
            target = outs[0].at[layer, :, columns]
        else:
            target = outs[1].at[layer, :, pl.ds((piece - 6) * tile, tile)]
        copies.append(pltpu.make_async_copy(wide_buffer.at[piece], target, out_sems.at[piece]))
        copies[-1].start()
    if slab == "attn" and layer == 0:
        for line in range(24):
            of_layer, which = line // 12, line % 12
            row = share + line % 3
            values = buffer[line // 3, row : row + 1, :share].astype(f32)
            if which < 8:
                outs[2 + which][of_layer : of_layer + 1, :] = values
            else:
                at = (which - 8) * share
                outs[10][of_layer : of_layer + 1, at : at + share] = values
    else:
        outs[-1][...] = jnp.zeros(outs[-1].shape, f32)
    finish(copies)


SMEM = pl.BlockSpec(memory_space=pltpu.SMEM)
VMEM = pl.BlockSpec(memory_space=pltpu.VMEM)
ANY = pl.BlockSpec(memory_space=pl.ANY)


def call(kernel, name, time, in_specs, out_specs, out_shape, scratch, args, aliases=()):
    return pl.pallas_call(
        kernel,
        name=name,
        in_specs=in_specs,
        out_specs=out_specs,
        out_shape=out_shape,
        scratch_shapes=scratch,
        input_output_aliases=dict(aliases),
        compiler_params=pltpu.CompilerParams(vmem_limit_bytes=VMEM_BYTES),
        cost_estimate=pl.CostEstimate(
            flops=int(time * 1.1e9), bytes_accessed=int(time * 3.6e6), transcendentals=0
        ),
    )(*args)


def shape(dims, kind):
    return jax.ShapeDtypeStruct(dims, kind)


def added(a, b):
    return (a.astype(f32) + b.astype(f32)).astype(low)


WAYS = ("zxy", "xyz", "yxz", "zyx", "xyz", "xyz")
BACKS = ("zy", "zy", "zy", "yz", "zy", "zy")
PLAN = (
    "out1", "in1", 0, 1, "attn1", "out0", "in0", 0, 1, "attn0", 1, 0, 2, 4, 3, 1, 2, 4, 1, 0, 5, 3, 2, 0, 4,
    1, 2, 0, 3, 2, 4, 5, 3, 0, 5, 4, 2, 3, 5, 1, 3, 5, 4, 2, 5, 4, 3, 5,
)
TIMES = {"out1": 20, "in1": 20, "attn1": 0.3, "out0": 2, "in0": 1, "attn0": 8}


class Order:
    def __init__(self, ids):
        self.ids = ids

    def wait(self, values):
        values, self.ids = lax.optimization_barrier((values, self.ids))
        return values


STEPS = {"x": ("narrow", 2), "y": ("wide", 1), "z": ("wide", 2)}


class Slab:
    def __init__(self, way, back, wide_count, kept, sent):
        self.kept = kept
        self.way, self.back = way, back
        self.rest = [1 << b for b in range(HALVINGS, wide_count.bit_length() - 1)]
        self.flying = swap(sent, "narrow", 1)
        self.stage = 0

    def step(self, order):
        received = order.wait(self.flying)
        stage, way = self.stage, self.way
        if stage < len(way):
            send = order.wait(added(self.kept[1], received[1]))
            self.kept = added(self.kept[0], received[0])
            self.flying = swap(send, *STEPS[way[stage]])
        elif stage < len(way) + 1 + len(self.back):
            if stage == len(way):
                piece = added(self.kept, received)
                for bit in self.rest[:-1]:
                    piece = added(piece, swap(piece, "wide", bit))
                self.kept = order.wait(piece)
                self.flying = swap(self.kept, "wide", self.rest[-1])
            else:
                if stage == len(way) + 1:
                    self.block = added(self.kept, received)[None]
                else:
                    self.block = jnp.concatenate([self.block, received], axis=0)
                self.block = order.wait(self.block)
                self.flying = swap(self.block, *STEPS[self.back[stage - len(way) - 1]])
        else:
            self.far = received
        self.stage += 1

    def ended(self):
        return self.stage == len(self.way) + len(self.back) + 2


def body(
    tables_in,
    cotangent,
    cell_ids,
    lengths,
    qkv_weight,
    q_bias,
    v_bias,
    o_weight,
    o_bias,
    norm1_gain,
    norm1_bias,
    in_weight,
    in_bias,
    out_weight,
    out_bias,
    norm2_gain,
    norm2_bias,
):
    tokens, width = tables_in.shape
    layers, share, ffn = in_weight.shape
    ffn_share = out_weight.shape[1]
    wide_count = lax.axis_size("wide")
    assert wide_count & (wide_count - 1) == 0 and wide_count > 1 << HALVINGS and lax.axis_size("narrow") == 4
    tile = ffn // 8
    me = lax.axis_index("narrow").astype(jnp.int32)
    wide_me = lax.axis_index("wide").astype(jnp.int32)
    y = wide_me & 1
    ids = jnp.stack([me, me ^ 1, me ^ 2, me ^ 3, y, wide_me & (2**HALVINGS - 1)])

    order = Order(ids)

    def half_of(weight, layer):
        rows = weight.shape[1] // 2
        return lax.dynamic_slice(weight, (layer, y * rows, 0), (1, rows, weight.shape[2]))[0]

    halves = []
    for layer in range(layers):
        joint = jnp.concatenate([half_of(qkv_weight, layer), half_of(o_weight, layer)], axis=1)
        halves += [joint, half_of(in_weight, layer), half_of(out_weight, layer)]
    near_x, far_x, diagonal = [None] * len(halves), [None] * len(halves), [None] * len(halves)
    core = [None] * 4
    own = (qkv_weight, o_weight, in_weight, out_weight)

    def group(i):
        return near_x[i], far_x[i], diagonal[i]

    def attn_weights(layer):
        return (qkv_weight, core[0], o_weight, core[1]) + group(3 * layer)

    def ffn_weights(layer):
        return (in_weight, core[2]) + group(3 * layer + 1) + (out_weight, core[3]) + group(3 * layer + 2)

    def in_order(low_one, high_one, bit):
        swapped = (me & bit) != 0
        return jnp.stack([jnp.where(swapped, high_one, low_one), jnp.where(swapped, low_one, high_one)])

    def send_x(*which):
        for i in which:
            near_x[i] = swap(order.wait(halves[i]), "narrow", 2)

    def group(i):
        return near_x[i], far_x[i], diagonal[i]

    def attn_weights(layer):
        return (qkv_weight, core[0], o_weight, core[1]) + group(3 * layer)

    def ffn_weights(layer):
        return (in_weight, core[2]) + group(3 * layer + 1) + (out_weight, core[3]) + group(3 * layer + 2)

    def in_order(low_one, high_one, bit):
        swapped = (me & bit) != 0
        return jnp.stack([jnp.where(swapped, high_one, low_one), jnp.where(swapped, low_one, high_one)])

    def send_x(*which):
        for i in which:
            near_x[i] = swap(order.wait(halves[i]), "narrow", 2)

    def send_core(i):
        core[i] = swap(order.wait(own[i]), "narrow", 1)

    def arrive(*events):
        for kind, i in events:
            if kind == "x":
                near_x[i] = order.wait(near_x[i])
                far_x[i] = swap(near_x[i], "wide", 1)
            elif kind == "y":
                far_x[i] = order.wait(far_x[i])
                diagonal[i] = swap(order.wait(jnp.concatenate([near_x[i], far_x[i]], axis=0)), "narrow", 1)
            elif kind == "d":
                diagonal[i] = order.wait(diagonal[i])
            else:
                core[i] = order.wait(core[i])

    send_x(0)
    core[0], core[1] = [swap(weight, "narrow", 1) for weight in order.wait(own[:2])]
    short = order.wait((q_bias, v_bias, o_bias, norm1_gain, norm1_bias, out_bias, norm2_gain, norm2_bias))
    packed = call(
        pack_kernel, "pack", 1, [VMEM] * 9, VMEM, shape((layers, 12, share), f32), [], tuple(short) + (in_bias,)
    )
    halves[1:], packed = order.wait((halves[1:], packed))
    near_x[0], core[0], core[1] = order.wait((near_x[0], core[0], core[1]))
    others = [lax.ppermute(packed, "narrow", [(i, i ^ away) for i in range(4)]) for away in (1, 2, 3)]
    far_x[0] = swap(near_x[0], "wide", 1)
    send_x(1)
    far_x[0], near_x[1], others = order.wait((far_x[0], near_x[1], others))
    packed = in_order(in_order(packed, others[0], 1), in_order(others[1], others[2], 1), 2)
    packed = packed.reshape(4, layers, 12, share)
    small = packed[:, :, :8].transpose(1, 2, 0, 3).reshape(layers, 8, width)
    full_in_bias = packed[:, :, 8:].transpose(1, 0, 2, 3).reshape(layers, 1, ffn)

    def begin_round(i):
        diagonal[i] = swap(order.wait(jnp.concatenate([near_x[i], far_x[i]], axis=0)), "narrow", 1)
        if i + 1 < len(halves):
            far_x[i + 1] = swap(near_x[i + 1], "wide", 1)
        if i + 2 < len(halves):
            send_x(i + 2)

    def end_round(i):
        if i + 2 < len(halves):
            far_x[i + 1], near_x[i + 2] = order.wait((far_x[i + 1], near_x[i + 2]))
        elif i + 1 < len(halves):
            far_x[i + 1] = order.wait(far_x[i + 1])

    def arrive(i):
        diagonal[i] = order.wait(diagonal[i])

    begin_round(0)
    core[2], core[3] = [swap(weight, "narrow", 1) for weight in order.wait(own[2:])]
    small, full_in_bias = order.wait((small, full_in_bias))
    arrive(0)
    core[2], core[3] = order.wait((core[2], core[3]))
    end_round(0)

    w_qkv = pltpu.VMEM((width, 3 * width), low)
    w_o = pltpu.VMEM((width, width), low)
    w_in = pltpu.VMEM((width, ffn), low)
    w_out = pltpu.VMEM((ffn, width), low)
    copy_sems = pltpu.SemaphoreType.DMA((12,))
    piece_sems = pltpu.SemaphoreType.DMA((16,))
    rows_f32 = shape((tokens, width), f32)
    rows_low = shape((tokens, width), low)
    column_f32 = shape((tokens, 1), f32)
    eight_f32 = shape((8, width), f32)

    def pieces(rows):
        return [shape((2, 2, 2, 2, rows, tile), low)] * 2

    def stage(rows):
        return pltpu.VMEM((2, 2, 2, 2, 2, rows, tile), low)

    def tie(outs, which):
        outs = list(outs)
        outs[which] = order.wait(outs[which])
        return outs

    def attn_forward(layer, x):
        x = order.wait(x)
        outs = call(
            functools.partial(attn_fwd_kernel, layer),
            "attn_fwd",
            2.6,
            [SMEM, SMEM] + [VMEM] * 3 + [ANY] * 7,
            [VMEM] * 5,
            [shape((tokens, 3 * width), low), shape((HEADS, tokens, tokens), low), rows_low, rows_f32, column_f32],
            [w_qkv, w_o, pltpu.VMEM((tokens, tokens), f32), copy_sems],
            (order.ids, lengths, x, cell_ids, small) + attn_weights(layer),
        )
        return tie(outs, 3)

    def ffn_forward(layer, unit_one):
        unit_one = order.wait(unit_one)
        outs = call(
            functools.partial(ffn_fwd_kernel, layer),
            "ffn_fwd",
            2,
            [SMEM] + [VMEM] * 3 + [ANY] * 10,
            [ANY] * 2 + [VMEM] * 3,
            [shape((tokens, ffn), low), shape((tokens, ffn), f32), rows_f32, column_f32, rows_low],
            [
                w_in,
                w_out,
                pltpu.VMEM((tokens, width), low),
                pltpu.VMEM((tokens, ffn), low),
                pltpu.VMEM((tokens, ffn), f32),
                copy_sems,
                piece_sems,
            ],
            (order.ids, unit_one, full_in_bias, small) + ffn_weights(layer),
        )
        return tie(outs, 4)

    def out_backward(layer, way, grad, unit_two, inverse_two, hidden):
        grad = order.wait(grad)
        outs = call(
            functools.partial(out_bwd_kernel, layer, way),
            "out_bwd",
            TIMES["out%d" % layer],
            [SMEM] + [VMEM] * 5,
            [VMEM] * 3 + [ANY] * 2,
            [rows_low, rows_f32, eight_f32] + pieces(share),
            [stage(share), pltpu.SemaphoreType.DMA((4,))],
            (order.ids, grad, unit_two, inverse_two, hidden, small),
        )
        return tie(outs, 0)

    def in_backward(layer, way, d_ffn, d_resid_two, unit_one, inverse_one, slope):
        d_ffn = order.wait(d_ffn)
        outs = call(
            functools.partial(in_bwd_kernel, layer, way),
            "in_bwd",
            TIMES["in%d" % layer],
            [SMEM] + [VMEM] * 6 + [ANY] * 10,
            [VMEM] * 3 + [ANY] * 2,
            [rows_f32, eight_f32, shape((1, ffn), f32)] + pieces(share),
            [
                w_in,
                w_out,
                pltpu.VMEM((tokens, ffn), low),
                pltpu.VMEM((width, tokens), low),
                stage(share),
                copy_sems,
                piece_sems,
            ],
            (order.ids, d_ffn, d_resid_two, unit_one, inverse_one, slope, small) + ffn_weights(layer),
        )
        return tie(outs, 0)

    def attn_backward(layer, way, d_resid, x, qkv_rows, probs, context, small_others):
        d_resid = order.wait(d_resid)
        rows = share + (SMALL_ROWS if small_others else 0)
        outs = call(
            functools.partial(attn_bwd_kernel, layer, way),
            "attn_bwd",
            TIMES["attn%d" % layer],
            [SMEM] + [VMEM] * 5 + [ANY] * 7 + [VMEM] * len(small_others),
            [VMEM] * 2 + [ANY] * 2,
            [rows_low, eight_f32] + pieces(rows),
            [
                w_qkv,
                w_o,
                pltpu.VMEM((tokens, width), low),
                pltpu.VMEM((tokens, width), low),
                pltpu.VMEM((tokens, 3 * width), low),
                pltpu.VMEM((width, tokens), low),
                stage(rows),
                copy_sems,
                piece_sems,
            ],
            (order.ids, d_resid, x, qkv_rows, probs, context) + attn_weights(layer) + tuple(small_others),
        )
        return tie(outs, 0)

    def unpack(layer, name, slab, earlier):
        dims = {
            "attn": [(layers, share, 3 * width), (layers, share, width)],
            "in": [(layers, share, ffn)],
            "out": [(layers, ffn_share, width)],
        }[name]
        last = name == "attn" and layer == 0
        extra = [(layers, share)] * 8 + [(layers, ffn_share)] if last else [(8, 128)]
        near, far = order.wait((slab.block, slab.far))
        rows = near.shape[2]
        outs = call(
            functools.partial(unpack_kernel, layer, name, slab.back, len(earlier)),
            "unpack",
            4,
            [SMEM] + [ANY] * (2 + len(earlier)),
            [ANY] * len(dims) + [VMEM] * len(extra),
            [shape(d, f32) for d in dims + extra],
            [
                pltpu.VMEM((8, rows, tile), low),
                pltpu.VMEM((8, share, tile), f32),
                pltpu.SemaphoreType.DMA((8,)),
                pltpu.SemaphoreType.DMA((8,)),
            ],
            (order.ids, near, far, *earlier),
            {3 + i: i for i in range(len(earlier))},
        )
        return tuple(tie(outs, 0))

    begin_round(1)
    first_attn = attn_forward(0, tables_in)
    arrive(1)
    end_round(1)
    begin_round(2)
    arrive(2)
    first_ffn = ffn_forward(0, first_attn[3])
    end_round(2)
    begin_round(3)
    arrive(3)
    second_attn = attn_forward(1, first_ffn[4])
    end_round(3)
    begin_round(4)
    arrive(4)
    end_round(4)
    begin_round(5)
    arrive(5)
    second_ffn = ffn_forward(1, second_attn[3])
    mixed_out = second_ffn[4]
    inputs = (tables_in, first_ffn[4])
    attn_kept, ffn_kept = (first_attn, second_attn), (first_ffn, second_ffn)

    slabs = [None] * 6
    grad = cotangent
    small_out, small_in, small_attn, bias_grads = [None] * 2, [None] * 2, [None] * 2, [None] * 2
    unpacked = {"attn": (), "in": (), "out": ()}
    for action in PLAN:
        if isinstance(action, int):
            slab = slabs[action]
            slab.step(order)
            if slab.ended():
                name = ("out", "in", "attn")[action % 3]
                unpacked[name] = unpack(layers - 1 - action // 3, name, slab, unpacked[name][: 2 if name == "attn" else 1])
            continue
        name, layer = action[:-1], int(action[-1])
        which = 3 * (layers - 1 - layer) + ("out", "in", "attn").index(name)
        way = WAYS[which]
        qkv_rows, probs, context, unit_one, inverse_one = attn_kept[layer]
        hidden, slope, unit_two, inverse_two, _ = ffn_kept[layer]
        if name == "out":
            d_ffn, d_resid_two, small_out[layer], kept, sent = out_backward(
                layer, way, grad, unit_two, inverse_two, hidden
            )
        elif name == "in":
            d_resid, small_in[layer], bias_grads[layer], kept, sent = in_backward(
                layer, way, d_ffn, d_resid_two, unit_one, inverse_one, slope
            )
        else:
            small_others = ()
            if layer == 0:
                small_others = (
                    small_out[0],
                    small_in[0],
                    bias_grads[0],
                    small_out[1],
                    small_in[1],
                    bias_grads[1],
                    small_attn[1],
                )
            grad, small_attn[layer], kept, sent = attn_backward(
                layer, way, d_resid, inputs[layer], qkv_rows, probs, context, small_others
            )
        slabs[which] = Slab(way, BACKS[which], wide_count, kept, sent)
    qkv_grad, o_grad, *vectors = unpacked["attn"]
    in_grad, out_grad = unpacked["in"][0], unpacked["out"][0]
    return (
        mixed_out,
        grad,
        qkv_grad,
        vectors[0],
        vectors[1],
        o_grad,
        vectors[2],
        vectors[3],
        vectors[4],
        in_grad,
        vectors[8],
        out_grad,
        vectors[5],
        vectors[6],
        vectors[7],
    )


def solution(mesh):
    by_table = P(("wide", "narrow"), None)
    matrix = P(None, "narrow", None)
    vector = P(None, "narrow")
    return jax.shard_map(
        body,
        mesh=mesh,
        in_specs=(
            by_table,
            by_table,
            by_table,
            P(("wide", "narrow")),
            matrix,
            vector,
            vector,
            matrix,
            vector,
            vector,
            vector,
            matrix,
            vector,
            matrix,
            vector,
            vector,
            vector,
        ),
        out_specs=(
            by_table,
            by_table,
            matrix,
            vector,
            vector,
            matrix,
            vector,
            vector,
            vector,
            matrix,
            vector,
            matrix,
            vector,
            vector,
            vector,
        ),
        check_vma=False,
    )
```

```python
import functools
import math

import jax
import jax.numpy as jnp
from jax import lax
from jax.experimental import pallas as pl
from jax.experimental.pallas import tpu as pltpu
from jax.sharding import PartitionSpec as P

HEADS = 12
norm_eps = 1e-12
masked_score = -1000000000.0
low = jnp.bfloat16
f32 = jnp.float32
VMEM_BYTES = 56 * 1024 * 1024
HALVINGS = 2


def swap(value, axis, bit):
    count = lax.axis_size(axis)
    return lax.ppermute(value, axis, [(i, i ^ bit) for i in range(count)])


def dot(a, b):
    return jnp.dot(a, b, preferred_element_type=f32)


def dot_nt(a, b):
    return lax.dot_general(a, b, (((1,), (1,)), ((), ())), preferred_element_type=f32)


def dot_tn(a, b):
    return lax.dot_general(a, b, (((0,), (0,)), ((), ())), preferred_element_type=f32)


def normalize(residual):
    center = residual - jnp.mean(residual, axis=-1, keepdims=True)
    inverse = lax.rsqrt(jnp.mean(center * center, axis=-1, keepdims=True) + norm_eps)
    return center * inverse, inverse


def normalize_back(grad_unit, unit, inverse):
    centered = grad_unit - jnp.mean(grad_unit, axis=-1, keepdims=True)
    return inverse * (centered - unit * jnp.mean(grad_unit * unit, axis=-1, keepdims=True))


def weight_copies(ids, layer, pieces, target, columns, sems, base):
    own, core, near_x, far_x, diagonal = pieces
    rows = own.shape[1]
    half = rows // 2
    n, y = ids[0], ids[4]
    copies = []

    def add(source, start, count):
        where = target.at[pl.ds(pl.multiple_of(start, half), count), :]
        copies.append(pltpu.make_async_copy(source, where, sems.at[base + len(copies)]))

    at = pl.ds(columns, target.shape[1])
    add(own.at[layer], n * rows, rows)
    add(core.at[layer], ids[1] * rows, rows)
    add(near_x.at[:, at], ids[2] * rows + y * half, half)
    add(far_x.at[:, at], ids[2] * rows + (1 - y) * half, half)
    add(diagonal.at[pl.ds(0, half), at], ids[3] * rows + y * half, half)
    add(diagonal.at[pl.ds(half, half), at], ids[3] * rows + (1 - y) * half, half)
    return copies


def begin(copies):
    for copy in copies:
        copy.start()


def finish(copies):
    for copy in copies:
        copy.wait()


def attn_copies(layer, ids, refs, w_qkv, w_o, sems):
    qkv_own, qkv_core, o_own, o_core = refs[:4]
    halves = refs[4:]
    qkv = weight_copies(ids, layer, (qkv_own, qkv_core) + halves, w_qkv, 0, sems, 0)
    o = weight_copies(ids, layer, (o_own, o_core) + halves, w_o, w_qkv.shape[1], sems, 6)
    return qkv, o


def ffn_copies(layer, ids, refs, w_in, w_out, sems):
    in_copies = weight_copies(ids, layer, refs[:5], w_in, 0, sems, 0)
    out_copies = weight_copies(ids, layer, refs[5:], w_out, 0, sems, 6)
    return in_copies, out_copies


def pack_kernel(*refs):
    shorts, in_bias, packed = refs[:8], refs[8], refs[9]
    layers, share = shorts[0].shape
    for layer in range(layers):
        for i, short in enumerate(shorts):
            packed[layer, i : i + 1, :] = short[layer : layer + 1, :].astype(f32)
        for i in range(4):
            packed[layer, 8 + i : 9 + i, :] = in_bias[layer : layer + 1, i * share : (i + 1) * share].astype(f32)


def attn_fwd_kernel(layer, ids, length, x, cell_row, small, *rest):
    weights, rest = rest[:7], rest[7:]
    qkv_rows, probs, context, unit_out, inverse_out, w_qkv, w_o, mask, sems = rest
    tokens, width = x.shape
    qkv_copies, o_copies = attn_copies(layer, ids, weights, w_qkv, w_o, sems)
    begin(qkv_copies)
    begin(o_copies)
    position = lax.broadcasted_iota(jnp.int32, (tokens, 1), 0)
    query_cell = cell_row[...]
    square = (tokens, tokens)
    diagonal = lax.broadcasted_iota(jnp.int32, square, 0) == lax.broadcasted_iota(jnp.int32, square, 1)
    key_cell = jnp.sum(jnp.where(diagonal, query_cell, 0), axis=1, keepdims=True)
    allowed = (query_cell == key_cell) | (key_cell == 0) | (query_cell == 0)
    allowed = allowed & (position < length[0])
    mask[...] = jnp.where(allowed, 0.0, masked_score)
    scale = 1.0 / math.sqrt(width // HEADS)
    finish(qkv_copies)
    for part in range(3):
        columns = slice(part * width, (part + 1) * width)
        rows = dot(x[...], w_qkv[:, columns])
        if part != 1:
            rows = rows + small[layer, part // 2 : part // 2 + 1, :]
        if part == 0:
            rows = rows * scale
        qkv_rows[:, columns] = rows.astype(low)

    pair_width = 2 * width // HEADS
    first = lax.broadcasted_iota(jnp.int32, (1, pair_width), 1) < pair_width // 2

    for pair in range(HEADS // 2):
        at = slice(pair * pair_width, (pair + 1) * pair_width)
        query = qkv_rows[:, at]
        key = qkv_rows[:, width + at.start : width + at.stop]
        value = qkv_rows[:, 2 * width + at.start : 2 * width + at.stop]
        sides = []
        for side in range(2):
            mine = first if side == 0 else jnp.logical_not(first)
            scores = dot_nt(key, jnp.where(mine, query, jnp.zeros_like(query))) + mask[...]
            shifted = jnp.exp(scores - jnp.max(scores, axis=0, keepdims=True))
            total = jnp.sum(shifted, axis=0, keepdims=True)
            prob = (shifted * (1.0 / total)).astype(low)
            probs[2 * pair + side] = prob
            sides.append(dot_tn(prob, value))
        context[:, at] = jnp.where(first, sides[0], sides[1]).astype(low)

    finish(o_copies)
    residual = x[...].astype(f32) + (dot(context[...], w_o[...]) + small[layer, 2:3, :])
    unit, inverse = normalize(residual)
    unit_out[...] = unit
    inverse_out[...] = inverse


def gelu_and_slope(x):
    t = 1.0 / (1.0 + (0.3275911 * math.sqrt(0.5)) * jnp.abs(x))
    bell = jnp.exp(-0.5 * x * x)
    series = 1.421413741 + t * (-1.453152027 + t * 1.061405429)
    series = t * (0.254829592 + t * (-0.284496736 + t * series))
    tail = 0.5 * series * bell
    cdf = jnp.where(x >= 0.0, 1.0 - tail, tail)
    return (x * cdf).astype(low), cdf + x * (bell * (1.0 / math.sqrt(2.0 * math.pi)))


def ffn_fwd_kernel(layer, ids, unit_one, in_bias, small, *rest):
    weights, rest = rest[:10], rest[10:]
    hidden_out, slope_out, unit_out, inverse_out, result = rest[:5]
    w_in, w_out, normed_low, hidden, slope, sems, out_sems = rest[5:]
    in_copies, out_copies = ffn_copies(layer, ids, weights, w_in, w_out, sems)
    begin(in_copies)
    begin(out_copies)
    normed = unit_one[...] * small[layer, 3:4, :] + small[layer, 4:5, :]
    normed_low[...] = normed.astype(low)
    finish(in_copies)
    tile = w_in.shape[1] // 4
    going = []
    for t in range(4):
        columns = pl.ds(t * tile, tile)
        pre = dot(normed_low[...], w_in[:, columns]) + in_bias[layer, :, columns]
        hidden[:, columns], slope[:, columns] = gelu_and_slope(pre)
        leaving = [
            pltpu.make_async_copy(hidden.at[:, columns], hidden_out.at[:, columns], out_sems.at[2 * t]),
            pltpu.make_async_copy(slope.at[:, columns], slope_out.at[:, columns], out_sems.at[2 * t + 1]),
        ]
        begin(leaving)
        going += leaving

    finish(out_copies)
    residual = unit_one[...] * small[layer, 3:4, :] + small[layer, 4:5, :] + (dot(hidden[...], w_out[...]) + small[layer, 5:6, :])
    unit, inverse = normalize(residual)
    unit_out[...] = unit
    inverse_out[...] = inverse
    result[...] = (unit * small[layer, 6:7, :] + small[layer, 7:8, :]).astype(low)
    finish(going)


WIDE_BIT = {"y": 0, "z": 1}


def place_of(ids, owner, piece, way):
    away = None if owner is None else ids[0] ^ owner
    off = None if piece is None else piece ^ ids[5]
    place = [None if away is None else away & 1]
    for name in way:
        if name == "x":
            place.append(pl.ds(0, 2) if away is None else away >> 1)
        else:
            place.append(pl.ds(0, 2) if off is None else (off >> WIDE_BIT[name]) & 1)
    return tuple(place) + (pl.ds(0, 2) if piece is None else piece >> 2,)


def store_rows(stage, ids, product, piece, way):
    share = product.shape[0] // 4
    for owner in range(4):
        block = product[owner * share : (owner + 1) * share].astype(low)
        stage[place_of(ids, owner, piece, way) + (pl.ds(0, share),)] = block


def piece_copies(stage, ids, piece, way, kept, sent, sems, turn):
    at = place_of(ids, None, piece, way)[1:]
    copies = [
        pltpu.make_async_copy(stage.at[(1,) + at], sent.at[at], sems.at[2 * turn]),
        pltpu.make_async_copy(stage.at[(0,) + at], kept.at[at], sems.at[2 * turn + 1]),
    ]
    begin(copies)
    return copies


def out_bwd_kernel(layer, way, ids, grad, unit_two, inverse_two, hidden, small, *rest):
    d_ffn, d_resid_two, small_grads, kept, sent, stage, out_sems = rest
    g = grad[...].astype(f32)
    unit = unit_two[...]
    small_grads[0:1, :] = jnp.sum(g * unit, axis=0, keepdims=True)
    small_grads[1:2, :] = jnp.sum(g, axis=0, keepdims=True)
    d_two = normalize_back(g * small[layer, 6:7, :], unit, inverse_two[...])
    d_resid_two[...] = d_two
    d_low = d_two.astype(low)
    d_ffn[...] = d_low
    small_grads[2:3, :] = jnp.sum(d_low.astype(f32), axis=0, keepdims=True)
    small_grads[3:8, :] = jnp.zeros((5, unit.shape[1]), f32)
    tile = hidden.shape[1] // 8
    share = d_ffn.shape[1] // 4
    waits = []
    for owner in range(4):
        for half in range(2):
            columns = slice((2 * owner + half) * tile, (2 * owner + half + 1) * tile)
            out_grad = dot_tn(hidden[:, columns], d_ffn[...])
            for row_group in range(2):
                for column_group in range(2):
                    piece = (half * 2 + row_group) * 2 + column_group
                    block = out_grad[
                        row_group * share : (row_group + 1) * share,
                        column_group * tile : (column_group + 1) * tile,
                    ]
                    stage[place_of(ids, owner, piece, way)] = block.astype(low)
        core, *at = place_of(ids, owner, None, way)
        at = tuple(at)
        to_kept = pltpu.make_async_copy(stage.at[(0,) + at], kept.at[at], out_sems.at[owner])
        to_sent = pltpu.make_async_copy(stage.at[(1,) + at], sent.at[at], out_sems.at[owner])
        pl.when(core == 0)(to_kept.start)
        pl.when(core == 1)(to_sent.start)
        waits.append(to_kept)
    finish(waits)


def in_bwd_kernel(layer, way, ids, d_ffn, unit_one, inverse_one, small, resid_in, slope_in, *rest):
    weights, rest = rest[:10], rest[10:]
    d_resid, small_grads, in_bias_grad, kept, sent = rest[:5]
    w_in, w_out, d_pre, normed_t, slope, d_resid_two, stage, sems, out_sems, more_sems = rest[5:]
    in_copies, out_copies = ffn_copies(layer, ids, weights, w_in, w_out, sems)
    slope_copy = pltpu.make_async_copy(slope_in, slope, more_sems.at[0])
    resid_copy = pltpu.make_async_copy(resid_in, d_resid_two, more_sems.at[1])
    begin(out_copies + [slope_copy] + in_copies + [resid_copy])
    normed = unit_one[...] * small[layer, 3:4, :] + small[layer, 4:5, :]
    normed_t[...] = normed.astype(low).T
    finish(out_copies)
    tile = w_in.shape[1] // 4
    going = []
    slope_copy.wait()
    for t in range(4):
        columns = slice(t * tile, (t + 1) * tile)
        d_hidden = dot_nt(d_ffn[...], w_out[columns, :])
        d_tile = (d_hidden * slope[:, columns]).astype(low)
        d_pre[:, columns] = d_tile
        in_bias_grad[:, columns] = jnp.sum(d_tile.astype(f32), axis=0, keepdims=True)
        product = dot(normed_t[...], d_tile)
        for half in range(2):
            piece = 2 * t + half
            store_rows(stage, ids, product[:, half * tile // 2 : (half + 1) * tile // 2], piece, way)
            going += piece_copies(stage, ids, piece, way, kept, sent, out_sems, piece)
    resid_copy.wait()
    finish(in_copies)
    d_normed = d_resid_two[...] + dot_nt(d_pre[...], w_in[...])
    unit = unit_one[...]
    small_grads[0:1, :] = jnp.sum(d_normed * unit, axis=0, keepdims=True)
    small_grads[1:2, :] = jnp.sum(d_normed, axis=0, keepdims=True)
    small_grads[2:8, :] = jnp.zeros((6, unit.shape[1]), f32)
    d_resid[...] = normalize_back(d_normed * small[layer, 3:4, :], unit, inverse_one[...])
    finish(going)


def attn_bwd_kernel(layer, way, ids, d_resid, x, qkv_rows, probs, context, *rest):
    weights, others, rest = rest[:7], rest[7:-13], rest[-13:]
    d_input, small_grads, kept, sent = rest[:4]
    w_qkv, w_o, d_attn, d_context, d_qkv, x_t, stage, sems, out_sems = rest[4:]
    tokens, width = x.shape
    qkv_copies, o_copies = attn_copies(layer, ids, weights, w_qkv, w_o, sems)
    begin(o_copies)
    begin(qkv_copies)
    d_low = d_resid[...].astype(low)
    d_attn[...] = d_low
    small_grads[2:3, :] = jnp.sum(d_low.astype(f32), axis=0, keepdims=True)
    x_t[...] = x[...].T
    tile = width // 2
    product = dot_tn(context[...], d_attn[...])
    for half in range(2):
        store_rows(stage, ids, product[:, half * tile : (half + 1) * tile], 6 + half, way)
    finish(o_copies)
    d_context[...] = dot_nt(d_attn[...], w_o[...]).astype(low)
    pair_width = 2 * width // HEADS
    first = lax.broadcasted_iota(jnp.int32, (1, pair_width), 1) < pair_width // 2
    scale = 1.0 / math.sqrt(width // HEADS)

    for pair in range(HEADS // 2):
        at_query = slice(pair * pair_width, (pair + 1) * pair_width)
        at_key = slice(width + at_query.start, width + at_query.stop)
        at_value = slice(2 * width + at_query.start, 2 * width + at_query.stop)
        query, key, value = qkv_rows[:, at_query], qkv_rows[:, at_key], qkv_rows[:, at_value]
        d_ctx = d_context[:, at_query]
        sides = []
        for side in range(2):
            mine = first if side == 0 else jnp.logical_not(first)
            prob_low = probs[2 * pair + side]
            prob = prob_low.astype(f32)
            d_prob = dot_nt(value, jnp.where(mine, d_ctx, jnp.zeros_like(d_ctx)))
            inner = jnp.sum(prob * d_prob, axis=0, keepdims=True)
            d_scores = (prob * (d_prob - inner)).astype(low)
            sides.append((dot_tn(d_scores, key), dot(d_scores, query), dot(prob_low, d_ctx)))
        d_qkv[:, at_query] = (jnp.where(first, sides[0][0], sides[1][0]) * scale).astype(low)
        d_qkv[:, at_key] = jnp.where(first, sides[0][1], sides[1][1]).astype(low)
        d_qkv[:, at_value] = jnp.where(first, sides[0][2], sides[1][2]).astype(low)

    small_grads[0:1, :] = jnp.sum(d_qkv[:, :width].astype(f32), axis=0, keepdims=True)
    small_grads[1:2, :] = jnp.sum(d_qkv[:, 2 * width :].astype(f32), axis=0, keepdims=True)
    small_grads[3:8, :] = jnp.zeros((5, width), f32)
    if others:
        share = width // 4
        sources = small_sources(layer, small_grads, others)
        for owner in range(4):
            for piece in range(8):
                lines = []
                for source, row, start, step in sources[3 * piece : 3 * piece + 3]:
                    line = source[row : row + 1, start + owner * step : start + owner * step + share]
                    lines.append(jnp.concatenate([line, jnp.zeros_like(line)], axis=1))
                lines.append(jnp.zeros((SMALL_ROWS - 3, tile), f32))
                block = jnp.concatenate(lines, axis=0).astype(low)
                stage[place_of(ids, owner, piece, way) + (pl.ds(share, SMALL_ROWS),)] = block
    going = []
    for part in (3, 0, 1, 2):
        if part < 3:
            product = dot(x_t[...], d_qkv[:, part * width : (part + 1) * width])
        for half in range(2):
            piece = 2 * part + half
            if part < 3:
                store_rows(stage, ids, product[:, half * tile : (half + 1) * tile], piece, way)
            going += piece_copies(stage, ids, piece, way, kept, sent, out_sems, piece)
    finish(qkv_copies)
    d_input[...] = (d_resid[...] + dot_nt(d_qkv[...], w_qkv[...])).astype(low)
    finish(going)


SMALL_ROWS = 16
SMALL_LINES = (("attn", 0), ("attn", 1), ("attn", 2), ("in", 0), ("in", 1), ("out", 2), ("out", 0), ("out", 1))


def small_sources(layer, own, others):
    found = []
    out_0, in_0, bias_0, out_1, in_1, bias_1, attn_1 = others
    refs = ({"attn": own, "in": in_0, "out": out_0}, {"attn": attn_1, "in": in_1, "out": out_1})
    width = own.shape[1]
    for of_layer, bias in zip(refs, (bias_0, bias_1)):
        found += [(of_layer[name], row, 0, width // 4) for name, row in SMALL_LINES]
        found += [(bias, 0, i * (width // 4), width) for i in range(4)]
    return found


def unpack_kernel(layer, slab, back, earlier, ids, near, far, *rest):
    outs = rest[earlier:-4]
    buffer, wide_buffer, in_sems, out_sems = rest[-4:]
    share, tile = wide_buffer.shape[1:]

    def fetch(piece, ref, index):
        return pltpu.make_async_copy(ref.at[index], buffer.at[piece], in_sems.at[piece])

    for piece in range(8):
        off = piece ^ ids[5]
        inner, outer = [(off >> WIDE_BIT[name]) & 1 for name in back]
        pl.when(outer == 0)(fetch(piece, near, (inner, piece >> 2)).start)
        pl.when(outer == 1)(fetch(piece, far, (inner, piece >> 2)).start)

    copies = []
    for piece in range(8):
        fetch(piece, near, (0, 0)).wait()
        wide_buffer[piece] = buffer[piece, :share].astype(f32)
        columns = pl.ds(piece * tile, tile)
        if slab == "in":
            target = outs[0].at[layer, :, columns]
        elif slab == "out":
            rows = pl.ds((piece // 2) * share, share)
            target = outs[0].at[layer, rows, pl.ds((piece % 2) * tile, tile)]
        elif piece < 6:
            target = outs[0].at[layer, :, columns]
        else:
            target = outs[1].at[layer, :, pl.ds((piece - 6) * tile, tile)]
        copies.append(pltpu.make_async_copy(wide_buffer.at[piece], target, out_sems.at[piece]))
        copies[-1].start()
    if slab == "attn" and layer == 0:
        for line in range(24):
            of_layer, which = line // 12, line % 12
            row = share + line % 3
            values = buffer[line // 3, row : row + 1, :share].astype(f32)
            if which < 8:
                outs[2 + which][of_layer : of_layer + 1, :] = values
            else:
                at = (which - 8) * share
                outs[10][of_layer : of_layer + 1, at : at + share] = values
    else:
        outs[-1][...] = jnp.zeros(outs[-1].shape, f32)
    finish(copies)


SMEM = pl.BlockSpec(memory_space=pltpu.SMEM)
VMEM = pl.BlockSpec(memory_space=pltpu.VMEM)
ANY = pl.BlockSpec(memory_space=pl.ANY)


def call(kernel, name, time, in_specs, out_specs, out_shape, scratch, args, aliases=()):
    return pl.pallas_call(
        kernel,
        name=name,
        in_specs=in_specs,
        out_specs=out_specs,
        out_shape=out_shape,
        scratch_shapes=scratch,
        input_output_aliases=dict(aliases),
        compiler_params=pltpu.CompilerParams(vmem_limit_bytes=VMEM_BYTES),
        cost_estimate=pl.CostEstimate(
            flops=int(time * 1.1e9), bytes_accessed=int(time * 3.6e6), transcendentals=0
        ),
    )(*args)


def shape(dims, kind):
    return jax.ShapeDtypeStruct(dims, kind)


def added(a, b):
    return (a.astype(f32) + b.astype(f32)).astype(low)


WAYS = ("zxy", "xyz", "yxz", "zyx", "xyz", "xyz")
BACKS = ("zy", "zy", "zy", "yz", "zy", "zy")
PLAN = (
    "out1", "in1", 0, 1, "attn1", "out0", "in0", 0, 1, "attn0", 1, 0, 2, 4, 3, 1, 2, 4, 1, 0, 5, 3, 2, 0, 4,
    1, 2, 0, 3, 2, 4, 5, 3, 0, 5, 4, 2, 3, 5, 1, 3, 5, 4, 2, 5, 4, 3, 5,
)
FORWARD = (
    "h0", "g1", "g0", "h1", "g3", "h5", "h2", "g2", "c2", "h3", "x2", "x1", "c0", "pack", "x0", "h4", "c3",
    "y2", "x3", "sm", "y1", "y0", "c1", "A", "d1", "d2", "d0", "x5", "attn1", "y3", "x4", "y5", "ffn1", "y4",
    "d3", "attn2", "d4", "d5", "ffn2",
)
TIMES = {
    "pack": 2, "attn1": 0.3, "ffn1": 0.3, "attn2": 3, "ffn2": 8,
    "out_bwd1": 20, "in_bwd1": 20, "attn_bwd1": 0.3, "out_bwd0": 2, "in_bwd0": 1, "attn_bwd0": 8,
}


class Order:
    def __init__(self, ids):
        self.ids = ids

    def wait(self, values):
        values, self.ids = lax.optimization_barrier((values, self.ids))
        return values


STEPS = {"x": ("narrow", 2), "y": ("wide", 1), "z": ("wide", 2)}


class Slab:
    def __init__(self, way, back, wide_count, kept, sent):
        self.kept = kept
        self.way, self.back = way, back
        self.rest = [1 << b for b in range(HALVINGS, wide_count.bit_length() - 1)]
        self.flying = swap(sent, "narrow", 1)
        self.stage = 0

    def step(self, order):
        received = order.wait(self.flying)
        stage, way = self.stage, self.way
        if stage < len(way):
            send = order.wait(added(self.kept[1], received[1]))
            self.kept = added(self.kept[0], received[0])
            self.flying = swap(send, *STEPS[way[stage]])
        elif stage < len(way) + 1 + len(self.back):
            if stage == len(way):
                piece = added(self.kept, received)
                for bit in self.rest[:-1]:
                    piece = added(piece, swap(piece, "wide", bit))
                self.kept = order.wait(piece)
                self.flying = swap(self.kept, "wide", self.rest[-1])
            else:
                if stage == len(way) + 1:
                    self.block = added(self.kept, received)[None]
                else:
                    self.block = jnp.concatenate([self.block, received], axis=0)
                self.block = order.wait(self.block)
                self.flying = swap(self.block, *STEPS[self.back[stage - len(way) - 1]])
        else:
            self.far = received
        self.stage += 1

    def ended(self):
        return self.stage == len(self.way) + len(self.back) + 2


def body(
    tables_in,
    cotangent,
    cell_ids,
    lengths,
    qkv_weight,
    q_bias,
    v_bias,
    o_weight,
    o_bias,
    norm1_gain,
    norm1_bias,
    in_weight,
    in_bias,
    out_weight,
    out_bias,
    norm2_gain,
    norm2_bias,
):
    tokens, width = tables_in.shape
    layers, share, ffn = in_weight.shape
    ffn_share = out_weight.shape[1]
    wide_count = lax.axis_size("wide")
    assert wide_count & (wide_count - 1) == 0 and wide_count > 1 << HALVINGS and lax.axis_size("narrow") == 4
    tile = ffn // 8
    me = lax.axis_index("narrow").astype(jnp.int32)
    wide_me = lax.axis_index("wide").astype(jnp.int32)
    y = wide_me & 1
    ids = jnp.stack([me, me ^ 1, me ^ 2, me ^ 3, y, wide_me & (2**HALVINGS - 1)])

    order = Order(ids)

    def half_of(weight, layer):
        rows = weight.shape[1] // 2
        return lax.dynamic_slice(weight, (layer, y * rows, 0), (1, rows, weight.shape[2]))[0]

    halves = []
    for layer in range(layers):
        joint = jnp.concatenate([half_of(qkv_weight, layer), half_of(o_weight, layer)], axis=1)
        halves += [joint, half_of(in_weight, layer), half_of(out_weight, layer)]
    near_x, far_x, diagonal = [None] * len(halves), [None] * len(halves), [None] * len(halves)
    core = [None] * 4
    own = (qkv_weight, o_weight, in_weight, out_weight)

    def group(i):
        return near_x[i], far_x[i], diagonal[i]

    def attn_weights(layer):
        return (qkv_weight, core[0], o_weight, core[1]) + group(3 * layer)

    def ffn_weights(layer):
        return (in_weight, core[2]) + group(3 * layer + 1) + (out_weight, core[3]) + group(3 * layer + 2)

    def in_order(low_one, high_one, bit):
        swapped = (me & bit) != 0
        return jnp.stack([jnp.where(swapped, high_one, low_one), jnp.where(swapped, low_one, high_one)])

    def send_x(*which):
        for i in which:
            near_x[i] = swap(order.wait(halves[i]), "narrow", 2)

    def group(i):
        return near_x[i], far_x[i], diagonal[i]

    def attn_weights(layer):
        return (qkv_weight, core[0], o_weight, core[1]) + group(3 * layer)

    def ffn_weights(layer):
        return (in_weight, core[2]) + group(3 * layer + 1) + (out_weight, core[3]) + group(3 * layer + 2)

    def in_order(low_one, high_one, bit):
        swapped = (me & bit) != 0
        return jnp.stack([jnp.where(swapped, high_one, low_one), jnp.where(swapped, low_one, high_one)])

    def send_x(*which):
        for i in which:
            near_x[i] = swap(order.wait(halves[i]), "narrow", 2)

    def send_core(i):
        core[i] = swap(order.wait(own[i]), "narrow", 1)

    def arrive(*events):
        for kind, i in events:
            if kind == "x":
                near_x[i] = order.wait(near_x[i])
                far_x[i] = swap(near_x[i], "wide", 1)
            elif kind == "y":
                far_x[i] = order.wait(far_x[i])
                diagonal[i] = swap(order.wait(jnp.concatenate([near_x[i], far_x[i]], axis=0)), "narrow", 1)
            elif kind == "d":
                diagonal[i] = order.wait(diagonal[i])
            else:
                core[i] = order.wait(core[i])

    w_qkv = pltpu.VMEM((width, 3 * width), low)
    w_o = pltpu.VMEM((width, width), low)
    w_in = pltpu.VMEM((width, ffn), low)
    w_out = pltpu.VMEM((ffn, width), low)
    copy_sems = pltpu.SemaphoreType.DMA((12,))
    piece_sems = pltpu.SemaphoreType.DMA((16,))
    rows_f32 = shape((tokens, width), f32)
    rows_low = shape((tokens, width), low)
    column_f32 = shape((tokens, 1), f32)
    eight_f32 = shape((8, width), f32)

    def pieces(rows):
        return [shape((2, 2, 2, 2, rows, tile), low)] * 2

    def stage(rows):
        return pltpu.VMEM((2, 2, 2, 2, 2, rows, tile), low)

    def tie(outs, which):
        outs = list(outs)
        outs[which] = order.wait(outs[which])
        return outs

    def attn_forward(layer, x):
        x = order.wait(x)
        outs = call(
            functools.partial(attn_fwd_kernel, layer),
            "attn_fwd",
            TIMES["attn%d" % (layer + 1)],
            [SMEM, SMEM] + [VMEM] * 3 + [ANY] * 7,
            [VMEM] * 5,
            [shape((tokens, 3 * width), low), shape((HEADS, tokens, tokens), low), rows_low, rows_f32, column_f32],
            [w_qkv, w_o, pltpu.VMEM((tokens, tokens), f32), copy_sems],
            (order.ids, lengths, x, cell_ids, small) + attn_weights(layer),
        )
        return tie(outs, 3)

    def ffn_forward(layer, unit_one):
        unit_one = order.wait(unit_one)
        outs = call(
            functools.partial(ffn_fwd_kernel, layer),
            "ffn_fwd",
            TIMES["ffn%d" % (layer + 1)],
            [SMEM] + [VMEM] * 3 + [ANY] * 10,
            [ANY] * 2 + [VMEM] * 3,
            [shape((tokens, ffn), low), shape((tokens, ffn), f32), rows_f32, column_f32, rows_low],
            [
                w_in,
                w_out,
                pltpu.VMEM((tokens, width), low),
                pltpu.VMEM((tokens, ffn), low),
                pltpu.VMEM((tokens, ffn), f32),
                copy_sems,
                piece_sems,
            ],
            (order.ids, unit_one, full_in_bias, small) + ffn_weights(layer),
        )
        return tie(outs, 4)

    def out_backward(layer, way, grad, unit_two, inverse_two, hidden):
        grad = order.wait(grad)
        outs = call(
            functools.partial(out_bwd_kernel, layer, way),
            "out_bwd",
            TIMES["out_bwd%d" % layer],
            [SMEM] + [VMEM] * 5,
            [VMEM] * 3 + [ANY] * 2,
            [rows_low, rows_f32, eight_f32] + pieces(share),
            [stage(share), pltpu.SemaphoreType.DMA((4,))],
            (order.ids, grad, unit_two, inverse_two, hidden, small),
        )
        return tie(outs, 0)

    def in_backward(layer, way, d_ffn, d_resid_two, unit_one, inverse_one, slope):
        d_ffn = order.wait(d_ffn)
        outs = call(
            functools.partial(in_bwd_kernel, layer, way),
            "in_bwd",
            TIMES["in_bwd%d" % layer],
            [SMEM] + [VMEM] * 4 + [ANY] * 12,
            [VMEM] * 3 + [ANY] * 2,
            [rows_f32, eight_f32, shape((1, ffn), f32)] + pieces(share),
            [
                w_in,
                w_out,
                pltpu.VMEM((tokens, ffn), low),
                pltpu.VMEM((width, tokens), low),
                pltpu.VMEM((tokens, ffn), f32),
                pltpu.VMEM((tokens, width), f32),
                stage(share),
                copy_sems,
                piece_sems,
                pltpu.SemaphoreType.DMA((2,)),
            ],
            (order.ids, d_ffn, unit_one, inverse_one, small, d_resid_two, slope) + ffn_weights(layer),
        )
        return tie(outs, 0)

    def attn_backward(layer, way, d_resid, x, qkv_rows, probs, context, small_others):
        d_resid = order.wait(d_resid)
        rows = share + (SMALL_ROWS if small_others else 0)
        outs = call(
            functools.partial(attn_bwd_kernel, layer, way),
            "attn_bwd",
            TIMES["attn_bwd%d" % layer],
            [SMEM] + [VMEM] * 5 + [ANY] * 7 + [VMEM] * len(small_others),
            [VMEM] * 2 + [ANY] * 2,
            [rows_low, eight_f32] + pieces(rows),
            [
                w_qkv,
                w_o,
                pltpu.VMEM((tokens, width), low),
                pltpu.VMEM((tokens, width), low),
                pltpu.VMEM((tokens, 3 * width), low),
                pltpu.VMEM((width, tokens), low),
                stage(rows),
                copy_sems,
                piece_sems,
            ],
            (order.ids, d_resid, x, qkv_rows, probs, context) + attn_weights(layer) + tuple(small_others),
        )
        return tie(outs, 0)

    def unpack(layer, name, slab, earlier):
        dims = {
            "attn": [(layers, share, 3 * width), (layers, share, width)],
            "in": [(layers, share, ffn)],
            "out": [(layers, ffn_share, width)],
        }[name]
        last = name == "attn" and layer == 0
        extra = [(layers, share)] * 8 + [(layers, ffn_share)] if last else [(8, 128)]
        near, far = order.wait((slab.block, slab.far))
        rows = near.shape[2]
        outs = call(
            functools.partial(unpack_kernel, layer, name, slab.back, len(earlier)),
            "unpack",
            4,
            [SMEM] + [ANY] * (2 + len(earlier)),
            [ANY] * len(dims) + [VMEM] * len(extra),
            [shape(d, f32) for d in dims + extra],
            [
                pltpu.VMEM((8, rows, tile), low),
                pltpu.VMEM((8, share, tile), f32),
                pltpu.SemaphoreType.DMA((8,)),
                pltpu.SemaphoreType.DMA((8,)),
            ],
            (order.ids, near, far, *earlier),
            {3 + i: i for i in range(len(earlier))},
        )
        return tuple(tie(outs, 0))

    short = (q_bias, v_bias, o_bias, norm1_gain, norm1_bias, out_bias, norm2_gain, norm2_bias)
    for token in FORWARD:
        kind, i = (token[0], int(token[1])) if len(token) == 2 and token[1].isdigit() else (token, None)
        if kind == "h":
            send_x(i)
        elif kind == "g":
            core[i] = swap(order.wait(own[i]), "narrow", 1)
        elif kind == "x":
            near_x[i] = order.wait(near_x[i])
            far_x[i] = swap(near_x[i], "wide", 1)
        elif kind == "y":
            far_x[i] = order.wait(far_x[i])
            diagonal[i] = swap(order.wait(jnp.concatenate([near_x[i], far_x[i]], axis=0)), "narrow", 1)
        elif kind == "d":
            diagonal[i] = order.wait(diagonal[i])
        elif kind == "c":
            core[i] = order.wait(core[i])
        elif token == "pack":
            packed = call(
                pack_kernel,
                "pack",
                TIMES["pack"],
                [VMEM] * 9,
                VMEM,
                shape((layers, 12, share), f32),
                [],
                tuple(order.wait(short)) + (in_bias,),
            )
            packed = order.wait(packed)
            others = [lax.ppermute(packed, "narrow", [(j, j ^ away) for j in range(4)]) for away in (1, 2, 3)]
        elif token == "sm":
            others = order.wait(others)
        elif token == "A":
            packed = in_order(in_order(packed, others[0], 1), in_order(others[1], others[2], 1), 2)
            packed = packed.reshape(4, layers, 12, share)
            small = packed[:, :, :8].transpose(1, 2, 0, 3).reshape(layers, 8, width)
            full_in_bias = packed[:, :, 8:].transpose(1, 0, 2, 3).reshape(layers, 1, ffn)
            small, full_in_bias = order.wait((small, full_in_bias))
        elif token == "attn1":
            first_attn = attn_forward(0, tables_in)
        elif token == "ffn1":
            first_ffn = ffn_forward(0, first_attn[3])
        elif token == "attn2":
            second_attn = attn_forward(1, first_ffn[4])
        else:
            second_ffn = ffn_forward(1, second_attn[3])
    mixed_out = second_ffn[4]
    inputs = (tables_in, first_ffn[4])
    attn_kept, ffn_kept = (first_attn, second_attn), (first_ffn, second_ffn)

    slabs = [None] * 6
    grad = cotangent
    small_out, small_in, small_attn, bias_grads = [None] * 2, [None] * 2, [None] * 2, [None] * 2
    unpacked = {"attn": (), "in": (), "out": ()}
    for action in PLAN:
        if isinstance(action, int):
            slab = slabs[action]
            slab.step(order)
            if slab.ended():
                name = ("out", "in", "attn")[action % 3]
                unpacked[name] = unpack(layers - 1 - action // 3, name, slab, unpacked[name][: 2 if name == "attn" else 1])
            continue
        name, layer = action[:-1], int(action[-1])
        which = 3 * (layers - 1 - layer) + ("out", "in", "attn").index(name)
        way = WAYS[which]
        qkv_rows, probs, context, unit_one, inverse_one = attn_kept[layer]
        hidden, slope, unit_two, inverse_two, _ = ffn_kept[layer]
        if name == "out":
            d_ffn, d_resid_two, small_out[layer], kept, sent = out_backward(
                layer, way, grad, unit_two, inverse_two, hidden
            )
        elif name == "in":
            d_resid, small_in[layer], bias_grads[layer], kept, sent = in_backward(
                layer, way, d_ffn, d_resid_two, unit_one, inverse_one, slope
            )
        else:
            small_others = ()
            if layer == 0:
                small_others = (
                    small_out[0],
                    small_in[0],
                    bias_grads[0],
                    small_out[1],
                    small_in[1],
                    bias_grads[1],
                    small_attn[1],
                )
            grad, small_attn[layer], kept, sent = attn_backward(
                layer, way, d_resid, inputs[layer], qkv_rows, probs, context, small_others
            )
        slabs[which] = Slab(way, BACKS[which], wide_count, kept, sent)
    qkv_grad, o_grad, *vectors = unpacked["attn"]
    in_grad, out_grad = unpacked["in"][0], unpacked["out"][0]
    return (
        mixed_out,
        grad,
        qkv_grad,
        vectors[0],
        vectors[1],
        o_grad,
        vectors[2],
        vectors[3],
        vectors[4],
        in_grad,
        vectors[8],
        out_grad,
        vectors[5],
        vectors[6],
        vectors[7],
    )


def solution(mesh):
    by_table = P(("wide", "narrow"), None)
    matrix = P(None, "narrow", None)
    vector = P(None, "narrow")
    return jax.shard_map(
        body,
        mesh=mesh,
        in_specs=(
            by_table,
            by_table,
            by_table,
            P(("wide", "narrow")),
            matrix,
            vector,
            vector,
            matrix,
            vector,
            vector,
            vector,
            matrix,
            vector,
            matrix,
            vector,
            vector,
            vector,
        ),
        out_specs=(
            by_table,
            by_table,
            matrix,
            vector,
            vector,
            matrix,
            vector,
            vector,
            vector,
            matrix,
            vector,
            matrix,
            vector,
            vector,
            vector,
        ),
        check_vma=False,
    )
```

```python
import functools
import math

import jax
import jax.numpy as jnp
from jax import lax
from jax.experimental import pallas as pl
from jax.experimental.pallas import tpu as pltpu
from jax.sharding import PartitionSpec as P

HEADS = 12
norm_eps = 1e-12
masked_score = -1000000000.0
low = jnp.bfloat16
f32 = jnp.float32
VMEM_BYTES = 56 * 1024 * 1024
HALVINGS = 2


def swap(value, axis, bit):
    count = lax.axis_size(axis)
    return lax.ppermute(value, axis, [(i, i ^ bit) for i in range(count)])


def dot(a, b):
    return jnp.dot(a, b, preferred_element_type=f32)


def dot_nt(a, b):
    return lax.dot_general(a, b, (((1,), (1,)), ((), ())), preferred_element_type=f32)


def dot_tn(a, b):
    return lax.dot_general(a, b, (((0,), (0,)), ((), ())), preferred_element_type=f32)


def normalize(residual):
    center = residual - jnp.mean(residual, axis=-1, keepdims=True)
    inverse = lax.rsqrt(jnp.mean(center * center, axis=-1, keepdims=True) + norm_eps)
    return center * inverse, inverse


def normalize_back(grad_unit, unit, inverse):
    centered = grad_unit - jnp.mean(grad_unit, axis=-1, keepdims=True)
    return inverse * (centered - unit * jnp.mean(grad_unit * unit, axis=-1, keepdims=True))


def position(wide_bits, mode):
    y, z = wide_bits & 1, wide_bits >> 1
    return {"hy": y, "hz": z}.get(mode, wide_bits)


def weight_copies(ids, layer, pieces, mode, target, columns, sems, base):
    own, core, near, diagonal = pieces
    rows = own.shape[1]
    parts = 4 if mode[0] == "q" else 2
    step = rows // parts
    copies = []

    def add(source, start, count):
        where = target.at[pl.ds(pl.multiple_of(start, step), count), :]
        copies.append(pltpu.make_async_copy(source, where, sems.at[base + len(copies)]))

    add(own.at[layer], ids[0] * rows, rows)
    add(core.at[layer], ids[1] * rows, rows)
    at = pl.ds(columns, target.shape[1])
    for shard, owner in ((near, ids[2]), (diagonal, ids[3])):
        for part in range(parts):
            start = owner * rows + (position(ids[5], mode) ^ part) * step
            add(shard.at[pl.ds(part * step, step), at], start, step)
    return copies


def begin(copies):
    for copy in copies:
        copy.start()


def finish(copies):
    for copy in copies:
        copy.wait()


def attn_copies(layer, ids, refs, mode, w_qkv, w_o, sems):
    qkv_own, qkv_core, o_own, o_core, near, diagonal = refs
    qkv = weight_copies(ids, layer, (qkv_own, qkv_core, near, diagonal), mode, w_qkv, 0, sems, 0)
    o = weight_copies(ids, layer, (o_own, o_core, near, diagonal), mode, w_o, w_qkv.shape[1], sems, 10)
    return qkv, o


def pack_kernel(*refs):
    shorts, in_bias, packed = refs[:8], refs[8], refs[9]
    layers, share = shorts[0].shape
    for layer in range(layers):
        for i, short in enumerate(shorts):
            packed[layer, i : i + 1, :] = short[layer : layer + 1, :].astype(f32)
        for i in range(4):
            packed[layer, 8 + i : 9 + i, :] = in_bias[layer : layer + 1, i * share : (i + 1) * share].astype(f32)


def attn_fwd_kernel(layer, mode, ids, length, x, cell_row, small, *rest):
    weights, rest = rest[:6], rest[6:]
    qkv_rows, probs, context, unit_out, inverse_out, w_qkv, w_o, mask, sems = rest
    tokens, width = x.shape
    qkv_copies, o_copies = attn_copies(layer, ids, weights, mode, w_qkv, w_o, sems)
    begin(qkv_copies)
    begin(o_copies)
    position = lax.broadcasted_iota(jnp.int32, (tokens, 1), 0)
    query_cell = cell_row[...]
    square = (tokens, tokens)
    diagonal = lax.broadcasted_iota(jnp.int32, square, 0) == lax.broadcasted_iota(jnp.int32, square, 1)
    key_cell = jnp.sum(jnp.where(diagonal, query_cell, 0), axis=1, keepdims=True)
    allowed = (query_cell == key_cell) | (key_cell == 0) | (query_cell == 0)
    allowed = allowed & (position < length[0])
    mask[...] = jnp.where(allowed, 0.0, masked_score)
    scale = 1.0 / math.sqrt(width // HEADS)
    finish(qkv_copies)
    for part in range(3):
        columns = slice(part * width, (part + 1) * width)
        rows = dot(x[...], w_qkv[:, columns])
        if part != 1:
            rows = rows + small[layer, part // 2 : part // 2 + 1, :]
        if part == 0:
            rows = rows * scale
        qkv_rows[:, columns] = rows.astype(low)

    pair_width = 2 * width // HEADS
    first = lax.broadcasted_iota(jnp.int32, (1, pair_width), 1) < pair_width // 2

    for pair in range(HEADS // 2):
        at = slice(pair * pair_width, (pair + 1) * pair_width)
        query = qkv_rows[:, at]
        key = qkv_rows[:, width + at.start : width + at.stop]
        value = qkv_rows[:, 2 * width + at.start : 2 * width + at.stop]
        sides = []
        for side in range(2):
            mine = first if side == 0 else jnp.logical_not(first)
            scores = dot_nt(key, jnp.where(mine, query, jnp.zeros_like(query))) + mask[...]
            shifted = jnp.exp(scores - jnp.max(scores, axis=0, keepdims=True))
            total = jnp.sum(shifted, axis=0, keepdims=True)
            prob = (shifted * (1.0 / total)).astype(low)
            probs[2 * pair + side] = prob
            sides.append(dot_tn(prob, value))
        context[:, at] = jnp.where(first, sides[0], sides[1]).astype(low)

    finish(o_copies)
    residual = x[...].astype(f32) + (dot(context[...], w_o[...]) + small[layer, 2:3, :])
    unit, inverse = normalize(residual)
    unit_out[...] = unit
    inverse_out[...] = inverse


def gelu_and_slope(x):
    t = 1.0 / (1.0 + (0.3275911 * math.sqrt(0.5)) * jnp.abs(x))
    bell = jnp.exp(-0.5 * x * x)
    series = 1.421413741 + t * (-1.453152027 + t * 1.061405429)
    series = t * (0.254829592 + t * (-0.284496736 + t * series))
    tail = 0.5 * series * bell
    cdf = jnp.where(x >= 0.0, 1.0 - tail, tail)
    return (x * cdf).astype(low), cdf + x * (bell * (1.0 / math.sqrt(2.0 * math.pi)))


def ffn_in_kernel(layer, mode, ids, unit_one, in_bias, small, *rest):
    weights, rest = rest[:4], rest[4:]
    hidden_out, slope_out, w_in, normed_low, hidden, slope, sems, out_sems = rest
    copies = weight_copies(ids, layer, weights, mode, w_in, 0, sems, 0)
    begin(copies)
    normed = unit_one[...] * small[layer, 3:4, :] + small[layer, 4:5, :]
    normed_low[...] = normed.astype(low)
    finish(copies)
    tile = w_in.shape[1] // 4
    going = []
    for t in range(4):
        columns = pl.ds(t * tile, tile)
        pre = dot(normed_low[...], w_in[:, columns]) + in_bias[layer, :, columns]
        hidden[:, columns], slope[:, columns] = gelu_and_slope(pre)
        leaving = [
            pltpu.make_async_copy(hidden.at[:, columns], hidden_out.at[:, columns], out_sems.at[2 * t]),
            pltpu.make_async_copy(slope.at[:, columns], slope_out.at[:, columns], out_sems.at[2 * t + 1]),
        ]
        begin(leaving)
        going += leaving
    finish(going)


def ffn_out_kernel(layer, mode, ids, unit_one, hidden, small, *rest):
    weights, rest = rest[:4], rest[4:]
    unit_out, inverse_out, result, w_out, sems = rest
    copies = weight_copies(ids, layer, weights, mode, w_out, 0, sems, 0)
    begin(copies)
    normed = unit_one[...] * small[layer, 3:4, :] + small[layer, 4:5, :]
    finish(copies)
    unit, inverse = normalize(normed + (dot(hidden[...], w_out[...]) + small[layer, 5:6, :]))
    unit_out[...] = unit
    inverse_out[...] = inverse
    result[...] = (unit * small[layer, 6:7, :] + small[layer, 7:8, :]).astype(low)


WIDE_BIT = {"y": 0, "z": 1}


def place_of(ids, owner, piece, way):
    away = None if owner is None else ids[0] ^ owner
    off = None if piece is None else piece ^ ids[5]
    place = [None if away is None else away & 1]
    for name in way:
        if name == "x":
            place.append(pl.ds(0, 2) if away is None else away >> 1)
        else:
            place.append(pl.ds(0, 2) if off is None else (off >> WIDE_BIT[name]) & 1)
    return tuple(place) + (pl.ds(0, 2) if piece is None else piece >> 2,)


def store_rows(stage, ids, product, piece, way):
    share = product.shape[0] // 4
    for owner in range(4):
        block = product[owner * share : (owner + 1) * share].astype(low)
        stage[place_of(ids, owner, piece, way) + (pl.ds(0, share),)] = block


def piece_copies(stage, ids, piece, way, kept, sent, sems, turn):
    at = place_of(ids, None, piece, way)[1:]
    copies = [
        pltpu.make_async_copy(stage.at[(1,) + at], sent.at[at], sems.at[2 * turn]),
        pltpu.make_async_copy(stage.at[(0,) + at], kept.at[at], sems.at[2 * turn + 1]),
    ]
    begin(copies)
    return copies


def out_bwd_kernel(layer, way, ids, grad, unit_two, inverse_two, hidden, small, *rest):
    d_ffn, d_resid_two, small_grads, kept, sent, stage, out_sems = rest
    g = grad[...].astype(f32)
    unit = unit_two[...]
    small_grads[0:1, :] = jnp.sum(g * unit, axis=0, keepdims=True)
    small_grads[1:2, :] = jnp.sum(g, axis=0, keepdims=True)
    d_two = normalize_back(g * small[layer, 6:7, :], unit, inverse_two[...])
    d_resid_two[...] = d_two
    d_low = d_two.astype(low)
    d_ffn[...] = d_low
    small_grads[2:3, :] = jnp.sum(d_low.astype(f32), axis=0, keepdims=True)
    small_grads[3:8, :] = jnp.zeros((5, unit.shape[1]), f32)
    tile = hidden.shape[1] // 8
    share = d_ffn.shape[1] // 4
    waits = []
    for owner in range(4):
        for half in range(2):
            columns = slice((2 * owner + half) * tile, (2 * owner + half + 1) * tile)
            out_grad = dot_tn(hidden[:, columns], d_ffn[...])
            for row_group in range(2):
                for column_group in range(2):
                    piece = (half * 2 + row_group) * 2 + column_group
                    block = out_grad[
                        row_group * share : (row_group + 1) * share,
                        column_group * tile : (column_group + 1) * tile,
                    ]
                    stage[place_of(ids, owner, piece, way)] = block.astype(low)
        core, *at = place_of(ids, owner, None, way)
        at = tuple(at)
        to_kept = pltpu.make_async_copy(stage.at[(0,) + at], kept.at[at], out_sems.at[owner])
        to_sent = pltpu.make_async_copy(stage.at[(1,) + at], sent.at[at], out_sems.at[owner])
        pl.when(core == 0)(to_kept.start)
        pl.when(core == 1)(to_sent.start)
        waits.append(to_kept)
    finish(waits)


def in_bwd_kernel(layer, way, modes, ids, d_ffn, unit_one, inverse_one, small, resid_in, slope_in, *rest):
    weights, rest = rest[:8], rest[8:]
    d_resid, small_grads, in_bias_grad, kept, sent = rest[:5]
    w_in, w_out, d_pre, normed_t, slope, d_resid_two, stage, sems, out_sems, more_sems = rest[5:]
    in_copies = weight_copies(ids, layer, weights[:4], modes[0], w_in, 0, sems, 0)
    out_copies = weight_copies(ids, layer, weights[4:], modes[1], w_out, 0, sems, 10)
    slope_copy = pltpu.make_async_copy(slope_in, slope, more_sems.at[0])
    resid_copy = pltpu.make_async_copy(resid_in, d_resid_two, more_sems.at[1])
    begin(out_copies + [slope_copy] + in_copies + [resid_copy])
    normed = unit_one[...] * small[layer, 3:4, :] + small[layer, 4:5, :]
    normed_t[...] = normed.astype(low).T
    finish(out_copies)
    tile = w_in.shape[1] // 4
    going = []
    slope_copy.wait()
    for t in range(4):
        columns = slice(t * tile, (t + 1) * tile)
        d_hidden = dot_nt(d_ffn[...], w_out[columns, :])
        d_tile = (d_hidden * slope[:, columns]).astype(low)
        d_pre[:, columns] = d_tile
        in_bias_grad[:, columns] = jnp.sum(d_tile.astype(f32), axis=0, keepdims=True)
        product = dot(normed_t[...], d_tile)
        for half in range(2):
            piece = 2 * t + half
            store_rows(stage, ids, product[:, half * tile // 2 : (half + 1) * tile // 2], piece, way)
            going += piece_copies(stage, ids, piece, way, kept, sent, out_sems, piece)
    resid_copy.wait()
    finish(in_copies)
    d_normed = d_resid_two[...] + dot_nt(d_pre[...], w_in[...])
    unit = unit_one[...]
    small_grads[0:1, :] = jnp.sum(d_normed * unit, axis=0, keepdims=True)
    small_grads[1:2, :] = jnp.sum(d_normed, axis=0, keepdims=True)
    small_grads[2:8, :] = jnp.zeros((6, unit.shape[1]), f32)
    d_resid[...] = normalize_back(d_normed * small[layer, 3:4, :], unit, inverse_one[...])
    finish(going)


def attn_bwd_kernel(layer, way, mode, ids, d_resid, x, qkv_rows, probs, context, *rest):
    weights, others, rest = rest[:6], rest[6:-13], rest[-13:]
    d_input, small_grads, kept, sent = rest[:4]
    w_qkv, w_o, d_attn, d_context, d_qkv, x_t, stage, sems, out_sems = rest[4:]
    tokens, width = x.shape
    qkv_copies, o_copies = attn_copies(layer, ids, weights, mode, w_qkv, w_o, sems)
    begin(o_copies)
    begin(qkv_copies)
    d_low = d_resid[...].astype(low)
    d_attn[...] = d_low
    small_grads[2:3, :] = jnp.sum(d_low.astype(f32), axis=0, keepdims=True)
    x_t[...] = x[...].T
    tile = width // 2
    product = dot_tn(context[...], d_attn[...])
    for half in range(2):
        store_rows(stage, ids, product[:, half * tile : (half + 1) * tile], 6 + half, way)
    finish(o_copies)
    d_context[...] = dot_nt(d_attn[...], w_o[...]).astype(low)
    pair_width = 2 * width // HEADS
    first = lax.broadcasted_iota(jnp.int32, (1, pair_width), 1) < pair_width // 2
    scale = 1.0 / math.sqrt(width // HEADS)

    for pair in range(HEADS // 2):
        at_query = slice(pair * pair_width, (pair + 1) * pair_width)
        at_key = slice(width + at_query.start, width + at_query.stop)
        at_value = slice(2 * width + at_query.start, 2 * width + at_query.stop)
        query, key, value = qkv_rows[:, at_query], qkv_rows[:, at_key], qkv_rows[:, at_value]
        d_ctx = d_context[:, at_query]
        sides = []
        for side in range(2):
            mine = first if side == 0 else jnp.logical_not(first)
            prob_low = probs[2 * pair + side]
            prob = prob_low.astype(f32)
            d_prob = dot_nt(value, jnp.where(mine, d_ctx, jnp.zeros_like(d_ctx)))
            inner = jnp.sum(prob * d_prob, axis=0, keepdims=True)
            d_scores = (prob * (d_prob - inner)).astype(low)
            sides.append((dot_tn(d_scores, key), dot(d_scores, query), dot(prob_low, d_ctx)))
        d_qkv[:, at_query] = (jnp.where(first, sides[0][0], sides[1][0]) * scale).astype(low)
        d_qkv[:, at_key] = jnp.where(first, sides[0][1], sides[1][1]).astype(low)
        d_qkv[:, at_value] = jnp.where(first, sides[0][2], sides[1][2]).astype(low)

    small_grads[0:1, :] = jnp.sum(d_qkv[:, :width].astype(f32), axis=0, keepdims=True)
    small_grads[1:2, :] = jnp.sum(d_qkv[:, 2 * width :].astype(f32), axis=0, keepdims=True)
    small_grads[3:8, :] = jnp.zeros((5, width), f32)
    if others:
        share = width // 4
        sources = small_sources(layer, small_grads, others)
        for owner in range(4):
            for piece in range(8):
                lines = []
                for source, row, start, step in sources[3 * piece : 3 * piece + 3]:
                    line = source[row : row + 1, start + owner * step : start + owner * step + share]
                    lines.append(jnp.concatenate([line, jnp.zeros_like(line)], axis=1))
                lines.append(jnp.zeros((SMALL_ROWS - 3, tile), f32))
                block = jnp.concatenate(lines, axis=0).astype(low)
                stage[place_of(ids, owner, piece, way) + (pl.ds(share, SMALL_ROWS),)] = block
    going = []
    for part in (3, 0, 1, 2):
        if part < 3:
            product = dot(x_t[...], d_qkv[:, part * width : (part + 1) * width])
        for half in range(2):
            piece = 2 * part + half
            if part < 3:
                store_rows(stage, ids, product[:, half * tile : (half + 1) * tile], piece, way)
            going += piece_copies(stage, ids, piece, way, kept, sent, out_sems, piece)
    finish(qkv_copies)
    d_input[...] = (d_resid[...] + dot_nt(d_qkv[...], w_qkv[...])).astype(low)
    finish(going)


SMALL_ROWS = 16
SMALL_LINES = (("attn", 0), ("attn", 1), ("attn", 2), ("in", 0), ("in", 1), ("out", 2), ("out", 0), ("out", 1))


def small_sources(layer, own, others):
    found = []
    out_0, in_0, bias_0, out_1, in_1, bias_1, attn_1 = others
    refs = ({"attn": own, "in": in_0, "out": out_0}, {"attn": attn_1, "in": in_1, "out": out_1})
    width = own.shape[1]
    for of_layer, bias in zip(refs, (bias_0, bias_1)):
        found += [(of_layer[name], row, 0, width // 4) for name, row in SMALL_LINES]
        found += [(bias, 0, i * (width // 4), width) for i in range(4)]
    return found


def unpack_kernel(layer, slab, back, earlier, ids, near, far, *rest):
    outs = rest[earlier:-4]
    buffer, wide_buffer, in_sems, out_sems = rest[-4:]
    share, tile = wide_buffer.shape[1:]

    def fetch(piece, ref, index):
        return pltpu.make_async_copy(ref.at[index], buffer.at[piece], in_sems.at[piece])

    for piece in range(8):
        off = piece ^ ids[5]
        inner, outer = [(off >> WIDE_BIT[name]) & 1 for name in back]
        pl.when(outer == 0)(fetch(piece, near, (inner, piece >> 2)).start)
        pl.when(outer == 1)(fetch(piece, far, (inner, piece >> 2)).start)

    copies = []
    for piece in range(8):
        fetch(piece, near, (0, 0)).wait()
        wide_buffer[piece] = buffer[piece, :share].astype(f32)
        columns = pl.ds(piece * tile, tile)
        if slab == "in":
            target = outs[0].at[layer, :, columns]
        elif slab == "out":
            rows = pl.ds((piece // 2) * share, share)
            target = outs[0].at[layer, rows, pl.ds((piece % 2) * tile, tile)]
        elif piece < 6:
            target = outs[0].at[layer, :, columns]
        else:
            target = outs[1].at[layer, :, pl.ds((piece - 6) * tile, tile)]
        copies.append(pltpu.make_async_copy(wide_buffer.at[piece], target, out_sems.at[piece]))
        copies[-1].start()
    if slab == "attn" and layer == 0:
        for line in range(24):
            of_layer, which = line // 12, line % 12
            row = share + line % 3
            values = buffer[line // 3, row : row + 1, :share].astype(f32)
            if which < 8:
                outs[2 + which][of_layer : of_layer + 1, :] = values
            else:
                at = (which - 8) * share
                outs[10][of_layer : of_layer + 1, at : at + share] = values
    else:
        outs[-1][...] = jnp.zeros(outs[-1].shape, f32)
    finish(copies)


SMEM = pl.BlockSpec(memory_space=pltpu.SMEM)
VMEM = pl.BlockSpec(memory_space=pltpu.VMEM)
ANY = pl.BlockSpec(memory_space=pl.ANY)


def call(kernel, name, time, in_specs, out_specs, out_shape, scratch, args, aliases=()):
    return pl.pallas_call(
        kernel,
        name=name,
        in_specs=in_specs,
        out_specs=out_specs,
        out_shape=out_shape,
        scratch_shapes=scratch,
        input_output_aliases=dict(aliases),
        compiler_params=pltpu.CompilerParams(vmem_limit_bytes=VMEM_BYTES),
        cost_estimate=pl.CostEstimate(
            flops=int(time * 1.1e9), bytes_accessed=int(time * 3.6e6), transcendentals=0
        ),
    )(*args)


def shape(dims, kind):
    return jax.ShapeDtypeStruct(dims, kind)


def added(a, b):
    return (a.astype(f32) + b.astype(f32)).astype(low)


WAYS = ("zxy", "xyz", "yxz", "zyx", "xyz", "xyz")
BACKS = ("zy", "zy", "zy", "yz", "zy", "zy")
PLAN = (
    "out1", "in1", 0, 1, "attn1", "out0", "in0", 0, 1, "attn0", 1, 0, 2, 4, 3, 1, 2, 4, 1, 0, 5, 3, 2, 0, 4,
    1, 2, 0, 3, 2, 4, 5, 3, 0, 5, 4, 2, 3, 5, 1, 3, 5, 4, 2, 5, 4, 3, 5,
)
MODES = ("qy", "hz", "qy", "hy", "qy", "hz")
FORWARD = (
    "h4", "h0", "h5", "g0", "g3", "pack", "sm", "h2", "h1", "g1", "x0", "g2", "c0", "h3", "c3", "A", "x2",
    "c2", "z0", "y0", "y2", "z2", "x1", "q0", "c1", "x3", "q2", "z1", "d0", "attn1", "x4", "d1", "fi1", "z4",
    "d2", "y3", "y4", "x5", "fo1", "d3", "attn2", "q4", "z5", "d4", "fi2", "d5", "fo2",
)
TIMES = {
    "pack": 3, "attn1": 0.3, "fi1": 0.3, "fo1": 8, "attn2": 0.3, "fi2": 1, "fo2": 5,
    "out_bwd1": 20, "in_bwd1": 20, "attn_bwd1": 0.3, "out_bwd0": 2, "in_bwd0": 1, "attn_bwd0": 8,
}


class Order:
    def __init__(self, ids):
        self.ids = ids

    def wait(self, values):
        values, self.ids = lax.optimization_barrier((values, self.ids))
        return values


STEPS = {"x": ("narrow", 2), "y": ("wide", 1), "z": ("wide", 2)}


class Slab:
    def __init__(self, way, back, wide_count, kept, sent):
        self.kept = kept
        self.way, self.back = way, back
        self.rest = [1 << b for b in range(HALVINGS, wide_count.bit_length() - 1)]
        self.flying = swap(sent, "narrow", 1)
        self.stage = 0

    def step(self, order):
        received = order.wait(self.flying)
        stage, way = self.stage, self.way
        if stage < len(way):
            send = order.wait(added(self.kept[1], received[1]))
            self.kept = added(self.kept[0], received[0])
            self.flying = swap(send, *STEPS[way[stage]])
        elif stage < len(way) + 1 + len(self.back):
            if stage == len(way):
                piece = added(self.kept, received)
                for bit in self.rest[:-1]:
                    piece = added(piece, swap(piece, "wide", bit))
                self.kept = order.wait(piece)
                self.flying = swap(self.kept, "wide", self.rest[-1])
            else:
                if stage == len(way) + 1:
                    self.block = added(self.kept, received)[None]
                else:
                    self.block = jnp.concatenate([self.block, received], axis=0)
                self.block = order.wait(self.block)
                self.flying = swap(self.block, *STEPS[self.back[stage - len(way) - 1]])
        else:
            self.far = received
        self.stage += 1

    def ended(self):
        return self.stage == len(self.way) + len(self.back) + 2


def body(
    tables_in,
    cotangent,
    cell_ids,
    lengths,
    qkv_weight,
    q_bias,
    v_bias,
    o_weight,
    o_bias,
    norm1_gain,
    norm1_bias,
    in_weight,
    in_bias,
    out_weight,
    out_bias,
    norm2_gain,
    norm2_bias,
):
    tokens, width = tables_in.shape
    layers, share, ffn = in_weight.shape
    ffn_share = out_weight.shape[1]
    wide_count = lax.axis_size("wide")
    assert wide_count & (wide_count - 1) == 0 and wide_count > 1 << HALVINGS and lax.axis_size("narrow") == 4
    tile = ffn // 8
    me = lax.axis_index("narrow").astype(jnp.int32)
    wide_me = lax.axis_index("wide").astype(jnp.int32)
    y = wide_me & 1
    ids = jnp.stack([me, me ^ 1, me ^ 2, me ^ 3, y, wide_me & (2**HALVINGS - 1)])

    order = Order(ids)

    def part_of(weight, layer, mode):
        rows = weight.shape[1] // (4 if mode[0] == "q" else 2)
        start = position(wide_me & 3, mode) * rows
        return lax.dynamic_slice(weight, (layer, start, 0), (1, rows, weight.shape[2]))[0]

    own = (qkv_weight, o_weight, in_weight, out_weight)
    parts = []
    for layer in range(layers):
        attn_mode, in_mode, out_mode = MODES[3 * layer : 3 * layer + 3]
        joint = [part_of(weight, layer, attn_mode) for weight in own[:2]]
        parts += [jnp.concatenate(joint, axis=1), part_of(in_weight, layer, in_mode), part_of(out_weight, layer, out_mode)]
    near, diagonal, core = [None] * 6, [None] * 6, [None] * 4
    transfers = [{} for _ in range(6)]

    def joined(i, *names):
        near[i] = order.wait(jnp.concatenate([transfers[i][name] for name in names], axis=0))
        transfers[i]["d"] = swap(near[i], "narrow", 1)

    def weight_step(kind, i):
        moving, mode = transfers[i], MODES[i]
        if kind == "h":
            moving["x"] = swap(order.wait(parts[i]), "narrow", 2)
            return
        moving[kind] = order.wait(moving[kind])
        if kind == "x":
            for name, bit in (("y", 1), ("z", 2)):
                if mode[0] == "q" or mode[1] == name:
                    moving[name] = swap(moving["x"], "wide", bit)
        elif kind == "d":
            diagonal[i] = moving["d"]
        elif kind == "q":
            joined(i, "x", "y", "z", "q")
        elif mode[0] == "h":
            joined(i, "x", kind)
        elif mode[1] != kind:
            moving["q"] = swap(moving[kind], "wide", 1 if mode[1] == "y" else 2)

    def in_order(low_one, high_one, bit):
        swapped = (me & bit) != 0
        return jnp.stack([jnp.where(swapped, high_one, low_one), jnp.where(swapped, low_one, high_one)])

    def attn_weights(layer):
        return (qkv_weight, core[0], o_weight, core[1], near[3 * layer], diagonal[3 * layer])

    def in_weights(layer):
        return (in_weight, core[2], near[3 * layer + 1], diagonal[3 * layer + 1])

    def out_weights(layer):
        return (out_weight, core[3], near[3 * layer + 2], diagonal[3 * layer + 2])

    w_qkv = pltpu.VMEM((width, 3 * width), low)
    w_o = pltpu.VMEM((width, width), low)
    w_in = pltpu.VMEM((width, ffn), low)
    w_out = pltpu.VMEM((ffn, width), low)
    copy_sems = pltpu.SemaphoreType.DMA((20,))
    piece_sems = pltpu.SemaphoreType.DMA((16,))
    rows_f32 = shape((tokens, width), f32)
    rows_low = shape((tokens, width), low)
    column_f32 = shape((tokens, 1), f32)
    eight_f32 = shape((8, width), f32)

    def pieces(rows):
        return [shape((2, 2, 2, 2, rows, tile), low)] * 2

    def stage(rows):
        return pltpu.VMEM((2, 2, 2, 2, 2, rows, tile), low)

    def tie(outs, which):
        outs = list(outs)
        outs[which] = order.wait(outs[which])
        return outs

    def attn_forward(layer, x):
        x = order.wait(x)
        outs = call(
            functools.partial(attn_fwd_kernel, layer, MODES[3 * layer]),
            "attn_fwd",
            TIMES["attn%d" % (layer + 1)],
            [SMEM, SMEM] + [VMEM] * 3 + [ANY] * 6,
            [VMEM] * 5,
            [shape((tokens, 3 * width), low), shape((HEADS, tokens, tokens), low), rows_low, rows_f32, column_f32],
            [w_qkv, w_o, pltpu.VMEM((tokens, tokens), f32), copy_sems],
            (order.ids, lengths, x, cell_ids, small) + attn_weights(layer),
        )
        return tie(outs, 3)

    def ffn_in(layer, unit_one):
        unit_one = order.wait(unit_one)
        outs = call(
            functools.partial(ffn_in_kernel, layer, MODES[3 * layer + 1]),
            "ffn_in",
            TIMES["fi%d" % (layer + 1)],
            [SMEM] + [VMEM] * 3 + [ANY] * 4,
            [ANY] * 2,
            [shape((tokens, ffn), low), shape((tokens, ffn), f32)],
            [
                w_in,
                pltpu.VMEM((tokens, width), low),
                pltpu.VMEM((tokens, ffn), low),
                pltpu.VMEM((tokens, ffn), f32),
                copy_sems,
                piece_sems,
            ],
            (order.ids, unit_one, full_in_bias, small) + in_weights(layer),
        )
        return tie(outs, 0)

    def ffn_out(layer, unit_one, hidden):
        hidden = order.wait(hidden)
        outs = call(
            functools.partial(ffn_out_kernel, layer, MODES[3 * layer + 2]),
            "ffn_out",
            TIMES["fo%d" % (layer + 1)],
            [SMEM] + [VMEM] * 3 + [ANY] * 4,
            [VMEM] * 3,
            [rows_f32, column_f32, rows_low],
            [w_out, copy_sems],
            (order.ids, unit_one, hidden, small) + out_weights(layer),
        )
        return tie(outs, 2)

    def out_backward(layer, way, grad, unit_two, inverse_two, hidden):
        grad = order.wait(grad)
        outs = call(
            functools.partial(out_bwd_kernel, layer, way),
            "out_bwd",
            TIMES["out_bwd%d" % layer],
            [SMEM] + [VMEM] * 5,
            [VMEM] * 3 + [ANY] * 2,
            [rows_low, rows_f32, eight_f32] + pieces(share),
            [stage(share), pltpu.SemaphoreType.DMA((4,))],
            (order.ids, grad, unit_two, inverse_two, hidden, small),
        )
        return tie(outs, 0)

    def in_backward(layer, way, d_ffn, d_resid_two, unit_one, inverse_one, slope):
        d_ffn = order.wait(d_ffn)
        outs = call(
            functools.partial(in_bwd_kernel, layer, way, MODES[3 * layer + 1 : 3 * layer + 3]),
            "in_bwd",
            TIMES["in_bwd%d" % layer],
            [SMEM] + [VMEM] * 4 + [ANY] * 10,
            [VMEM] * 3 + [ANY] * 2,
            [rows_f32, eight_f32, shape((1, ffn), f32)] + pieces(share),
            [
                w_in,
                w_out,
                pltpu.VMEM((tokens, ffn), low),
                pltpu.VMEM((width, tokens), low),
                pltpu.VMEM((tokens, ffn), f32),
                pltpu.VMEM((tokens, width), f32),
                stage(share),
                copy_sems,
                piece_sems,
                pltpu.SemaphoreType.DMA((2,)),
            ],
            (order.ids, d_ffn, unit_one, inverse_one, small, d_resid_two, slope)
            + in_weights(layer)
            + out_weights(layer),
        )
        return tie(outs, 0)

    def attn_backward(layer, way, d_resid, x, qkv_rows, probs, context, small_others):
        d_resid = order.wait(d_resid)
        rows = share + (SMALL_ROWS if small_others else 0)
        outs = call(
            functools.partial(attn_bwd_kernel, layer, way, MODES[3 * layer]),
            "attn_bwd",
            TIMES["attn_bwd%d" % layer],
            [SMEM] + [VMEM] * 5 + [ANY] * 6 + [VMEM] * len(small_others),
            [VMEM] * 2 + [ANY] * 2,
            [rows_low, eight_f32] + pieces(rows),
            [
                w_qkv,
                w_o,
                pltpu.VMEM((tokens, width), low),
                pltpu.VMEM((tokens, width), low),
                pltpu.VMEM((tokens, 3 * width), low),
                pltpu.VMEM((width, tokens), low),
                stage(rows),
                copy_sems,
                piece_sems,
            ],
            (order.ids, d_resid, x, qkv_rows, probs, context) + attn_weights(layer) + tuple(small_others),
        )
        return tie(outs, 0)

    def unpack(layer, name, slab, earlier):
        dims = {
            "attn": [(layers, share, 3 * width), (layers, share, width)],
            "in": [(layers, share, ffn)],
            "out": [(layers, ffn_share, width)],
        }[name]
        last = name == "attn" and layer == 0
        extra = [(layers, share)] * 8 + [(layers, ffn_share)] if last else [(8, 128)]
        near, far = order.wait((slab.block, slab.far))
        rows = near.shape[2]
        outs = call(
            functools.partial(unpack_kernel, layer, name, slab.back, len(earlier)),
            "unpack",
            4,
            [SMEM] + [ANY] * (2 + len(earlier)),
            [ANY] * len(dims) + [VMEM] * len(extra),
            [shape(d, f32) for d in dims + extra],
            [
                pltpu.VMEM((8, rows, tile), low),
                pltpu.VMEM((8, share, tile), f32),
                pltpu.SemaphoreType.DMA((8,)),
                pltpu.SemaphoreType.DMA((8,)),
            ],
            (order.ids, near, far, *earlier),
            {3 + i: i for i in range(len(earlier))},
        )
        return tuple(tie(outs, 0))

    short = (q_bias, v_bias, o_bias, norm1_gain, norm1_bias, out_bias, norm2_gain, norm2_bias)
    inputs, attn_kept, ffn_kept = [tables_in], [], []
    for token in FORWARD:
        kind, i = (token[0], int(token[1])) if len(token) == 2 and token[1].isdigit() else (token, None)
        if kind == "g":
            core[i] = swap(order.wait(own[i]), "narrow", 1)
        elif kind == "c":
            core[i] = order.wait(core[i])
        elif i is not None:
            weight_step(kind, i)
        elif token == "pack":
            packed = call(
                pack_kernel,
                "pack",
                TIMES["pack"],
                [VMEM] * 9,
                VMEM,
                shape((layers, 12, share), f32),
                [],
                tuple(order.wait(short)) + (in_bias,),
            )
            packed = order.wait(packed)
            others = [lax.ppermute(packed, "narrow", [(j, j ^ away) for j in range(4)]) for away in (1, 2, 3)]
        elif token == "sm":
            others = order.wait(others)
        elif token == "A":
            packed = in_order(in_order(packed, others[0], 1), in_order(others[1], others[2], 1), 2)
            packed = packed.reshape(4, layers, 12, share)
            small = packed[:, :, :8].transpose(1, 2, 0, 3).reshape(layers, 8, width)
            full_in_bias = packed[:, :, 8:].transpose(1, 0, 2, 3).reshape(layers, 1, ffn)
            small, full_in_bias = order.wait((small, full_in_bias))
        elif token[:-1] == "attn":
            attn_kept.append(attn_forward(int(token[-1]) - 1, inputs[-1]))
        elif token[:-1] == "fi":
            ffn_kept.append(ffn_in(int(token[-1]) - 1, attn_kept[-1][3]))
        else:
            ffn_kept[-1] += ffn_out(int(token[-1]) - 1, attn_kept[-1][3], ffn_kept[-1][0])
            inputs.append(ffn_kept[-1][4])
    mixed_out = inputs[-1]

    slabs = [None] * 6
    grad = cotangent
    small_out, small_in, small_attn, bias_grads = [None] * 2, [None] * 2, [None] * 2, [None] * 2
    unpacked = {"attn": (), "in": (), "out": ()}
    for action in PLAN:
        if isinstance(action, int):
            slab = slabs[action]
            slab.step(order)
            if slab.ended():
                name = ("out", "in", "attn")[action % 3]
                unpacked[name] = unpack(layers - 1 - action // 3, name, slab, unpacked[name][: 2 if name == "attn" else 1])
            continue
        name, layer = action[:-1], int(action[-1])
        which = 3 * (layers - 1 - layer) + ("out", "in", "attn").index(name)
        way = WAYS[which]
        qkv_rows, probs, context, unit_one, inverse_one = attn_kept[layer]
        hidden, slope, unit_two, inverse_two, _ = ffn_kept[layer]
        if name == "out":
            d_ffn, d_resid_two, small_out[layer], kept, sent = out_backward(
                layer, way, grad, unit_two, inverse_two, hidden
            )
        elif name == "in":
            d_resid, small_in[layer], bias_grads[layer], kept, sent = in_backward(
                layer, way, d_ffn, d_resid_two, unit_one, inverse_one, slope
            )
        else:
            small_others = ()
            if layer == 0:
                small_others = (
                    small_out[0],
                    small_in[0],
                    bias_grads[0],
                    small_out[1],
                    small_in[1],
                    bias_grads[1],
                    small_attn[1],
                )
            grad, small_attn[layer], kept, sent = attn_backward(
                layer, way, d_resid, inputs[layer], qkv_rows, probs, context, small_others
            )
        slabs[which] = Slab(way, BACKS[which], wide_count, kept, sent)
    qkv_grad, o_grad, *vectors = unpacked["attn"]
    in_grad, out_grad = unpacked["in"][0], unpacked["out"][0]
    return (
        mixed_out,
        grad,
        qkv_grad,
        vectors[0],
        vectors[1],
        o_grad,
        vectors[2],
        vectors[3],
        vectors[4],
        in_grad,
        vectors[8],
        out_grad,
        vectors[5],
        vectors[6],
        vectors[7],
    )


def solution(mesh):
    by_table = P(("wide", "narrow"), None)
    matrix = P(None, "narrow", None)
    vector = P(None, "narrow")
    return jax.shard_map(
        body,
        mesh=mesh,
        in_specs=(
            by_table,
            by_table,
            by_table,
            P(("wide", "narrow")),
            matrix,
            vector,
            vector,
            matrix,
            vector,
            vector,
            vector,
            matrix,
            vector,
            matrix,
            vector,
            vector,
            vector,
        ),
        out_specs=(
            by_table,
            by_table,
            matrix,
            vector,
            vector,
            matrix,
            vector,
            vector,
            vector,
            matrix,
            vector,
            matrix,
            vector,
            vector,
            vector,
        ),
        check_vma=False,
    )
```

```python
import functools
import math

import jax
import jax.numpy as jnp
from jax import lax
from jax.experimental import pallas as pl
from jax.experimental.pallas import tpu as pltpu
from jax.sharding import PartitionSpec as P

HEADS = 12
norm_eps = 1e-12
masked_score = -1000000000.0
low = jnp.bfloat16
f32 = jnp.float32
VMEM_BYTES = 56 * 1024 * 1024
HALVINGS = 2


def swap(value, axis, bit):
    count = lax.axis_size(axis)
    return lax.ppermute(value, axis, [(i, i ^ bit) for i in range(count)])


def dot(a, b):
    return jnp.dot(a, b, preferred_element_type=f32)


def dot_nt(a, b):
    return lax.dot_general(a, b, (((1,), (1,)), ((), ())), preferred_element_type=f32)


def dot_tn(a, b):
    return lax.dot_general(a, b, (((0,), (0,)), ((), ())), preferred_element_type=f32)


def normalize(residual):
    center = residual - jnp.mean(residual, axis=-1, keepdims=True)
    inverse = lax.rsqrt(jnp.mean(center * center, axis=-1, keepdims=True) + norm_eps)
    return center * inverse, inverse


def normalize_back(grad_unit, unit, inverse):
    centered = grad_unit - jnp.mean(grad_unit, axis=-1, keepdims=True)
    return inverse * (centered - unit * jnp.mean(grad_unit * unit, axis=-1, keepdims=True))


def position(wide_bits, mode):
    y, z = wide_bits & 1, wide_bits >> 1
    return {"hy": y, "hz": z}.get(mode, wide_bits)


def weight_copies(ids, layer, pieces, mode, target, columns, sems, base):
    own, core, near, diagonal = pieces
    rows = own.shape[1]
    parts = 4 if mode[0] == "q" else 2
    step = rows // parts
    copies = []

    def add(source, start, count):
        where = target.at[pl.ds(pl.multiple_of(start, step), count), :]
        copies.append(pltpu.make_async_copy(source, where, sems.at[base + len(copies)]))

    add(own.at[layer], ids[0] * rows, rows)
    add(core.at[layer], ids[1] * rows, rows)
    at = pl.ds(columns, target.shape[1])
    for shard, owner in ((near, ids[2]), (diagonal, ids[3])):
        for part in range(parts):
            start = owner * rows + (position(ids[5], mode) ^ part) * step
            add(shard.at[pl.ds(part * step, step), at], start, step)
    return copies


def begin(copies):
    for copy in copies:
        copy.start()


def finish(copies):
    for copy in copies:
        copy.wait()


def attn_copies(layer, ids, refs, mode, w_qkv, w_o, sems):
    qkv_own, qkv_core, o_own, o_core, near, diagonal = refs
    qkv = weight_copies(ids, layer, (qkv_own, qkv_core, near, diagonal), mode, w_qkv, 0, sems, 0)
    o = weight_copies(ids, layer, (o_own, o_core, near, diagonal), mode, w_o, w_qkv.shape[1], sems, 10)
    return qkv, o


def pack_kernel(*refs):
    shorts, in_bias, packed = refs[:8], refs[8], refs[9]
    layers, share = shorts[0].shape
    for layer in range(layers):
        for i, short in enumerate(shorts):
            packed[layer, i : i + 1, :] = short[layer : layer + 1, :].astype(f32)
        for i in range(4):
            packed[layer, 8 + i : 9 + i, :] = in_bias[layer : layer + 1, i * share : (i + 1) * share].astype(f32)


def attn_fwd_kernel(layer, mode, ids, length, x, cell_row, small, *rest):
    weights, rest = rest[:6], rest[6:]
    qkv_rows, probs, context, unit_out, inverse_out, w_qkv, w_o, mask, sems = rest
    tokens, width = x.shape
    qkv_copies, o_copies = attn_copies(layer, ids, weights, mode, w_qkv, w_o, sems)
    begin(qkv_copies)
    begin(o_copies)
    position = lax.broadcasted_iota(jnp.int32, (tokens, 1), 0)
    query_cell = cell_row[...]
    square = (tokens, tokens)
    diagonal = lax.broadcasted_iota(jnp.int32, square, 0) == lax.broadcasted_iota(jnp.int32, square, 1)
    key_cell = jnp.sum(jnp.where(diagonal, query_cell, 0), axis=1, keepdims=True)
    allowed = (query_cell == key_cell) | (key_cell == 0) | (query_cell == 0)
    allowed = allowed & (position < length[0])
    mask[...] = jnp.where(allowed, 0.0, masked_score)
    scale = 1.0 / math.sqrt(width // HEADS)
    finish(qkv_copies)
    for part in range(3):
        columns = slice(part * width, (part + 1) * width)
        rows = dot(x[...], w_qkv[:, columns])
        if part != 1:
            rows = rows + small[layer, part // 2 : part // 2 + 1, :]
        if part == 0:
            rows = rows * scale
        qkv_rows[:, columns] = rows.astype(low)

    pair_width = 2 * width // HEADS
    first = lax.broadcasted_iota(jnp.int32, (1, pair_width), 1) < pair_width // 2

    for pair in range(HEADS // 2):
        at = slice(pair * pair_width, (pair + 1) * pair_width)
        query = qkv_rows[:, at]
        key = qkv_rows[:, width + at.start : width + at.stop]
        value = qkv_rows[:, 2 * width + at.start : 2 * width + at.stop]
        sides = []
        for side in range(2):
            mine = first if side == 0 else jnp.logical_not(first)
            scores = dot_nt(key, jnp.where(mine, query, jnp.zeros_like(query))) + mask[...]
            shifted = jnp.exp(scores - jnp.max(scores, axis=0, keepdims=True))
            total = jnp.sum(shifted, axis=0, keepdims=True)
            prob = (shifted * (1.0 / total)).astype(low)
            probs[2 * pair + side] = prob
            sides.append(dot_tn(prob, value))
        context[:, at] = jnp.where(first, sides[0], sides[1]).astype(low)

    finish(o_copies)
    residual = x[...].astype(f32) + (dot(context[...], w_o[...]) + small[layer, 2:3, :])
    unit, inverse = normalize(residual)
    unit_out[...] = unit
    inverse_out[...] = inverse


def gelu_and_slope(x):
    t = 1.0 / (1.0 + (0.3275911 * math.sqrt(0.5)) * jnp.abs(x))
    bell = jnp.exp(-0.5 * x * x)
    series = 1.421413741 + t * (-1.453152027 + t * 1.061405429)
    series = t * (0.254829592 + t * (-0.284496736 + t * series))
    tail = 0.5 * series * bell
    cdf = jnp.where(x >= 0.0, 1.0 - tail, tail)
    return (x * cdf).astype(low), cdf + x * (bell * (1.0 / math.sqrt(2.0 * math.pi)))


def ffn_fwd_kernel(layer, modes, ids, unit_one, in_bias, small, *rest):
    weights, rest = rest[:8], rest[8:]
    hidden_out, slope_out, unit_out, inverse_out, result = rest[:5]
    w_in, w_out, normed_low, hidden, slope, sems, out_sems = rest[5:]
    in_copies = weight_copies(ids, layer, weights[:4], modes[0], w_in, 0, sems, 0)
    out_copies = weight_copies(ids, layer, weights[4:], modes[1], w_out, 0, sems, 10)
    begin(in_copies)
    begin(out_copies)
    normed = unit_one[...] * small[layer, 3:4, :] + small[layer, 4:5, :]
    normed_low[...] = normed.astype(low)
    finish(in_copies)
    tile = w_in.shape[1] // 4
    going = []
    for t in range(4):
        columns = pl.ds(t * tile, tile)
        pre = dot(normed_low[...], w_in[:, columns]) + in_bias[layer, :, columns]
        hidden[:, columns], slope[:, columns] = gelu_and_slope(pre)
        leaving = [
            pltpu.make_async_copy(hidden.at[:, columns], hidden_out.at[:, columns], out_sems.at[2 * t]),
            pltpu.make_async_copy(slope.at[:, columns], slope_out.at[:, columns], out_sems.at[2 * t + 1]),
        ]
        begin(leaving)
        going += leaving

    finish(out_copies)
    residual = unit_one[...] * small[layer, 3:4, :] + small[layer, 4:5, :] + (dot(hidden[...], w_out[...]) + small[layer, 5:6, :])
    unit, inverse = normalize(residual)
    unit_out[...] = unit
    inverse_out[...] = inverse
    result[...] = (unit * small[layer, 6:7, :] + small[layer, 7:8, :]).astype(low)
    finish(going)


WIDE_BIT = {"y": 0, "z": 1}


def place_of(ids, owner, piece, way):
    away = None if owner is None else ids[0] ^ owner
    off = None if piece is None else piece ^ ids[5]
    place = [None if away is None else away & 1]
    for name in way:
        if name == "x":
            place.append(pl.ds(0, 2) if away is None else away >> 1)
        else:
            place.append(pl.ds(0, 2) if off is None else (off >> WIDE_BIT[name]) & 1)
    return tuple(place) + (pl.ds(0, 2) if piece is None else piece >> 2,)


def store_rows(stage, ids, product, piece, way):
    share = product.shape[0] // 4
    for owner in range(4):
        block = product[owner * share : (owner + 1) * share].astype(low)
        stage[place_of(ids, owner, piece, way) + (pl.ds(0, share),)] = block


def piece_copies(stage, ids, piece, way, kept, sent, sems, turn):
    at = place_of(ids, None, piece, way)[1:]
    copies = [
        pltpu.make_async_copy(stage.at[(1,) + at], sent.at[at], sems.at[2 * turn]),
        pltpu.make_async_copy(stage.at[(0,) + at], kept.at[at], sems.at[2 * turn + 1]),
    ]
    begin(copies)
    return copies


def out_bwd_kernel(layer, way, ids, *refs):
    finish(out_part(layer, way, ids, *refs))


def out_part(layer, way, ids, grad, unit_two, inverse_two, hidden, small, *rest):
    d_ffn, d_resid_two, small_grads, kept, sent, stage, out_sems = rest
    g = grad[...].astype(f32)
    unit = unit_two[...]
    small_grads[0:1, :] = jnp.sum(g * unit, axis=0, keepdims=True)
    small_grads[1:2, :] = jnp.sum(g, axis=0, keepdims=True)
    d_two = normalize_back(g * small[layer, 6:7, :], unit, inverse_two[...])
    d_resid_two[...] = d_two
    d_low = d_two.astype(low)
    d_ffn[...] = d_low
    small_grads[2:3, :] = jnp.sum(d_low.astype(f32), axis=0, keepdims=True)
    small_grads[3:8, :] = jnp.zeros((5, unit.shape[1]), f32)
    tile = hidden.shape[1] // 8
    share = d_ffn.shape[1] // 4
    waits = []
    for owner in range(4):
        for half in range(2):
            columns = slice((2 * owner + half) * tile, (2 * owner + half + 1) * tile)
            out_grad = dot_tn(hidden[:, columns], d_ffn[...])
            for row_group in range(2):
                for column_group in range(2):
                    piece = (half * 2 + row_group) * 2 + column_group
                    block = out_grad[
                        row_group * share : (row_group + 1) * share,
                        column_group * tile : (column_group + 1) * tile,
                    ]
                    stage[place_of(ids, owner, piece, way)] = block.astype(low)
        core, *at = place_of(ids, owner, None, way)
        at = tuple(at)
        to_kept = pltpu.make_async_copy(stage.at[(0,) + at], kept.at[at], out_sems.at[owner])
        to_sent = pltpu.make_async_copy(stage.at[(1,) + at], sent.at[at], out_sems.at[owner])
        pl.when(core == 0)(to_kept.start)
        pl.when(core == 1)(to_sent.start)
        waits.append(to_kept)
    return waits


def in_bwd_kernel(layer, way, modes, ids, d_ffn, unit_one, inverse_one, small, resid_in, slope_in, *rest):
    weights, rest = rest[:8], rest[8:]
    outs, (w_in, w_out, d_pre, normed_t, slope, d_resid_two, stage, sems, out_sems, more_sems) = rest[:5], rest[5:]
    in_copies = weight_copies(ids, layer, weights[:4], modes[0], w_in, 0, sems, 0)
    out_copies = weight_copies(ids, layer, weights[4:], modes[1], w_out, 0, sems, 10)
    slope_copy = pltpu.make_async_copy(slope_in, slope, more_sems.at[0])
    resid_copy = pltpu.make_async_copy(resid_in, d_resid_two, more_sems.at[1])
    begin(out_copies + [slope_copy] + in_copies + [resid_copy])
    late = (out_copies + [slope_copy], in_copies + [resid_copy])
    refs = (d_ffn, d_resid_two, unit_one, inverse_one, small, slope, w_in, w_out, d_pre, normed_t, stage, out_sems)
    finish(in_part(layer, way, ids, late, *refs, *outs))


def in_part(layer, way, ids, late, d_ffn, d_resid_two, unit_one, inverse_one, small, slope, w_in, w_out, *rest):
    d_pre, normed_t, stage, out_sems, d_resid, small_grads, in_bias_grad, kept, sent = rest
    normed = unit_one[...] * small[layer, 3:4, :] + small[layer, 4:5, :]
    normed_t[...] = normed.astype(low).T
    finish(late[0])
    tile = w_in.shape[1] // 4
    going = []
    for t in range(4):
        columns = slice(t * tile, (t + 1) * tile)
        d_hidden = dot_nt(d_ffn[...], w_out[columns, :])
        d_tile = (d_hidden * slope[:, columns]).astype(low)
        d_pre[:, columns] = d_tile
        in_bias_grad[:, columns] = jnp.sum(d_tile.astype(f32), axis=0, keepdims=True)
        product = dot(normed_t[...], d_tile)
        for half in range(2):
            piece = 2 * t + half
            store_rows(stage, ids, product[:, half * tile // 2 : (half + 1) * tile // 2], piece, way)
            going += piece_copies(stage, ids, piece, way, kept, sent, out_sems, piece)
    finish(late[1])
    d_normed = d_resid_two[...] + dot_nt(d_pre[...], w_in[...])
    unit = unit_one[...]
    small_grads[0:1, :] = jnp.sum(d_normed * unit, axis=0, keepdims=True)
    small_grads[1:2, :] = jnp.sum(d_normed, axis=0, keepdims=True)
    small_grads[2:8, :] = jnp.zeros((6, unit.shape[1]), f32)
    d_resid[...] = normalize_back(d_normed * small[layer, 3:4, :], unit, inverse_one[...])
    return going


def ffn_bwd_kernel(layer, ways, modes, ids, grad, unit_two, inverse_two, hidden, unit_one, inverse_one, small, *rest):
    slope_in, weights, rest = rest[0], rest[1:9], rest[9:]
    out_small, out_kept, out_sent = rest[:3]
    outs, rest = rest[3:8], rest[8:]
    w_in, w_out, d_ffn, d_resid_two, d_pre, normed_t, slope, out_stage, stage, sems, owner_sems, out_sems, slope_sem = rest
    in_copies = weight_copies(ids, layer, weights[:4], modes[0], w_in, 0, sems, 0)
    out_copies = weight_copies(ids, layer, weights[4:], modes[1], w_out, 0, sems, 10)
    slope_copy = pltpu.make_async_copy(slope_in, slope, slope_sem.at[0])
    begin(out_copies + [slope_copy] + in_copies)
    refs = (grad, unit_two, inverse_two, hidden, small, d_ffn, d_resid_two, out_small, out_kept, out_sent)
    going = out_part(layer, ways[0], ids, *refs, out_stage, owner_sems)
    refs = (d_ffn, d_resid_two, unit_one, inverse_one, small, slope, w_in, w_out, d_pre, normed_t, stage, out_sems)
    going += in_part(layer, ways[1], ids, (out_copies + [slope_copy], in_copies), *refs, *outs)
    finish(going)


def attn_bwd_kernel(layer, way, mode, ids, d_resid, x, qkv_rows, probs, context, *rest):
    weights, others, rest = rest[:6], rest[6:-13], rest[-13:]
    d_input, small_grads, kept, sent = rest[:4]
    w_qkv, w_o, d_attn, d_context, d_qkv, x_t, stage, sems, out_sems = rest[4:]
    tokens, width = x.shape
    qkv_copies, o_copies = attn_copies(layer, ids, weights, mode, w_qkv, w_o, sems)
    begin(o_copies)
    begin(qkv_copies)
    d_low = d_resid[...].astype(low)
    d_attn[...] = d_low
    small_grads[2:3, :] = jnp.sum(d_low.astype(f32), axis=0, keepdims=True)
    x_t[...] = x[...].T
    tile = width // 2
    product = dot_tn(context[...], d_attn[...])
    for half in range(2):
        store_rows(stage, ids, product[:, half * tile : (half + 1) * tile], 6 + half, way)
    finish(o_copies)
    d_context[...] = dot_nt(d_attn[...], w_o[...]).astype(low)
    pair_width = 2 * width // HEADS
    first = lax.broadcasted_iota(jnp.int32, (1, pair_width), 1) < pair_width // 2
    scale = 1.0 / math.sqrt(width // HEADS)

    for pair in range(HEADS // 2):
        at_query = slice(pair * pair_width, (pair + 1) * pair_width)
        at_key = slice(width + at_query.start, width + at_query.stop)
        at_value = slice(2 * width + at_query.start, 2 * width + at_query.stop)
        query, key, value = qkv_rows[:, at_query], qkv_rows[:, at_key], qkv_rows[:, at_value]
        d_ctx = d_context[:, at_query]
        sides = []
        for side in range(2):
            mine = first if side == 0 else jnp.logical_not(first)
            prob_low = probs[2 * pair + side]
            prob = prob_low.astype(f32)
            d_prob = dot_nt(value, jnp.where(mine, d_ctx, jnp.zeros_like(d_ctx)))
            inner = jnp.sum(prob * d_prob, axis=0, keepdims=True)
            d_scores = (prob * (d_prob - inner)).astype(low)
            sides.append((dot_tn(d_scores, key), dot(d_scores, query), dot(prob_low, d_ctx)))
        d_qkv[:, at_query] = (jnp.where(first, sides[0][0], sides[1][0]) * scale).astype(low)
        d_qkv[:, at_key] = jnp.where(first, sides[0][1], sides[1][1]).astype(low)
        d_qkv[:, at_value] = jnp.where(first, sides[0][2], sides[1][2]).astype(low)

    small_grads[0:1, :] = jnp.sum(d_qkv[:, :width].astype(f32), axis=0, keepdims=True)
    small_grads[1:2, :] = jnp.sum(d_qkv[:, 2 * width :].astype(f32), axis=0, keepdims=True)
    small_grads[3:8, :] = jnp.zeros((5, width), f32)
    if others:
        share = width // 4
        sources = small_sources(layer, small_grads, others)
        for owner in range(4):
            for piece in range(8):
                lines = []
                for source, row, start, step in sources[3 * piece : 3 * piece + 3]:
                    line = source[row : row + 1, start + owner * step : start + owner * step + share]
                    lines.append(jnp.concatenate([line, jnp.zeros_like(line)], axis=1))
                lines.append(jnp.zeros((SMALL_ROWS - 3, tile), f32))
                block = jnp.concatenate(lines, axis=0).astype(low)
                stage[place_of(ids, owner, piece, way) + (pl.ds(share, SMALL_ROWS),)] = block
    going = []
    for part in (3, 0, 1, 2):
        if part < 3:
            product = dot(x_t[...], d_qkv[:, part * width : (part + 1) * width])
        for half in range(2):
            piece = 2 * part + half
            if part < 3:
                store_rows(stage, ids, product[:, half * tile : (half + 1) * tile], piece, way)
            going += piece_copies(stage, ids, piece, way, kept, sent, out_sems, piece)
    finish(qkv_copies)
    d_input[...] = (d_resid[...] + dot_nt(d_qkv[...], w_qkv[...])).astype(low)
    finish(going)


SMALL_ROWS = 16
SMALL_LINES = (("attn", 0), ("attn", 1), ("attn", 2), ("in", 0), ("in", 1), ("out", 2), ("out", 0), ("out", 1))


def small_sources(layer, own, others):
    found = []
    out_0, in_0, bias_0, out_1, in_1, bias_1, attn_1 = others
    refs = ({"attn": own, "in": in_0, "out": out_0}, {"attn": attn_1, "in": in_1, "out": out_1})
    width = own.shape[1]
    for of_layer, bias in zip(refs, (bias_0, bias_1)):
        found += [(of_layer[name], row, 0, width // 4) for name, row in SMALL_LINES]
        found += [(bias, 0, i * (width // 4), width) for i in range(4)]
    return found


def unpack_kernel(layer, slab, back, earlier, ids, near, far, *rest):
    outs = rest[earlier:-4]
    buffer, wide_buffer, in_sems, out_sems = rest[-4:]
    share, tile = wide_buffer.shape[1:]

    def fetch(piece, ref, index):
        return pltpu.make_async_copy(ref.at[index], buffer.at[piece], in_sems.at[piece])

    for piece in range(8):
        off = piece ^ ids[5]
        inner, outer = [(off >> WIDE_BIT[name]) & 1 for name in back]
        pl.when(outer == 0)(fetch(piece, near, (inner, piece >> 2)).start)
        pl.when(outer == 1)(fetch(piece, far, (inner, piece >> 2)).start)

    copies = []
    for piece in range(8):
        fetch(piece, near, (0, 0)).wait()
        wide_buffer[piece] = buffer[piece, :share].astype(f32)
        columns = pl.ds(piece * tile, tile)
        if slab == "in":
            target = outs[0].at[layer, :, columns]
        elif slab == "out":
            rows = pl.ds((piece // 2) * share, share)
            target = outs[0].at[layer, rows, pl.ds((piece % 2) * tile, tile)]
        elif piece < 6:
            target = outs[0].at[layer, :, columns]
        else:
            target = outs[1].at[layer, :, pl.ds((piece - 6) * tile, tile)]
        copies.append(pltpu.make_async_copy(wide_buffer.at[piece], target, out_sems.at[piece]))
        copies[-1].start()
    if slab == "attn" and layer == 0:
        for line in range(24):
            of_layer, which = line // 12, line % 12
            row = share + line % 3
            values = buffer[line // 3, row : row + 1, :share].astype(f32)
            if which < 8:
                outs[2 + which][of_layer : of_layer + 1, :] = values
            else:
                at = (which - 8) * share
                outs[10][of_layer : of_layer + 1, at : at + share] = values
    else:
        outs[-1][...] = jnp.zeros(outs[-1].shape, f32)
    finish(copies)


SMEM = pl.BlockSpec(memory_space=pltpu.SMEM)
VMEM = pl.BlockSpec(memory_space=pltpu.VMEM)
ANY = pl.BlockSpec(memory_space=pl.ANY)


def call(kernel, name, time, in_specs, out_specs, out_shape, scratch, args, aliases=()):
    return pl.pallas_call(
        kernel,
        name=name,
        in_specs=in_specs,
        out_specs=out_specs,
        out_shape=out_shape,
        scratch_shapes=scratch,
        input_output_aliases=dict(aliases),
        compiler_params=pltpu.CompilerParams(vmem_limit_bytes=VMEM_BYTES),
        cost_estimate=pl.CostEstimate(
            flops=int(time * 1.1e9), bytes_accessed=int(time * 3.6e6), transcendentals=0
        ),
    )(*args)


def shape(dims, kind):
    return jax.ShapeDtypeStruct(dims, kind)


def added(a, b):
    return (a.astype(f32) + b.astype(f32)).astype(low)


WAYS = ("zxy", "xyz", "yxz", "zyx", "xyz", "xyz")
BACKS = ("yz", "zy", "zy", "yz", "zy", "zy")
PLAN = (
    "out1", "in1", 0, 1, "attn1", "out0", "in0", 0, 1, "attn0", 1, 0, 2, 4, 3, 1, 2, 4, 1, 0, 5, 3, 2, 0, 4,
    0, 1, 2, 3, 2, 4, 5, 3, 0, 5, 4, 2, 5, 1, 3, 5, 4, 3, 2, 5, 4, 3, 5,
)
MODES = ("hy", "hy", "hz", "hy", "hy", "hy")
FORWARD = (
    "h0", "g1", "g0", "h1", "g3", "h5", "h2", "g2", "c2", "h3", "x2", "x1", "z2", "c0", "pack", "x0", "h4",
    "c3", "x3", "sm", "y1", "y0", "c1", "A", "d2", "d0", "x5", "attn1", "y3", "d1", "x4", "y5", "ffn1", "y4",
    "d3", "attn2", "d4", "d5", "ffn2",
)
TIMES = {
    "pack": 3, "attn1": 0.3, "ffn1": 0.3, "attn2": 3, "ffn2": 8,
    "out_bwd1": 20.0, "in_bwd1": 20.0, "attn_bwd1": 0.3, "out_bwd0": 2.0, "in_bwd0": 1.0, "attn_bwd0": 8.0,
}


class Order:
    def __init__(self, ids):
        self.ids = ids

    def wait(self, values):
        values, self.ids = lax.optimization_barrier((values, self.ids))
        return values


STEPS = {"x": ("narrow", 2), "y": ("wide", 1), "z": ("wide", 2)}


class Slab:
    def __init__(self, way, back, wide_count, kept, sent):
        self.kept = kept
        self.way, self.back = way, back
        self.rest = [1 << b for b in range(HALVINGS, wide_count.bit_length() - 1)]
        self.flying = swap(sent, "narrow", 1)
        self.stage = 0

    def step(self, order):
        received = order.wait(self.flying)
        stage, way = self.stage, self.way
        if stage < len(way):
            send = order.wait(added(self.kept[1], received[1]))
            self.kept = added(self.kept[0], received[0])
            self.flying = swap(send, *STEPS[way[stage]])
        elif stage < len(way) + 1 + len(self.back):
            if stage == len(way):
                piece = added(self.kept, received)
                for bit in self.rest[:-1]:
                    piece = added(piece, swap(piece, "wide", bit))
                self.kept = order.wait(piece)
                self.flying = swap(self.kept, "wide", self.rest[-1])
            else:
                if stage == len(way) + 1:
                    self.block = added(self.kept, received)[None]
                else:
                    self.block = jnp.concatenate([self.block, received], axis=0)
                self.block = order.wait(self.block)
                self.flying = swap(self.block, *STEPS[self.back[stage - len(way) - 1]])
        else:
            self.far = received
        self.stage += 1

    def ended(self):
        return self.stage == len(self.way) + len(self.back) + 2


def body(
    tables_in,
    cotangent,
    cell_ids,
    lengths,
    qkv_weight,
    q_bias,
    v_bias,
    o_weight,
    o_bias,
    norm1_gain,
    norm1_bias,
    in_weight,
    in_bias,
    out_weight,
    out_bias,
    norm2_gain,
    norm2_bias,
):
    tokens, width = tables_in.shape
    layers, share, ffn = in_weight.shape
    ffn_share = out_weight.shape[1]
    wide_count = lax.axis_size("wide")
    assert wide_count & (wide_count - 1) == 0 and wide_count > 1 << HALVINGS and lax.axis_size("narrow") == 4
    tile = ffn // 8
    me = lax.axis_index("narrow").astype(jnp.int32)
    wide_me = lax.axis_index("wide").astype(jnp.int32)
    y = wide_me & 1
    ids = jnp.stack([me, me ^ 1, me ^ 2, me ^ 3, y, wide_me & (2**HALVINGS - 1)])

    order = Order(ids)

    def part_of(weight, layer, mode):
        rows = weight.shape[1] // (4 if mode[0] == "q" else 2)
        start = position(wide_me & 3, mode) * rows
        return lax.dynamic_slice(weight, (layer, start, 0), (1, rows, weight.shape[2]))[0]

    own = (qkv_weight, o_weight, in_weight, out_weight)
    parts = []
    for layer in range(layers):
        attn_mode, in_mode, out_mode = MODES[3 * layer : 3 * layer + 3]
        joint = [part_of(weight, layer, attn_mode) for weight in own[:2]]
        parts += [jnp.concatenate(joint, axis=1), part_of(in_weight, layer, in_mode), part_of(out_weight, layer, out_mode)]
    near, diagonal, core = [None] * 6, [None] * 6, [None] * 4
    transfers = [{} for _ in range(6)]

    def joined(i, *names):
        near[i] = order.wait(jnp.concatenate([transfers[i][name] for name in names], axis=0))
        transfers[i]["d"] = swap(near[i], "narrow", 1)

    def weight_step(kind, i):
        moving, mode = transfers[i], MODES[i]
        if kind == "h":
            moving["x"] = swap(order.wait(parts[i]), "narrow", 2)
            return
        moving[kind] = order.wait(moving[kind])
        if kind == "x":
            for name, bit in (("y", 1), ("z", 2)):
                if mode[0] == "q" or mode[1] == name:
                    moving[name] = swap(moving["x"], "wide", bit)
        elif kind == "d":
            diagonal[i] = moving["d"]
        elif kind == "q":
            joined(i, "x", "y", "z", "q")
        elif mode[0] == "h":
            joined(i, "x", kind)
        elif mode[1] != kind:
            moving["q"] = swap(moving[kind], "wide", 1 if mode[1] == "y" else 2)

    def in_order(low_one, high_one, bit):
        swapped = (me & bit) != 0
        return jnp.stack([jnp.where(swapped, high_one, low_one), jnp.where(swapped, low_one, high_one)])

    def attn_weights(layer):
        return (qkv_weight, core[0], o_weight, core[1], near[3 * layer], diagonal[3 * layer])

    def in_weights(layer):
        return (in_weight, core[2], near[3 * layer + 1], diagonal[3 * layer + 1])

    def out_weights(layer):
        return (out_weight, core[3], near[3 * layer + 2], diagonal[3 * layer + 2])

    w_qkv = pltpu.VMEM((width, 3 * width), low)
    w_o = pltpu.VMEM((width, width), low)
    w_in = pltpu.VMEM((width, ffn), low)
    w_out = pltpu.VMEM((ffn, width), low)
    copy_sems = pltpu.SemaphoreType.DMA((20,))
    piece_sems = pltpu.SemaphoreType.DMA((16,))
    rows_f32 = shape((tokens, width), f32)
    rows_low = shape((tokens, width), low)
    column_f32 = shape((tokens, 1), f32)
    eight_f32 = shape((8, width), f32)

    def pieces(rows):
        return [shape((2, 2, 2, 2, rows, tile), low)] * 2

    def stage(rows):
        return pltpu.VMEM((2, 2, 2, 2, 2, rows, tile), low)

    def tie(outs, which):
        outs = list(outs)
        outs[which] = order.wait(outs[which])
        return outs

    def attn_forward(layer, x):
        x = order.wait(x)
        outs = call(
            functools.partial(attn_fwd_kernel, layer, MODES[3 * layer]),
            "attn_fwd",
            TIMES["attn%d" % (layer + 1)],
            [SMEM, SMEM] + [VMEM] * 3 + [ANY] * 6,
            [VMEM] * 5,
            [shape((tokens, 3 * width), low), shape((HEADS, tokens, tokens), low), rows_low, rows_f32, column_f32],
            [w_qkv, w_o, pltpu.VMEM((tokens, tokens), f32), copy_sems],
            (order.ids, lengths, x, cell_ids, small) + attn_weights(layer),
        )
        return tie(outs, 3)

    def ffn_forward(layer, unit_one):
        unit_one = order.wait(unit_one)
        outs = call(
            functools.partial(ffn_fwd_kernel, layer, MODES[3 * layer + 1 : 3 * layer + 3]),
            "ffn_fwd",
            TIMES["ffn%d" % (layer + 1)],
            [SMEM] + [VMEM] * 3 + [ANY] * 8,
            [ANY] * 2 + [VMEM] * 3,
            [shape((tokens, ffn), low), shape((tokens, ffn), f32), rows_f32, column_f32, rows_low],
            [
                w_in,
                w_out,
                pltpu.VMEM((tokens, width), low),
                pltpu.VMEM((tokens, ffn), low),
                pltpu.VMEM((tokens, ffn), f32),
                copy_sems,
                piece_sems,
            ],
            (order.ids, unit_one, full_in_bias, small) + in_weights(layer) + out_weights(layer),
        )
        return tie(outs, 4)

    def out_backward(layer, way, grad, unit_two, inverse_two, hidden):
        grad = order.wait(grad)
        outs = call(
            functools.partial(out_bwd_kernel, layer, way),
            "out_bwd",
            TIMES["out_bwd%d" % layer],
            [SMEM] + [VMEM] * 5,
            [VMEM] * 3 + [ANY] * 2,
            [rows_low, rows_f32, eight_f32] + pieces(share),
            [stage(share), pltpu.SemaphoreType.DMA((4,))],
            (order.ids, grad, unit_two, inverse_two, hidden, small),
        )
        return tie(outs, 0)

    def in_backward(layer, way, d_ffn, d_resid_two, unit_one, inverse_one, slope):
        d_ffn = order.wait(d_ffn)
        outs = call(
            functools.partial(in_bwd_kernel, layer, way, MODES[3 * layer + 1 : 3 * layer + 3]),
            "in_bwd",
            TIMES["in_bwd%d" % layer],
            [SMEM] + [VMEM] * 4 + [ANY] * 10,
            [VMEM] * 3 + [ANY] * 2,
            [rows_f32, eight_f32, shape((1, ffn), f32)] + pieces(share),
            [
                w_in,
                w_out,
                pltpu.VMEM((tokens, ffn), low),
                pltpu.VMEM((width, tokens), low),
                pltpu.VMEM((tokens, ffn), f32),
                pltpu.VMEM((tokens, width), f32),
                stage(share),
                copy_sems,
                piece_sems,
                pltpu.SemaphoreType.DMA((2,)),
            ],
            (order.ids, d_ffn, unit_one, inverse_one, small, d_resid_two, slope)
            + in_weights(layer)
            + out_weights(layer),
        )
        return tie(outs, 0)

    def ffn_backward(layer, ways, grad, attn_part, ffn_part):
        grad = order.wait(grad)
        hidden, slope, unit_two, inverse_two, _ = ffn_part
        outs = call(
            functools.partial(ffn_bwd_kernel, layer, ways, MODES[3 * layer + 1 : 3 * layer + 3]),
            "ffn_bwd",
            TIMES["in_bwd%d" % layer],
            [SMEM] + [VMEM] * 7 + [ANY] * 9,
            [VMEM] + [ANY] * 2 + [VMEM] * 3 + [ANY] * 2,
            [eight_f32] + pieces(share) + [rows_f32, eight_f32, shape((1, ffn), f32)] + pieces(share),
            [
                w_in,
                w_out,
                pltpu.VMEM((tokens, width), low),
                pltpu.VMEM((tokens, width), f32),
                pltpu.VMEM((tokens, ffn), low),
                pltpu.VMEM((width, tokens), low),
                pltpu.VMEM((tokens, ffn), f32),
                stage(share),
                stage(share),
                copy_sems,
                pltpu.SemaphoreType.DMA((4,)),
                piece_sems,
                pltpu.SemaphoreType.DMA((1,)),
            ],
            (order.ids, grad, unit_two, inverse_two, hidden, attn_part[3], attn_part[4], small, slope)
            + in_weights(layer)
            + out_weights(layer),
        )
        return tie(outs, 3)

    def attn_backward(layer, way, d_resid, x, qkv_rows, probs, context, small_others):
        d_resid = order.wait(d_resid)
        rows = share + (SMALL_ROWS if small_others else 0)
        outs = call(
            functools.partial(attn_bwd_kernel, layer, way, MODES[3 * layer]),
            "attn_bwd",
            TIMES["attn_bwd%d" % layer],
            [SMEM] + [VMEM] * 5 + [ANY] * 6 + [VMEM] * len(small_others),
            [VMEM] * 2 + [ANY] * 2,
            [rows_low, eight_f32] + pieces(rows),
            [
                w_qkv,
                w_o,
                pltpu.VMEM((tokens, width), low),
                pltpu.VMEM((tokens, width), low),
                pltpu.VMEM((tokens, 3 * width), low),
                pltpu.VMEM((width, tokens), low),
                stage(rows),
                copy_sems,
                piece_sems,
            ],
            (order.ids, d_resid, x, qkv_rows, probs, context) + attn_weights(layer) + tuple(small_others),
        )
        return tie(outs, 0)

    def unpack(layer, name, slab, earlier):
        dims = {
            "attn": [(layers, share, 3 * width), (layers, share, width)],
            "in": [(layers, share, ffn)],
            "out": [(layers, ffn_share, width)],
        }[name]
        last = name == "attn" and layer == 0
        extra = [(layers, share)] * 8 + [(layers, ffn_share)] if last else [(8, 128)]
        near, far = order.wait((slab.block, slab.far))
        rows = near.shape[2]
        outs = call(
            functools.partial(unpack_kernel, layer, name, slab.back, len(earlier)),
            "unpack",
            4,
            [SMEM] + [ANY] * (2 + len(earlier)),
            [ANY] * len(dims) + [VMEM] * len(extra),
            [shape(d, f32) for d in dims + extra],
            [
                pltpu.VMEM((8, rows, tile), low),
                pltpu.VMEM((8, share, tile), f32),
                pltpu.SemaphoreType.DMA((8,)),
                pltpu.SemaphoreType.DMA((8,)),
            ],
            (order.ids, near, far, *earlier),
            {3 + i: i for i in range(len(earlier))},
        )
        return tuple(tie(outs, 0))

    short = (q_bias, v_bias, o_bias, norm1_gain, norm1_bias, out_bias, norm2_gain, norm2_bias)
    inputs, attn_kept, ffn_kept = [tables_in], [], []
    for token in FORWARD:
        kind, i = (token[0], int(token[1])) if len(token) == 2 and token[1].isdigit() else (token, None)
        if kind == "g":
            core[i] = swap(order.wait(own[i]), "narrow", 1)
        elif kind == "c":
            core[i] = order.wait(core[i])
        elif i is not None:
            weight_step(kind, i)
        elif token == "pack":
            packed = call(
                pack_kernel,
                "pack",
                TIMES["pack"],
                [VMEM] * 9,
                VMEM,
                shape((layers, 12, share), f32),
                [],
                tuple(order.wait(short)) + (in_bias,),
            )
            packed = order.wait(packed)
            others = [lax.ppermute(packed, "narrow", [(j, j ^ away) for j in range(4)]) for away in (1, 2, 3)]
        elif token == "sm":
            others = order.wait(others)
        elif token == "A":
            packed = in_order(in_order(packed, others[0], 1), in_order(others[1], others[2], 1), 2)
            packed = packed.reshape(4, layers, 12, share)
            small = packed[:, :, :8].transpose(1, 2, 0, 3).reshape(layers, 8, width)
            full_in_bias = packed[:, :, 8:].transpose(1, 0, 2, 3).reshape(layers, 1, ffn)
            small, full_in_bias = order.wait((small, full_in_bias))
        elif token[:-1] == "attn":
            attn_kept.append(attn_forward(int(token[-1]) - 1, inputs[-1]))
        else:
            ffn_kept.append(ffn_forward(int(token[-1]) - 1, attn_kept[-1][3]))
            inputs.append(ffn_kept[-1][4])
    mixed_out = inputs[-1]

    slabs = [None] * 6
    grad = cotangent
    small_out, small_in, small_attn, bias_grads = [None] * 2, [None] * 2, [None] * 2, [None] * 2
    unpacked = {"attn": (), "in": (), "out": ()}
    for action in PLAN:
        if isinstance(action, int):
            slab = slabs[action]
            slab.step(order)
            if slab.ended():
                name = ("out", "in", "attn")[action % 3]
                unpacked[name] = unpack(layers - 1 - action // 3, name, slab, unpacked[name][: 2 if name == "attn" else 1])
            continue
        name, layer = action[:-1], int(action[-1])
        which = 3 * (layers - 1 - layer) + ("out", "in", "attn").index(name)
        way = WAYS[which]
        qkv_rows, probs, context, unit_one, inverse_one = attn_kept[layer]
        hidden, slope, unit_two, inverse_two, _ = ffn_kept[layer]
        if name == "out" and layer == 0:
            continue
        if name == "in" and layer == 0:
            outs = ffn_backward(layer, WAYS[which - 1 : which + 1], grad, attn_kept[layer], ffn_kept[layer])
            small_out[layer], out_kept, out_sent, d_resid, small_in[layer], bias_grads[layer], kept, sent = outs
            slabs[which - 1] = Slab(WAYS[which - 1], BACKS[which - 1], wide_count, out_kept, out_sent)
        elif name == "out":
            d_ffn, d_resid_two, small_out[layer], kept, sent = out_backward(
                layer, way, grad, unit_two, inverse_two, hidden
            )
        elif name == "in":
            d_resid, small_in[layer], bias_grads[layer], kept, sent = in_backward(
                layer, way, d_ffn, d_resid_two, unit_one, inverse_one, slope
            )
        else:
            small_others = ()
            if layer == 0:
                small_others = (
                    small_out[0],
                    small_in[0],
                    bias_grads[0],
                    small_out[1],
                    small_in[1],
                    bias_grads[1],
                    small_attn[1],
                )
            grad, small_attn[layer], kept, sent = attn_backward(
                layer, way, d_resid, inputs[layer], qkv_rows, probs, context, small_others
            )
        slabs[which] = Slab(way, BACKS[which], wide_count, kept, sent)
    qkv_grad, o_grad, *vectors = unpacked["attn"]
    in_grad, out_grad = unpacked["in"][0], unpacked["out"][0]
    return (
        mixed_out,
        grad,
        qkv_grad,
        vectors[0],
        vectors[1],
        o_grad,
        vectors[2],
        vectors[3],
        vectors[4],
        in_grad,
        vectors[8],
        out_grad,
        vectors[5],
        vectors[6],
        vectors[7],
    )


def solution(mesh):
    by_table = P(("wide", "narrow"), None)
    matrix = P(None, "narrow", None)
    vector = P(None, "narrow")
    return jax.shard_map(
        body,
        mesh=mesh,
        in_specs=(
            by_table,
            by_table,
            by_table,
            P(("wide", "narrow")),
            matrix,
            vector,
            vector,
            matrix,
            vector,
            vector,
            vector,
            matrix,
            vector,
            matrix,
            vector,
            vector,
            vector,
        ),
        out_specs=(
            by_table,
            by_table,
            matrix,
            vector,
            vector,
            matrix,
            vector,
            vector,
            vector,
            matrix,
            vector,
            matrix,
            vector,
            vector,
            vector,
        ),
        check_vma=False,
    )
```

```python
import functools
import math

import jax
import jax.numpy as jnp
from jax import lax
from jax.experimental import pallas as pl
from jax.experimental.pallas import tpu as pltpu
from jax.sharding import PartitionSpec as P

HEADS = 12
norm_eps = 1e-12
masked_score = -1000000000.0
low = jnp.bfloat16
f32 = jnp.float32
VMEM_BYTES = 56 * 1024 * 1024
HALVINGS = 2


def swap(value, axis, bit):
    count = lax.axis_size(axis)
    return lax.ppermute(value, axis, [(i, i ^ bit) for i in range(count)])


def dot(a, b):
    return jnp.dot(a, b, preferred_element_type=f32)


def dot_nt(a, b):
    return lax.dot_general(a, b, (((1,), (1,)), ((), ())), preferred_element_type=f32)


def dot_tn(a, b):
    return lax.dot_general(a, b, (((0,), (0,)), ((), ())), preferred_element_type=f32)


def normalize(residual):
    center = residual - jnp.mean(residual, axis=-1, keepdims=True)
    inverse = lax.rsqrt(jnp.mean(center * center, axis=-1, keepdims=True) + norm_eps)
    return center * inverse, inverse


def normalize_back(grad_unit, unit, inverse):
    centered = grad_unit - jnp.mean(grad_unit, axis=-1, keepdims=True)
    return inverse * (centered - unit * jnp.mean(grad_unit * unit, axis=-1, keepdims=True))


def position(wide_bits, mode):
    y, z = wide_bits & 1, wide_bits >> 1
    return {"hy": y, "hz": z}.get(mode, wide_bits)


def weight_copies(ids, layer, pieces, mode, target, columns, sems, base):
    own, core, near, diagonal = pieces
    rows = own.shape[1]
    parts = 4 if mode[0] == "q" else 2
    step = rows // parts
    copies = []

    def add(source, start, count):
        where = target.at[pl.ds(pl.multiple_of(start, step), count), :]
        copies.append(pltpu.make_async_copy(source, where, sems.at[base + len(copies)]))

    add(own.at[layer], ids[0] * rows, rows)
    add(core.at[layer], ids[1] * rows, rows)
    at = pl.ds(columns, target.shape[1])
    for shard, owner in ((near, ids[2]), (diagonal, ids[3])):
        for part in range(parts):
            start = owner * rows + (position(ids[5], mode) ^ part) * step
            add(shard.at[pl.ds(part * step, step), at], start, step)
    return copies


def begin(copies):
    for copy in copies:
        copy.start()


def finish(copies):
    for copy in copies:
        copy.wait()


def attn_copies(layer, ids, refs, mode, w_qkv, w_o, sems):
    qkv_own, qkv_core, o_own, o_core, near, diagonal = refs
    qkv = weight_copies(ids, layer, (qkv_own, qkv_core, near, diagonal), mode, w_qkv, 0, sems, 0)
    o = weight_copies(ids, layer, (o_own, o_core, near, diagonal), mode, w_o, w_qkv.shape[1], sems, 10)
    return qkv, o


def cut_kernel(slabs, ids, qkv, o, w_in, w_out, *rest):
    outs, sems = rest[:-1], rest[-1]
    copies = []
    for slab, out in zip(slabs, outs):
        layer, which = divmod(slab, 3)
        begins = 0
        for weight in ((qkv, o), (w_in,), (w_out,))[which]:
            rows = out.shape[0]
            start = pl.multiple_of(position(ids[5], MODES[slab]) * rows, rows)
            source = weight.at[layer, pl.ds(start, rows), :]
            target = out.at[:, pl.ds(begins, weight.shape[2])]
            copies.append(pltpu.make_async_copy(source, target, sems.at[len(copies)]))
            begins += weight.shape[2]
    begin(copies)
    finish(copies)


def pack_kernel(*refs):
    shorts, in_bias, packed = refs[:8], refs[8], refs[9]
    layers, share = shorts[0].shape
    for layer in range(layers):
        for i, short in enumerate(shorts):
            packed[layer, i : i + 1, :] = short[layer : layer + 1, :].astype(f32)
        for i in range(4):
            packed[layer, 8 + i : 9 + i, :] = in_bias[layer : layer + 1, i * share : (i + 1) * share].astype(f32)


def attn_fwd_kernel(layer, mode, ids, length, x, cell_row, small, *rest):
    weights, rest = rest[:6], rest[6:]
    qkv_rows, probs, context, unit_out, inverse_out, w_qkv, w_o, mask, sems = rest
    tokens, width = x.shape
    qkv_copies, o_copies = attn_copies(layer, ids, weights, mode, w_qkv, w_o, sems)
    begin(qkv_copies)
    begin(o_copies)
    position = lax.broadcasted_iota(jnp.int32, (tokens, 1), 0)
    query_cell = cell_row[...]
    square = (tokens, tokens)
    diagonal = lax.broadcasted_iota(jnp.int32, square, 0) == lax.broadcasted_iota(jnp.int32, square, 1)
    key_cell = jnp.sum(jnp.where(diagonal, query_cell, 0), axis=1, keepdims=True)
    allowed = (query_cell == key_cell) | (key_cell == 0) | (query_cell == 0)
    allowed = allowed & (position < length[0])
    mask[...] = jnp.where(allowed, 0.0, masked_score)
    scale = 1.0 / math.sqrt(width // HEADS)
    finish(qkv_copies)
    for part in range(3):
        columns = slice(part * width, (part + 1) * width)
        rows = dot(x[...], w_qkv[:, columns])
        if part != 1:
            rows = rows + small[layer, part // 2 : part // 2 + 1, :]
        if part == 0:
            rows = rows * scale
        qkv_rows[:, columns] = rows.astype(low)

    pair_width = 2 * width // HEADS
    first = lax.broadcasted_iota(jnp.int32, (1, pair_width), 1) < pair_width // 2

    for pair in range(HEADS // 2):
        at = slice(pair * pair_width, (pair + 1) * pair_width)
        query = qkv_rows[:, at]
        key = qkv_rows[:, width + at.start : width + at.stop]
        value = qkv_rows[:, 2 * width + at.start : 2 * width + at.stop]
        sides = []
        for side in range(2):
            mine = first if side == 0 else jnp.logical_not(first)
            scores = dot_nt(key, jnp.where(mine, query, jnp.zeros_like(query))) + mask[...]
            shifted = jnp.exp(scores - jnp.max(scores, axis=0, keepdims=True))
            total = jnp.sum(shifted, axis=0, keepdims=True)
            prob = (shifted * (1.0 / total)).astype(low)
            probs[2 * pair + side] = prob
            sides.append(dot_tn(prob, value))
        context[:, at] = jnp.where(first, sides[0], sides[1]).astype(low)

    finish(o_copies)
    residual = x[...].astype(f32) + (dot(context[...], w_o[...]) + small[layer, 2:3, :])
    unit, inverse = normalize(residual)
    unit_out[...] = unit
    inverse_out[...] = inverse


def gelu_and_slope(x):
    t = 1.0 / (1.0 + (0.3275911 * math.sqrt(0.5)) * jnp.abs(x))
    bell = jnp.exp(-0.5 * x * x)
    series = 1.421413741 + t * (-1.453152027 + t * 1.061405429)
    series = t * (0.254829592 + t * (-0.284496736 + t * series))
    tail = 0.5 * series * bell
    cdf = jnp.where(x >= 0.0, 1.0 - tail, tail)
    return (x * cdf).astype(low), cdf + x * (bell * (1.0 / math.sqrt(2.0 * math.pi)))


def ffn_fwd_kernel(layer, modes, ids, unit_one, in_bias, small, *rest):
    weights, rest = rest[:8], rest[8:]
    hidden_out, slope_out, unit_out, inverse_out, result = rest[:5]
    w_in, w_out, normed_low, hidden, slope, sems, out_sems = rest[5:]
    in_copies = weight_copies(ids, layer, weights[:4], modes[0], w_in, 0, sems, 0)
    out_copies = weight_copies(ids, layer, weights[4:], modes[1], w_out, 0, sems, 10)
    begin(in_copies)
    begin(out_copies)
    normed = unit_one[...] * small[layer, 3:4, :] + small[layer, 4:5, :]
    normed_low[...] = normed.astype(low)
    finish(in_copies)
    tile = w_in.shape[1] // 4
    going = []
    for t in range(4):
        columns = pl.ds(t * tile, tile)
        pre = dot(normed_low[...], w_in[:, columns]) + in_bias[layer, :, columns]
        hidden[:, columns], slope[:, columns] = gelu_and_slope(pre)
        leaving = [
            pltpu.make_async_copy(hidden.at[:, columns], hidden_out.at[:, columns], out_sems.at[2 * t]),
            pltpu.make_async_copy(slope.at[:, columns], slope_out.at[:, columns], out_sems.at[2 * t + 1]),
        ]
        begin(leaving)
        going += leaving

    finish(out_copies)
    residual = unit_one[...] * small[layer, 3:4, :] + small[layer, 4:5, :] + (dot(hidden[...], w_out[...]) + small[layer, 5:6, :])
    unit, inverse = normalize(residual)
    unit_out[...] = unit
    inverse_out[...] = inverse
    result[...] = (unit * small[layer, 6:7, :] + small[layer, 7:8, :]).astype(low)
    finish(going)


WIDE_BIT = {"y": 0, "z": 1}


def place_of(ids, owner, piece, way):
    away = None if owner is None else ids[0] ^ owner
    off = None if piece is None else piece ^ ids[5]
    place = [None if away is None else away & 1]
    for name in way:
        if name == "x":
            place.append(pl.ds(0, 2) if away is None else away >> 1)
        else:
            place.append(pl.ds(0, 2) if off is None else (off >> WIDE_BIT[name]) & 1)
    return tuple(place) + (pl.ds(0, 2) if piece is None else piece >> 2,)


def store_rows(stage, ids, product, piece, way):
    share = product.shape[0] // 4
    for owner in range(4):
        block = product[owner * share : (owner + 1) * share].astype(low)
        stage[place_of(ids, owner, piece, way) + (pl.ds(0, share),)] = block


def piece_copies(stage, ids, piece, way, kept, sent, sems, turn):
    at = place_of(ids, None, piece, way)[1:]
    copies = [
        pltpu.make_async_copy(stage.at[(1,) + at], sent.at[at], sems.at[2 * turn]),
        pltpu.make_async_copy(stage.at[(0,) + at], kept.at[at], sems.at[2 * turn + 1]),
    ]
    begin(copies)
    return copies


def out_bwd_kernel(layer, way, ids, *refs):
    finish(out_part(layer, way, ids, *refs))


def out_part(layer, way, ids, grad, unit_two, inverse_two, hidden, small, *rest):
    d_ffn, d_resid_two, small_grads, kept, sent, stage, out_sems = rest
    g = grad[...].astype(f32)
    unit = unit_two[...]
    small_grads[0:1, :] = jnp.sum(g * unit, axis=0, keepdims=True)
    small_grads[1:2, :] = jnp.sum(g, axis=0, keepdims=True)
    d_two = normalize_back(g * small[layer, 6:7, :], unit, inverse_two[...])
    d_resid_two[...] = d_two
    d_low = d_two.astype(low)
    d_ffn[...] = d_low
    small_grads[2:3, :] = jnp.sum(d_low.astype(f32), axis=0, keepdims=True)
    small_grads[3:8, :] = jnp.zeros((5, unit.shape[1]), f32)
    tile = hidden.shape[1] // 8
    share = d_ffn.shape[1] // 4
    waits = []
    for owner in range(4):
        for half in range(2):
            columns = slice((2 * owner + half) * tile, (2 * owner + half + 1) * tile)
            out_grad = dot_tn(hidden[:, columns], d_ffn[...])
            for row_group in range(2):
                for column_group in range(2):
                    piece = (half * 2 + row_group) * 2 + column_group
                    block = out_grad[
                        row_group * share : (row_group + 1) * share,
                        column_group * tile : (column_group + 1) * tile,
                    ]
                    stage[place_of(ids, owner, piece, way)] = block.astype(low)
        core, *at = place_of(ids, owner, None, way)
        at = tuple(at)
        to_kept = pltpu.make_async_copy(stage.at[(0,) + at], kept.at[at], out_sems.at[owner])
        to_sent = pltpu.make_async_copy(stage.at[(1,) + at], sent.at[at], out_sems.at[owner])
        pl.when(core == 0)(to_kept.start)
        pl.when(core == 1)(to_sent.start)
        waits.append(to_kept)
    return waits


def in_bwd_kernel(layer, way, modes, ids, d_ffn, unit_one, inverse_one, small, resid_in, slope_in, *rest):
    weights, rest = rest[:8], rest[8:]
    outs, (w_in, w_out, d_pre, normed_t, slope, d_resid_two, stage, sems, out_sems, more_sems) = rest[:5], rest[5:]
    in_copies = weight_copies(ids, layer, weights[:4], modes[0], w_in, 0, sems, 0)
    out_copies = weight_copies(ids, layer, weights[4:], modes[1], w_out, 0, sems, 10)
    slope_copy = pltpu.make_async_copy(slope_in, slope, more_sems.at[0])
    resid_copy = pltpu.make_async_copy(resid_in, d_resid_two, more_sems.at[1])
    begin(out_copies + [slope_copy] + in_copies + [resid_copy])
    late = (out_copies + [slope_copy], in_copies + [resid_copy])
    refs = (d_ffn, d_resid_two, unit_one, inverse_one, small, slope, w_in, w_out, d_pre, normed_t, stage, out_sems)
    finish(in_part(layer, way, ids, late, *refs, *outs))


def in_part(layer, way, ids, late, d_ffn, d_resid_two, unit_one, inverse_one, small, slope, w_in, w_out, *rest):
    d_pre, normed_t, stage, out_sems, d_resid, small_grads, in_bias_grad, kept, sent = rest
    normed = unit_one[...] * small[layer, 3:4, :] + small[layer, 4:5, :]
    normed_t[...] = normed.astype(low).T
    finish(late[0])
    tile = w_in.shape[1] // 4
    going = []
    for t in range(4):
        columns = slice(t * tile, (t + 1) * tile)
        d_hidden = dot_nt(d_ffn[...], w_out[columns, :])
        d_tile = (d_hidden * slope[:, columns]).astype(low)
        d_pre[:, columns] = d_tile
        in_bias_grad[:, columns] = jnp.sum(d_tile.astype(f32), axis=0, keepdims=True)
        product = dot(normed_t[...], d_tile)
        for half in range(2):
            piece = 2 * t + half
            store_rows(stage, ids, product[:, half * tile // 2 : (half + 1) * tile // 2], piece, way)
            going += piece_copies(stage, ids, piece, way, kept, sent, out_sems, piece)
    finish(late[1])
    d_normed = d_resid_two[...] + dot_nt(d_pre[...], w_in[...])
    unit = unit_one[...]
    small_grads[0:1, :] = jnp.sum(d_normed * unit, axis=0, keepdims=True)
    small_grads[1:2, :] = jnp.sum(d_normed, axis=0, keepdims=True)
    small_grads[2:8, :] = jnp.zeros((6, unit.shape[1]), f32)
    d_resid[...] = normalize_back(d_normed * small[layer, 3:4, :], unit, inverse_one[...])
    return going


def ffn_bwd_kernel(layer, ways, modes, ids, grad, unit_two, inverse_two, hidden, unit_one, inverse_one, small, *rest):
    slope_in, weights, rest = rest[0], rest[1:9], rest[9:]
    out_small, out_kept, out_sent = rest[:3]
    outs, rest = rest[3:8], rest[8:]
    w_in, w_out, d_ffn, d_resid_two, d_pre, normed_t, slope, out_stage, stage, sems, owner_sems, out_sems, slope_sem = rest
    in_copies = weight_copies(ids, layer, weights[:4], modes[0], w_in, 0, sems, 0)
    out_copies = weight_copies(ids, layer, weights[4:], modes[1], w_out, 0, sems, 10)
    slope_copy = pltpu.make_async_copy(slope_in, slope, slope_sem.at[0])
    begin(out_copies + [slope_copy] + in_copies)
    refs = (grad, unit_two, inverse_two, hidden, small, d_ffn, d_resid_two, out_small, out_kept, out_sent)
    going = out_part(layer, ways[0], ids, *refs, out_stage, owner_sems)
    refs = (d_ffn, d_resid_two, unit_one, inverse_one, small, slope, w_in, w_out, d_pre, normed_t, stage, out_sems)
    going += in_part(layer, ways[1], ids, (out_copies + [slope_copy], in_copies), *refs, *outs)
    finish(going)


def attn_bwd_kernel(layer, way, mode, ids, d_resid, x, qkv_rows, probs, context, *rest):
    weights, others, rest = rest[:6], rest[6:-13], rest[-13:]
    d_input, small_grads, kept, sent = rest[:4]
    w_qkv, w_o, d_attn, d_context, d_qkv, x_t, stage, sems, out_sems = rest[4:]
    tokens, width = x.shape
    qkv_copies, o_copies = attn_copies(layer, ids, weights, mode, w_qkv, w_o, sems)
    begin(o_copies)
    begin(qkv_copies)
    d_low = d_resid[...].astype(low)
    d_attn[...] = d_low
    small_grads[2:3, :] = jnp.sum(d_low.astype(f32), axis=0, keepdims=True)
    x_t[...] = x[...].T
    tile = width // 2
    product = dot_tn(context[...], d_attn[...])
    for half in range(2):
        store_rows(stage, ids, product[:, half * tile : (half + 1) * tile], 6 + half, way)
    finish(o_copies)
    d_context[...] = dot_nt(d_attn[...], w_o[...]).astype(low)
    pair_width = 2 * width // HEADS
    first = lax.broadcasted_iota(jnp.int32, (1, pair_width), 1) < pair_width // 2
    scale = 1.0 / math.sqrt(width // HEADS)

    for pair in range(HEADS // 2):
        at_query = slice(pair * pair_width, (pair + 1) * pair_width)
        at_key = slice(width + at_query.start, width + at_query.stop)
        at_value = slice(2 * width + at_query.start, 2 * width + at_query.stop)
        query, key, value = qkv_rows[:, at_query], qkv_rows[:, at_key], qkv_rows[:, at_value]
        d_ctx = d_context[:, at_query]
        sides = []
        for side in range(2):
            mine = first if side == 0 else jnp.logical_not(first)
            prob_low = probs[2 * pair + side]
            prob = prob_low.astype(f32)
            d_prob = dot_nt(value, jnp.where(mine, d_ctx, jnp.zeros_like(d_ctx)))
            inner = jnp.sum(prob * d_prob, axis=0, keepdims=True)
            d_scores = (prob * (d_prob - inner)).astype(low)
            sides.append((dot_tn(d_scores, key), dot(d_scores, query), dot(prob_low, d_ctx)))
        d_qkv[:, at_query] = (jnp.where(first, sides[0][0], sides[1][0]) * scale).astype(low)
        d_qkv[:, at_key] = jnp.where(first, sides[0][1], sides[1][1]).astype(low)
        d_qkv[:, at_value] = jnp.where(first, sides[0][2], sides[1][2]).astype(low)

    small_grads[0:1, :] = jnp.sum(d_qkv[:, :width].astype(f32), axis=0, keepdims=True)
    small_grads[1:2, :] = jnp.sum(d_qkv[:, 2 * width :].astype(f32), axis=0, keepdims=True)
    small_grads[3:8, :] = jnp.zeros((5, width), f32)
    if others:
        share = width // 4
        sources = small_sources(layer, small_grads, others)
        for owner in range(4):
            for piece in range(8):
                lines = []
                for source, row, start, step in sources[3 * piece : 3 * piece + 3]:
                    line = source[row : row + 1, start + owner * step : start + owner * step + share]
                    lines.append(jnp.concatenate([line, jnp.zeros_like(line)], axis=1))
                lines.append(jnp.zeros((SMALL_ROWS - 3, tile), f32))
                block = jnp.concatenate(lines, axis=0).astype(low)
                stage[place_of(ids, owner, piece, way) + (pl.ds(share, SMALL_ROWS),)] = block
    going = []
    for part in (3, 0, 1, 2):
        if part < 3:
            product = dot(x_t[...], d_qkv[:, part * width : (part + 1) * width])
        for half in range(2):
            piece = 2 * part + half
            if part < 3:
                store_rows(stage, ids, product[:, half * tile : (half + 1) * tile], piece, way)
            going += piece_copies(stage, ids, piece, way, kept, sent, out_sems, piece)
    finish(qkv_copies)
    d_input[...] = (d_resid[...] + dot_nt(d_qkv[...], w_qkv[...])).astype(low)
    finish(going)


SMALL_ROWS = 16
SMALL_LINES = (("attn", 0), ("attn", 1), ("attn", 2), ("in", 0), ("in", 1), ("out", 2), ("out", 0), ("out", 1))


def small_sources(layer, own, others):
    found = []
    out_0, in_0, bias_0, out_1, in_1, bias_1, attn_1 = others
    refs = ({"attn": own, "in": in_0, "out": out_0}, {"attn": attn_1, "in": in_1, "out": out_1})
    width = own.shape[1]
    for of_layer, bias in zip(refs, (bias_0, bias_1)):
        found += [(of_layer[name], row, 0, width // 4) for name, row in SMALL_LINES]
        found += [(bias, 0, i * (width // 4), width) for i in range(4)]
    return found


def unpack_kernel(layer, slab, back, far, earlier, ids, *rest):
    halves = rest[: 2 if slab == "attn" and layer == 0 and far else 1]
    outs = rest[len(halves) + earlier : -5]
    buffer, wide_buffer, lines, in_sems, out_sems = rest[-5:]
    share, tile = wide_buffer.shape[1:]

    def piece_of(far_side, inner, last):
        bits = {back[0]: inner, back[1]: far_side}
        return ((ids[5] ^ (bits["y"] | bits["z"] << 1)) & 3) | last << 2

    pieces = [(inner, last) for inner in range(2) for last in range(2)]
    arriving = []
    for slot, place in enumerate(pieces):
        arriving.append(pltpu.make_async_copy(halves[0].at[place], buffer.at[slot], in_sems.at[slot]))
    small = []
    for side, half in enumerate(halves if len(halves) == 2 else ()):
        for place in pieces:
            target = lines.at[piece_of(1 - side, *place)]
            source = half.at[place + (pl.ds(share, SMALL_ROWS),)]
            small.append(pltpu.make_async_copy(source, target, in_sems.at[4 + len(small)]))
    begin(arriving + small)
    waits = []
    for slot, place in enumerate(pieces):
        piece = piece_of(int(far), *place)
        arriving[slot].wait()
        wide_buffer[slot] = buffer[slot, :share].astype(f32)
        source, sem = wide_buffer.at[slot], out_sems.at[slot]

        def columns(at):
            return pl.ds(pl.multiple_of(at * tile, tile), tile)

        if slab == "out":
            rows = pl.ds(pl.multiple_of((piece >> 1) * share, share), share)
            copies = [pltpu.make_async_copy(source, outs[0].at[layer, rows, columns(piece & 1)], sem)]
            copies[0].start()
        elif slab == "in":
            copies = [pltpu.make_async_copy(source, outs[0].at[layer, :, columns(piece)], sem)]
            copies[0].start()
        else:
            in_qkv, in_o = jnp.minimum(piece, 5), jnp.maximum(piece - 6, 0)
            copies = [
                pltpu.make_async_copy(source, outs[0].at[layer, :, columns(in_qkv)], sem),
                pltpu.make_async_copy(source, outs[1].at[layer, :, columns(in_o)], sem),
            ]
            pl.when(piece < 6)(copies[0].start)
            pl.when(piece >= 6)(copies[1].start)
        waits.append(copies[0])
    if small:
        finish(small)
        for line in range(24):
            of_layer, which = line // 12, line % 12
            values = lines[line // 3, line % 3 : line % 3 + 1, :share].astype(f32)
            if which < 8:
                outs[2 + which][of_layer : of_layer + 1, :] = values
            else:
                at = (which - 8) * share
                outs[10][of_layer : of_layer + 1, at : at + share] = values
    else:
        outs[-1][...] = jnp.zeros(outs[-1].shape, f32)
    finish(waits)


SMEM = pl.BlockSpec(memory_space=pltpu.SMEM)
VMEM = pl.BlockSpec(memory_space=pltpu.VMEM)
ANY = pl.BlockSpec(memory_space=pl.ANY)


def call(kernel, name, time, in_specs, out_specs, out_shape, scratch, args, aliases=()):
    return pl.pallas_call(
        kernel,
        name=name,
        in_specs=in_specs,
        out_specs=out_specs,
        out_shape=out_shape,
        scratch_shapes=scratch,
        input_output_aliases=dict(aliases),
        compiler_params=pltpu.CompilerParams(vmem_limit_bytes=VMEM_BYTES),
        cost_estimate=pl.CostEstimate(
            flops=int(time * 1.1e9), bytes_accessed=int(time * 3.6e6), transcendentals=0
        ),
    )(*args)


def shape(dims, kind):
    return jax.ShapeDtypeStruct(dims, kind)


def added(a, b):
    return (a.astype(f32) + b.astype(f32)).astype(low)


WAYS = ("zxy", "xyz", "yxz", "zyx", "xyz", "xyz")
BACKS = ("yz", "zy", "zy", "yz", "zy", "zy")
PLAN = (
    "out1", "in1", 0, 1, "attn1", "out0", "in0", 0, 1, "attn0", 1, 0, 2, 4, 1, 3, 1, 2, 4, 0, 5, 3, 2, 0, 4,
    0, 1, 2, 3, 2, 4, 5, 3, 0, 5, 4, 2, 5, 1, 3, 5, 4, 3, 2, 5, 4, 3, 5,
)
MODES = ("qz", "hz", "qy", "qz", "qy", "hy")
FORWARD = (
    "h0", "g0", "g2", "cut", "x0", "h2", "h3", "c0", "g3", "pack", "h1", "x2", "h5", "h4", "g1", "y0", "z0",
    "x3", "z2", "y2", "y3", "c3", "q0", "x5", "q2", "z3", "x1", "q3", "y5", "x4", "z1", "sm", "A", "y4", "d0",
    "z4", "c1", "attn1", "c2", "d3", "d1", "q4", "d2", "ffn1", "d4", "d5", "attn2", "ffn2",
)
TIMES = {
    "pack": 1, "attn1": 5, "ffn1": 13, "attn2": 3, "ffn2": 8,
    "out_bwd1": 3, "in_bwd1": 20.0, "attn_bwd1": 0.3, "out_bwd0": 2.0, "in_bwd0": 1.0, "attn_bwd0": 8.0,
}


class Order:
    def __init__(self, ids):
        self.ids = ids

    def wait(self, values):
        values, self.ids = lax.optimization_barrier((values, self.ids))
        return values


STEPS = {"x": ("narrow", 2), "y": ("wide", 1), "z": ("wide", 2)}


class Slab:
    def __init__(self, way, back, wide_count, kept, sent):
        self.kept = kept
        self.way, self.back = way, back
        self.rest = [1 << b for b in range(HALVINGS, wide_count.bit_length() - 1)]
        self.flying = swap(sent, "narrow", 1)
        self.stage = 0

    def step(self, order):
        received = order.wait(self.flying)
        stage, way = self.stage, self.way
        if stage < len(way):
            send = order.wait(added(self.kept[1], received[1]))
            self.kept = added(self.kept[0], received[0])
            self.flying = swap(send, *STEPS[way[stage]])
        elif stage < len(way) + 1 + len(self.back):
            if stage == len(way):
                piece = added(self.kept, received)
                for bit in self.rest[:-1]:
                    piece = added(piece, swap(piece, "wide", bit))
                self.kept = order.wait(piece)
                self.flying = swap(self.kept, "wide", self.rest[-1])
            else:
                if stage == len(way) + 1:
                    self.block = added(self.kept, received)[None]
                else:
                    self.block = jnp.concatenate([self.block, received], axis=0)
                self.block = order.wait(self.block)
                self.flying = swap(self.block, *STEPS[self.back[stage - len(way) - 1]])
        else:
            self.far = received
        self.stage += 1

    def ended(self):
        return self.stage == len(self.way) + len(self.back) + 2


def body(
    tables_in,
    cotangent,
    cell_ids,
    lengths,
    qkv_weight,
    q_bias,
    v_bias,
    o_weight,
    o_bias,
    norm1_gain,
    norm1_bias,
    in_weight,
    in_bias,
    out_weight,
    out_bias,
    norm2_gain,
    norm2_bias,
):
    tokens, width = tables_in.shape
    layers, share, ffn = in_weight.shape
    ffn_share = out_weight.shape[1]
    wide_count = lax.axis_size("wide")
    assert wide_count & (wide_count - 1) == 0 and wide_count > 1 << HALVINGS and lax.axis_size("narrow") == 4
    tile = ffn // 8
    me = lax.axis_index("narrow").astype(jnp.int32)
    wide_me = lax.axis_index("wide").astype(jnp.int32)
    y = wide_me & 1
    ids = jnp.stack([me, me ^ 1, me ^ 2, me ^ 3, y, wide_me & (2**HALVINGS - 1)])

    order = Order(ids)

    own = (qkv_weight, o_weight, in_weight, out_weight)
    parts = [None] * 6

    def cut(*slabs):
        outs = []
        for slab in slabs:
            weight = (qkv_weight, in_weight, out_weight)[slab % 3]
            columns = 4 * width if slab % 3 == 0 else weight.shape[2]
            outs.append(shape((weight.shape[1] // (4 if MODES[slab][0] == "q" else 2), columns), low))
        results = call(
            functools.partial(cut_kernel, slabs),
            "cut",
            1,
            [SMEM] + [ANY] * 4,
            [ANY] * len(slabs),
            outs,
            [pltpu.SemaphoreType.DMA((8,))],
            (order.ids, *own),
        )
        for slab, part in zip(slabs, results):
            parts[slab] = part

    first_slab = [int(token[1]) for token in FORWARD if token[0] == "h"][0]
    cut(first_slab)
    near, diagonal, core = [None] * 6, [None] * 6, [None] * 4
    transfers = [{} for _ in range(6)]

    def joined(i, *names):
        near[i] = order.wait(jnp.concatenate([transfers[i][name] for name in names], axis=0))
        transfers[i]["d"] = swap(near[i], "narrow", 1)

    def weight_step(kind, i):
        moving, mode = transfers[i], MODES[i]
        if kind == "h":
            moving["x"] = swap(order.wait(parts[i]), "narrow", 2)
            return
        moving[kind] = order.wait(moving[kind])
        if kind == "x":
            for name, bit in (("y", 1), ("z", 2)):
                if mode[0] == "q" or mode[1] == name:
                    moving[name] = swap(moving["x"], "wide", bit)
        elif kind == "d":
            diagonal[i] = moving["d"]
        elif kind == "q":
            joined(i, "x", "y", "z", "q")
        elif mode[0] == "h":
            joined(i, "x", kind)
        elif mode[1] != kind:
            moving["q"] = swap(moving[kind], "wide", 1 if mode[1] == "y" else 2)

    def in_order(low_one, high_one, bit):
        swapped = (me & bit) != 0
        return jnp.stack([jnp.where(swapped, high_one, low_one), jnp.where(swapped, low_one, high_one)])

    def attn_weights(layer):
        return (qkv_weight, core[0], o_weight, core[1], near[3 * layer], diagonal[3 * layer])

    def in_weights(layer):
        return (in_weight, core[2], near[3 * layer + 1], diagonal[3 * layer + 1])

    def out_weights(layer):
        return (out_weight, core[3], near[3 * layer + 2], diagonal[3 * layer + 2])

    w_qkv = pltpu.VMEM((width, 3 * width), low)
    w_o = pltpu.VMEM((width, width), low)
    w_in = pltpu.VMEM((width, ffn), low)
    w_out = pltpu.VMEM((ffn, width), low)
    copy_sems = pltpu.SemaphoreType.DMA((20,))
    piece_sems = pltpu.SemaphoreType.DMA((16,))
    rows_f32 = shape((tokens, width), f32)
    rows_low = shape((tokens, width), low)
    column_f32 = shape((tokens, 1), f32)
    eight_f32 = shape((8, width), f32)

    def pieces(rows):
        return [shape((2, 2, 2, 2, rows, tile), low)] * 2

    def stage(rows):
        return pltpu.VMEM((2, 2, 2, 2, 2, rows, tile), low)

    def tie(outs, which):
        outs = list(outs)
        outs[which] = order.wait(outs[which])
        return outs

    def attn_forward(layer, x):
        x = order.wait(x)
        outs = call(
            functools.partial(attn_fwd_kernel, layer, MODES[3 * layer]),
            "attn_fwd",
            TIMES["attn%d" % (layer + 1)],
            [SMEM, SMEM] + [VMEM] * 3 + [ANY] * 6,
            [VMEM] * 5,
            [shape((tokens, 3 * width), low), shape((HEADS, tokens, tokens), low), rows_low, rows_f32, column_f32],
            [w_qkv, w_o, pltpu.VMEM((tokens, tokens), f32), copy_sems],
            (order.ids, lengths, x, cell_ids, small) + attn_weights(layer),
        )
        return tie(outs, 3)

    def ffn_forward(layer, unit_one):
        unit_one = order.wait(unit_one)
        outs = call(
            functools.partial(ffn_fwd_kernel, layer, MODES[3 * layer + 1 : 3 * layer + 3]),
            "ffn_fwd",
            TIMES["ffn%d" % (layer + 1)],
            [SMEM] + [VMEM] * 3 + [ANY] * 8,
            [ANY] * 2 + [VMEM] * 3,
            [shape((tokens, ffn), low), shape((tokens, ffn), f32), rows_f32, column_f32, rows_low],
            [
                w_in,
                w_out,
                pltpu.VMEM((tokens, width), low),
                pltpu.VMEM((tokens, ffn), low),
                pltpu.VMEM((tokens, ffn), f32),
                copy_sems,
                piece_sems,
            ],
            (order.ids, unit_one, full_in_bias, small) + in_weights(layer) + out_weights(layer),
        )
        return tie(outs, 4)

    def out_backward(layer, way, grad, unit_two, inverse_two, hidden):
        grad = order.wait(grad)
        outs = call(
            functools.partial(out_bwd_kernel, layer, way),
            "out_bwd",
            TIMES["out_bwd%d" % layer],
            [SMEM] + [VMEM] * 5,
            [VMEM] * 3 + [ANY] * 2,
            [rows_low, rows_f32, eight_f32] + pieces(share),
            [stage(share), pltpu.SemaphoreType.DMA((4,))],
            (order.ids, grad, unit_two, inverse_two, hidden, small),
        )
        return tie(outs, 0)

    def in_backward(layer, way, d_ffn, d_resid_two, unit_one, inverse_one, slope):
        d_ffn = order.wait(d_ffn)
        outs = call(
            functools.partial(in_bwd_kernel, layer, way, MODES[3 * layer + 1 : 3 * layer + 3]),
            "in_bwd",
            TIMES["in_bwd%d" % layer],
            [SMEM] + [VMEM] * 4 + [ANY] * 10,
            [VMEM] * 3 + [ANY] * 2,
            [rows_f32, eight_f32, shape((1, ffn), f32)] + pieces(share),
            [
                w_in,
                w_out,
                pltpu.VMEM((tokens, ffn), low),
                pltpu.VMEM((width, tokens), low),
                pltpu.VMEM((tokens, ffn), f32),
                pltpu.VMEM((tokens, width), f32),
                stage(share),
                copy_sems,
                piece_sems,
                pltpu.SemaphoreType.DMA((2,)),
            ],
            (order.ids, d_ffn, unit_one, inverse_one, small, d_resid_two, slope)
            + in_weights(layer)
            + out_weights(layer),
        )
        return tie(outs, 0)

    def ffn_backward(layer, ways, grad, attn_part, ffn_part):
        grad = order.wait(grad)
        hidden, slope, unit_two, inverse_two, _ = ffn_part
        outs = call(
            functools.partial(ffn_bwd_kernel, layer, ways, MODES[3 * layer + 1 : 3 * layer + 3]),
            "ffn_bwd",
            TIMES["in_bwd%d" % layer],
            [SMEM] + [VMEM] * 7 + [ANY] * 9,
            [VMEM] + [ANY] * 2 + [VMEM] * 3 + [ANY] * 2,
            [eight_f32] + pieces(share) + [rows_f32, eight_f32, shape((1, ffn), f32)] + pieces(share),
            [
                w_in,
                w_out,
                pltpu.VMEM((tokens, width), low),
                pltpu.VMEM((tokens, width), f32),
                pltpu.VMEM((tokens, ffn), low),
                pltpu.VMEM((width, tokens), low),
                pltpu.VMEM((tokens, ffn), f32),
                stage(share),
                stage(share),
                copy_sems,
                pltpu.SemaphoreType.DMA((4,)),
                piece_sems,
                pltpu.SemaphoreType.DMA((1,)),
            ],
            (order.ids, grad, unit_two, inverse_two, hidden, attn_part[3], attn_part[4], small, slope)
            + in_weights(layer)
            + out_weights(layer),
        )
        return tie(outs, 3)

    def attn_backward(layer, way, d_resid, x, qkv_rows, probs, context, small_others):
        d_resid = order.wait(d_resid)
        rows = share + (SMALL_ROWS if small_others else 0)
        outs = call(
            functools.partial(attn_bwd_kernel, layer, way, MODES[3 * layer]),
            "attn_bwd",
            TIMES["attn_bwd%d" % layer],
            [SMEM] + [VMEM] * 5 + [ANY] * 6 + [VMEM] * len(small_others),
            [VMEM] * 2 + [ANY] * 2,
            [rows_low, eight_f32] + pieces(rows),
            [
                w_qkv,
                w_o,
                pltpu.VMEM((tokens, width), low),
                pltpu.VMEM((tokens, width), low),
                pltpu.VMEM((tokens, 3 * width), low),
                pltpu.VMEM((width, tokens), low),
                stage(rows),
                copy_sems,
                piece_sems,
            ],
            (order.ids, d_resid, x, qkv_rows, probs, context) + attn_weights(layer) + tuple(small_others),
        )
        return tie(outs, 0)

    def unpack(layer, name, slab, far, earlier):
        dims = {
            "attn": [(layers, share, 3 * width), (layers, share, width)],
            "in": [(layers, share, ffn)],
            "out": [(layers, ffn_share, width)],
        }[name]
        last = name == "attn" and layer == 0 and far
        extra = [(layers, share)] * 8 + [(layers, ffn_share)] if last else [(8, 128)]
        halves = [slab.far if far else slab.block] + ([slab.block] if last else [])
        halves[0] = order.wait(halves[0])
        rows = slab.block.shape[2]
        outs = call(
            functools.partial(unpack_kernel, layer, name, slab.back, far, len(earlier)),
            "unpack",
            2,
            [SMEM] + [ANY] * (len(halves) + len(earlier)),
            [ANY] * len(dims) + [VMEM] * len(extra),
            [shape(d, f32) for d in dims + extra],
            [
                pltpu.VMEM((4, rows, tile), low),
                pltpu.VMEM((4, share, tile), f32),
                pltpu.VMEM((8, SMALL_ROWS, tile), low),
                pltpu.SemaphoreType.DMA((12,)),
                pltpu.SemaphoreType.DMA((4,)),
            ],
            (order.ids, *halves, *earlier),
            {1 + len(halves) + i: i for i in range(len(earlier))},
        )
        return tuple(tie(outs, 0))

    short = (q_bias, v_bias, o_bias, norm1_gain, norm1_bias, out_bias, norm2_gain, norm2_bias)
    inputs, attn_kept, ffn_kept = [tables_in], [], []
    for token in FORWARD:
        kind, i = (token[0], int(token[1])) if len(token) == 2 and token[1].isdigit() else (token, None)
        if token == "cut":
            cut(*[slab for slab in range(6) if slab != first_slab])
        elif kind == "g":
            core[i] = swap(order.wait(own[i]), "narrow", 1)
        elif kind == "c":
            core[i] = order.wait(core[i])
        elif i is not None:
            weight_step(kind, i)
        elif token == "pack":
            packed = call(
                pack_kernel,
                "pack",
                TIMES["pack"],
                [VMEM] * 9,
                VMEM,
                shape((layers, 12, share), f32),
                [],
                tuple(order.wait(short)) + (in_bias,),
            )
            packed = order.wait(packed)
            others = [lax.ppermute(packed, "narrow", [(j, j ^ away) for j in range(4)]) for away in (1, 2, 3)]
        elif token == "sm":
            others = order.wait(others)
        elif token == "A":
            packed = in_order(in_order(packed, others[0], 1), in_order(others[1], others[2], 1), 2)
            packed = packed.reshape(4, layers, 12, share)
            small = packed[:, :, :8].transpose(1, 2, 0, 3).reshape(layers, 8, width)
            full_in_bias = packed[:, :, 8:].transpose(1, 0, 2, 3).reshape(layers, 1, ffn)
            small, full_in_bias = order.wait((small, full_in_bias))
        elif token[:-1] == "attn":
            attn_kept.append(attn_forward(int(token[-1]) - 1, inputs[-1]))
        else:
            ffn_kept.append(ffn_forward(int(token[-1]) - 1, attn_kept[-1][3]))
            inputs.append(ffn_kept[-1][4])
    mixed_out = inputs[-1]

    slabs = [None] * 6
    grad = cotangent
    small_out, small_in, small_attn, bias_grads = [None] * 2, [None] * 2, [None] * 2, [None] * 2
    unpacked = {"attn": (), "in": (), "out": ()}
    for action in PLAN:
        if isinstance(action, int):
            slab = slabs[action]
            slab.step(order)
            name = ("out", "in", "attn")[action % 3]
            if slab.stage >= len(slab.way) + len(slab.back) + 1:
                earlier = unpacked[name][: 2 if name == "attn" else 1]
                unpacked[name] = unpack(layers - 1 - action // 3, name, slab, slab.ended(), earlier)
            continue
        name, layer = action[:-1], int(action[-1])
        which = 3 * (layers - 1 - layer) + ("out", "in", "attn").index(name)
        way = WAYS[which]
        qkv_rows, probs, context, unit_one, inverse_one = attn_kept[layer]
        hidden, slope, unit_two, inverse_two, _ = ffn_kept[layer]
        if name == "out" and layer == 0:
            continue
        if name == "in" and layer == 0:
            outs = ffn_backward(layer, WAYS[which - 1 : which + 1], grad, attn_kept[layer], ffn_kept[layer])
            small_out[layer], out_kept, out_sent, d_resid, small_in[layer], bias_grads[layer], kept, sent = outs
            slabs[which - 1] = Slab(WAYS[which - 1], BACKS[which - 1], wide_count, out_kept, out_sent)
        elif name == "out":
            d_ffn, d_resid_two, small_out[layer], kept, sent = out_backward(
                layer, way, grad, unit_two, inverse_two, hidden
            )
        elif name == "in":
            d_resid, small_in[layer], bias_grads[layer], kept, sent = in_backward(
                layer, way, d_ffn, d_resid_two, unit_one, inverse_one, slope
            )
        else:
            small_others = ()
            if layer == 0:
                small_others = (
                    small_out[0],
                    small_in[0],
                    bias_grads[0],
                    small_out[1],
                    small_in[1],
                    bias_grads[1],
                    small_attn[1],
                )
            grad, small_attn[layer], kept, sent = attn_backward(
                layer, way, d_resid, inputs[layer], qkv_rows, probs, context, small_others
            )
        slabs[which] = Slab(way, BACKS[which], wide_count, kept, sent)
    qkv_grad, o_grad, *vectors = unpacked["attn"]
    in_grad, out_grad = unpacked["in"][0], unpacked["out"][0]
    return (
        mixed_out,
        grad,
        qkv_grad,
        vectors[0],
        vectors[1],
        o_grad,
        vectors[2],
        vectors[3],
        vectors[4],
        in_grad,
        vectors[8],
        out_grad,
        vectors[5],
        vectors[6],
        vectors[7],
    )


def solution(mesh):
    by_table = P(("wide", "narrow"), None)
    matrix = P(None, "narrow", None)
    vector = P(None, "narrow")
    return jax.shard_map(
        body,
        mesh=mesh,
        in_specs=(
            by_table,
            by_table,
            by_table,
            P(("wide", "narrow")),
            matrix,
            vector,
            vector,
            matrix,
            vector,
            vector,
            vector,
            matrix,
            vector,
            matrix,
            vector,
            vector,
            vector,
        ),
        out_specs=(
            by_table,
            by_table,
            matrix,
            vector,
            vector,
            matrix,
            vector,
            vector,
            vector,
            matrix,
            vector,
            matrix,
            vector,
            vector,
            vector,
        ),
        check_vma=False,
    )
```

```python
import functools
import math

import jax
import jax.numpy as jnp
from jax import lax
from jax.experimental import pallas as pl
from jax.experimental.pallas import tpu as pltpu
from jax.sharding import PartitionSpec as P

HEADS = 12
norm_eps = 1e-12
masked_score = -1000000000.0
low = jnp.bfloat16
f32 = jnp.float32
VMEM_BYTES = 56 * 1024 * 1024
HALVINGS = 2


def swap(value, axis, bit):
    count = lax.axis_size(axis)
    return lax.ppermute(value, axis, [(i, i ^ bit) for i in range(count)])


def dot(a, b):
    return jnp.dot(a, b, preferred_element_type=f32)


def dot_nt(a, b):
    return lax.dot_general(a, b, (((1,), (1,)), ((), ())), preferred_element_type=f32)


def dot_tn(a, b):
    return lax.dot_general(a, b, (((0,), (0,)), ((), ())), preferred_element_type=f32)


def normalize(residual):
    center = residual - jnp.mean(residual, axis=-1, keepdims=True)
    inverse = lax.rsqrt(jnp.mean(center * center, axis=-1, keepdims=True) + norm_eps)
    return center * inverse, inverse


def normalize_back(grad_unit, unit, inverse):
    centered = grad_unit - jnp.mean(grad_unit, axis=-1, keepdims=True)
    return inverse * (centered - unit * jnp.mean(grad_unit * unit, axis=-1, keepdims=True))


def position(wide_bits, mode):
    y, z = wide_bits & 1, wide_bits >> 1
    return {"hy": y, "hz": z}.get(mode, wide_bits)


def weight_copies(ids, layer, pieces, mode, target, columns, sems, base):
    own, core, near, diagonal = pieces
    rows = own.shape[1]
    parts = 4 if mode[0] == "q" else 2
    step = rows // parts
    copies = []

    def add(source, start, count):
        where = target.at[pl.ds(pl.multiple_of(start, step), count), :]
        copies.append(pltpu.make_async_copy(source, where, sems.at[base + len(copies)]))

    add(own.at[layer], ids[0] * rows, rows)
    add(core.at[layer], ids[1] * rows, rows)
    at = pl.ds(columns, target.shape[1])
    for shard, owner in ((near, ids[2]), (diagonal, ids[3])):
        for part in range(parts):
            start = owner * rows + (position(ids[5], mode) ^ part) * step
            add(shard.at[pl.ds(part * step, step), at], start, step)
    return copies


def begin(copies):
    for copy in copies:
        copy.start()


def finish(copies):
    for copy in copies:
        copy.wait()


def attn_copies(layer, ids, refs, mode, w_qkv, w_o, sems):
    qkv_own, qkv_core, o_own, o_core, near, diagonal = refs
    qkv = weight_copies(ids, layer, (qkv_own, qkv_core, near, diagonal), mode, w_qkv, 0, sems, 0)
    o = weight_copies(ids, layer, (o_own, o_core, near, diagonal), mode, w_o, w_qkv.shape[1], sems, 10)
    return qkv, o


def cut_kernel(slabs, ids, qkv, o, w_in, w_out, *rest):
    outs, sems = rest[:-1], rest[-1]
    copies = []
    for slab, out in zip(slabs, outs):
        layer, which = divmod(slab, 3)
        begins = 0
        for weight in ((qkv, o), (w_in,), (w_out,))[which]:
            rows = out.shape[0]
            start = pl.multiple_of(position(ids[5], MODES[slab]) * rows, rows)
            source = weight.at[layer, pl.ds(start, rows), :]
            target = out.at[:, pl.ds(begins, weight.shape[2])]
            copies.append(pltpu.make_async_copy(source, target, sems.at[len(copies)]))
            begins += weight.shape[2]
    begin(copies)
    finish(copies)


def pack_kernel(*refs):
    shorts, in_bias, packed = refs[:8], refs[8], refs[9]
    layers, share = shorts[0].shape
    for layer in range(layers):
        for i, short in enumerate(shorts):
            packed[layer, i : i + 1, :] = short[layer : layer + 1, :].astype(f32)
        for i in range(4):
            packed[layer, 8 + i : 9 + i, :] = in_bias[layer : layer + 1, i * share : (i + 1) * share].astype(f32)


def attn_fwd_kernel(layer, mode, ids, length, x, cell_row, small, *rest):
    weights, rest = rest[:6], rest[6:]
    qkv_rows, probs, context, unit_out, inverse_out, w_qkv, w_o, mask, sems = rest
    tokens, width = x.shape
    qkv_copies, o_copies = attn_copies(layer, ids, weights, mode, w_qkv, w_o, sems)
    begin(qkv_copies)
    begin(o_copies)
    position = lax.broadcasted_iota(jnp.int32, (tokens, 1), 0)
    query_cell = cell_row[...]
    square = (tokens, tokens)
    diagonal = lax.broadcasted_iota(jnp.int32, square, 0) == lax.broadcasted_iota(jnp.int32, square, 1)
    key_cell = jnp.sum(jnp.where(diagonal, query_cell, 0), axis=1, keepdims=True)
    allowed = (query_cell == key_cell) | (key_cell == 0) | (query_cell == 0)
    allowed = allowed & (position < length[0])
    mask[...] = jnp.where(allowed, 0.0, masked_score)
    scale = 1.0 / math.sqrt(width // HEADS)
    finish(qkv_copies)
    for part in range(3):
        columns = slice(part * width, (part + 1) * width)
        rows = dot(x[...], w_qkv[:, columns])
        if part != 1:
            rows = rows + small[layer, part // 2 : part // 2 + 1, :]
        if part == 0:
            rows = rows * scale
        qkv_rows[:, columns] = rows.astype(low)

    pair_width = 2 * width // HEADS
    first = lax.broadcasted_iota(jnp.int32, (1, pair_width), 1) < pair_width // 2

    for pair in range(HEADS // 2):
        at = slice(pair * pair_width, (pair + 1) * pair_width)
        query = qkv_rows[:, at]
        key = qkv_rows[:, width + at.start : width + at.stop]
        value = qkv_rows[:, 2 * width + at.start : 2 * width + at.stop]
        sides = []
        for side in range(2):
            mine = first if side == 0 else jnp.logical_not(first)
            scores = dot_nt(key, jnp.where(mine, query, jnp.zeros_like(query))) + mask[...]
            shifted = jnp.exp(scores - jnp.max(scores, axis=0, keepdims=True))
            total = jnp.sum(shifted, axis=0, keepdims=True)
            prob = (shifted * (1.0 / total)).astype(low)
            probs[2 * pair + side] = prob
            sides.append(dot_tn(prob, value))
        context[:, at] = jnp.where(first, sides[0], sides[1]).astype(low)

    finish(o_copies)
    residual = x[...].astype(f32) + (dot(context[...], w_o[...]) + small[layer, 2:3, :])
    unit, inverse = normalize(residual)
    unit_out[...] = unit
    inverse_out[...] = inverse


def gelu_and_slope(x):
    t = 1.0 / (1.0 + (0.3275911 * math.sqrt(0.5)) * jnp.abs(x))
    bell = jnp.exp(-0.5 * x * x)
    series = 1.421413741 + t * (-1.453152027 + t * 1.061405429)
    series = t * (0.254829592 + t * (-0.284496736 + t * series))
    tail = 0.5 * series * bell
    cdf = jnp.where(x >= 0.0, 1.0 - tail, tail)
    return (x * cdf).astype(low), cdf + x * (bell * (1.0 / math.sqrt(2.0 * math.pi)))


def ffn_fwd_kernel(layer, modes, ids, unit_one, in_bias, small, *rest):
    weights, rest = rest[:8], rest[8:]
    hidden_out, slope_out, unit_out, inverse_out, result = rest[:5]
    w_in, w_out, normed_low, hidden, slope, sems, out_sems = rest[5:]
    in_copies = weight_copies(ids, layer, weights[:4], modes[0], w_in, 0, sems, 0)
    out_copies = weight_copies(ids, layer, weights[4:], modes[1], w_out, 0, sems, 10)
    begin(in_copies)
    begin(out_copies)
    normed = unit_one[...] * small[layer, 3:4, :] + small[layer, 4:5, :]
    normed_low[...] = normed.astype(low)
    finish(in_copies)
    tile = w_in.shape[1] // 4
    going = []
    for t in range(4):
        columns = pl.ds(t * tile, tile)
        pre = dot(normed_low[...], w_in[:, columns]) + in_bias[layer, :, columns]
        hidden[:, columns], slope[:, columns] = gelu_and_slope(pre)
        leaving = [
            pltpu.make_async_copy(hidden.at[:, columns], hidden_out.at[:, columns], out_sems.at[2 * t]),
            pltpu.make_async_copy(slope.at[:, columns], slope_out.at[:, columns], out_sems.at[2 * t + 1]),
        ]
        begin(leaving)
        going += leaving

    finish(out_copies)
    residual = unit_one[...] * small[layer, 3:4, :] + small[layer, 4:5, :] + (dot(hidden[...], w_out[...]) + small[layer, 5:6, :])
    unit, inverse = normalize(residual)
    unit_out[...] = unit
    inverse_out[...] = inverse
    result[...] = (unit * small[layer, 6:7, :] + small[layer, 7:8, :]).astype(low)
    finish(going)


WIDE_BIT = {"y": 0, "z": 1}


def place_of(ids, owner, piece, way):
    away = None if owner is None else ids[0] ^ owner
    off = None if piece is None else piece ^ ids[5]
    place = [None if away is None else away & 1]
    for name in way:
        if name == "x":
            place.append(pl.ds(0, 2) if away is None else away >> 1)
        else:
            place.append(pl.ds(0, 2) if off is None else (off >> WIDE_BIT[name]) & 1)
    return tuple(place) + (pl.ds(0, 2) if piece is None else piece >> 2,)


def store_rows(stage, ids, product, piece, way):
    share = product.shape[0] // 4
    for owner in range(4):
        block = product[owner * share : (owner + 1) * share].astype(low)
        stage[place_of(ids, owner, piece, way) + (pl.ds(0, share),)] = block


def piece_copies(stage, ids, piece, way, kept, sent, sems, turn):
    at = place_of(ids, None, piece, way)[1:]
    copies = [
        pltpu.make_async_copy(stage.at[(1,) + at], sent.at[at], sems.at[2 * turn]),
        pltpu.make_async_copy(stage.at[(0,) + at], kept.at[at], sems.at[2 * turn + 1]),
    ]
    begin(copies)
    return copies


def out_bwd_kernel(layer, way, ids, *refs):
    finish(out_part(layer, way, ids, *refs))


def out_part(layer, way, ids, grad, unit_two, inverse_two, hidden, small, *rest):
    d_ffn, d_resid_two, small_grads, kept, sent, stage, out_sems = rest
    g = grad[...].astype(f32)
    unit = unit_two[...]
    small_grads[0:1, :] = jnp.sum(g * unit, axis=0, keepdims=True)
    small_grads[1:2, :] = jnp.sum(g, axis=0, keepdims=True)
    d_two = normalize_back(g * small[layer, 6:7, :], unit, inverse_two[...])
    d_resid_two[...] = d_two
    d_low = d_two.astype(low)
    d_ffn[...] = d_low
    small_grads[2:3, :] = jnp.sum(d_low.astype(f32), axis=0, keepdims=True)
    small_grads[3:8, :] = jnp.zeros((5, unit.shape[1]), f32)
    tile = hidden.shape[1] // 8
    share = d_ffn.shape[1] // 4
    waits = []
    for owner in range(4):
        for half in range(2):
            columns = slice((2 * owner + half) * tile, (2 * owner + half + 1) * tile)
            out_grad = dot_tn(hidden[:, columns], d_ffn[...])
            for row_group in range(2):
                for column_group in range(2):
                    piece = (half * 2 + row_group) * 2 + column_group
                    block = out_grad[
                        row_group * share : (row_group + 1) * share,
                        column_group * tile : (column_group + 1) * tile,
                    ]
                    stage[place_of(ids, owner, piece, way)] = block.astype(low)
        core, *at = place_of(ids, owner, None, way)
        at = tuple(at)
        to_kept = pltpu.make_async_copy(stage.at[(0,) + at], kept.at[at], out_sems.at[owner])
        to_sent = pltpu.make_async_copy(stage.at[(1,) + at], sent.at[at], out_sems.at[owner])
        pl.when(core == 0)(to_kept.start)
        pl.when(core == 1)(to_sent.start)
        waits.append(to_kept)
    return waits


def in_bwd_kernel(layer, way, modes, ids, d_ffn, unit_one, inverse_one, small, resid_in, slope_in, *rest):
    weights, rest = rest[:8], rest[8:]
    outs, (w_in, w_out, d_pre, normed_t, slope, d_resid_two, stage, sems, out_sems, more_sems) = rest[:5], rest[5:]
    in_copies = weight_copies(ids, layer, weights[:4], modes[0], w_in, 0, sems, 0)
    out_copies = weight_copies(ids, layer, weights[4:], modes[1], w_out, 0, sems, 10)
    slope_copy = pltpu.make_async_copy(slope_in, slope, more_sems.at[0])
    resid_copy = pltpu.make_async_copy(resid_in, d_resid_two, more_sems.at[1])
    begin(out_copies + [slope_copy] + in_copies + [resid_copy])
    late = (out_copies + [slope_copy], in_copies + [resid_copy])
    refs = (d_ffn, d_resid_two, unit_one, inverse_one, small, slope, w_in, w_out, d_pre, normed_t, stage, out_sems)
    finish(in_part(layer, way, ids, late, *refs, *outs))


def in_part(layer, way, ids, late, d_ffn, d_resid_two, unit_one, inverse_one, small, slope, w_in, w_out, *rest):
    d_pre, normed_t, stage, out_sems, d_resid, small_grads, in_bias_grad, kept, sent = rest
    normed = unit_one[...] * small[layer, 3:4, :] + small[layer, 4:5, :]
    normed_t[...] = normed.astype(low).T
    finish(late[0])
    tile = w_in.shape[1] // 4
    going = []
    for t in range(4):
        columns = slice(t * tile, (t + 1) * tile)
        d_hidden = dot_nt(d_ffn[...], w_out[columns, :])
        d_tile = (d_hidden * slope[:, columns]).astype(low)
        d_pre[:, columns] = d_tile
        in_bias_grad[:, columns] = jnp.sum(d_tile.astype(f32), axis=0, keepdims=True)
        product = dot(normed_t[...], d_tile)
        for half in range(2):
            piece = 2 * t + half
            store_rows(stage, ids, product[:, half * tile // 2 : (half + 1) * tile // 2], piece, way)
            going += piece_copies(stage, ids, piece, way, kept, sent, out_sems, piece)
    finish(late[1])
    d_normed = d_resid_two[...] + dot_nt(d_pre[...], w_in[...])
    unit = unit_one[...]
    small_grads[0:1, :] = jnp.sum(d_normed * unit, axis=0, keepdims=True)
    small_grads[1:2, :] = jnp.sum(d_normed, axis=0, keepdims=True)
    small_grads[2:8, :] = jnp.zeros((6, unit.shape[1]), f32)
    d_resid[...] = normalize_back(d_normed * small[layer, 3:4, :], unit, inverse_one[...])
    return going


def ffn_bwd_kernel(layer, ways, modes, ids, grad, unit_two, inverse_two, hidden, unit_one, inverse_one, small, *rest):
    slope_in, weights, rest = rest[0], rest[1:9], rest[9:]
    out_small, out_kept, out_sent = rest[:3]
    outs, rest = rest[3:8], rest[8:]
    w_in, w_out, d_ffn, d_resid_two, d_pre, normed_t, slope, out_stage, stage, sems, owner_sems, out_sems, slope_sem = rest
    in_copies = weight_copies(ids, layer, weights[:4], modes[0], w_in, 0, sems, 0)
    out_copies = weight_copies(ids, layer, weights[4:], modes[1], w_out, 0, sems, 10)
    slope_copy = pltpu.make_async_copy(slope_in, slope, slope_sem.at[0])
    begin(out_copies + [slope_copy] + in_copies)
    refs = (grad, unit_two, inverse_two, hidden, small, d_ffn, d_resid_two, out_small, out_kept, out_sent)
    going = out_part(layer, ways[0], ids, *refs, out_stage, owner_sems)
    refs = (d_ffn, d_resid_two, unit_one, inverse_one, small, slope, w_in, w_out, d_pre, normed_t, stage, out_sems)
    going += in_part(layer, ways[1], ids, (out_copies + [slope_copy], in_copies), *refs, *outs)
    finish(going)


def attn_bwd_kernel(layer, way, mode, ids, d_resid, x, qkv_rows, probs, context, *rest):
    weights, others, rest = rest[:6], rest[6:-13], rest[-13:]
    d_input, small_grads, kept, sent = rest[:4]
    w_qkv, w_o, d_attn, d_context, d_qkv, x_t, stage, sems, out_sems = rest[4:]
    tokens, width = x.shape
    qkv_copies, o_copies = attn_copies(layer, ids, weights, mode, w_qkv, w_o, sems)
    begin(o_copies)
    begin(qkv_copies)
    d_low = d_resid[...].astype(low)
    d_attn[...] = d_low
    small_grads[2:3, :] = jnp.sum(d_low.astype(f32), axis=0, keepdims=True)
    x_t[...] = x[...].T
    tile = width // 2
    product = dot_tn(context[...], d_attn[...])
    for half in range(2):
        store_rows(stage, ids, product[:, half * tile : (half + 1) * tile], 6 + half, way)
    finish(o_copies)
    d_context[...] = dot_nt(d_attn[...], w_o[...]).astype(low)
    pair_width = 2 * width // HEADS
    first = lax.broadcasted_iota(jnp.int32, (1, pair_width), 1) < pair_width // 2
    scale = 1.0 / math.sqrt(width // HEADS)

    for pair in range(HEADS // 2):
        at_query = slice(pair * pair_width, (pair + 1) * pair_width)
        at_key = slice(width + at_query.start, width + at_query.stop)
        at_value = slice(2 * width + at_query.start, 2 * width + at_query.stop)
        query, key, value = qkv_rows[:, at_query], qkv_rows[:, at_key], qkv_rows[:, at_value]
        d_ctx = d_context[:, at_query]
        sides = []
        for side in range(2):
            mine = first if side == 0 else jnp.logical_not(first)
            prob_low = probs[2 * pair + side]
            prob = prob_low.astype(f32)
            d_prob = dot_nt(value, jnp.where(mine, d_ctx, jnp.zeros_like(d_ctx)))
            inner = jnp.sum(prob * d_prob, axis=0, keepdims=True)
            d_scores = (prob * (d_prob - inner)).astype(low)
            sides.append((dot_tn(d_scores, key), dot(d_scores, query), dot(prob_low, d_ctx)))
        d_qkv[:, at_query] = (jnp.where(first, sides[0][0], sides[1][0]) * scale).astype(low)
        d_qkv[:, at_key] = jnp.where(first, sides[0][1], sides[1][1]).astype(low)
        d_qkv[:, at_value] = jnp.where(first, sides[0][2], sides[1][2]).astype(low)

    small_grads[0:1, :] = jnp.sum(d_qkv[:, :width].astype(f32), axis=0, keepdims=True)
    small_grads[1:2, :] = jnp.sum(d_qkv[:, 2 * width :].astype(f32), axis=0, keepdims=True)
    small_grads[3:8, :] = jnp.zeros((5, width), f32)
    if others:
        share = width // 4
        sources = small_sources(layer, small_grads, others)
        for owner in range(4):
            for piece in range(8):
                lines = []
                for source, row, start, step in sources[3 * piece : 3 * piece + 3]:
                    line = source[row : row + 1, start + owner * step : start + owner * step + share]
                    lines.append(jnp.concatenate([line, jnp.zeros_like(line)], axis=1))
                lines.append(jnp.zeros((SMALL_ROWS - 3, tile), f32))
                block = jnp.concatenate(lines, axis=0).astype(low)
                stage[place_of(ids, owner, piece, way) + (pl.ds(share, SMALL_ROWS),)] = block
    going = []
    for part in (3, 0, 1, 2):
        if part < 3:
            product = dot(x_t[...], d_qkv[:, part * width : (part + 1) * width])
        for half in range(2):
            piece = 2 * part + half
            if part < 3:
                store_rows(stage, ids, product[:, half * tile : (half + 1) * tile], piece, way)
            going += piece_copies(stage, ids, piece, way, kept, sent, out_sems, piece)
    finish(qkv_copies)
    d_input[...] = (d_resid[...] + dot_nt(d_qkv[...], w_qkv[...])).astype(low)
    finish(going)


SMALL_ROWS = 16
SMALL_LINES = (("attn", 0), ("attn", 1), ("attn", 2), ("in", 0), ("in", 1), ("out", 2), ("out", 0), ("out", 1))


def small_sources(layer, own, others):
    found = []
    out_0, in_0, bias_0, out_1, in_1, bias_1, attn_1 = others
    refs = ({"attn": own, "in": in_0, "out": out_0}, {"attn": attn_1, "in": in_1, "out": out_1})
    width = own.shape[1]
    for of_layer, bias in zip(refs, (bias_0, bias_1)):
        found += [(of_layer[name], row, 0, width // 4) for name, row in SMALL_LINES]
        found += [(bias, 0, i * (width // 4), width) for i in range(4)]
    return found


def unpack_kernel(layer, slab, back, earlier, ids, near, far, *rest):
    outs = rest[earlier:-4]
    buffer, wide_buffer, in_sems, out_sems = rest[-4:]
    share, tile = wide_buffer.shape[1:]

    def fetch(piece, ref, index):
        return pltpu.make_async_copy(ref.at[index], buffer.at[piece], in_sems.at[piece])

    for piece in range(8):
        off = piece ^ ids[5]
        inner, outer = [(off >> WIDE_BIT[name]) & 1 for name in back]
        pl.when(outer == 0)(fetch(piece, near, (inner, piece >> 2)).start)
        pl.when(outer == 1)(fetch(piece, far, (inner, piece >> 2)).start)

    copies = []
    for piece in range(8):
        fetch(piece, near, (0, 0)).wait()
        wide_buffer[piece] = buffer[piece, :share].astype(f32)
        columns = pl.ds(piece * tile, tile)
        if slab == "in":
            target = outs[0].at[layer, :, columns]
        elif slab == "out":
            rows = pl.ds((piece // 2) * share, share)
            target = outs[0].at[layer, rows, pl.ds((piece % 2) * tile, tile)]
        elif piece < 6:
            target = outs[0].at[layer, :, columns]
        else:
            target = outs[1].at[layer, :, pl.ds((piece - 6) * tile, tile)]
        copies.append(pltpu.make_async_copy(wide_buffer.at[piece], target, out_sems.at[piece]))
        copies[-1].start()
    if slab == "attn" and layer == 0:
        for line in range(24):
            of_layer, which = line // 12, line % 12
            row = share + line % 3
            values = buffer[line // 3, row : row + 1, :share].astype(f32)
            if which < 8:
                outs[2 + which][of_layer : of_layer + 1, :] = values
            else:
                at = (which - 8) * share
                outs[10][of_layer : of_layer + 1, at : at + share] = values
    else:
        outs[-1][...] = jnp.zeros(outs[-1].shape, f32)
    finish(copies)


SMEM = pl.BlockSpec(memory_space=pltpu.SMEM)
VMEM = pl.BlockSpec(memory_space=pltpu.VMEM)
ANY = pl.BlockSpec(memory_space=pl.ANY)


def call(kernel, name, time, in_specs, out_specs, out_shape, scratch, args, aliases=()):
    return pl.pallas_call(
        kernel,
        name=name,
        in_specs=in_specs,
        out_specs=out_specs,
        out_shape=out_shape,
        scratch_shapes=scratch,
        input_output_aliases=dict(aliases),
        compiler_params=pltpu.CompilerParams(vmem_limit_bytes=VMEM_BYTES),
        cost_estimate=pl.CostEstimate(
            flops=int(time * 1.1e9), bytes_accessed=int(time * 3.6e6), transcendentals=0
        ),
    )(*args)


def shape(dims, kind):
    return jax.ShapeDtypeStruct(dims, kind)


def added(a, b):
    return (a.astype(f32) + b.astype(f32)).astype(low)


WAYS = ("zxy", "xyz", "yxz", "zyx", "xyz", "xyz")
BACKS = ("yz", "zy", "zy", "yz", "zy", "zy")
PLAN = (
    "out1", "in1", 0, 1, "attn1", "out0", "in0", 0, 1, "attn0", 1, 0, 2, 4, 1, 0, 3, 1, 2, 4, 0, 5, 3, 2, 4,
    0, 1, 2, 3, 2, 4, 5, 3, 0, 5, 4, 2, 5, 1, 3, 5, 4, 3, 2, 5, 4, 3, 5,
)
MODES = ("qz", "hz", "qy", "qz", "qy", "hy")
FORWARD = (
    "h0", "g0", "g2", "cut", "x0", "h2", "h3", "c0", "g3", "pack", "h1", "x2", "h5", "h4", "g1", "y0", "z0",
    "x3", "z2", "y2", "y3", "c3", "q0", "x5", "q2", "z3", "x1", "q3", "y5", "x4", "z1", "sm", "A", "y4", "d0",
    "z4", "c1", "attn1", "c2", "d3", "d1", "q4", "d2", "ffn1", "d4", "d5", "attn2", "ffn2",
)
TIMES = {
    "pack": 1, "attn1": 5, "ffn1": 13, "attn2": 3, "ffn2": 8,
    "out_bwd1": 3, "in_bwd1": 20.0, "attn_bwd1": 0.3, "out_bwd0": 2.0, "in_bwd0": 1.0, "attn_bwd0": 8.0,
}


class Order:
    def __init__(self, ids):
        self.ids = ids

    def wait(self, values):
        values, self.ids = lax.optimization_barrier((values, self.ids))
        return values


STEPS = {"x": ("narrow", 2), "y": ("wide", 1), "z": ("wide", 2)}


class Slab:
    def __init__(self, way, back, wide_count, kept, sent):
        self.kept = kept
        self.way, self.back = way, back
        self.rest = [1 << b for b in range(HALVINGS, wide_count.bit_length() - 1)]
        self.flying = swap(sent, "narrow", 1)
        self.stage = 0

    def step(self, order):
        received = order.wait(self.flying)
        stage, way = self.stage, self.way
        if stage < len(way):
            send = order.wait(added(self.kept[1], received[1]))
            self.kept = added(self.kept[0], received[0])
            self.flying = swap(send, *STEPS[way[stage]])
        elif stage < len(way) + 1 + len(self.back):
            if stage == len(way):
                piece = added(self.kept, received)
                for bit in self.rest[:-1]:
                    piece = added(piece, swap(piece, "wide", bit))
                self.kept = order.wait(piece)
                self.flying = swap(self.kept, "wide", self.rest[-1])
            else:
                if stage == len(way) + 1:
                    self.block = added(self.kept, received)[None]
                else:
                    self.block = jnp.concatenate([self.block, received], axis=0)
                self.block = order.wait(self.block)
                self.flying = swap(self.block, *STEPS[self.back[stage - len(way) - 1]])
        else:
            self.far = received
        self.stage += 1

    def ended(self):
        return self.stage == len(self.way) + len(self.back) + 2


def body(
    tables_in,
    cotangent,
    cell_ids,
    lengths,
    qkv_weight,
    q_bias,
    v_bias,
    o_weight,
    o_bias,
    norm1_gain,
    norm1_bias,
    in_weight,
    in_bias,
    out_weight,
    out_bias,
    norm2_gain,
    norm2_bias,
):
    tokens, width = tables_in.shape
    layers, share, ffn = in_weight.shape
    ffn_share = out_weight.shape[1]
    wide_count = lax.axis_size("wide")
    assert wide_count & (wide_count - 1) == 0 and wide_count > 1 << HALVINGS and lax.axis_size("narrow") == 4
    tile = ffn // 8
    me = lax.axis_index("narrow").astype(jnp.int32)
    wide_me = lax.axis_index("wide").astype(jnp.int32)
    y = wide_me & 1
    ids = jnp.stack([me, me ^ 1, me ^ 2, me ^ 3, y, wide_me & (2**HALVINGS - 1)])

    order = Order(ids)

    own = (qkv_weight, o_weight, in_weight, out_weight)
    parts = [None] * 6

    def cut(*slabs):
        outs = []
        for slab in slabs:
            weight = (qkv_weight, in_weight, out_weight)[slab % 3]
            columns = 4 * width if slab % 3 == 0 else weight.shape[2]
            outs.append(shape((weight.shape[1] // (4 if MODES[slab][0] == "q" else 2), columns), low))
        results = call(
            functools.partial(cut_kernel, slabs),
            "cut",
            1,
            [SMEM] + [ANY] * 4,
            [VMEM] * len(slabs),
            outs,
            [pltpu.SemaphoreType.DMA((8,))],
            (order.ids, *own),
        )
        for slab, part in zip(slabs, results):
            parts[slab] = part

    first_slab = [int(token[1]) for token in FORWARD if token[0] == "h"][0]
    cut(first_slab)
    near, diagonal, core = [None] * 6, [None] * 6, [None] * 4
    transfers = [{} for _ in range(6)]

    def joined(i, *names):
        near[i] = order.wait(jnp.concatenate([transfers[i][name] for name in names], axis=0))
        transfers[i]["d"] = swap(near[i], "narrow", 1)

    def weight_step(kind, i):
        moving, mode = transfers[i], MODES[i]
        if kind == "h":
            moving["x"] = swap(order.wait(parts[i]), "narrow", 2)
            return
        moving[kind] = order.wait(moving[kind])
        if kind == "x":
            for name, bit in (("y", 1), ("z", 2)):
                if mode[0] == "q" or mode[1] == name:
                    moving[name] = swap(moving["x"], "wide", bit)
        elif kind == "d":
            diagonal[i] = moving["d"]
        elif kind == "q":
            joined(i, "x", "y", "z", "q")
        elif mode[0] == "h":
            joined(i, "x", kind)
        elif mode[1] != kind:
            moving["q"] = swap(moving[kind], "wide", 1 if mode[1] == "y" else 2)

    def in_order(low_one, high_one, bit):
        swapped = (me & bit) != 0
        return jnp.stack([jnp.where(swapped, high_one, low_one), jnp.where(swapped, low_one, high_one)])

    def attn_weights(layer):
        return (qkv_weight, core[0], o_weight, core[1], near[3 * layer], diagonal[3 * layer])

    def in_weights(layer):
        return (in_weight, core[2], near[3 * layer + 1], diagonal[3 * layer + 1])

    def out_weights(layer):
        return (out_weight, core[3], near[3 * layer + 2], diagonal[3 * layer + 2])

    w_qkv = pltpu.VMEM((width, 3 * width), low)
    w_o = pltpu.VMEM((width, width), low)
    w_in = pltpu.VMEM((width, ffn), low)
    w_out = pltpu.VMEM((ffn, width), low)
    copy_sems = pltpu.SemaphoreType.DMA((20,))
    piece_sems = pltpu.SemaphoreType.DMA((16,))
    rows_f32 = shape((tokens, width), f32)
    rows_low = shape((tokens, width), low)
    column_f32 = shape((tokens, 1), f32)
    eight_f32 = shape((8, width), f32)

    def pieces(rows):
        return [shape((2, 2, 2, 2, rows, tile), low)] * 2

    def stage(rows):
        return pltpu.VMEM((2, 2, 2, 2, 2, rows, tile), low)

    def tie(outs, which):
        outs = list(outs)
        outs[which] = order.wait(outs[which])
        return outs

    def attn_forward(layer, x):
        x = order.wait(x)
        outs = call(
            functools.partial(attn_fwd_kernel, layer, MODES[3 * layer]),
            "attn_fwd",
            TIMES["attn%d" % (layer + 1)],
            [SMEM, SMEM] + [VMEM] * 3 + [ANY] * 6,
            [VMEM] * 5,
            [shape((tokens, 3 * width), low), shape((HEADS, tokens, tokens), low), rows_low, rows_f32, column_f32],
            [w_qkv, w_o, pltpu.VMEM((tokens, tokens), f32), copy_sems],
            (order.ids, lengths, x, cell_ids, small) + attn_weights(layer),
        )
        return tie(outs, 3)

    def ffn_forward(layer, unit_one):
        unit_one = order.wait(unit_one)
        outs = call(
            functools.partial(ffn_fwd_kernel, layer, MODES[3 * layer + 1 : 3 * layer + 3]),
            "ffn_fwd",
            TIMES["ffn%d" % (layer + 1)],
            [SMEM] + [VMEM] * 3 + [ANY] * 8,
            [ANY] * 2 + [VMEM] * 3,
            [shape((tokens, ffn), low), shape((tokens, ffn), f32), rows_f32, column_f32, rows_low],
            [
                w_in,
                w_out,
                pltpu.VMEM((tokens, width), low),
                pltpu.VMEM((tokens, ffn), low),
                pltpu.VMEM((tokens, ffn), f32),
                copy_sems,
                piece_sems,
            ],
            (order.ids, unit_one, full_in_bias, small) + in_weights(layer) + out_weights(layer),
        )
        return tie(outs, 4)

    def out_backward(layer, way, grad, unit_two, inverse_two, hidden):
        grad = order.wait(grad)
        outs = call(
            functools.partial(out_bwd_kernel, layer, way),
            "out_bwd",
            TIMES["out_bwd%d" % layer],
            [SMEM] + [VMEM] * 5,
            [VMEM] * 3 + [ANY] * 2,
            [rows_low, rows_f32, eight_f32] + pieces(share),
            [stage(share), pltpu.SemaphoreType.DMA((4,))],
            (order.ids, grad, unit_two, inverse_two, hidden, small),
        )
        return tie(outs, 0)

    def in_backward(layer, way, d_ffn, d_resid_two, unit_one, inverse_one, slope):
        d_ffn = order.wait(d_ffn)
        outs = call(
            functools.partial(in_bwd_kernel, layer, way, MODES[3 * layer + 1 : 3 * layer + 3]),
            "in_bwd",
            TIMES["in_bwd%d" % layer],
            [SMEM] + [VMEM] * 4 + [ANY] * 10,
            [VMEM] * 3 + [ANY] * 2,
            [rows_f32, eight_f32, shape((1, ffn), f32)] + pieces(share),
            [
                w_in,
                w_out,
                pltpu.VMEM((tokens, ffn), low),
                pltpu.VMEM((width, tokens), low),
                pltpu.VMEM((tokens, ffn), f32),
                pltpu.VMEM((tokens, width), f32),
                stage(share),
                copy_sems,
                piece_sems,
                pltpu.SemaphoreType.DMA((2,)),
            ],
            (order.ids, d_ffn, unit_one, inverse_one, small, d_resid_two, slope)
            + in_weights(layer)
            + out_weights(layer),
        )
        return tie(outs, 0)

    def ffn_backward(layer, ways, grad, attn_part, ffn_part):
        grad = order.wait(grad)
        hidden, slope, unit_two, inverse_two, _ = ffn_part
        outs = call(
            functools.partial(ffn_bwd_kernel, layer, ways, MODES[3 * layer + 1 : 3 * layer + 3]),
            "ffn_bwd",
            TIMES["in_bwd%d" % layer],
            [SMEM] + [VMEM] * 7 + [ANY] * 9,
            [VMEM] + [ANY] * 2 + [VMEM] * 3 + [ANY] * 2,
            [eight_f32] + pieces(share) + [rows_f32, eight_f32, shape((1, ffn), f32)] + pieces(share),
            [
                w_in,
                w_out,
                pltpu.VMEM((tokens, width), low),
                pltpu.VMEM((tokens, width), f32),
                pltpu.VMEM((tokens, ffn), low),
                pltpu.VMEM((width, tokens), low),
                pltpu.VMEM((tokens, ffn), f32),
                stage(share),
                stage(share),
                copy_sems,
                pltpu.SemaphoreType.DMA((4,)),
                piece_sems,
                pltpu.SemaphoreType.DMA((1,)),
            ],
            (order.ids, grad, unit_two, inverse_two, hidden, attn_part[3], attn_part[4], small, slope)
            + in_weights(layer)
            + out_weights(layer),
        )
        return tie(outs, 3)

    def attn_backward(layer, way, d_resid, x, qkv_rows, probs, context, small_others):
        d_resid = order.wait(d_resid)
        rows = share + (SMALL_ROWS if small_others else 0)
        outs = call(
            functools.partial(attn_bwd_kernel, layer, way, MODES[3 * layer]),
            "attn_bwd",
            TIMES["attn_bwd%d" % layer],
            [SMEM] + [VMEM] * 5 + [ANY] * 6 + [VMEM] * len(small_others),
            [VMEM] * 2 + [ANY] * 2,
            [rows_low, eight_f32] + pieces(rows),
            [
                w_qkv,
                w_o,
                pltpu.VMEM((tokens, width), low),
                pltpu.VMEM((tokens, width), low),
                pltpu.VMEM((tokens, 3 * width), low),
                pltpu.VMEM((width, tokens), low),
                stage(rows),
                copy_sems,
                piece_sems,
            ],
            (order.ids, d_resid, x, qkv_rows, probs, context) + attn_weights(layer) + tuple(small_others),
        )
        return tie(outs, 0)

    def unpack(layer, name, slab, earlier):
        dims = {
            "attn": [(layers, share, 3 * width), (layers, share, width)],
            "in": [(layers, share, ffn)],
            "out": [(layers, ffn_share, width)],
        }[name]
        last = name == "attn" and layer == 0
        extra = [(layers, share)] * 8 + [(layers, ffn_share)] if last else [(8, 128)]
        near, far = order.wait((slab.block, slab.far))
        rows = near.shape[2]
        outs = call(
            functools.partial(unpack_kernel, layer, name, slab.back, len(earlier)),
            "unpack",
            4,
            [SMEM] + [ANY] * (2 + len(earlier)),
            [ANY] * len(dims) + [VMEM] * len(extra),
            [shape(d, f32) for d in dims + extra],
            [
                pltpu.VMEM((8, rows, tile), low),
                pltpu.VMEM((8, share, tile), f32),
                pltpu.SemaphoreType.DMA((8,)),
                pltpu.SemaphoreType.DMA((8,)),
            ],
            (order.ids, near, far, *earlier),
            {3 + i: i for i in range(len(earlier))},
        )
        return tuple(tie(outs, 0))

    short = (q_bias, v_bias, o_bias, norm1_gain, norm1_bias, out_bias, norm2_gain, norm2_bias)
    inputs, attn_kept, ffn_kept = [tables_in], [], []
    for token in FORWARD:
        kind, i = (token[0], int(token[1])) if len(token) == 2 and token[1].isdigit() else (token, None)
        if token == "cut":
            cut(*[slab for slab in range(6) if slab != first_slab])
        elif kind == "g":
            core[i] = swap(order.wait(own[i]), "narrow", 1)
        elif kind == "c":
            core[i] = order.wait(core[i])
        elif i is not None:
            weight_step(kind, i)
        elif token == "pack":
            packed = call(
                pack_kernel,
                "pack",
                TIMES["pack"],
                [VMEM] * 9,
                VMEM,
                shape((layers, 12, share), f32),
                [],
                tuple(order.wait(short)) + (in_bias,),
            )
            packed = order.wait(packed)
            others = [lax.ppermute(packed, "narrow", [(j, j ^ away) for j in range(4)]) for away in (1, 2, 3)]
        elif token == "sm":
            others = order.wait(others)
        elif token == "A":
            packed = in_order(in_order(packed, others[0], 1), in_order(others[1], others[2], 1), 2)
            packed = packed.reshape(4, layers, 12, share)
            small = packed[:, :, :8].transpose(1, 2, 0, 3).reshape(layers, 8, width)
            full_in_bias = packed[:, :, 8:].transpose(1, 0, 2, 3).reshape(layers, 1, ffn)
            small, full_in_bias = order.wait((small, full_in_bias))
        elif token[:-1] == "attn":
            attn_kept.append(attn_forward(int(token[-1]) - 1, inputs[-1]))
        else:
            ffn_kept.append(ffn_forward(int(token[-1]) - 1, attn_kept[-1][3]))
            inputs.append(ffn_kept[-1][4])
    mixed_out = inputs[-1]

    slabs = [None] * 6
    grad = cotangent
    small_out, small_in, small_attn, bias_grads = [None] * 2, [None] * 2, [None] * 2, [None] * 2
    unpacked = {"attn": (), "in": (), "out": ()}
    for action in PLAN:
        if isinstance(action, int):
            slab = slabs[action]
            slab.step(order)
            if slab.ended():
                name = ("out", "in", "attn")[action % 3]
                unpacked[name] = unpack(layers - 1 - action // 3, name, slab, unpacked[name][: 2 if name == "attn" else 1])
            continue
        name, layer = action[:-1], int(action[-1])
        which = 3 * (layers - 1 - layer) + ("out", "in", "attn").index(name)
        way = WAYS[which]
        qkv_rows, probs, context, unit_one, inverse_one = attn_kept[layer]
        hidden, slope, unit_two, inverse_two, _ = ffn_kept[layer]
        if name == "out" and layer == 0:
            continue
        if name == "in" and layer == 0:
            outs = ffn_backward(layer, WAYS[which - 1 : which + 1], grad, attn_kept[layer], ffn_kept[layer])
            small_out[layer], out_kept, out_sent, d_resid, small_in[layer], bias_grads[layer], kept, sent = outs
            slabs[which - 1] = Slab(WAYS[which - 1], BACKS[which - 1], wide_count, out_kept, out_sent)
        elif name == "out":
            d_ffn, d_resid_two, small_out[layer], kept, sent = out_backward(
                layer, way, grad, unit_two, inverse_two, hidden
            )
        elif name == "in":
            d_resid, small_in[layer], bias_grads[layer], kept, sent = in_backward(
                layer, way, d_ffn, d_resid_two, unit_one, inverse_one, slope
            )
        else:
            small_others = ()
            if layer == 0:
                small_others = (
                    small_out[0],
                    small_in[0],
                    bias_grads[0],
                    small_out[1],
                    small_in[1],
                    bias_grads[1],
                    small_attn[1],
                )
            grad, small_attn[layer], kept, sent = attn_backward(
                layer, way, d_resid, inputs[layer], qkv_rows, probs, context, small_others
            )
        slabs[which] = Slab(way, BACKS[which], wide_count, kept, sent)
    qkv_grad, o_grad, *vectors = unpacked["attn"]
    in_grad, out_grad = unpacked["in"][0], unpacked["out"][0]
    return (
        mixed_out,
        grad,
        qkv_grad,
        vectors[0],
        vectors[1],
        o_grad,
        vectors[2],
        vectors[3],
        vectors[4],
        in_grad,
        vectors[8],
        out_grad,
        vectors[5],
        vectors[6],
        vectors[7],
    )


def solution(mesh):
    by_table = P(("wide", "narrow"), None)
    matrix = P(None, "narrow", None)
    vector = P(None, "narrow")
    return jax.shard_map(
        body,
        mesh=mesh,
        in_specs=(
            by_table,
            by_table,
            by_table,
            P(("wide", "narrow")),
            matrix,
            vector,
            vector,
            matrix,
            vector,
            vector,
            vector,
            matrix,
            vector,
            matrix,
            vector,
            vector,
            vector,
        ),
        out_specs=(
            by_table,
            by_table,
            matrix,
            vector,
            vector,
            matrix,
            vector,
            vector,
            vector,
            matrix,
            vector,
            matrix,
            vector,
            vector,
            vector,
        ),
        check_vma=False,
    )
```

```python
import functools
import math

import jax
import jax.numpy as jnp
from jax import lax
from jax.experimental import pallas as pl
from jax.experimental.pallas import tpu as pltpu
from jax.sharding import PartitionSpec as P

HEADS = 12
norm_eps = 1e-12
masked_score = -1000000000.0
low = jnp.bfloat16
f32 = jnp.float32
VMEM_BYTES = 56 * 1024 * 1024
HALVINGS = 2


def swap(value, axis, bit):
    count = lax.axis_size(axis)
    return lax.ppermute(value, axis, [(i, i ^ bit) for i in range(count)])


def dot(a, b):
    return jnp.dot(a, b, preferred_element_type=f32)


def dot_nt(a, b):
    return lax.dot_general(a, b, (((1,), (1,)), ((), ())), preferred_element_type=f32)


def dot_tn(a, b):
    return lax.dot_general(a, b, (((0,), (0,)), ((), ())), preferred_element_type=f32)


def normalize(residual):
    center = residual - jnp.mean(residual, axis=-1, keepdims=True)
    inverse = lax.rsqrt(jnp.mean(center * center, axis=-1, keepdims=True) + norm_eps)
    return center * inverse, inverse


def normalize_back(grad_unit, unit, inverse):
    centered = grad_unit - jnp.mean(grad_unit, axis=-1, keepdims=True)
    return inverse * (centered - unit * jnp.mean(grad_unit * unit, axis=-1, keepdims=True))


def position(wide_bits, mode):
    y, z = wide_bits & 1, wide_bits >> 1
    return {"hy": y, "hz": z}.get(mode, wide_bits)


def weight_copies(ids, layer, pieces, mode, target, columns, sems, base):
    own, core, near, diagonal = pieces
    rows = own.shape[1]
    parts = 4 if mode[0] == "q" else 2
    step = rows // parts
    copies = []

    def add(source, start, count):
        where = target.at[pl.ds(pl.multiple_of(start, step), count), :]
        copies.append(pltpu.make_async_copy(source, where, sems.at[base + len(copies)]))

    add(own.at[layer], ids[0] * rows, rows)
    add(core.at[layer], ids[1] * rows, rows)
    at = pl.ds(columns, target.shape[1])
    for shard, owner in ((near, ids[2]), (diagonal, ids[3])):
        for part in range(parts):
            start = owner * rows + (position(ids[5], mode) ^ part) * step
            add(shard.at[pl.ds(part * step, step), at], start, step)
    return copies


def begin(copies):
    for copy in copies:
        copy.start()


def finish(copies):
    for copy in copies:
        copy.wait()


def attn_copies(layer, ids, refs, mode, w_qkv, w_o, sems):
    qkv_own, qkv_core, o_own, o_core, near, diagonal = refs
    qkv = weight_copies(ids, layer, (qkv_own, qkv_core, near, diagonal), mode, w_qkv, 0, sems, 0)
    o = weight_copies(ids, layer, (o_own, o_core, near, diagonal), mode, w_o, w_qkv.shape[1], sems, 10)
    return qkv, o


def cut_kernel(slabs, ids, qkv, o, w_in, w_out, *rest):
    outs, sems = rest[:-1], rest[-1]
    copies = []
    for slab, out in zip(slabs, outs):
        layer, which = divmod(slab, 3)
        begins = 0
        for weight in ((qkv, o), (w_in,), (w_out,))[which]:
            rows = out.shape[0]
            start = pl.multiple_of(position(ids[5], MODES[slab]) * rows, rows)
            source = weight.at[layer, pl.ds(start, rows), :]
            target = out.at[:, pl.ds(begins, weight.shape[2])]
            copies.append(pltpu.make_async_copy(source, target, sems.at[len(copies)]))
            begins += weight.shape[2]
    begin(copies)
    finish(copies)


def pack_kernel(*refs):
    shorts, in_bias, packed = refs[:8], refs[8], refs[9]
    layers, share = shorts[0].shape
    for layer in range(layers):
        for i, short in enumerate(shorts):
            packed[layer, i : i + 1, :] = short[layer : layer + 1, :].astype(f32)
        for i in range(4):
            packed[layer, 8 + i : 9 + i, :] = in_bias[layer : layer + 1, i * share : (i + 1) * share].astype(f32)


def attn_fwd_kernel(layer, mode, ids, length, x, cell_row, small, *rest):
    weights, rest = rest[:6], rest[6:]
    qkv_rows, probs, context, unit_out, inverse_out, w_qkv, w_o, mask, sems = rest
    tokens, width = x.shape
    qkv_copies, o_copies = attn_copies(layer, ids, weights, mode, w_qkv, w_o, sems)
    begin(qkv_copies)
    begin(o_copies)
    position = lax.broadcasted_iota(jnp.int32, (tokens, 1), 0)
    query_cell = cell_row[...]
    square = (tokens, tokens)
    diagonal = lax.broadcasted_iota(jnp.int32, square, 0) == lax.broadcasted_iota(jnp.int32, square, 1)
    key_cell = jnp.sum(jnp.where(diagonal, query_cell, 0), axis=1, keepdims=True)
    allowed = (query_cell == key_cell) | (key_cell == 0) | (query_cell == 0)
    allowed = allowed & (position < length[0])
    mask[...] = jnp.where(allowed, 0.0, masked_score)
    scale = 1.0 / math.sqrt(width // HEADS)
    finish(qkv_copies)
    for part in range(3):
        columns = slice(part * width, (part + 1) * width)
        rows = dot(x[...], w_qkv[:, columns])
        if part != 1:
            rows = rows + small[layer, part // 2 : part // 2 + 1, :]
        if part == 0:
            rows = rows * scale
        qkv_rows[:, columns] = rows.astype(low)

    pair_width = 2 * width // HEADS
    first = lax.broadcasted_iota(jnp.int32, (1, pair_width), 1) < pair_width // 2

    for pair in range(HEADS // 2):
        at = slice(pair * pair_width, (pair + 1) * pair_width)
        query = qkv_rows[:, at]
        key = qkv_rows[:, width + at.start : width + at.stop]
        value = qkv_rows[:, 2 * width + at.start : 2 * width + at.stop]
        sides = []
        for side in range(2):
            mine = first if side == 0 else jnp.logical_not(first)
            scores = dot_nt(key, jnp.where(mine, query, jnp.zeros_like(query))) + mask[...]
            shifted = jnp.exp(scores - jnp.max(scores, axis=0, keepdims=True))
            total = jnp.sum(shifted, axis=0, keepdims=True)
            prob = (shifted * (1.0 / total)).astype(low)
            probs[2 * pair + side] = prob
            sides.append(dot_tn(prob, value))
        context[:, at] = jnp.where(first, sides[0], sides[1]).astype(low)

    finish(o_copies)
    residual = x[...].astype(f32) + (dot(context[...], w_o[...]) + small[layer, 2:3, :])
    unit, inverse = normalize(residual)
    unit_out[...] = unit
    inverse_out[...] = inverse


def gelu_and_slope(x):
    t = 1.0 / (1.0 + (0.3275911 * math.sqrt(0.5)) * jnp.abs(x))
    bell = jnp.exp(-0.5 * x * x)
    series = 1.421413741 + t * (-1.453152027 + t * 1.061405429)
    series = t * (0.254829592 + t * (-0.284496736 + t * series))
    tail = 0.5 * series * bell
    cdf = jnp.where(x >= 0.0, 1.0 - tail, tail)
    return (x * cdf).astype(low), cdf + x * (bell * (1.0 / math.sqrt(2.0 * math.pi)))


def ffn_fwd_kernel(layer, modes, ids, unit_one, in_bias, small, *rest):
    weights, rest = rest[:8], rest[8:]
    hidden_out, slope_out, unit_out, inverse_out, result = rest[:5]
    w_in, w_out, normed_low, hidden, slope, sems, out_sems = rest[5:]
    in_copies = weight_copies(ids, layer, weights[:4], modes[0], w_in, 0, sems, 0)
    out_copies = weight_copies(ids, layer, weights[4:], modes[1], w_out, 0, sems, 10)
    begin(in_copies)
    begin(out_copies)
    normed = unit_one[...] * small[layer, 3:4, :] + small[layer, 4:5, :]
    normed_low[...] = normed.astype(low)
    finish(in_copies)
    tile = w_in.shape[1] // 4
    going = []
    for t in range(4):
        columns = pl.ds(t * tile, tile)
        pre = dot(normed_low[...], w_in[:, columns]) + in_bias[layer, :, columns]
        hidden[:, columns], slope[:, columns] = gelu_and_slope(pre)
        leaving = [
            pltpu.make_async_copy(hidden.at[:, columns], hidden_out.at[:, columns], out_sems.at[2 * t]),
            pltpu.make_async_copy(slope.at[:, columns], slope_out.at[:, columns], out_sems.at[2 * t + 1]),
        ]
        begin(leaving)
        going += leaving

    finish(out_copies)
    residual = unit_one[...] * small[layer, 3:4, :] + small[layer, 4:5, :] + (dot(hidden[...], w_out[...]) + small[layer, 5:6, :])
    unit, inverse = normalize(residual)
    unit_out[...] = unit
    inverse_out[...] = inverse
    result[...] = (unit * small[layer, 6:7, :] + small[layer, 7:8, :]).astype(low)
    finish(going)


WIDE_BIT = {"y": 0, "z": 1}


def place_of(ids, owner, piece, way):
    away = None if owner is None else ids[0] ^ owner
    off = None if piece is None else piece ^ ids[5]
    place = [None if away is None else away & 1]
    for name in way:
        if name == "x":
            place.append(pl.ds(0, 2) if away is None else away >> 1)
        else:
            place.append(pl.ds(0, 2) if off is None else (off >> WIDE_BIT[name]) & 1)
    return tuple(place) + (pl.ds(0, 2) if piece is None else piece >> 2,)


def store_rows(stage, ids, product, piece, way):
    share = product.shape[0] // 4
    for owner in range(4):
        block = product[owner * share : (owner + 1) * share].astype(low)
        stage[place_of(ids, owner, piece, way) + (pl.ds(0, share),)] = block


def piece_copies(stage, ids, piece, way, kept, sent, sems, turn):
    at = place_of(ids, None, piece, way)[1:]
    copies = [
        pltpu.make_async_copy(stage.at[(1,) + at], sent.at[at], sems.at[2 * turn]),
        pltpu.make_async_copy(stage.at[(0,) + at], kept.at[at], sems.at[2 * turn + 1]),
    ]
    begin(copies)
    return copies


def out_bwd_kernel(layer, way, ids, *refs):
    finish(out_part(layer, way, ids, *refs))


def out_part(layer, way, ids, grad, unit_two, inverse_two, hidden, small, *rest):
    d_ffn, d_resid_two, small_grads, kept, sent, stage, out_sems = rest
    g = grad[...].astype(f32)
    unit = unit_two[...]
    small_grads[0:1, :] = jnp.sum(g * unit, axis=0, keepdims=True)
    small_grads[1:2, :] = jnp.sum(g, axis=0, keepdims=True)
    d_two = normalize_back(g * small[layer, 6:7, :], unit, inverse_two[...])
    d_resid_two[...] = d_two
    d_low = d_two.astype(low)
    d_ffn[...] = d_low
    small_grads[2:3, :] = jnp.sum(d_low.astype(f32), axis=0, keepdims=True)
    small_grads[3:8, :] = jnp.zeros((5, unit.shape[1]), f32)
    tile = hidden.shape[1] // 8
    share = d_ffn.shape[1] // 4
    waits = []
    for owner in range(4):
        for half in range(2):
            columns = slice((2 * owner + half) * tile, (2 * owner + half + 1) * tile)
            out_grad = dot_tn(hidden[:, columns], d_ffn[...])
            for row_group in range(2):
                for column_group in range(2):
                    piece = (half * 2 + row_group) * 2 + column_group
                    block = out_grad[
                        row_group * share : (row_group + 1) * share,
                        column_group * tile : (column_group + 1) * tile,
                    ]
                    stage[place_of(ids, owner, piece, way)] = block.astype(low)
        core, *at = place_of(ids, owner, None, way)
        at = tuple(at)
        to_kept = pltpu.make_async_copy(stage.at[(0,) + at], kept.at[at], out_sems.at[owner])
        to_sent = pltpu.make_async_copy(stage.at[(1,) + at], sent.at[at], out_sems.at[owner])
        pl.when(core == 0)(to_kept.start)
        pl.when(core == 1)(to_sent.start)
        waits.append(to_kept)
    return waits


def in_bwd_kernel(layer, way, modes, ids, d_ffn, unit_one, inverse_one, small, resid_in, slope_in, *rest):
    weights, rest = rest[:8], rest[8:]
    outs, (w_in, w_out, d_pre, normed_t, slope, d_resid_two, stage, sems, out_sems, more_sems) = rest[:5], rest[5:]
    in_copies = weight_copies(ids, layer, weights[:4], modes[0], w_in, 0, sems, 0)
    out_copies = weight_copies(ids, layer, weights[4:], modes[1], w_out, 0, sems, 10)
    slope_copy = pltpu.make_async_copy(slope_in, slope, more_sems.at[0])
    resid_copy = pltpu.make_async_copy(resid_in, d_resid_two, more_sems.at[1])
    begin(out_copies + [slope_copy] + in_copies + [resid_copy])
    late = (out_copies + [slope_copy], in_copies + [resid_copy])
    refs = (d_ffn, d_resid_two, unit_one, inverse_one, small, slope, w_in, w_out, d_pre, normed_t, stage, out_sems)
    finish(in_part(layer, way, ids, late, *refs, *outs))


def in_part(layer, way, ids, late, d_ffn, d_resid_two, unit_one, inverse_one, small, slope, w_in, w_out, *rest):
    d_pre, normed_t, stage, out_sems, d_resid, small_grads, in_bias_grad, kept, sent = rest
    normed = unit_one[...] * small[layer, 3:4, :] + small[layer, 4:5, :]
    normed_t[...] = normed.astype(low).T
    finish(late[0])
    tile = w_in.shape[1] // 4
    going = []
    for t in range(4):
        columns = slice(t * tile, (t + 1) * tile)
        d_hidden = dot_nt(d_ffn[...], w_out[columns, :])
        d_tile = (d_hidden * slope[:, columns]).astype(low)
        d_pre[:, columns] = d_tile
        in_bias_grad[:, columns] = jnp.sum(d_tile.astype(f32), axis=0, keepdims=True)
        product = dot(normed_t[...], d_tile)
        for half in range(2):
            piece = 2 * t + half
            store_rows(stage, ids, product[:, half * tile // 2 : (half + 1) * tile // 2], piece, way)
            going += piece_copies(stage, ids, piece, way, kept, sent, out_sems, piece)
    finish(late[1])
    d_normed = d_resid_two[...] + dot_nt(d_pre[...], w_in[...])
    unit = unit_one[...]
    small_grads[0:1, :] = jnp.sum(d_normed * unit, axis=0, keepdims=True)
    small_grads[1:2, :] = jnp.sum(d_normed, axis=0, keepdims=True)
    small_grads[2:8, :] = jnp.zeros((6, unit.shape[1]), f32)
    d_resid[...] = normalize_back(d_normed * small[layer, 3:4, :], unit, inverse_one[...])
    return going


def ffn_bwd_kernel(layer, ways, modes, ids, grad, unit_two, inverse_two, hidden, unit_one, inverse_one, small, *rest):
    slope_in, weights, rest = rest[0], rest[1:9], rest[9:]
    out_small, out_kept, out_sent = rest[:3]
    outs, rest = rest[3:8], rest[8:]
    w_in, w_out, d_ffn, d_resid_two, d_pre, normed_t, slope, out_stage, stage, sems, owner_sems, out_sems, slope_sem = rest
    in_copies = weight_copies(ids, layer, weights[:4], modes[0], w_in, 0, sems, 0)
    out_copies = weight_copies(ids, layer, weights[4:], modes[1], w_out, 0, sems, 10)
    slope_copy = pltpu.make_async_copy(slope_in, slope, slope_sem.at[0])
    begin(out_copies + [slope_copy] + in_copies)
    refs = (grad, unit_two, inverse_two, hidden, small, d_ffn, d_resid_two, out_small, out_kept, out_sent)
    going = out_part(layer, ways[0], ids, *refs, out_stage, owner_sems)
    refs = (d_ffn, d_resid_two, unit_one, inverse_one, small, slope, w_in, w_out, d_pre, normed_t, stage, out_sems)
    going += in_part(layer, ways[1], ids, (out_copies + [slope_copy], in_copies), *refs, *outs)
    finish(going)


def attn_bwd_kernel(layer, way, mode, ids, d_resid, x, qkv_rows, probs, context, *rest):
    weights, others, rest = rest[:6], rest[6:-13], rest[-13:]
    d_input, small_grads, kept, sent = rest[:4]
    w_qkv, w_o, d_attn, d_context, d_qkv, x_t, stage, sems, out_sems = rest[4:]
    tokens, width = x.shape
    qkv_copies, o_copies = attn_copies(layer, ids, weights, mode, w_qkv, w_o, sems)
    begin(o_copies)
    begin(qkv_copies)
    d_low = d_resid[...].astype(low)
    d_attn[...] = d_low
    small_grads[2:3, :] = jnp.sum(d_low.astype(f32), axis=0, keepdims=True)
    x_t[...] = x[...].T
    tile = width // 2
    product = dot_tn(context[...], d_attn[...])
    for half in range(2):
        store_rows(stage, ids, product[:, half * tile : (half + 1) * tile], 6 + half, way)
    finish(o_copies)
    d_context[...] = dot_nt(d_attn[...], w_o[...]).astype(low)
    pair_width = 2 * width // HEADS
    first = lax.broadcasted_iota(jnp.int32, (1, pair_width), 1) < pair_width // 2
    scale = 1.0 / math.sqrt(width // HEADS)

    for pair in range(HEADS // 2):
        at_query = slice(pair * pair_width, (pair + 1) * pair_width)
        at_key = slice(width + at_query.start, width + at_query.stop)
        at_value = slice(2 * width + at_query.start, 2 * width + at_query.stop)
        query, key, value = qkv_rows[:, at_query], qkv_rows[:, at_key], qkv_rows[:, at_value]
        d_ctx = d_context[:, at_query]
        sides = []
        for side in range(2):
            mine = first if side == 0 else jnp.logical_not(first)
            prob_low = probs[2 * pair + side]
            prob = prob_low.astype(f32)
            d_prob = dot_nt(value, jnp.where(mine, d_ctx, jnp.zeros_like(d_ctx)))
            inner = jnp.sum(prob * d_prob, axis=0, keepdims=True)
            d_scores = (prob * (d_prob - inner)).astype(low)
            sides.append((dot_tn(d_scores, key), dot(d_scores, query), dot(prob_low, d_ctx)))
        d_qkv[:, at_query] = (jnp.where(first, sides[0][0], sides[1][0]) * scale).astype(low)
        d_qkv[:, at_key] = jnp.where(first, sides[0][1], sides[1][1]).astype(low)
        d_qkv[:, at_value] = jnp.where(first, sides[0][2], sides[1][2]).astype(low)

    small_grads[0:1, :] = jnp.sum(d_qkv[:, :width].astype(f32), axis=0, keepdims=True)
    small_grads[1:2, :] = jnp.sum(d_qkv[:, 2 * width :].astype(f32), axis=0, keepdims=True)
    small_grads[3:8, :] = jnp.zeros((5, width), f32)
    if others:
        share = width // 4
        sources = small_sources(layer, small_grads, others)
        for owner in range(4):
            for piece in range(8):
                lines = []
                for source, row, start, step in sources[3 * piece : 3 * piece + 3]:
                    line = source[row : row + 1, start + owner * step : start + owner * step + share]
                    lines.append(jnp.concatenate([line, jnp.zeros_like(line)], axis=1))
                lines.append(jnp.zeros((SMALL_ROWS - 3, tile), f32))
                block = jnp.concatenate(lines, axis=0).astype(low)
                stage[place_of(ids, owner, piece, way) + (pl.ds(share, SMALL_ROWS),)] = block
    going = []
    for part in (3, 0, 1, 2):
        if part < 3:
            product = dot(x_t[...], d_qkv[:, part * width : (part + 1) * width])
        for half in range(2):
            piece = 2 * part + half
            if part < 3:
                store_rows(stage, ids, product[:, half * tile : (half + 1) * tile], piece, way)
            going += piece_copies(stage, ids, piece, way, kept, sent, out_sems, piece)
    finish(qkv_copies)
    d_input[...] = (d_resid[...] + dot_nt(d_qkv[...], w_qkv[...])).astype(low)
    finish(going)


SMALL_ROWS = 16
SMALL_LINES = (("attn", 0), ("attn", 1), ("attn", 2), ("in", 0), ("in", 1), ("out", 2), ("out", 0), ("out", 1))


def small_sources(layer, own, others):
    found = []
    out_0, in_0, bias_0, out_1, in_1, bias_1, attn_1 = others
    refs = ({"attn": own, "in": in_0, "out": out_0}, {"attn": attn_1, "in": in_1, "out": out_1})
    width = own.shape[1]
    for of_layer, bias in zip(refs, (bias_0, bias_1)):
        found += [(of_layer[name], row, 0, width // 4) for name, row in SMALL_LINES]
        found += [(bias, 0, i * (width // 4), width) for i in range(4)]
    return found


def unpack_kernel(layer, slab, back, earlier, ids, near, far, *rest):
    outs = rest[earlier:-4]
    buffer, wide_buffer, in_sems, out_sems = rest[-4:]
    share, tile = wide_buffer.shape[1:]

    def fetch(piece, ref, index):
        return pltpu.make_async_copy(ref.at[index], buffer.at[piece], in_sems.at[piece])

    for piece in range(8):
        off = piece ^ ids[5]
        inner, outer = [(off >> WIDE_BIT[name]) & 1 for name in back]
        pl.when(outer == 0)(fetch(piece, near, (inner, piece >> 2)).start)
        pl.when(outer == 1)(fetch(piece, far, (inner, piece >> 2)).start)

    copies = []
    for piece in range(8):
        fetch(piece, near, (0, 0)).wait()
        wide_buffer[piece] = buffer[piece, :share].astype(f32)
        columns = pl.ds(piece * tile, tile)
        if slab == "in":
            target = outs[0].at[layer, :, columns]
        elif slab == "out":
            rows = pl.ds((piece // 2) * share, share)
            target = outs[0].at[layer, rows, pl.ds((piece % 2) * tile, tile)]
        elif piece < 6:
            target = outs[0].at[layer, :, columns]
        else:
            target = outs[1].at[layer, :, pl.ds((piece - 6) * tile, tile)]
        copies.append(pltpu.make_async_copy(wide_buffer.at[piece], target, out_sems.at[piece]))
        copies[-1].start()
    if slab == "attn" and layer == 0:
        for line in range(24):
            of_layer, which = line // 12, line % 12
            row = share + line % 3
            values = buffer[line // 3, row : row + 1, :share].astype(f32)
            if which < 8:
                outs[2 + which][of_layer : of_layer + 1, :] = values
            else:
                at = (which - 8) * share
                outs[10][of_layer : of_layer + 1, at : at + share] = values
    else:
        outs[-1][...] = jnp.zeros(outs[-1].shape, f32)
    finish(copies)


SMEM = pl.BlockSpec(memory_space=pltpu.SMEM)
VMEM = pl.BlockSpec(memory_space=pltpu.VMEM)
ANY = pl.BlockSpec(memory_space=pl.ANY)


def call(kernel, name, time, in_specs, out_specs, out_shape, scratch, args, aliases=()):
    return pl.pallas_call(
        kernel,
        name=name,
        in_specs=in_specs,
        out_specs=out_specs,
        out_shape=out_shape,
        scratch_shapes=scratch,
        input_output_aliases=dict(aliases),
        compiler_params=pltpu.CompilerParams(vmem_limit_bytes=VMEM_BYTES),
        cost_estimate=pl.CostEstimate(
            flops=int(time * 1.1e9), bytes_accessed=int(time * 3.6e6), transcendentals=0
        ),
    )(*args)


def shape(dims, kind):
    return jax.ShapeDtypeStruct(dims, kind)


def added(a, b):
    return (a.astype(f32) + b.astype(f32)).astype(low)


WAYS = ("zxy", "xyz", "yxz", "zyx", "xyz", "xyz")
BACKS = ("yz", "zy", "zy", "yz", "zy", "zy")
PLAN = (
    "out1", "in1", 0, 1, "attn1", "out0", "in0", 0, 1, "attn0", 1, 0, 2, 4, 1, 3, 0, 1, 2, 4, 0, 5, 2, 3, 4,
    0, 1, 2, 3, 2, 4, 5, 3, 0, 5, 4, 2, 5, 1, 3, 5, 4, 3, 2, 5, 4, 3, 5,
)
MODES = ("qz", "hz", "qy", "qz", "qy", "hy")
FORWARD = (
    "h0", "g0", "g2", "cut", "x0", "h2", "h3", "g3", "g1", "c0", "pack", "x2", "h5", "z0", "h4", "y0", "h1",
    "x3", "z2", "y2", "y3", "c3", "q0", "x5", "q2", "z3", "x1", "q3", "sm", "y5", "x4", "z1", "A", "y4", "d0",
    "z4", "c1", "attn1", "c2", "d3", "d1", "q4", "d2", "ffn1", "d4", "d5", "attn2", "ffn2",
)
TIMES = {
    "pack": 1, "attn1": 5, "ffn1": 13, "attn2": 0.3, "ffn2": 8,
    "out_bwd1": 3, "in_bwd1": 20.0, "attn_bwd1": 0.3, "out_bwd0": 2.0, "in_bwd0": 1.0, "attn_bwd0": 8.0,
}


class Order:
    def __init__(self, ids):
        self.ids = ids

    def wait(self, values):
        values, self.ids = lax.optimization_barrier((values, self.ids))
        return values


STEPS = {"x": ("narrow", 2), "y": ("wide", 1), "z": ("wide", 2)}


class Slab:
    def __init__(self, way, back, wide_count, kept, sent):
        self.kept = kept
        self.way, self.back = way, back
        self.rest = [1 << b for b in range(HALVINGS, wide_count.bit_length() - 1)]
        self.flying = swap(sent, "narrow", 1)
        self.stage = 0

    def step(self, order):
        received = order.wait(self.flying)
        stage, way = self.stage, self.way
        if stage < len(way):
            send = order.wait(added(self.kept[1], received[1]))
            self.kept = added(self.kept[0], received[0])
            self.flying = swap(send, *STEPS[way[stage]])
        elif stage < len(way) + 1 + len(self.back):
            if stage == len(way):
                piece = added(self.kept, received)
                for bit in self.rest[:-1]:
                    piece = added(piece, swap(piece, "wide", bit))
                self.kept = order.wait(piece)
                self.flying = swap(self.kept, "wide", self.rest[-1])
            else:
                if stage == len(way) + 1:
                    self.block = added(self.kept, received)[None]
                else:
                    self.block = jnp.concatenate([self.block, received], axis=0)
                self.block = order.wait(self.block)
                self.flying = swap(self.block, *STEPS[self.back[stage - len(way) - 1]])
        else:
            self.far = received
        self.stage += 1

    def ended(self):
        return self.stage == len(self.way) + len(self.back) + 2


def body(
    tables_in,
    cotangent,
    cell_ids,
    lengths,
    qkv_weight,
    q_bias,
    v_bias,
    o_weight,
    o_bias,
    norm1_gain,
    norm1_bias,
    in_weight,
    in_bias,
    out_weight,
    out_bias,
    norm2_gain,
    norm2_bias,
):
    tokens, width = tables_in.shape
    layers, share, ffn = in_weight.shape
    ffn_share = out_weight.shape[1]
    wide_count = lax.axis_size("wide")
    assert wide_count & (wide_count - 1) == 0 and wide_count > 1 << HALVINGS and lax.axis_size("narrow") == 4
    tile = ffn // 8
    me = lax.axis_index("narrow").astype(jnp.int32)
    wide_me = lax.axis_index("wide").astype(jnp.int32)
    y = wide_me & 1
    ids = jnp.stack([me, me ^ 1, me ^ 2, me ^ 3, y, wide_me & (2**HALVINGS - 1)])

    order = Order(ids)

    own = (qkv_weight, o_weight, in_weight, out_weight)
    parts = [None] * 6

    def cut(*slabs):
        outs = []
        for slab in slabs:
            weight = (qkv_weight, in_weight, out_weight)[slab % 3]
            columns = 4 * width if slab % 3 == 0 else weight.shape[2]
            outs.append(shape((weight.shape[1] // (4 if MODES[slab][0] == "q" else 2), columns), low))
        results = call(
            functools.partial(cut_kernel, slabs),
            "cut",
            1,
            [SMEM] + [ANY] * 4,
            [VMEM] * len(slabs),
            outs,
            [pltpu.SemaphoreType.DMA((8,))],
            (order.ids, *own),
        )
        for slab, part in zip(slabs, results):
            parts[slab] = part

    first_slab = [int(token[1]) for token in FORWARD if token[0] == "h"][0]
    cut(first_slab)
    near, diagonal, core = [None] * 6, [None] * 6, [None] * 4
    transfers = [{} for _ in range(6)]

    def joined(i, *names):
        near[i] = order.wait(jnp.concatenate([transfers[i][name] for name in names], axis=0))
        transfers[i]["d"] = swap(near[i], "narrow", 1)

    def weight_step(kind, i):
        moving, mode = transfers[i], MODES[i]
        if kind == "h":
            moving["x"] = swap(order.wait(parts[i]), "narrow", 2)
            return
        moving[kind] = order.wait(moving[kind])
        if kind == "x":
            for name, bit in (("y", 1), ("z", 2)):
                if mode[0] == "q" or mode[1] == name:
                    moving[name] = swap(moving["x"], "wide", bit)
        elif kind == "d":
            diagonal[i] = moving["d"]
        elif kind == "q":
            joined(i, "x", "y", "z", "q")
        elif mode[0] == "h":
            joined(i, "x", kind)
        elif mode[1] != kind:
            moving["q"] = swap(moving[kind], "wide", 1 if mode[1] == "y" else 2)

    def in_order(low_one, high_one, bit):
        swapped = (me & bit) != 0
        return jnp.stack([jnp.where(swapped, high_one, low_one), jnp.where(swapped, low_one, high_one)])

    def attn_weights(layer):
        return (qkv_weight, core[0], o_weight, core[1], near[3 * layer], diagonal[3 * layer])

    def in_weights(layer):
        return (in_weight, core[2], near[3 * layer + 1], diagonal[3 * layer + 1])

    def out_weights(layer):
        return (out_weight, core[3], near[3 * layer + 2], diagonal[3 * layer + 2])

    w_qkv = pltpu.VMEM((width, 3 * width), low)
    w_o = pltpu.VMEM((width, width), low)
    w_in = pltpu.VMEM((width, ffn), low)
    w_out = pltpu.VMEM((ffn, width), low)
    copy_sems = pltpu.SemaphoreType.DMA((20,))
    piece_sems = pltpu.SemaphoreType.DMA((16,))
    rows_f32 = shape((tokens, width), f32)
    rows_low = shape((tokens, width), low)
    column_f32 = shape((tokens, 1), f32)
    eight_f32 = shape((8, width), f32)

    def pieces(rows):
        return [shape((2, 2, 2, 2, rows, tile), low)] * 2

    def stage(rows):
        return pltpu.VMEM((2, 2, 2, 2, 2, rows, tile), low)

    def tie(outs, which):
        outs = list(outs)
        outs[which] = order.wait(outs[which])
        return outs

    def attn_forward(layer, x):
        x = order.wait(x)
        outs = call(
            functools.partial(attn_fwd_kernel, layer, MODES[3 * layer]),
            "attn_fwd",
            TIMES["attn%d" % (layer + 1)],
            [SMEM, SMEM] + [VMEM] * 3 + [ANY] * 6,
            [VMEM] * 5,
            [shape((tokens, 3 * width), low), shape((HEADS, tokens, tokens), low), rows_low, rows_f32, column_f32],
            [w_qkv, w_o, pltpu.VMEM((tokens, tokens), f32), copy_sems],
            (order.ids, lengths, x, cell_ids, small) + attn_weights(layer),
        )
        return tie(outs, 3)

    def ffn_forward(layer, unit_one):
        unit_one = order.wait(unit_one)
        outs = call(
            functools.partial(ffn_fwd_kernel, layer, MODES[3 * layer + 1 : 3 * layer + 3]),
            "ffn_fwd",
            TIMES["ffn%d" % (layer + 1)],
            [SMEM] + [VMEM] * 3 + [ANY] * 8,
            [ANY] * 2 + [VMEM] * 3,
            [shape((tokens, ffn), low), shape((tokens, ffn), f32), rows_f32, column_f32, rows_low],
            [
                w_in,
                w_out,
                pltpu.VMEM((tokens, width), low),
                pltpu.VMEM((tokens, ffn), low),
                pltpu.VMEM((tokens, ffn), f32),
                copy_sems,
                piece_sems,
            ],
            (order.ids, unit_one, full_in_bias, small) + in_weights(layer) + out_weights(layer),
        )
        return tie(outs, 4)

    def out_backward(layer, way, grad, unit_two, inverse_two, hidden):
        grad = order.wait(grad)
        outs = call(
            functools.partial(out_bwd_kernel, layer, way),
            "out_bwd",
            TIMES["out_bwd%d" % layer],
            [SMEM] + [VMEM] * 5,
            [VMEM] * 3 + [ANY] * 2,
            [rows_low, rows_f32, eight_f32] + pieces(share),
            [stage(share), pltpu.SemaphoreType.DMA((4,))],
            (order.ids, grad, unit_two, inverse_two, hidden, small),
        )
        return tie(outs, 0)

    def in_backward(layer, way, d_ffn, d_resid_two, unit_one, inverse_one, slope):
        d_ffn = order.wait(d_ffn)
        outs = call(
            functools.partial(in_bwd_kernel, layer, way, MODES[3 * layer + 1 : 3 * layer + 3]),
            "in_bwd",
            TIMES["in_bwd%d" % layer],
            [SMEM] + [VMEM] * 4 + [ANY] * 10,
            [VMEM] * 3 + [ANY] * 2,
            [rows_f32, eight_f32, shape((1, ffn), f32)] + pieces(share),
            [
                w_in,
                w_out,
                pltpu.VMEM((tokens, ffn), low),
                pltpu.VMEM((width, tokens), low),
                pltpu.VMEM((tokens, ffn), f32),
                pltpu.VMEM((tokens, width), f32),
                stage(share),
                copy_sems,
                piece_sems,
                pltpu.SemaphoreType.DMA((2,)),
            ],
            (order.ids, d_ffn, unit_one, inverse_one, small, d_resid_two, slope)
            + in_weights(layer)
            + out_weights(layer),
        )
        return tie(outs, 0)

    def ffn_backward(layer, ways, grad, attn_part, ffn_part):
        grad = order.wait(grad)
        hidden, slope, unit_two, inverse_two, _ = ffn_part
        outs = call(
            functools.partial(ffn_bwd_kernel, layer, ways, MODES[3 * layer + 1 : 3 * layer + 3]),
            "ffn_bwd",
            TIMES["in_bwd%d" % layer],
            [SMEM] + [VMEM] * 7 + [ANY] * 9,
            [VMEM] + [ANY] * 2 + [VMEM] * 3 + [ANY] * 2,
            [eight_f32] + pieces(share) + [rows_f32, eight_f32, shape((1, ffn), f32)] + pieces(share),
            [
                w_in,
                w_out,
                pltpu.VMEM((tokens, width), low),
                pltpu.VMEM((tokens, width), f32),
                pltpu.VMEM((tokens, ffn), low),
                pltpu.VMEM((width, tokens), low),
                pltpu.VMEM((tokens, ffn), f32),
                stage(share),
                stage(share),
                copy_sems,
                pltpu.SemaphoreType.DMA((4,)),
                piece_sems,
                pltpu.SemaphoreType.DMA((1,)),
            ],
            (order.ids, grad, unit_two, inverse_two, hidden, attn_part[3], attn_part[4], small, slope)
            + in_weights(layer)
            + out_weights(layer),
        )
        return tie(outs, 3)

    def attn_backward(layer, way, d_resid, x, qkv_rows, probs, context, small_others):
        d_resid = order.wait(d_resid)
        rows = share + (SMALL_ROWS if small_others else 0)
        outs = call(
            functools.partial(attn_bwd_kernel, layer, way, MODES[3 * layer]),
            "attn_bwd",
            TIMES["attn_bwd%d" % layer],
            [SMEM] + [VMEM] * 5 + [ANY] * 6 + [VMEM] * len(small_others),
            [VMEM] * 2 + [ANY] * 2,
            [rows_low, eight_f32] + pieces(rows),
            [
                w_qkv,
                w_o,
                pltpu.VMEM((tokens, width), low),
                pltpu.VMEM((tokens, width), low),
                pltpu.VMEM((tokens, 3 * width), low),
                pltpu.VMEM((width, tokens), low),
                stage(rows),
                copy_sems,
                piece_sems,
            ],
            (order.ids, d_resid, x, qkv_rows, probs, context) + attn_weights(layer) + tuple(small_others),
        )
        return tie(outs, 0)

    def unpack(layer, name, slab, earlier):
        dims = {
            "attn": [(layers, share, 3 * width), (layers, share, width)],
            "in": [(layers, share, ffn)],
            "out": [(layers, ffn_share, width)],
        }[name]
        last = name == "attn" and layer == 0
        extra = [(layers, share)] * 8 + [(layers, ffn_share)] if last else [(8, 128)]
        near, far = order.wait((slab.block, slab.far))
        rows = near.shape[2]
        outs = call(
            functools.partial(unpack_kernel, layer, name, slab.back, len(earlier)),
            "unpack",
            4,
            [SMEM] + [ANY] * (2 + len(earlier)),
            [ANY] * len(dims) + [VMEM] * len(extra),
            [shape(d, f32) for d in dims + extra],
            [
                pltpu.VMEM((8, rows, tile), low),
                pltpu.VMEM((8, share, tile), f32),
                pltpu.SemaphoreType.DMA((8,)),
                pltpu.SemaphoreType.DMA((8,)),
            ],
            (order.ids, near, far, *earlier),
            {3 + i: i for i in range(len(earlier))},
        )
        return tuple(tie(outs, 0))

    short = (q_bias, v_bias, o_bias, norm1_gain, norm1_bias, out_bias, norm2_gain, norm2_bias)
    inputs, attn_kept, ffn_kept = [tables_in], [], []
    for token in FORWARD:
        kind, i = (token[0], int(token[1])) if len(token) == 2 and token[1].isdigit() else (token, None)
        if token == "cut":
            cut(*[slab for slab in range(6) if slab != first_slab])
        elif kind == "g":
            core[i] = swap(order.wait(own[i]), "narrow", 1)
        elif kind == "c":
            core[i] = order.wait(core[i])
        elif i is not None:
            weight_step(kind, i)
        elif token == "pack":
            packed = call(
                pack_kernel,
                "pack",
                TIMES["pack"],
                [VMEM] * 9,
                VMEM,
                shape((layers, 12, share), f32),
                [],
                tuple(order.wait(short)) + (in_bias,),
            )
            packed = order.wait(packed)
            others = [lax.ppermute(packed, "narrow", [(j, j ^ away) for j in range(4)]) for away in (1, 2, 3)]
        elif token == "sm":
            others = order.wait(others)
        elif token == "A":
            packed = in_order(in_order(packed, others[0], 1), in_order(others[1], others[2], 1), 2)
            packed = packed.reshape(4, layers, 12, share)
            small = packed[:, :, :8].transpose(1, 2, 0, 3).reshape(layers, 8, width)
            full_in_bias = packed[:, :, 8:].transpose(1, 0, 2, 3).reshape(layers, 1, ffn)
            small, full_in_bias = order.wait((small, full_in_bias))
        elif token[:-1] == "attn":
            attn_kept.append(attn_forward(int(token[-1]) - 1, inputs[-1]))
        else:
            ffn_kept.append(ffn_forward(int(token[-1]) - 1, attn_kept[-1][3]))
            inputs.append(ffn_kept[-1][4])
    mixed_out = inputs[-1]

    slabs = [None] * 6
    grad = cotangent
    small_out, small_in, small_attn, bias_grads = [None] * 2, [None] * 2, [None] * 2, [None] * 2
    unpacked = {"attn": (), "in": (), "out": ()}
    for action in PLAN:
        if isinstance(action, int):
            slab = slabs[action]
            slab.step(order)
            if slab.ended():
                name = ("out", "in", "attn")[action % 3]
                unpacked[name] = unpack(layers - 1 - action // 3, name, slab, unpacked[name][: 2 if name == "attn" else 1])
            continue
        name, layer = action[:-1], int(action[-1])
        which = 3 * (layers - 1 - layer) + ("out", "in", "attn").index(name)
        way = WAYS[which]
        qkv_rows, probs, context, unit_one, inverse_one = attn_kept[layer]
        hidden, slope, unit_two, inverse_two, _ = ffn_kept[layer]
        if name == "out" and layer == 0:
            continue
        if name == "in" and layer == 0:
            outs = ffn_backward(layer, WAYS[which - 1 : which + 1], grad, attn_kept[layer], ffn_kept[layer])
            small_out[layer], out_kept, out_sent, d_resid, small_in[layer], bias_grads[layer], kept, sent = outs
            slabs[which - 1] = Slab(WAYS[which - 1], BACKS[which - 1], wide_count, out_kept, out_sent)
        elif name == "out":
            d_ffn, d_resid_two, small_out[layer], kept, sent = out_backward(
                layer, way, grad, unit_two, inverse_two, hidden
            )
        elif name == "in":
            d_resid, small_in[layer], bias_grads[layer], kept, sent = in_backward(
                layer, way, d_ffn, d_resid_two, unit_one, inverse_one, slope
            )
        else:
            small_others = ()
            if layer == 0:
                small_others = (
                    small_out[0],
                    small_in[0],
                    bias_grads[0],
                    small_out[1],
                    small_in[1],
                    bias_grads[1],
                    small_attn[1],
                )
            grad, small_attn[layer], kept, sent = attn_backward(
                layer, way, d_resid, inputs[layer], qkv_rows, probs, context, small_others
            )
        slabs[which] = Slab(way, BACKS[which], wide_count, kept, sent)
    qkv_grad, o_grad, *vectors = unpacked["attn"]
    in_grad, out_grad = unpacked["in"][0], unpacked["out"][0]
    return (
        mixed_out,
        grad,
        qkv_grad,
        vectors[0],
        vectors[1],
        o_grad,
        vectors[2],
        vectors[3],
        vectors[4],
        in_grad,
        vectors[8],
        out_grad,
        vectors[5],
        vectors[6],
        vectors[7],
    )


def solution(mesh):
    by_table = P(("wide", "narrow"), None)
    matrix = P(None, "narrow", None)
    vector = P(None, "narrow")
    return jax.shard_map(
        body,
        mesh=mesh,
        in_specs=(
            by_table,
            by_table,
            by_table,
            P(("wide", "narrow")),
            matrix,
            vector,
            vector,
            matrix,
            vector,
            vector,
            vector,
            matrix,
            vector,
            matrix,
            vector,
            vector,
            vector,
        ),
        out_specs=(
            by_table,
            by_table,
            matrix,
            vector,
            vector,
            matrix,
            vector,
            vector,
            vector,
            matrix,
            vector,
            matrix,
            vector,
            vector,
            vector,
        ),
        check_vma=False,
    )
```

```python
import functools
import math

import jax
import jax.numpy as jnp
from jax import lax
from jax.experimental import pallas as pl
from jax.experimental.pallas import tpu as pltpu
from jax.sharding import PartitionSpec as P

HEADS = 12
norm_eps = 1e-12
masked_score = -1000000000.0
low = jnp.bfloat16
f32 = jnp.float32
VMEM_BYTES = 56 * 1024 * 1024
HALVINGS = 2


def swap(value, axis, bit):
    count = lax.axis_size(axis)
    return lax.ppermute(value, axis, [(i, i ^ bit) for i in range(count)])


def dot(a, b):
    return jnp.dot(a, b, preferred_element_type=f32)


def dot_nt(a, b):
    return lax.dot_general(a, b, (((1,), (1,)), ((), ())), preferred_element_type=f32)


def dot_tn(a, b):
    return lax.dot_general(a, b, (((0,), (0,)), ((), ())), preferred_element_type=f32)


def normalize(residual):
    center = residual - jnp.mean(residual, axis=-1, keepdims=True)
    inverse = lax.rsqrt(jnp.mean(center * center, axis=-1, keepdims=True) + norm_eps)
    return center * inverse, inverse


def normalize_back(grad_unit, unit, inverse):
    centered = grad_unit - jnp.mean(grad_unit, axis=-1, keepdims=True)
    return inverse * (centered - unit * jnp.mean(grad_unit * unit, axis=-1, keepdims=True))


def position(wide_bits, mode):
    y, z = wide_bits & 1, wide_bits >> 1
    return {"hy": y, "hz": z}.get(mode, wide_bits)


def weight_copies(ids, layer, pieces, mode, target, columns, sems, base):
    own, core, near, diagonal = pieces
    rows = own.shape[1]
    parts = 4 if mode[0] == "q" else 2
    step = rows // parts
    copies = []

    def add(source, start, count):
        where = target.at[pl.ds(pl.multiple_of(start, step), count), :]
        copies.append(pltpu.make_async_copy(source, where, sems.at[base + len(copies)]))

    add(own.at[layer], ids[0] * rows, rows)
    add(core.at[layer], ids[1] * rows, rows)
    at = pl.ds(columns, target.shape[1])
    for shard, owner in ((near, ids[2]), (diagonal, ids[3])):
        for part in range(parts):
            start = owner * rows + (position(ids[5], mode) ^ part) * step
            add(shard.at[pl.ds(part * step, step), at], start, step)
    return copies


def begin(copies):
    for copy in copies:
        copy.start()


def finish(copies):
    for copy in copies:
        copy.wait()


def attn_copies(layer, ids, refs, mode, w_qkv, w_o, sems):
    qkv_own, qkv_core, o_own, o_core, near, diagonal = refs
    qkv = weight_copies(ids, layer, (qkv_own, qkv_core, near, diagonal), mode, w_qkv, 0, sems, 0)
    o = weight_copies(ids, layer, (o_own, o_core, near, diagonal), mode, w_o, w_qkv.shape[1], sems, 10)
    return qkv, o


def cut_kernel(slabs, ids, qkv, o, w_in, w_out, *rest):
    outs, sems = rest[:-1], rest[-1]
    copies = []
    for slab, out in zip(slabs, outs):
        layer, which = divmod(slab, 3)
        begins = 0
        for weight in ((qkv, o), (w_in,), (w_out,))[which]:
            rows = out.shape[0]
            start = pl.multiple_of(position(ids[5], MODES[slab]) * rows, rows)
            source = weight.at[layer, pl.ds(start, rows), :]
            target = out.at[:, pl.ds(begins, weight.shape[2])]
            copies.append(pltpu.make_async_copy(source, target, sems.at[len(copies)]))
            begins += weight.shape[2]
    begin(copies)
    finish(copies)


def spread_kernel(ids, mine, near_core, near_x, diagonal, small, in_bias):
    share = mine.shape[2]
    for owner in range(4):
        away = ids[0] ^ owner
        lines = jnp.where(away < 2, jnp.where(away == 0, mine[...], near_core[...]), 0.0)
        lines = jnp.where(away < 2, lines, jnp.where(away == 2, near_x[...], diagonal[...]))
        for layer in range(mine.shape[0]):
            small[layer, :, owner * share : (owner + 1) * share] = lines[layer, :8]
            for i in range(4):
                at = (4 * owner + i) * share
                in_bias[layer, :, at : at + share] = lines[layer, 8 + i : 9 + i]


def pack_kernel(*refs):
    shorts, in_bias, packed = refs[:8], refs[8], refs[9]
    layers, share = shorts[0].shape
    for layer in range(layers):
        for i, short in enumerate(shorts):
            packed[layer, i : i + 1, :] = short[layer : layer + 1, :].astype(f32)
        for i in range(4):
            packed[layer, 8 + i : 9 + i, :] = in_bias[layer : layer + 1, i * share : (i + 1) * share].astype(f32)


def attn_fwd_kernel(layer, mode, ids, length, x, cell_row, small, *rest):
    weights, rest = rest[:6], rest[6:]
    qkv_rows, probs, context, unit_out, inverse_out, w_qkv, w_o, mask, sems = rest
    tokens, width = x.shape
    qkv_copies, o_copies = attn_copies(layer, ids, weights, mode, w_qkv, w_o, sems)
    begin(qkv_copies)
    begin(o_copies)
    position = lax.broadcasted_iota(jnp.int32, (tokens, 1), 0)
    query_cell = cell_row[...]
    square = (tokens, tokens)
    diagonal = lax.broadcasted_iota(jnp.int32, square, 0) == lax.broadcasted_iota(jnp.int32, square, 1)
    key_cell = jnp.sum(jnp.where(diagonal, query_cell, 0), axis=1, keepdims=True)
    allowed = (query_cell == key_cell) | (key_cell == 0) | (query_cell == 0)
    allowed = allowed & (position < length[0])
    mask[...] = jnp.where(allowed, 0.0, masked_score)
    scale = 1.0 / math.sqrt(width // HEADS)
    finish(qkv_copies)
    for part in range(3):
        columns = slice(part * width, (part + 1) * width)
        rows = dot(x[...], w_qkv[:, columns])
        if part != 1:
            rows = rows + small[layer, part // 2 : part // 2 + 1, :]
        if part == 0:
            rows = rows * scale
        qkv_rows[:, columns] = rows.astype(low)

    pair_width = 2 * width // HEADS
    first = lax.broadcasted_iota(jnp.int32, (1, pair_width), 1) < pair_width // 2

    for pair in range(HEADS // 2):
        at = slice(pair * pair_width, (pair + 1) * pair_width)
        query = qkv_rows[:, at]
        key = qkv_rows[:, width + at.start : width + at.stop]
        value = qkv_rows[:, 2 * width + at.start : 2 * width + at.stop]
        sides = []
        for side in range(2):
            mine = first if side == 0 else jnp.logical_not(first)
            scores = dot_nt(key, jnp.where(mine, query, jnp.zeros_like(query))) + mask[...]
            shifted = jnp.exp(scores - jnp.max(scores, axis=0, keepdims=True))
            total = jnp.sum(shifted, axis=0, keepdims=True)
            prob = (shifted * (1.0 / total)).astype(low)
            probs[2 * pair + side] = prob
            sides.append(dot_tn(prob, value))
        context[:, at] = jnp.where(first, sides[0], sides[1]).astype(low)

    finish(o_copies)
    residual = x[...].astype(f32) + (dot(context[...], w_o[...]) + small[layer, 2:3, :])
    unit, inverse = normalize(residual)
    unit_out[...] = unit
    inverse_out[...] = inverse


def gelu_and_slope(x):
    t = 1.0 / (1.0 + (0.3275911 * math.sqrt(0.5)) * jnp.abs(x))
    bell = jnp.exp(-0.5 * x * x)
    series = 1.421413741 + t * (-1.453152027 + t * 1.061405429)
    series = t * (0.254829592 + t * (-0.284496736 + t * series))
    tail = 0.5 * series * bell
    cdf = jnp.where(x >= 0.0, 1.0 - tail, tail)
    return (x * cdf).astype(low), cdf + x * (bell * (1.0 / math.sqrt(2.0 * math.pi)))


def ffn_fwd_kernel(layer, modes, ids, unit_one, in_bias, small, *rest):
    weights, rest = rest[:8], rest[8:]
    hidden_out, slope_out, unit_out, inverse_out, result = rest[:5]
    w_in, w_out, normed_low, hidden, slope, sems, out_sems = rest[5:]
    in_copies = weight_copies(ids, layer, weights[:4], modes[0], w_in, 0, sems, 0)
    out_copies = weight_copies(ids, layer, weights[4:], modes[1], w_out, 0, sems, 10)
    begin(in_copies)
    begin(out_copies)
    normed = unit_one[...] * small[layer, 3:4, :] + small[layer, 4:5, :]
    normed_low[...] = normed.astype(low)
    finish(in_copies)
    tile = w_in.shape[1] // 4
    going = []
    for t in range(4):
        columns = pl.ds(t * tile, tile)
        pre = dot(normed_low[...], w_in[:, columns]) + in_bias[layer, :, columns]
        hidden[:, columns], slope[:, columns] = gelu_and_slope(pre)
        leaving = [
            pltpu.make_async_copy(hidden.at[:, columns], hidden_out.at[:, columns], out_sems.at[2 * t]),
            pltpu.make_async_copy(slope.at[:, columns], slope_out.at[:, columns], out_sems.at[2 * t + 1]),
        ]
        begin(leaving)
        going += leaving

    finish(out_copies)
    residual = unit_one[...] * small[layer, 3:4, :] + small[layer, 4:5, :] + (dot(hidden[...], w_out[...]) + small[layer, 5:6, :])
    unit, inverse = normalize(residual)
    unit_out[...] = unit
    inverse_out[...] = inverse
    result[...] = (unit * small[layer, 6:7, :] + small[layer, 7:8, :]).astype(low)
    finish(going)


WIDE_BIT = {"y": 0, "z": 1}


def place_of(ids, owner, piece, way):
    away = None if owner is None else ids[0] ^ owner
    off = None if piece is None else piece ^ ids[5]
    place = [None if away is None else away & 1]
    for name in way:
        if name == "x":
            place.append(pl.ds(0, 2) if away is None else away >> 1)
        else:
            place.append(pl.ds(0, 2) if off is None else (off >> WIDE_BIT[name]) & 1)
    return tuple(place) + (pl.ds(0, 2) if piece is None else piece >> 2,)


def store_rows(stage, ids, product, piece, way):
    share = product.shape[0] // 4
    for owner in range(4):
        block = product[owner * share : (owner + 1) * share].astype(low)
        stage[place_of(ids, owner, piece, way) + (pl.ds(0, share),)] = block


def piece_copies(stage, ids, piece, way, kept, sent, sems, turn):
    at = place_of(ids, None, piece, way)[1:]
    copies = [
        pltpu.make_async_copy(stage.at[(1,) + at], sent.at[at], sems.at[2 * turn]),
        pltpu.make_async_copy(stage.at[(0,) + at], kept.at[at], sems.at[2 * turn + 1]),
    ]
    begin(copies)
    return copies


def out_bwd_kernel(layer, way, ids, *refs):
    finish(out_part(layer, way, ids, *refs))


def out_part(layer, way, ids, grad, unit_two, inverse_two, hidden, small, *rest):
    d_ffn, d_resid_two, small_grads, kept, sent, stage, out_sems = rest
    g = grad[...].astype(f32)
    unit = unit_two[...]
    small_grads[0:1, :] = jnp.sum(g * unit, axis=0, keepdims=True)
    small_grads[1:2, :] = jnp.sum(g, axis=0, keepdims=True)
    d_two = normalize_back(g * small[layer, 6:7, :], unit, inverse_two[...])
    d_resid_two[...] = d_two
    d_low = d_two.astype(low)
    d_ffn[...] = d_low
    small_grads[2:3, :] = jnp.sum(d_low.astype(f32), axis=0, keepdims=True)
    small_grads[3:8, :] = jnp.zeros((5, unit.shape[1]), f32)
    tile = hidden.shape[1] // 8
    share = d_ffn.shape[1] // 4
    waits = []
    for owner in range(4):
        for half in range(2):
            columns = slice((2 * owner + half) * tile, (2 * owner + half + 1) * tile)
            out_grad = dot_tn(hidden[:, columns], d_ffn[...])
            for row_group in range(2):
                for column_group in range(2):
                    piece = (half * 2 + row_group) * 2 + column_group
                    block = out_grad[
                        row_group * share : (row_group + 1) * share,
                        column_group * tile : (column_group + 1) * tile,
                    ]
                    stage[place_of(ids, owner, piece, way)] = block.astype(low)
        core, *at = place_of(ids, owner, None, way)
        at = tuple(at)
        to_kept = pltpu.make_async_copy(stage.at[(0,) + at], kept.at[at], out_sems.at[owner])
        to_sent = pltpu.make_async_copy(stage.at[(1,) + at], sent.at[at], out_sems.at[owner])
        pl.when(core == 0)(to_kept.start)
        pl.when(core == 1)(to_sent.start)
        waits.append(to_kept)
    return waits


def in_bwd_kernel(layer, way, modes, ids, d_ffn, unit_one, inverse_one, small, resid_in, slope_in, *rest):
    weights, rest = rest[:8], rest[8:]
    outs, (w_in, w_out, d_pre, normed_t, slope, d_resid_two, stage, sems, out_sems, more_sems) = rest[:5], rest[5:]
    in_copies = weight_copies(ids, layer, weights[:4], modes[0], w_in, 0, sems, 0)
    out_copies = weight_copies(ids, layer, weights[4:], modes[1], w_out, 0, sems, 10)
    slope_copy = pltpu.make_async_copy(slope_in, slope, more_sems.at[0])
    resid_copy = pltpu.make_async_copy(resid_in, d_resid_two, more_sems.at[1])
    begin(out_copies + [slope_copy] + in_copies + [resid_copy])
    late = (out_copies + [slope_copy], in_copies + [resid_copy])
    refs = (d_ffn, d_resid_two, unit_one, inverse_one, small, slope, w_in, w_out, d_pre, normed_t, stage, out_sems)
    finish(in_part(layer, way, ids, late, *refs, *outs))


def in_part(layer, way, ids, late, d_ffn, d_resid_two, unit_one, inverse_one, small, slope, w_in, w_out, *rest):
    d_pre, normed_t, stage, out_sems, d_resid, small_grads, in_bias_grad, kept, sent = rest
    normed = unit_one[...] * small[layer, 3:4, :] + small[layer, 4:5, :]
    normed_t[...] = normed.astype(low).T
    finish(late[0])
    tile = w_in.shape[1] // 4
    going = []
    for t in range(4):
        columns = slice(t * tile, (t + 1) * tile)
        d_hidden = dot_nt(d_ffn[...], w_out[columns, :])
        d_tile = (d_hidden * slope[:, columns]).astype(low)
        d_pre[:, columns] = d_tile
        in_bias_grad[:, columns] = jnp.sum(d_tile.astype(f32), axis=0, keepdims=True)
        product = dot(normed_t[...], d_tile)
        for half in range(2):
            piece = 2 * t + half
            store_rows(stage, ids, product[:, half * tile // 2 : (half + 1) * tile // 2], piece, way)
            going += piece_copies(stage, ids, piece, way, kept, sent, out_sems, piece)
    finish(late[1])
    d_normed = d_resid_two[...] + dot_nt(d_pre[...], w_in[...])
    unit = unit_one[...]
    small_grads[0:1, :] = jnp.sum(d_normed * unit, axis=0, keepdims=True)
    small_grads[1:2, :] = jnp.sum(d_normed, axis=0, keepdims=True)
    small_grads[2:8, :] = jnp.zeros((6, unit.shape[1]), f32)
    d_resid[...] = normalize_back(d_normed * small[layer, 3:4, :], unit, inverse_one[...])
    return going


def ffn_bwd_kernel(layer, ways, modes, ids, grad, unit_two, inverse_two, hidden, unit_one, inverse_one, small, *rest):
    slope_in, weights, rest = rest[0], rest[1:9], rest[9:]
    out_small, out_kept, out_sent = rest[:3]
    outs, rest = rest[3:8], rest[8:]
    w_in, w_out, d_ffn, d_resid_two, d_pre, normed_t, slope, out_stage, stage, sems, owner_sems, out_sems, slope_sem = rest
    in_copies = weight_copies(ids, layer, weights[:4], modes[0], w_in, 0, sems, 0)
    out_copies = weight_copies(ids, layer, weights[4:], modes[1], w_out, 0, sems, 10)
    slope_copy = pltpu.make_async_copy(slope_in, slope, slope_sem.at[0])
    begin(out_copies + [slope_copy] + in_copies)
    refs = (grad, unit_two, inverse_two, hidden, small, d_ffn, d_resid_two, out_small, out_kept, out_sent)
    going = out_part(layer, ways[0], ids, *refs, out_stage, owner_sems)
    refs = (d_ffn, d_resid_two, unit_one, inverse_one, small, slope, w_in, w_out, d_pre, normed_t, stage, out_sems)
    going += in_part(layer, ways[1], ids, (out_copies + [slope_copy], in_copies), *refs, *outs)
    finish(going)


def attn_bwd_kernel(layer, way, mode, ids, d_resid, x, qkv_rows, probs, context, *rest):
    weights, others, rest = rest[:6], rest[6:-13], rest[-13:]
    d_input, small_grads, kept, sent = rest[:4]
    w_qkv, w_o, d_attn, d_context, d_qkv, x_t, stage, sems, out_sems = rest[4:]
    tokens, width = x.shape
    qkv_copies, o_copies = attn_copies(layer, ids, weights, mode, w_qkv, w_o, sems)
    begin(o_copies)
    begin(qkv_copies)
    d_low = d_resid[...].astype(low)
    d_attn[...] = d_low
    small_grads[2:3, :] = jnp.sum(d_low.astype(f32), axis=0, keepdims=True)
    x_t[...] = x[...].T
    tile = width // 2
    product = dot_tn(context[...], d_attn[...])
    for half in range(2):
        store_rows(stage, ids, product[:, half * tile : (half + 1) * tile], 6 + half, way)
    finish(o_copies)
    d_context[...] = dot_nt(d_attn[...], w_o[...]).astype(low)
    pair_width = 2 * width // HEADS
    first = lax.broadcasted_iota(jnp.int32, (1, pair_width), 1) < pair_width // 2
    scale = 1.0 / math.sqrt(width // HEADS)

    for pair in range(HEADS // 2):
        at_query = slice(pair * pair_width, (pair + 1) * pair_width)
        at_key = slice(width + at_query.start, width + at_query.stop)
        at_value = slice(2 * width + at_query.start, 2 * width + at_query.stop)
        query, key, value = qkv_rows[:, at_query], qkv_rows[:, at_key], qkv_rows[:, at_value]
        d_ctx = d_context[:, at_query]
        sides = []
        for side in range(2):
            mine = first if side == 0 else jnp.logical_not(first)
            prob_low = probs[2 * pair + side]
            prob = prob_low.astype(f32)
            d_prob = dot_nt(value, jnp.where(mine, d_ctx, jnp.zeros_like(d_ctx)))
            inner = jnp.sum(prob * d_prob, axis=0, keepdims=True)
            d_scores = (prob * (d_prob - inner)).astype(low)
            sides.append((dot_tn(d_scores, key), dot(d_scores, query), dot(prob_low, d_ctx)))
        d_qkv[:, at_query] = (jnp.where(first, sides[0][0], sides[1][0]) * scale).astype(low)
        d_qkv[:, at_key] = jnp.where(first, sides[0][1], sides[1][1]).astype(low)
        d_qkv[:, at_value] = jnp.where(first, sides[0][2], sides[1][2]).astype(low)

    small_grads[0:1, :] = jnp.sum(d_qkv[:, :width].astype(f32), axis=0, keepdims=True)
    small_grads[1:2, :] = jnp.sum(d_qkv[:, 2 * width :].astype(f32), axis=0, keepdims=True)
    small_grads[3:8, :] = jnp.zeros((5, width), f32)
    if others:
        share = width // 4
        sources = small_sources(layer, small_grads, others)
        for owner in range(4):
            for piece in range(8):
                lines = []
                for source, row, start, step in sources[3 * piece : 3 * piece + 3]:
                    line = source[row : row + 1, start + owner * step : start + owner * step + share]
                    lines.append(jnp.concatenate([line, jnp.zeros_like(line)], axis=1))
                lines.append(jnp.zeros((SMALL_ROWS - 3, tile), f32))
                block = jnp.concatenate(lines, axis=0).astype(low)
                stage[place_of(ids, owner, piece, way) + (pl.ds(share, SMALL_ROWS),)] = block
    going = []
    for part in (3, 0, 1, 2):
        if part < 3:
            product = dot(x_t[...], d_qkv[:, part * width : (part + 1) * width])
        for half in range(2):
            piece = 2 * part + half
            if part < 3:
                store_rows(stage, ids, product[:, half * tile : (half + 1) * tile], piece, way)
            going += piece_copies(stage, ids, piece, way, kept, sent, out_sems, piece)
    finish(qkv_copies)
    d_input[...] = (d_resid[...] + dot_nt(d_qkv[...], w_qkv[...])).astype(low)
    finish(going)


SMALL_ROWS = 16
SMALL_LINES = (("attn", 0), ("attn", 1), ("attn", 2), ("in", 0), ("in", 1), ("out", 2), ("out", 0), ("out", 1))


def small_sources(layer, own, others):
    found = []
    out_0, in_0, bias_0, out_1, in_1, bias_1, attn_1 = others
    refs = ({"attn": own, "in": in_0, "out": out_0}, {"attn": attn_1, "in": in_1, "out": out_1})
    width = own.shape[1]
    for of_layer, bias in zip(refs, (bias_0, bias_1)):
        found += [(of_layer[name], row, 0, width // 4) for name, row in SMALL_LINES]
        found += [(bias, 0, i * (width // 4), width) for i in range(4)]
    return found


def unpack_kernel(layer, slab, back, earlier, ids, near, far, *rest):
    outs = rest[earlier:-4]
    buffer, wide_buffer, in_sems, out_sems = rest[-4:]
    share, tile = wide_buffer.shape[1:]

    def fetch(piece, ref, index):
        return pltpu.make_async_copy(ref.at[index], buffer.at[piece], in_sems.at[piece])

    for piece in range(8):
        off = piece ^ ids[5]
        inner, outer = [(off >> WIDE_BIT[name]) & 1 for name in back]
        pl.when(outer == 0)(fetch(piece, near, (inner, piece >> 2)).start)
        pl.when(outer == 1)(fetch(piece, far, (inner, piece >> 2)).start)

    copies = []
    for piece in range(8):
        fetch(piece, near, (0, 0)).wait()
        wide_buffer[piece] = buffer[piece, :share].astype(f32)
        columns = pl.ds(piece * tile, tile)
        if slab == "in":
            target = outs[0].at[layer, :, columns]
        elif slab == "out":
            rows = pl.ds((piece // 2) * share, share)
            target = outs[0].at[layer, rows, pl.ds((piece % 2) * tile, tile)]
        elif piece < 6:
            target = outs[0].at[layer, :, columns]
        else:
            target = outs[1].at[layer, :, pl.ds((piece - 6) * tile, tile)]
        copies.append(pltpu.make_async_copy(wide_buffer.at[piece], target, out_sems.at[piece]))
        copies[-1].start()
    if slab == "attn" and layer == 0:
        for line in range(24):
            of_layer, which = line // 12, line % 12
            row = share + line % 3
            values = buffer[line // 3, row : row + 1, :share].astype(f32)
            if which < 8:
                outs[2 + which][of_layer : of_layer + 1, :] = values
            else:
                at = (which - 8) * share
                outs[10][of_layer : of_layer + 1, at : at + share] = values
    else:
        outs[-1][...] = jnp.zeros(outs[-1].shape, f32)
    finish(copies)


SMEM = pl.BlockSpec(memory_space=pltpu.SMEM)
VMEM = pl.BlockSpec(memory_space=pltpu.VMEM)
ANY = pl.BlockSpec(memory_space=pl.ANY)


def call(kernel, name, time, in_specs, out_specs, out_shape, scratch, args, aliases=()):
    return pl.pallas_call(
        kernel,
        name=name,
        in_specs=in_specs,
        out_specs=out_specs,
        out_shape=out_shape,
        scratch_shapes=scratch,
        input_output_aliases=dict(aliases),
        compiler_params=pltpu.CompilerParams(vmem_limit_bytes=VMEM_BYTES),
        cost_estimate=pl.CostEstimate(
            flops=int(time * 1.1e9), bytes_accessed=int(time * 3.6e6), transcendentals=0
        ),
    )(*args)


def shape(dims, kind):
    return jax.ShapeDtypeStruct(dims, kind)


def added(a, b):
    return (a.astype(f32) + b.astype(f32)).astype(low)


WAYS = ("zxy", "xyz", "yxz", "zyx", "xyz", "xyz")
BACKS = ("yz", "zy", "zy", "yz", "zy", "zy")
PLAN = (
    "out1", "in1", 0, 1, "attn1", "out0", "in0", 0, 1, "attn0", 1, 0, 2, 4, 1, 3, 0, 1, 2, 4, 0, 5, 2, 3, 4,
    0, 1, 2, 3, 2, 4, 5, 3, 0, 5, 4, 2, 5, 1, 3, 5, 4, 3, 2, 5, 4, 3, 5,
)
MODES = ("qz", "hz", "qy", "qz", "qy", "hy")
FORWARD = (
    "h0", "g0", "g2", "cut", "x0", "h2", "h3", "g3", "g1", "c0", "pack", "x2", "h5", "z0", "h4", "y0", "h1",
    "x3", "z2", "y2", "y3", "c3", "q0", "x5", "q2", "z3", "x1", "q3", "sm", "y5", "x4", "z1", "A", "y4", "d0",
    "z4", "c1", "attn1", "c2", "d3", "d1", "q4", "d2", "ffn1", "d4", "d5", "attn2", "ffn2",
)
TIMES = {
    "pack": 1, "attn1": 5, "ffn1": 13, "attn2": 0.3, "ffn2": 8,
    "out_bwd1": 3, "in_bwd1": 20.0, "attn_bwd1": 0.3, "out_bwd0": 2.0, "in_bwd0": 1.0, "attn_bwd0": 8.0,
}


class Order:
    def __init__(self, ids):
        self.ids = ids

    def wait(self, values):
        values, self.ids = lax.optimization_barrier((values, self.ids))
        return values


STEPS = {"x": ("narrow", 2), "y": ("wide", 1), "z": ("wide", 2)}


class Slab:
    def __init__(self, way, back, wide_count, kept, sent):
        self.kept = kept
        self.way, self.back = way, back
        self.rest = [1 << b for b in range(HALVINGS, wide_count.bit_length() - 1)]
        self.flying = swap(sent, "narrow", 1)
        self.stage = 0

    def step(self, order):
        received = order.wait(self.flying)
        stage, way = self.stage, self.way
        if stage < len(way):
            send = order.wait(added(self.kept[1], received[1]))
            self.kept = added(self.kept[0], received[0])
            self.flying = swap(send, *STEPS[way[stage]])
        elif stage < len(way) + 1 + len(self.back):
            if stage == len(way):
                piece = added(self.kept, received)
                for bit in self.rest[:-1]:
                    piece = added(piece, swap(piece, "wide", bit))
                self.kept = order.wait(piece)
                self.flying = swap(self.kept, "wide", self.rest[-1])
            else:
                if stage == len(way) + 1:
                    self.block = added(self.kept, received)[None]
                else:
                    self.block = jnp.concatenate([self.block, received], axis=0)
                self.block = order.wait(self.block)
                self.flying = swap(self.block, *STEPS[self.back[stage - len(way) - 1]])
        else:
            self.far = received
        self.stage += 1

    def ended(self):
        return self.stage == len(self.way) + len(self.back) + 2


def body(
    tables_in,
    cotangent,
    cell_ids,
    lengths,
    qkv_weight,
    q_bias,
    v_bias,
    o_weight,
    o_bias,
    norm1_gain,
    norm1_bias,
    in_weight,
    in_bias,
    out_weight,
    out_bias,
    norm2_gain,
    norm2_bias,
):
    tokens, width = tables_in.shape
    layers, share, ffn = in_weight.shape
    ffn_share = out_weight.shape[1]
    wide_count = lax.axis_size("wide")
    assert wide_count & (wide_count - 1) == 0 and wide_count > 1 << HALVINGS and lax.axis_size("narrow") == 4
    tile = ffn // 8
    me = lax.axis_index("narrow").astype(jnp.int32)
    wide_me = lax.axis_index("wide").astype(jnp.int32)
    y = wide_me & 1
    ids = jnp.stack([me, me ^ 1, me ^ 2, me ^ 3, y, wide_me & (2**HALVINGS - 1)])

    order = Order(ids)

    own = (qkv_weight, o_weight, in_weight, out_weight)
    parts = [None] * 6

    def cut(*slabs):
        outs = []
        for slab in slabs:
            weight = (qkv_weight, in_weight, out_weight)[slab % 3]
            columns = 4 * width if slab % 3 == 0 else weight.shape[2]
            outs.append(shape((weight.shape[1] // (4 if MODES[slab][0] == "q" else 2), columns), low))
        results = call(
            functools.partial(cut_kernel, slabs),
            "cut",
            1,
            [SMEM] + [ANY] * 4,
            [VMEM] * len(slabs),
            outs,
            [pltpu.SemaphoreType.DMA((8,))],
            (order.ids, *own),
        )
        for slab, part in zip(slabs, results):
            parts[slab] = part

    first_slab = [int(token[1]) for token in FORWARD if token[0] == "h"][0]
    cut(first_slab)
    near, diagonal, core = [None] * 6, [None] * 6, [None] * 4
    transfers = [{} for _ in range(6)]

    def joined(i, *names):
        near[i] = order.wait(jnp.concatenate([transfers[i][name] for name in names], axis=0))
        transfers[i]["d"] = swap(near[i], "narrow", 1)

    def weight_step(kind, i):
        moving, mode = transfers[i], MODES[i]
        if kind == "h":
            moving["x"] = swap(order.wait(parts[i]), "narrow", 2)
            return
        moving[kind] = order.wait(moving[kind])
        if kind == "x":
            for name, bit in (("y", 1), ("z", 2)):
                if mode[0] == "q" or mode[1] == name:
                    moving[name] = swap(moving["x"], "wide", bit)
        elif kind == "d":
            diagonal[i] = moving["d"]
        elif kind == "q":
            joined(i, "x", "y", "z", "q")
        elif mode[0] == "h":
            joined(i, "x", kind)
        elif mode[1] != kind:
            moving["q"] = swap(moving[kind], "wide", 1 if mode[1] == "y" else 2)

    def attn_weights(layer):
        return (qkv_weight, core[0], o_weight, core[1], near[3 * layer], diagonal[3 * layer])

    def in_weights(layer):
        return (in_weight, core[2], near[3 * layer + 1], diagonal[3 * layer + 1])

    def out_weights(layer):
        return (out_weight, core[3], near[3 * layer + 2], diagonal[3 * layer + 2])

    w_qkv = pltpu.VMEM((width, 3 * width), low)
    w_o = pltpu.VMEM((width, width), low)
    w_in = pltpu.VMEM((width, ffn), low)
    w_out = pltpu.VMEM((ffn, width), low)
    copy_sems = pltpu.SemaphoreType.DMA((20,))
    piece_sems = pltpu.SemaphoreType.DMA((16,))
    rows_f32 = shape((tokens, width), f32)
    rows_low = shape((tokens, width), low)
    column_f32 = shape((tokens, 1), f32)
    eight_f32 = shape((8, width), f32)

    def pieces(rows):
        return [shape((2, 2, 2, 2, rows, tile), low)] * 2

    def stage(rows):
        return pltpu.VMEM((2, 2, 2, 2, 2, rows, tile), low)

    def tie(outs, which):
        outs = list(outs)
        outs[which] = order.wait(outs[which])
        return outs

    def attn_forward(layer, x):
        x = order.wait(x)
        outs = call(
            functools.partial(attn_fwd_kernel, layer, MODES[3 * layer]),
            "attn_fwd",
            TIMES["attn%d" % (layer + 1)],
            [SMEM, SMEM] + [VMEM] * 3 + [ANY] * 6,
            [VMEM] * 5,
            [shape((tokens, 3 * width), low), shape((HEADS, tokens, tokens), low), rows_low, rows_f32, column_f32],
            [w_qkv, w_o, pltpu.VMEM((tokens, tokens), f32), copy_sems],
            (order.ids, lengths, x, cell_ids, small) + attn_weights(layer),
        )
        return tie(outs, 3)

    def ffn_forward(layer, unit_one):
        unit_one = order.wait(unit_one)
        outs = call(
            functools.partial(ffn_fwd_kernel, layer, MODES[3 * layer + 1 : 3 * layer + 3]),
            "ffn_fwd",
            TIMES["ffn%d" % (layer + 1)],
            [SMEM] + [VMEM] * 3 + [ANY] * 8,
            [ANY] * 2 + [VMEM] * 3,
            [shape((tokens, ffn), low), shape((tokens, ffn), f32), rows_f32, column_f32, rows_low],
            [
                w_in,
                w_out,
                pltpu.VMEM((tokens, width), low),
                pltpu.VMEM((tokens, ffn), low),
                pltpu.VMEM((tokens, ffn), f32),
                copy_sems,
                piece_sems,
            ],
            (order.ids, unit_one, full_in_bias, small) + in_weights(layer) + out_weights(layer),
        )
        return tie(outs, 4)

    def out_backward(layer, way, grad, unit_two, inverse_two, hidden):
        grad = order.wait(grad)
        outs = call(
            functools.partial(out_bwd_kernel, layer, way),
            "out_bwd",
            TIMES["out_bwd%d" % layer],
            [SMEM] + [VMEM] * 5,
            [VMEM] * 3 + [ANY] * 2,
            [rows_low, rows_f32, eight_f32] + pieces(share),
            [stage(share), pltpu.SemaphoreType.DMA((4,))],
            (order.ids, grad, unit_two, inverse_two, hidden, small),
        )
        return tie(outs, 0)

    def in_backward(layer, way, d_ffn, d_resid_two, unit_one, inverse_one, slope):
        d_ffn = order.wait(d_ffn)
        outs = call(
            functools.partial(in_bwd_kernel, layer, way, MODES[3 * layer + 1 : 3 * layer + 3]),
            "in_bwd",
            TIMES["in_bwd%d" % layer],
            [SMEM] + [VMEM] * 4 + [ANY] * 10,
            [VMEM] * 3 + [ANY] * 2,
            [rows_f32, eight_f32, shape((1, ffn), f32)] + pieces(share),
            [
                w_in,
                w_out,
                pltpu.VMEM((tokens, ffn), low),
                pltpu.VMEM((width, tokens), low),
                pltpu.VMEM((tokens, ffn), f32),
                pltpu.VMEM((tokens, width), f32),
                stage(share),
                copy_sems,
                piece_sems,
                pltpu.SemaphoreType.DMA((2,)),
            ],
            (order.ids, d_ffn, unit_one, inverse_one, small, d_resid_two, slope)
            + in_weights(layer)
            + out_weights(layer),
        )
        return tie(outs, 0)

    def ffn_backward(layer, ways, grad, attn_part, ffn_part):
        grad = order.wait(grad)
        hidden, slope, unit_two, inverse_two, _ = ffn_part
        outs = call(
            functools.partial(ffn_bwd_kernel, layer, ways, MODES[3 * layer + 1 : 3 * layer + 3]),
            "ffn_bwd",
            TIMES["in_bwd%d" % layer],
            [SMEM] + [VMEM] * 7 + [ANY] * 9,
            [VMEM] + [ANY] * 2 + [VMEM] * 3 + [ANY] * 2,
            [eight_f32] + pieces(share) + [rows_f32, eight_f32, shape((1, ffn), f32)] + pieces(share),
            [
                w_in,
                w_out,
                pltpu.VMEM((tokens, width), low),
                pltpu.VMEM((tokens, width), f32),
                pltpu.VMEM((tokens, ffn), low),
                pltpu.VMEM((width, tokens), low),
                pltpu.VMEM((tokens, ffn), f32),
                stage(share),
                stage(share),
                copy_sems,
                pltpu.SemaphoreType.DMA((4,)),
                piece_sems,
                pltpu.SemaphoreType.DMA((1,)),
            ],
            (order.ids, grad, unit_two, inverse_two, hidden, attn_part[3], attn_part[4], small, slope)
            + in_weights(layer)
            + out_weights(layer),
        )
        return tie(outs, 3)

    def attn_backward(layer, way, d_resid, x, qkv_rows, probs, context, small_others):
        d_resid = order.wait(d_resid)
        rows = share + (SMALL_ROWS if small_others else 0)
        outs = call(
            functools.partial(attn_bwd_kernel, layer, way, MODES[3 * layer]),
            "attn_bwd",
            TIMES["attn_bwd%d" % layer],
            [SMEM] + [VMEM] * 5 + [ANY] * 6 + [VMEM] * len(small_others),
            [VMEM] * 2 + [ANY] * 2,
            [rows_low, eight_f32] + pieces(rows),
            [
                w_qkv,
                w_o,
                pltpu.VMEM((tokens, width), low),
                pltpu.VMEM((tokens, width), low),
                pltpu.VMEM((tokens, 3 * width), low),
                pltpu.VMEM((width, tokens), low),
                stage(rows),
                copy_sems,
                piece_sems,
            ],
            (order.ids, d_resid, x, qkv_rows, probs, context) + attn_weights(layer) + tuple(small_others),
        )
        return tie(outs, 0)

    def unpack(layer, name, slab, earlier):
        dims = {
            "attn": [(layers, share, 3 * width), (layers, share, width)],
            "in": [(layers, share, ffn)],
            "out": [(layers, ffn_share, width)],
        }[name]
        last = name == "attn" and layer == 0
        extra = [(layers, share)] * 8 + [(layers, ffn_share)] if last else [(8, 128)]
        near, far = order.wait((slab.block, slab.far))
        rows = near.shape[2]
        outs = call(
            functools.partial(unpack_kernel, layer, name, slab.back, len(earlier)),
            "unpack",
            4,
            [SMEM] + [ANY] * (2 + len(earlier)),
            [ANY] * len(dims) + [VMEM] * len(extra),
            [shape(d, f32) for d in dims + extra],
            [
                pltpu.VMEM((8, rows, tile), low),
                pltpu.VMEM((8, share, tile), f32),
                pltpu.SemaphoreType.DMA((8,)),
                pltpu.SemaphoreType.DMA((8,)),
            ],
            (order.ids, near, far, *earlier),
            {3 + i: i for i in range(len(earlier))},
        )
        return tuple(tie(outs, 0))

    short = (q_bias, v_bias, o_bias, norm1_gain, norm1_bias, out_bias, norm2_gain, norm2_bias)
    inputs, attn_kept, ffn_kept = [tables_in], [], []
    for token in FORWARD:
        kind, i = (token[0], int(token[1])) if len(token) == 2 and token[1].isdigit() else (token, None)
        if token == "cut":
            cut(*[slab for slab in range(6) if slab != first_slab])
        elif kind == "g":
            core[i] = swap(order.wait(own[i]), "narrow", 1)
        elif kind == "c":
            core[i] = order.wait(core[i])
        elif i is not None:
            weight_step(kind, i)
        elif token == "pack":
            packed = call(
                pack_kernel,
                "pack",
                TIMES["pack"],
                [VMEM] * 9,
                VMEM,
                shape((layers, 12, share), f32),
                [],
                tuple(order.wait(short)) + (in_bias,),
            )
            packed = order.wait(packed)
            others = [lax.ppermute(packed, "narrow", [(j, j ^ away) for j in range(4)]) for away in (1, 2, 3)]
        elif token == "sm":
            others = order.wait(others)
        elif token == "A":
            small, full_in_bias = call(
                spread_kernel,
                "spread",
                1,
                [SMEM] + [VMEM] * 4,
                [VMEM] * 2,
                [shape((layers, 8, width), f32), shape((layers, 1, ffn), f32)],
                [],
                (order.ids, packed, *others),
            )
            small, full_in_bias = order.wait((small, full_in_bias))
        elif token[:-1] == "attn":
            attn_kept.append(attn_forward(int(token[-1]) - 1, inputs[-1]))
        else:
            ffn_kept.append(ffn_forward(int(token[-1]) - 1, attn_kept[-1][3]))
            inputs.append(ffn_kept[-1][4])
    mixed_out = inputs[-1]

    slabs = [None] * 6
    grad = cotangent
    small_out, small_in, small_attn, bias_grads = [None] * 2, [None] * 2, [None] * 2, [None] * 2
    unpacked = {"attn": (), "in": (), "out": ()}
    for action in PLAN:
        if isinstance(action, int):
            slab = slabs[action]
            slab.step(order)
            if slab.ended():
                name = ("out", "in", "attn")[action % 3]
                unpacked[name] = unpack(layers - 1 - action // 3, name, slab, unpacked[name][: 2 if name == "attn" else 1])
            continue
        name, layer = action[:-1], int(action[-1])
        which = 3 * (layers - 1 - layer) + ("out", "in", "attn").index(name)
        way = WAYS[which]
        qkv_rows, probs, context, unit_one, inverse_one = attn_kept[layer]
        hidden, slope, unit_two, inverse_two, _ = ffn_kept[layer]
        if name == "out" and layer == 0:
            continue
        if name == "in" and layer == 0:
            outs = ffn_backward(layer, WAYS[which - 1 : which + 1], grad, attn_kept[layer], ffn_kept[layer])
            small_out[layer], out_kept, out_sent, d_resid, small_in[layer], bias_grads[layer], kept, sent = outs
            slabs[which - 1] = Slab(WAYS[which - 1], BACKS[which - 1], wide_count, out_kept, out_sent)
        elif name == "out":
            d_ffn, d_resid_two, small_out[layer], kept, sent = out_backward(
                layer, way, grad, unit_two, inverse_two, hidden
            )
        elif name == "in":
            d_resid, small_in[layer], bias_grads[layer], kept, sent = in_backward(
                layer, way, d_ffn, d_resid_two, unit_one, inverse_one, slope
            )
        else:
            small_others = ()
            if layer == 0:
                small_others = (
                    small_out[0],
                    small_in[0],
                    bias_grads[0],
                    small_out[1],
                    small_in[1],
                    bias_grads[1],
                    small_attn[1],
                )
            grad, small_attn[layer], kept, sent = attn_backward(
                layer, way, d_resid, inputs[layer], qkv_rows, probs, context, small_others
            )
        slabs[which] = Slab(way, BACKS[which], wide_count, kept, sent)
    qkv_grad, o_grad, *vectors = unpacked["attn"]
    in_grad, out_grad = unpacked["in"][0], unpacked["out"][0]
    return (
        mixed_out,
        grad,
        qkv_grad,
        vectors[0],
        vectors[1],
        o_grad,
        vectors[2],
        vectors[3],
        vectors[4],
        in_grad,
        vectors[8],
        out_grad,
        vectors[5],
        vectors[6],
        vectors[7],
    )


def solution(mesh):
    by_table = P(("wide", "narrow"), None)
    matrix = P(None, "narrow", None)
    vector = P(None, "narrow")
    return jax.shard_map(
        body,
        mesh=mesh,
        in_specs=(
            by_table,
            by_table,
            by_table,
            P(("wide", "narrow")),
            matrix,
            vector,
            vector,
            matrix,
            vector,
            vector,
            vector,
            matrix,
            vector,
            matrix,
            vector,
            vector,
            vector,
        ),
        out_specs=(
            by_table,
            by_table,
            matrix,
            vector,
            vector,
            matrix,
            vector,
            vector,
            vector,
            matrix,
            vector,
            matrix,
            vector,
            vector,
            vector,
        ),
        check_vma=False,
    )
```
